32 devices in a mesh: dp: 4 (over x, core), ctx: 8 (over z, y).
Axes of the slice: x: 2, y: 2, z: 4, core: 2. Of those that a mesh axis runs over, the one named last changes fastest.
Arguments:
- tokens: bfloat16 [4, 1024, 512], P('dp', 'ctx'), may hold values from -6 to 6
- mixer_gain: float32 [512], P(('dp', 'ctx')), may hold values from 0.1 to 1.9
- in_proj: float32 [512, 2048], P(('dp', 'ctx')), may hold values from -0.25 to 0.25
- conv_weight: float32 [1024, 4], P(('dp', 'ctx')), may hold values from -3 to 3
- conv_bias: float32 [1024], P(('dp', 'ctx')), may hold values from -3 to 3
- x_proj: float32 [1024, 64], P(('dp', 'ctx')), may hold values from -0.1875 to 0.1875
- dt_proj: float32 [32, 1024], P(None, ('dp', 'ctx')), may hold values from -1 to 1
- dt_bias: float32 [1024], P(('dp', 'ctx')), may hold values from -6 to 0
- a_log: float32 [1024, 16], P(('dp', 'ctx')), may hold values from -4 to 1
- d_skip: float32 [1024], P(('dp', 'ctx')), may hold values from 0.5 to 1.5
- out_proj: float32 [1024, 512], P(('dp', 'ctx')), may hold values from -0.75 to 0.75
- attn_gain: float32 [512], P(('dp', 'ctx')), may hold values from 0.1 to 1.9
- w_query: float32 [512, 512], P(('dp', 'ctx')), may hold values from -0.375 to 0.375
- w_key: float32 [512, 512], P(('dp', 'ctx')), may hold values from -0.375 to 0.375
- w_value: float32 [512, 512], P(('dp', 'ctx')), may hold values from -0.25 to 0.25
- w_output: float32 [512, 512], P(('dp', 'ctx')), may hold values from -2 to 2
- cotangent: bfloat16 [4, 1024, 512], P('dp', 'ctx'), may hold values from -6 to 6
Outputs:
- result: bfloat16 [4, 1024, 512], P('dp', 'ctx')
- grad_tokens: bfloat16 [4, 1024, 512], P('dp', 'ctx')
- grad_mixer_gain: float32 [512], P(('dp', 'ctx'))
- grad_in_proj: float32 [512, 2048], P(('dp', 'ctx'))
- grad_conv_weight: float32 [1024, 4], P(('dp', 'ctx'))
- grad_conv_bias: float32 [1024], P(('dp', 'ctx'))
- grad_x_proj: float32 [1024, 64], P(('dp', 'ctx'))
- grad_dt_proj: float32 [32, 1024], P(None, ('dp', 'ctx'))
- grad_dt_bias: float32 [1024], P(('dp', 'ctx'))
- grad_a_log: float32 [1024, 16], P(('dp', 'ctx'))
- grad_d_skip: float32 [1024], P(('dp', 'ctx'))
- grad_out_proj: float32 [1024, 512], P(('dp', 'ctx'))
- grad_attn_gain: float32 [512], P(('dp', 'ctx'))
- grad_w_query: float32 [512, 512], P(('dp', 'ctx'))
- grad_w_key: float32 [512, 512], P(('dp', 'ctx'))
- grad_w_value: float32 [512, 512], P(('dp', 'ctx'))
- grad_w_output: float32 [512, 512], P(('dp', 'ctx'))
The draws below stay inside these ranges and needn't reach their ends.
All inputs are finite; a program needn't handle non-finite values.
Results may differ from the reference program's by a relative error of at most 0.04.
The reference program's roundings to bfloat16 on the way count: a program that leaves them out, or rounds other values in their place, can miss the bound.
Values may be sent and summed in bfloat16 or wider, within the bound.
No kernel may reach another device: no remote copies, remote signals or barrier semaphores. Data moves between devices by JAX's collectives and lax.ppermute only.
A program may use at most 192 MiB of HBM per device.

```python
import math
import jax
import jax.numpy as jnp
from jax import lax

D = 512
E = 1024
NS = 16
RANK = 32
KW = 4
HEADS = 8
HDIM = 64
SEQS = 4
LEN = 1024


def block_scale(rng, dims, shards, least, top_value):
    gain = 1.0
    for axis_at, parts in shards:
        draws = jax.random.uniform(jax.random.fold_in(jax.random.fold_in(rng, 6), axis_at), (parts,), jnp.float32, least / len(shards), top_value / len(shards))
        gain = gain * jnp.repeat(jnp.exp(draws), dims[axis_at] // parts).reshape((-1,) + (1,) * (len(dims) - 1 - axis_at))
    return gain


def scatter_about(stream_key, dims, scale, limit, cuts=(), dtype=jnp.bfloat16):
    loudness = block_scale(stream_key, dims, cuts, -0.22, 0.18) if cuts else 1.0
    values = jax.random.normal(stream_key, dims, jnp.float32) * scale * loudness
    return jnp.minimum(jnp.maximum(values, -limit), limit).astype(dtype)


def setup_inputs(seed: int = 0) -> dict:
    key_list = jax.random.split(jax.random.key(seed), 18)
    tokens = scatter_about(key_list[0], (SEQS, LEN, D), 1.0, 6.0, ((0, 4), (1, 8)))
    mixer_gain = jnp.clip(1.0 + 0.18 * jax.random.normal(key_list[1], (D,), jnp.float32), 0.1, 1.9)
    in_proj = scatter_about(key_list[2], (D, 2 * E), D ** -0.5, 0.25, ((0, 32),), jnp.float32)
    conv_weight = scatter_about(key_list[3], (E, KW), KW ** -0.5, 3.0, ((0, 32),), jnp.float32)
    conv_bias = scatter_about(key_list[4], (E,), 0.5, 3.0, ((0, 32),), jnp.float32)
    x_proj = scatter_about(key_list[5], (E, RANK + 2 * NS), E ** -0.5, 0.1875, ((0, 32),), jnp.float32)
    dt_proj = scatter_about(key_list[6], (RANK, E), RANK ** -0.5, 1.0, ((1, 32),), jnp.float32)
    dt_bias = jnp.clip(-6.0 + 6.0 * jax.random.uniform(key_list[7], (E,), jnp.float32) ** block_scale(key_list[7], (E,), ((0, 32),), -0.2, 0.2), -6.0, 0.0)
    a_log = jnp.clip(-4.0 + 5.0 * jax.random.uniform(key_list[8], (E, NS), jnp.float32) ** block_scale(key_list[8], (E, NS), ((0, 32),), -0.2, 0.2), -4.0, 1.0)
    d_skip = jnp.clip(0.5 + 1.0 * jax.random.uniform(key_list[9], (E,), jnp.float32) ** block_scale(key_list[9], (E,), ((0, 32),), -0.2, 0.2), 0.5, 1.5)
    out_proj = scatter_about(key_list[10], (E, D), (E // 16) ** -0.5, 0.75, ((0, 32),), jnp.float32)
    attn_gain = jnp.clip(1.0 + 0.18 * jax.random.normal(key_list[11], (D,), jnp.float32), 0.1, 1.9)
    w_query = scatter_about(key_list[12], (D, D), (D // 2) ** -0.5, 0.375, ((0, 32),), jnp.float32)
    w_key = scatter_about(key_list[13], (D, D), (D // 2) ** -0.5, 0.375, ((0, 32),), jnp.float32)
    w_value = scatter_about(key_list[14], (D, D), D ** -0.5, 0.25, ((0, 32),), jnp.float32)
    w_output = scatter_about(key_list[15], (D, D), (D // 64) ** -0.5, 2.0, ((0, 32),), jnp.float32)
    cotangent = scatter_about(key_list[16], (SEQS, LEN, D), 1.0, 6.0, ((0, 4), (1, 8)))
    return {"tokens": tokens, "mixer_gain": mixer_gain, "in_proj": in_proj, "conv_weight": conv_weight, "conv_bias": conv_bias, "x_proj": x_proj, "dt_proj": dt_proj, "dt_bias": dt_bias, "a_log": a_log, "d_skip": d_skip, "out_proj": out_proj, "attn_gain": attn_gain, "w_query": w_query, "w_key": w_key, "w_value": w_value, "w_output": w_output, "cotangent": cotangent}


@jax.custom_vjp
def low(v):
    return lax.optimization_barrier(v.astype(jnp.bfloat16)).astype(jnp.float32)

@jax.custom_vjp
def low_back(v):
    return v

def low_keep(v):
    return (low(v), None)

def low_pass(kept, grad):
    return (grad,)

def back_keep(v):
    return (v, None)

def back_low(kept, grad):
    return (low(grad),)
low.defvjp(low_keep, low_pass)
low_back.defvjp(back_keep, back_low)
epsilon = 1e-05
masked_score = -1e+30

def hdot(left, right):
    return jnp.dot(left, right, precision=lax.Precision.HIGHEST)

def rms_scale(values, scale_gain):
    return values * lax.rsqrt(lax.optimization_barrier(jnp.mean(values * values, axis=-1, keepdims=True)) + epsilon) * scale_gain

def selective_scan(step_size, act_in, b_rows, c_rows, a_matrix):
    length = step_size.shape[0]
    block_rows = math.gcd(length, 64)

    def advance(carried, per_step):
        size_t, input_t, b_row, c_row = per_step
        carried = jnp.exp(size_t[None, :] * a_matrix) * carried + (size_t * input_t)[None, :] * b_row[:, None]
        return (carried, lax.optimization_barrier(jnp.sum(carried * c_row[:, None], axis=0)))

    def block_scan(carried, stacked):
        return lax.scan(advance, carried, stacked)
    stacked = tuple((array_in.reshape((length // block_rows, block_rows) + array_in.shape[1:]) for array_in in (step_size, act_in, b_rows, c_rows)))
    start_state = jnp.zeros(a_matrix.shape, jnp.float32)
    _, outputs = lax.scan(jax.checkpoint(block_scan), start_state, stacked)
    return outputs.reshape(step_size.shape)

def attention(queries, key_rows, value_rows):
    length = queries.shape[0]
    block_rows = math.gcd(length, 512)
    query_heads = queries.reshape(length // block_rows, block_rows, HEADS, HDIM)
    key_heads = key_rows.reshape(length, HEADS, HDIM)
    value_heads = value_rows.reshape(length, HEADS, HDIM)
    key_pos = jnp.arange(length)

    def one_block(per_block):
        query_block, first_row = per_block
        scores = low_back(jnp.einsum('qhd,khd->hqk', query_block, key_heads, precision=lax.Precision.HIGHEST) * HDIM ** (-0.5))
        query_pos = first_row + jnp.arange(block_rows)
        allowed = key_pos[None, None, :] <= query_pos[None, :, None]
        scores = jnp.where(allowed, scores, masked_score)
        top_score = lax.optimization_barrier(jnp.max(scores, axis=-1, keepdims=True))
        expo = jnp.where(allowed, jnp.exp(scores - top_score), 0.0)
        softmax_p = expo / lax.optimization_barrier(jnp.sum(expo, axis=-1, keepdims=True))
        output_block = jnp.einsum('hqk,khd->qhd', low(softmax_p), value_heads, precision=lax.Precision.HIGHEST)
        return output_block.reshape(block_rows, HEADS * HDIM)
    firsts = jnp.arange(length // block_rows) * block_rows
    return lax.map(jax.checkpoint(one_block), (query_heads, firsts)).reshape(length, HEADS * HDIM)

def layer(tokens_seq, weights):
    mixer_gain, in_proj, conv_weight, conv_bias, x_proj, dt_proj, dt_bias, a_log, d_skip, out_proj, attn_gain, w_query, w_key, w_value, w_output = weights
    length = tokens_seq.shape[0]
    normed_one = low(rms_scale(tokens_seq, mixer_gain))
    mixed_in = low_back(hdot(normed_one, in_proj))
    u_pre = mixed_in[:, :E]
    gate_z = mixed_in[:, E:]
    padded = jnp.concatenate([jnp.zeros((KW - 1, E), jnp.float32), u_pre], axis=0)
    conv_out = conv_bias + sum((padded[tap_k:tap_k + length] * conv_weight[:, tap_k] for tap_k in range(KW)))
    act_u = low(jax.nn.silu(conv_out))
    projected = low_back(hdot(act_u, x_proj))
    dt_low = low(projected[:, :RANK])
    b_rows = projected[:, RANK:RANK + NS]
    c_rows = projected[:, RANK + NS:]
    step_size = jax.nn.softplus(low_back(hdot(dt_low, dt_proj)) + dt_bias)
    a_matrix = -jnp.exp(a_log).T
    mamba_y = selective_scan(step_size, act_u, b_rows, c_rows, a_matrix) + d_skip * act_u
    gated = low(mamba_y * jax.nn.silu(gate_z))
    middle = tokens_seq + low_back(hdot(gated, out_proj))
    normed_two = low(rms_scale(middle, attn_gain))
    queries = low(low_back(hdot(normed_two, w_query)))
    key_rows = low(low_back(hdot(normed_two, w_key)))
    value_rows = low(low_back(hdot(normed_two, w_value)))
    attended = low(low_back(attention(queries, key_rows, value_rows)))
    return middle + low_back(hdot(attended, w_output))

def reference(tokens, mixer_gain, in_proj, conv_weight, conv_bias, x_proj, dt_proj, dt_bias, a_log, d_skip, out_proj, attn_gain, w_query, w_key, w_value, w_output, cotangent):
    params = (mixer_gain, in_proj, conv_weight, conv_bias, x_proj, dt_proj, dt_bias, a_log, d_skip, out_proj, attn_gain, w_query, w_key, w_value, w_output)

    def forward(inputs, weights):
        lowered = tuple((low(master) for master in weights))

        def one_seq(sequence):
            return layer(sequence, lowered)
        return lax.map(jax.checkpoint(one_seq), inputs)
    outcome, pullback = jax.vjp(forward, tokens.astype(jnp.float32), params)
    grad_in, gradients = pullback(cotangent.astype(jnp.float32))
    return (outcome.astype(jnp.bfloat16), grad_in.astype(jnp.bfloat16), gradients[0], gradients[1], gradients[2], gradients[3], gradients[4], gradients[5], gradients[6], gradients[7], gradients[8], gradients[9], gradients[10], gradients[11], gradients[12], gradients[13], gradients[14])
```

```python
import functools

import jax
import jax.numpy as jnp
from jax import lax
from jax.experimental import pallas as pl
from jax.experimental.pallas import tpu as pltpu
from jax.sharding import PartitionSpec as P

D = 512
E = 1024
NS = 16
RANK = 32
KW = 4
HEADS = 8
HDIM = 64
LG = 8
HALO = 16
BLOCKS = 32
ALL = ("dp", "ctx")
EPS = 1e-05
LOG2E = 1.4426950408889634
LN2 = 0.6931471805599453
F32 = jnp.float32
BF16 = jnp.bfloat16
VM = pl.BlockSpec(memory_space=pltpu.VMEM)

Z_MASKS = (0, 2, 4, 6)
XY_MASKS = (0, 1, 16, 17)
CORE = 8
HALF_MASKS = tuple(xy | zz for xy in XY_MASKS for zz in Z_MASKS)
FULL_MASKS = HALF_MASKS + tuple(mask | CORE for mask in HALF_MASKS)
CHUNK_MASKS = tuple((c & 1) | (8 if c & 2 else 0) | (16 if c & 4 else 0) for c in range(8))

ROW_X = 0
ROW_DT = 64
ROW_A = 96
ROW_CW = 112
ROW_CB = 116
ROW_DB = 117
ROW_SK = 118
ROW_G1 = 119
ROW_G2 = 120
SMALL_ROWS = 128


def call(kernel, outs, scratch=(), limit=40, **kwargs):
    return pl.pallas_call(
        kernel,
        out_shape=[jax.ShapeDtypeStruct(shape, dtype) for shape, dtype in outs],
        out_specs=[VM] * len(outs),
        scratch_shapes=list(scratch),
        compiler_params=pltpu.CompilerParams(vmem_limit_bytes=limit * 2**20),
        **kwargs,
    )


def run(kernel, ins, outs, scratch=(), limit=40):
    return call(kernel, outs, scratch, limit, in_specs=[VM] * len(ins))(*ins)


def nn(left, right):
    return lax.dot_general(left, right, (((1,), (0,)), ((), ())), preferred_element_type=F32)


def nt(left, right):
    return lax.dot_general(left, right, (((1,), (1,)), ((), ())), preferred_element_type=F32)


def tn(left, right):
    return lax.dot_general(left, right, (((0,), (0,)), ((), ())), preferred_element_type=F32)


def sigmoid(value):
    return 1.0 / (1.0 + jnp.exp(-value))


class Plan:
    def __init__(self, mesh):
        self.dp, self.ctx = mesh.shape["dp"], mesh.shape["ctx"]
        self.fast = (self.dp, self.ctx) == (4, 8)
        self.chunks = self.ctx
        if self.fast:
            self.grad_masks = (FULL_MASKS[:16], FULL_MASKS[16:])
        else:
            self.grad_masks = (tuple(range(BLOCKS)),)

    def place(self, seq, chunk):
        return CHUNK_MASKS[chunk] | (seq << 1)

    def me(self):
        if self.fast:
            return lax.axis_index("dp") * 8 + lax.axis_index("ctx")
        return 0

    def chunk(self):
        if self.fast:
            lin = lax.axis_index("dp") * 8 + lax.axis_index("ctx")
            return (lin & 1) + ((lin >> 3) & 1) * 2 + ((lin >> 4) & 1) * 4
        return lax.axis_index("ctx")

    def order(self):
        return self.chunk() if self.fast else 0


def send(value, mask):
    return lax.ppermute(value, ALL, [(i, i ^ mask) for i in range(32)])


def fill(target, pieces, masks, me, rows, row_in, first_col):
    at = 0
    for piece in pieces:
        for k in range(piece.shape[0] // rows):
            block = me ^ masks[at]
            target[pl.ds(pl.multiple_of(block * row_in[1], 16), row_in[1]), first_col : first_col + piece.shape[1]] = (
                piece[k * rows + row_in[0] : k * rows + row_in[0] + row_in[1], :]
            )
            at += 1


def spread(target, source):
    count = source.shape[0]
    for s in range(LG):
        target[pl.ds(s, count, stride=LG), :] = source[:, s * 128 : (s + 1) * 128]


def gathered(source, count):
    return jnp.concatenate([source[pl.ds(s, count, stride=LG), :] for s in range(LG)], axis=1)


def broadcast_rows(target, proj, first):
    for n in range(NS):
        target[n] = jnp.broadcast_to(proj[:, first + n : first + n + 1], target.shape[1:])


def at8(ref, index):
    return ref[pl.ds(pl.multiple_of(index * 8, 8), 8), :]


def front_kernel(plan, nu, nz, masks, *refs):
    tok, halo, pm, gain = refs[:4]
    u_pieces, z_pieces = refs[4 : 4 + nu], refs[4 + nu : 4 + nu + nz]
    (normed, u_out, z_out, conv_out, act_out, proj_out, sig_out, dt3, au3, a3, state, weight, bx) = refs[4 + nu + nz :]
    me = plan.me()
    fill(weight, u_pieces, masks, me, 16, (0, 16), 0)
    fill(weight, z_pieces, masks, me, 16, (0, 16), E)
    tokens = tok.shape[0]
    x = jnp.concatenate([halo[...].astype(F32), tok[...].astype(F32)], axis=0)
    r = lax.rsqrt(jnp.mean(x * x, axis=-1, keepdims=True) + EPS)
    low = (x * r * gain[...]).astype(BF16)
    normed[...] = low
    u_out[...] = nn(low, weight[:, :E])
    z_out[...] = nn(low[HALO:], weight[:, E:])
    conv = pm[ROW_CB : ROW_CB + 1, :]
    for k in range(KW):
        conv = conv + pm[ROW_CW + k : ROW_CW + k + 1, :] * u_out[HALO - 3 + k : HALO - 3 + k + tokens, :]
    conv_out[...] = conv
    act = (conv * sigmoid(conv)).astype(BF16)
    act_out[...] = act
    proj = nt(act, pm[ROW_X : ROW_X + 64, :].astype(BF16))
    proj_out[:, :64] = proj
    proj_out[:, 64:] = jnp.zeros((tokens, 64), F32)
    pre = nn(proj[:, :RANK].astype(BF16), pm[ROW_DT : ROW_DT + RANK, :].astype(BF16)) + pm[ROW_DB : ROW_DB + 1, :]
    sig_out[...] = sigmoid(pre)
    step = jnp.maximum(pre, 0.0) + jnp.log1p(jnp.exp(-jnp.abs(pre)))
    spread(dt3, step)
    spread(au3, act.astype(F32))
    spread(a3, -LOG2E * jnp.exp(pm[ROW_A : ROW_A + NS, :]))
    broadcast_rows(bx, proj, RANK)
    decay = [a3[8 * n : 8 * n + 8, :] for n in range(NS)]

    def advance(t, carried):
        held, total = carried
        size = at8(dt3, t)
        drive = size * at8(au3, t)
        held = tuple(
            jnp.exp2(size * decay[n]) * held[n] + drive * bx[n, pl.ds(t, 1), :] for n in range(NS)
        )
        return held, total + size

    zero = jnp.zeros((8, 128), F32)
    held, total = lax.fori_loop(0, tokens, advance, ((zero,) * NS, zero), unroll=4)
    for n in range(0, NS, 2):
        state[8 * n : 8 * n + 16, :] = jnp.concatenate([held[n], held[n + 1]], axis=0).astype(BF16)
    state[128:144, :] = jnp.concatenate([total, zero], axis=0).astype(BF16)


def load_states(target, pieces):
    at = 0
    for piece in pieces:
        rows = piece.shape[0]
        target[at : at + rows, :] = piece[...].astype(F32)
        at += rows


def mid_kernel(plan, ns, nb, masks, *refs):
    tok, dt3, au3, proj, a3, z_in, pm, gain, cot = refs[:9]
    states = refs[9 : 9 + ns]
    one, two = refs[9 + ns : 9 + ns + nb], refs[9 + ns + nb : 9 + ns + 2 * nb]
    pay, mamba, gated_out, middle_out, entry, states_f, w_out, w_q, w_k, w_v, w_o, y3, bx, cx = refs[9 + ns + 2 * nb :]
    tokens = tok.shape[0]
    fill_attention(plan, one, two, masks, w_out, w_q, w_k, w_v, w_o)
    load_states(states_f, states)
    broadcast_rows(bx, proj, RANK)
    broadcast_rows(cx, proj, RANK + NS)
    decay = [a3[8 * n : 8 * n + 8, :] for n in range(NS)]
    zero = jnp.zeros((8, 128), F32)
    order = plan.order()

    def combine(j, held):
        base = (j ^ order) * 144
        total = states_f[pl.ds(pl.multiple_of(base + 128, 8), 8), :]
        return tuple(
            jnp.exp2(total * decay[n]) * held[n] + states_f[pl.ds(pl.multiple_of(base + 8 * n, 8), 8), :]
            for n in range(NS)
        )

    held = lax.fori_loop(0, plan.chunk(), combine, (zero,) * NS)
    for n in range(NS):
        entry[8 * n : 8 * n + 8, :] = held[n]

    def advance(t, held):
        size = at8(dt3, t)
        drive = size * at8(au3, t)
        held = tuple(
            jnp.exp2(size * decay[n]) * held[n] + drive * bx[n, pl.ds(t, 1), :] for n in range(NS)
        )
        y = held[0] * cx[0, pl.ds(t, 1), :]
        for n in range(1, NS):
            y = y + held[n] * cx[n, pl.ds(t, 1), :]
        y3[pl.ds(pl.multiple_of(t * 8, 8), 8), :] = y
        return held

    lax.fori_loop(0, tokens, advance, held, unroll=4)
    act = gathered(au3, tokens)
    y = gathered(y3, tokens) + pm[ROW_SK : ROW_SK + 1, :] * act
    mamba[...] = y
    z = z_in[...]
    gated = (y * (z * sigmoid(z))).astype(BF16)
    gated_out[...] = gated
    middle = tok[...].astype(F32) + nn(gated, w_out[...])
    middle_out[...] = middle
    r = lax.rsqrt(jnp.mean(middle * middle, axis=-1, keepdims=True) + EPS)
    low = (middle * r * gain[...]).astype(BF16)
    quads = (
        nn(low, w_q[...]).astype(BF16),
        nn(low, w_k[...]).astype(BF16),
        nn(low, w_v[...]).astype(BF16),
        nt(cot[...], w_o[...]).astype(BF16),
    )
    for h in range(HEADS):
        for i, part in enumerate(quads):
            pay[h * tokens : (h + 1) * tokens, i * HDIM : (i + 1) * HDIM] = part[:, h * HDIM : (h + 1) * HDIM]


def fill_attention(plan, one, two, masks, w_out, w_q, w_k, w_v, w_o):
    me = plan.me()
    fill(w_out, one, masks, me, 48, (0, 32), 0)
    fill(w_q, one, masks, me, 48, (32, 16), 0)
    fill(w_k, two, masks, me, 48, (0, 16), 0)
    fill(w_v, two, masks, me, 48, (16, 16), 0)
    fill(w_o, two, masks, me, 48, (32, 16), 0)


def attention_kernel(pay, back, q_s, k_s, v_s, g_s, kt, vt, dk, dv):
    length = pay.shape[0]
    rows = 256
    q_s[...] = pay[:, :HDIM]
    k_s[...] = pay[:, HDIM : 2 * HDIM]
    v_s[...] = pay[:, 2 * HDIM : 3 * HDIM]
    g_s[...] = pay[:, 3 * HDIM :]
    kt[...] = k_s[...].T
    vt[...] = v_s[...].T
    dk[...] = jnp.zeros_like(dk)
    dv[...] = jnp.zeros_like(dv)
    scale = HDIM**-0.5
    key_at = lax.broadcasted_iota(jnp.int32, (rows, rows), 0)
    query_at = lax.broadcasted_iota(jnp.int32, (rows, rows), 1)
    for i in range(length // rows):
        first, last = i * rows, (i + 1) * rows
        query = q_s[first:last, :]
        grad = g_s[first:last, :]
        scores = nt(k_s[:last, :], query) * scale
        diagonal = jnp.where(key_at <= query_at, scores[first:, :], -1e30)
        scores = diagonal if i == 0 else jnp.concatenate([scores[:first, :], diagonal], axis=0)
        expo = jnp.exp(scores - jnp.max(scores, axis=0, keepdims=True))
        soft = expo * (1.0 / jnp.sum(expo, axis=0, keepdims=True))
        soft_low = soft.astype(BF16)
        grad_p = nt(v_s[:last, :], grad)
        dot = jnp.sum(soft * grad_p, axis=0, keepdims=True)
        grad_s = (soft * (grad_p - dot)).astype(BF16)
        raw = nn(vt[:, :last], soft_low)
        grad_q = nn(kt[:, :last], grad_s) * scale
        back[first:last, :HDIM] = raw.T.astype(BF16)
        back[first:last, HDIM : 2 * HDIM] = grad_q.T.astype(BF16)
        dk[:last, :] += nn(grad_s, query)
        dv[:last, :] += nn(soft_low, grad)
    back[:, 2 * HDIM : 3 * HDIM] = (dk[...] * scale).astype(BF16)
    back[:, 3 * HDIM :] = dv[...].astype(BF16)


def states_kernel(dt3, au3, proj, a3, entry, all_states, bx):
    tokens = dt3.shape[0] // LG
    broadcast_rows(bx, proj, RANK)
    decay = [a3[8 * n : 8 * n + 8, :] for n in range(NS)]

    def advance(t, held):
        size = at8(dt3, t)
        drive = size * at8(au3, t)
        base = pl.multiple_of(t * 128, 128)
        fresh = []
        for n in range(NS):
            all_states[pl.ds(base + 8 * n, 8), :] = held[n]
            fresh.append(jnp.exp2(size * decay[n]) * held[n] + drive * bx[n, pl.ds(t, 1), :])
        return tuple(fresh)

    held = tuple(entry[8 * n : 8 * n + 8, :] for n in range(NS))
    held = lax.fori_loop(0, tokens, advance, held, unroll=4)
    for n in range(NS):
        all_states[tokens * 128 + 8 * n : tokens * 128 + 8 * n + 8, :] = held[n]


def turn_kernel(plan, nb, masks, *refs):
    got, middle, cot, gain, z_in, mamba, dt3, proj, a3 = refs[:9]
    one, two = refs[9 : 9 + nb], refs[9 + nb : 9 + 2 * nb]
    (att, gq, gk, gv, grad_middle, mix, gz, gy3, state, gain_grad, w_out, w_q, w_k, w_v, w_o, cx) = refs[9 + 2 * nb :]
    tokens = middle.shape[0]
    fill_attention(plan, one, two, masks, w_out, w_q, w_k, w_v, w_o)
    broadcast_rows(cx, proj, RANK + NS)
    for h in range(HEADS):
        for i, part in enumerate((att, gq, gk, gv)):
            part[:, h * HDIM : (h + 1) * HDIM] = got[h * tokens : (h + 1) * tokens, i * HDIM : (i + 1) * HDIM]
    grad_n = nt(gq[...], w_q[...]) + nt(gk[...], w_k[...]) + nt(gv[...], w_v[...])
    mid = middle[...]
    r = lax.rsqrt(jnp.mean(mid * mid, axis=-1, keepdims=True) + EPS)
    gain_grad[...] = jnp.sum(grad_n * mid * r, axis=0, keepdims=True)
    q = grad_n * gain[...]
    gm = cot[...].astype(F32) + r * q - mid * (r * r * r) * jnp.mean(q * mid, axis=-1, keepdims=True)
    grad_middle[...] = gm
    low = gm.astype(BF16)
    mix[...] = low
    grad_gated = nt(low, w_out[...])
    z = z_in[...]
    s = sigmoid(z)
    spread(gy3, grad_gated * (z * s))
    gz[...] = (grad_gated * mamba[...] * (s * (1.0 + z * (1.0 - s)))).astype(BF16)
    decay = [a3[8 * n : 8 * n + 8, :] for n in range(NS)]

    def retreat(i, carried):
        t = tokens - 1 - i
        size = at8(dt3, t)
        grad = at8(gy3, t)
        return tuple(
            jnp.exp2(size * decay[n]) * (carried[n] + grad * cx[n, pl.ds(t, 1), :]) for n in range(NS)
        )

    zero = jnp.zeros((8, 128), F32)
    carried = lax.fori_loop(0, tokens, retreat, (zero,) * NS, unroll=4)
    for n in range(0, NS, 2):
        state[8 * n : 8 * n + 16, :] = jnp.concatenate([carried[n], carried[n + 1]], axis=0).astype(BF16)


def pack_blocks(plan, outs, source, rows, out_rows, first):
    me = plan.me()
    for out, masks in zip(outs, plan.grad_masks):
        for k, mask in enumerate(masks):
            block = me ^ mask
            out[k * out_rows + first : k * out_rows + first + rows, :] = source[
                pl.ds(pl.multiple_of(block * rows, 16), rows), :
            ].astype(BF16)


def weights_kernel(plan, no, nb, masks, *refs):
    att, gq, gk, gv, mix, gated, middle, gain, cot = refs[:9]
    two = refs[9 : 9 + nb]
    refs = refs[9 + nb :]
    result, one_out, two_out = refs[0], refs[1 : 1 + no], refs[1 + no : 1 + 2 * no]
    w_o, small, large = refs[1 + 2 * no :]
    fill(w_o, two, masks, plan.me(), 48, (32, 16), 0)
    mid = middle[...]
    result[...] = (mid + nn(att[...], w_o[...])).astype(BF16)
    r = lax.rsqrt(jnp.mean(mid * mid, axis=-1, keepdims=True) + EPS)
    low = (mid * r * gain[...]).astype(BF16)
    large[...] = tn(gated[...], mix[...])
    pack_blocks(plan, one_out, large, 32, 48, 0)
    small[...] = tn(low, gq[...])
    pack_blocks(plan, one_out, small, 16, 48, 32)
    small[...] = tn(low, gk[...])
    pack_blocks(plan, two_out, small, 16, 48, 0)
    small[...] = tn(low, gv[...])
    pack_blocks(plan, two_out, small, 16, 48, 16)
    small[...] = tn(att[...], cot[...])
    pack_blocks(plan, two_out, small, 16, 48, 32)


def gate_weights_kernel(plan, no, *refs):
    normed, gz = refs[:2]
    outs = refs[2 : 2 + no]
    (large,) = refs[2 + no :]
    large[...] = tn(normed[HALO:, :], gz[...])
    pack_blocks(plan, outs, large, 16, 16, 0)


def back_kernel(plan, ns, no, *refs):
    dt3, au3, gy3, a3, proj, pm, all_states, sig, act, conv_in, u_in, normed = refs[:12]
    states, laters = refs[12 : 12 + ns], refs[12 + ns : 12 + 2 * ns]
    refs = refs[12 + 2 * ns :]
    u_blocks = refs[:no]
    small_grads, gu_out = refs[no : no + 2]
    (states_f, laters_f, bx, cx, grads, gs3, ga3, gal, skip3, low_rank, padded, large) = refs[no + 2 :]
    tokens = dt3.shape[0] // LG
    load_states(states_f, states)
    load_states(laters_f, laters)
    broadcast_rows(bx, proj, RANK)
    broadcast_rows(cx, proj, RANK + NS)
    decay = [a3[8 * n : 8 * n + 8, :] for n in range(NS)]
    zero = jnp.zeros((8, 128), F32)
    order = plan.order()
    spread(skip3, pm[ROW_SK : ROW_SK + 1, :])
    skip = skip3[...]

    def combine(i, held):
        j = plan.chunks - 1 - i
        total = states_f[pl.ds(pl.multiple_of((j ^ order) * 144 + 128, 8), 8), :]
        base = (j ^ order) * 128
        return tuple(
            jnp.exp2(total * decay[n]) * held[n] + laters_f[pl.ds(pl.multiple_of(base + 8 * n, 8), 8), :]
            for n in range(NS)
        )

    carried = lax.fori_loop(0, plan.chunks - 1 - plan.chunk(), combine, (zero,) * NS)
    gal[...] = jnp.zeros_like(gal)

    def retreat(i, state):
        carried, skipped = state
        t = tokens - 1 - i
        size, value, grad = at8(dt3, t), at8(au3, t), at8(gy3, t)
        base = pl.multiple_of(t * 128, 128)
        from_b = zero
        from_a = zero
        fresh = []
        for n in range(NS):
            g = carried[n] + grad * cx[n, pl.ds(t, 1), :]
            grads[pl.ds(base + 8 * n, 8), :] = g
            w = jnp.exp2(size * decay[n]) * g
            q = w * all_states[pl.ds(base + 8 * n, 8), :]
            from_a = from_a + decay[n] * q
            from_b = from_b + g * bx[n, pl.ds(t, 1), :]
            gal[8 * n : 8 * n + 8, :] += size * q
            fresh.append(w)
        at = pl.ds(pl.multiple_of(t * 8, 8), 8)
        gs3[at, :] = from_a * LN2 + from_b * value
        ga3[at, :] = from_b * size + skip * grad
        return tuple(fresh), skipped + grad * value

    _, skipped = lax.fori_loop(0, tokens, retreat, (carried, zero), unroll=2)

    span = 16
    row_t = lax.broadcasted_iota(jnp.int32, (span, span * NS), 0)
    col_t = lax.broadcasted_iota(jnp.int32, (span, span * NS), 1) // NS
    pick = (
        lax.broadcasted_iota(jnp.int32, (span * NS, NS), 0) % NS
        == lax.broadcasted_iota(jnp.int32, (span * NS, NS), 1)
    ).astype(BF16)
    for block in range(tokens // span):
        total_b = jnp.zeros((span, span * NS), F32)
        total_c = jnp.zeros((span, span * NS), F32)
        for s in range(LG):
            rows = pl.ds(block * span * 8 + s, span, stride=LG)
            grad_rows = grads[pl.ds(block * span * 128 + s, span * NS, stride=LG), :].astype(BF16)
            held_rows = all_states[pl.ds((block * span + 1) * 128 + s, span * NS, stride=LG), :].astype(BF16)
            total_b = total_b + nt((dt3[rows, :] * au3[rows, :]).astype(BF16), grad_rows)
            total_c = total_c + nt(gy3[rows, :].astype(BF16), held_rows)
        own_b = jnp.where(row_t == col_t, total_b, 0.0).astype(BF16)
        own_c = jnp.where(row_t == col_t, total_c, 0.0).astype(BF16)
        low_rank[block * span : (block + 1) * span, RANK : RANK + NS] = nn(own_b, pick)
        low_rank[block * span : (block + 1) * span, RANK + NS : RANK + 2 * NS] = nn(own_c, pick)

    grad_pre = gathered(gs3, tokens) * sig[...]
    grad_pre_low = grad_pre.astype(BF16)
    low_rank[:, :RANK] = nt(grad_pre_low, pm[ROW_DT : ROW_DT + RANK, :].astype(BF16))
    projected = low_rank[:, :64].astype(BF16)
    small_grads[ROW_X : ROW_X + 64, :] = tn(projected, act[...])
    small_grads[ROW_DT : ROW_DT + RANK, :] = tn(proj[:, :RANK].astype(BF16), grad_pre_low)
    true_a = -jnp.exp(pm[ROW_A : ROW_A + NS, :])
    small_grads[ROW_A : ROW_A + NS, :] = gathered(gal, NS) * true_a
    small_grads[ROW_DB : ROW_DB + 1, :] = jnp.sum(grad_pre, axis=0, keepdims=True)
    skip3[...] = skipped
    small_grads[ROW_SK : ROW_SK + 1, :] = gathered(skip3, 1)
    small_grads[ROW_G1:, :] = jnp.zeros((SMALL_ROWS - ROW_G1, E), F32)
    conv = conv_in[...]
    s = sigmoid(conv)
    grad_act = gathered(ga3, tokens) + nn(projected, pm[ROW_X : ROW_X + 64, :].astype(BF16))
    grad_conv = grad_act * (s * (1.0 + conv * (1.0 - s)))
    small_grads[ROW_CB : ROW_CB + 1, :] = jnp.sum(grad_conv, axis=0, keepdims=True)
    for k in range(KW):
        small_grads[ROW_CW + k : ROW_CW + k + 1, :] = jnp.sum(
            grad_conv * u_in[HALO - 3 + k : HALO - 3 + k + tokens, :], axis=0, keepdims=True
        )
    padded[:HALO, :] = jnp.zeros((HALO, E), F32)
    padded[HALO : HALO + tokens, :] = grad_conv
    padded[HALO + tokens :, :] = jnp.zeros((HALO, E), F32)
    gu = jnp.zeros((HALO + tokens, E), F32)
    for k in range(KW):
        gu = gu + pm[ROW_CW + k : ROW_CW + k + 1, :] * padded[3 - k : 3 - k + HALO + tokens, :]
    gu_low = gu.astype(BF16)
    gu_out[...] = gu_low
    large[...] = tn(normed[...], gu_low)
    pack_blocks(plan, u_blocks, large, 16, 16, 0)


def last_kernel(plan, nu, nz, masks, *refs):
    tok, halo, gain, gu, gz, grad_middle = refs[:6]
    u_pieces, z_pieces = refs[6 : 6 + nu], refs[6 + nu : 6 + nu + nz]
    own, before, gain_grad, weight = refs[6 + nu + nz :]
    me = plan.me()
    fill(weight, u_pieces, masks, me, 16, (0, 16), 0)
    fill(weight, z_pieces, masks, me, 16, (0, 16), E)
    x = jnp.concatenate([halo[...].astype(F32), tok[...].astype(F32)], axis=0)
    r = lax.rsqrt(jnp.mean(x * x, axis=-1, keepdims=True) + EPS)
    from_z = nt(gz[...], weight[:, E:])
    grad_n = nt(gu[...], weight[:, :E]) + jnp.concatenate([jnp.zeros((HALO, D), F32), from_z], axis=0)
    gain_grad[...] = jnp.sum(grad_n * x * r, axis=0, keepdims=True)
    q = grad_n * gain[...]
    base = r * q - x * (r * r * r) * jnp.mean(q * x, axis=-1, keepdims=True)
    own[...] = (grad_middle[...] + base[HALO:, :]).astype(BF16)
    before[...] = base[:HALO, :].astype(BF16)


def sum_split_kernel(count, *refs):
    ins, outs = refs[:-count], refs[-count:]
    rows = outs[0].shape[0]
    for i, out in enumerate(outs):
        part = slice(i * rows, (i + 1) * rows)
        total = ins[0][part, :].astype(F32)
        for other in ins[1:]:
            total = total + other[part, :].astype(F32)
        out[...] = total.astype(out.dtype)


def sum_split(ins, count, dtype):
    rows, cols = ins[0].shape
    return run(
        functools.partial(sum_split_kernel, count), ins, [((rows // count, cols), dtype)] * count
    )


def gather_blocks(value):
    held = jnp.concatenate([value] + [send(value, mask) for mask in Z_MASKS[1:]], axis=0)
    near = [held] + [send(held, mask) for mask in XY_MASKS[1:]]
    return near + [send(part, CORE) for part in near]


def gather_small(value, rows):
    lin = lax.axis_index("dp") * 8 + lax.axis_index("ctx")
    for bit in (1, 2, 4, 8, 16):
        other = send(value, bit)
        high = (lin & bit) != 0
        value = jnp.concatenate([jnp.where(high, other, value), jnp.where(high, value, other)], axis=0)
    return value


def reduce_blocks(keep, give, dtype):
    parts = sum_split([keep, send(give, CORE)], 4, BF16)
    parts = sum_split(
        [parts[0]] + [send(part, mask) for part, mask in zip(parts[1:], XY_MASKS[1:])], 4, BF16
    )
    return sum_split(
        [parts[0]] + [send(part, mask) for part, mask in zip(parts[1:], Z_MASKS[1:])], 1, dtype
    )[0]


def reduce_small(value):
    lin = lax.axis_index("dp") * 8 + lax.axis_index("ctx")
    for bit in (16, 8, 4, 2, 1):
        high = (lin & bit) != 0
        other = jnp.where(high, value[0], value[1])
        value = jnp.where(high, value[1], value[0]) + send(other, bit)
    return value


def body(plan, *args):
    (tokens, mixer_gain, in_proj, conv_weight, conv_bias, x_proj, dt_proj, dt_bias, a_log, d_skip, out_proj,
     attn_gain, w_query, w_key, w_value, w_output, cotangent) = args
    count = tokens.shape[1]
    tok0, cot0 = tokens.reshape(count, D), cotangent.reshape(count, D)
    chunks = plan.chunks
    low = lambda value: value.astype(BF16)
    devices = plan.dp * plan.ctx
    share, width = E // devices, D // devices
    smalls = jnp.concatenate(
        [x_proj.T, dt_proj, a_log.T, conv_weight.T, conv_bias[None], dt_bias[None], d_skip[None],
         jnp.pad(mixer_gain, (0, share - width))[None], jnp.pad(attn_gain, (0, share - width))[None],
         jnp.zeros((SMALL_ROWS - ROW_G2 - 1, share), F32)], axis=0).astype(BF16)
    pack_one = jnp.concatenate([low(out_proj), low(w_query)], axis=0)
    pack_two = jnp.concatenate([low(w_key), low(w_value), low(w_output)], axis=0)
    if plan.fast:
        masks = FULL_MASKS
        home = [(s * 8 + c, plan.place(s, c)) for s in range(4) for c in range(8)]
        tok = lax.ppermute(tok0, ALL, home)
        halo = lax.ppermute(
            tok0[count - HALO :], ALL, [(s * 8 + c, plan.place(s, c + 1)) for s in range(4) for c in range(7)]
        )
        small_all = gather_small(
            smalls.reshape(4, 32, share).transpose(1, 0, 2).reshape(1, 32, 128), 32)
        small_all = small_all.reshape(BLOCKS, 32, 4, share).transpose(2, 1, 0, 3).reshape(SMALL_ROWS, E)
        u_pieces = gather_blocks(low(in_proj[:, :E]))
        z_pieces = gather_blocks(low(in_proj[:, E:]))
        one = gather_blocks(pack_one)
        two = gather_blocks(pack_two)
        cot = lax.ppermute(cot0, ALL, home)
    else:
        masks = tuple(range(BLOCKS))
        tok, cot = tok0, cot0
        halo = lax.ppermute(tok0[count - HALO :], "ctx", [(c, c + 1) for c in range(chunks - 1)])
        small_all = lax.all_gather(smalls, ALL, axis=1, tiled=True)
        whole = lambda value: lax.all_gather(low(value), ALL, axis=0, tiled=True)
        u_pieces, z_pieces = [whole(in_proj[:, :E])], [whole(in_proj[:, E:])]
        out_all, q_all, k_all, v_all, o_all = (whole(w) for w in (out_proj, w_query, w_key, w_value, w_output))
        cut = lambda value, rows: value.reshape(BLOCKS, rows, D)
        one = [jnp.concatenate([cut(out_all, 32), cut(q_all, 16)], axis=1).reshape(-1, D)]
        two = [jnp.concatenate([cut(k_all, 16), cut(v_all, 16), cut(o_all, 16)], axis=1).reshape(-1, D)]
    pm = small_all.astype(F32)
    gain_of = lambda row: pm[row].reshape(devices, share)[:, :width].reshape(1, D)
    gain_one, gain_two = gain_of(ROW_G1), gain_of(ROW_G2)

    nu, nz, nb, no = len(u_pieces), len(z_pieces), len(one), len(plan.grad_masks)
    rows3 = count * LG
    (normed, u_pre, z, conv, act, proj, sig, dt3, au3, a3, state) = run(
        functools.partial(front_kernel, plan, nu, nz, masks),
        [tok, halo, pm, gain_one, *u_pieces, *z_pieces],
        [((HALO + count, D), BF16), ((HALO + count, E), F32), ((count, E), F32), ((count, E), F32),
         ((count, E), BF16), ((count, 128), F32), ((count, E), F32), ((rows3, 128), F32), ((rows3, 128), F32),
         ((128, 128), F32), ((144, 128), BF16)],
        [pltpu.VMEM((D, 2 * E), BF16), pltpu.VMEM((NS, count, 128), F32)],
    )
    if plan.fast:
        states = [state] + [send(state, mask) for mask in CHUNK_MASKS[1:]]
    else:
        states = [lax.all_gather(state, "ctx", axis=0, tiled=True)]
    ns = len(states)
    weights = [pltpu.VMEM((E, D), BF16)] + [pltpu.VMEM((D, D), BF16)] * 4
    rows_scratch = pltpu.VMEM((NS, count, 128), F32)
    pay, mamba, gated, middle, entry = run(
        functools.partial(mid_kernel, plan, ns, nb, masks),
        [tok, dt3, au3, proj, a3, z, pm, gain_two, cot, *states, *one, *two],
        [((HEADS * count, 4 * HDIM), BF16), ((count, E), F32), ((count, E), BF16), ((count, D), F32), ((128, 128), F32)],
        [pltpu.VMEM((144 * chunks, 128), F32), *weights, pltpu.VMEM((rows3, 128), F32), rows_scratch, rows_scratch],
    )
    got = attend(plan, pay, count)
    (all_states,) = run(
        states_kernel, [dt3, au3, proj, a3, entry], [(((count + 1) * 128, 128), F32)], [rows_scratch]
    )
    (att, gq, gk, gv, grad_middle, mix, gz, gy3, later, gain_grad_two) = run(
        functools.partial(turn_kernel, plan, nb, masks),
        [got, middle, cot, gain_two, z, mamba, dt3, proj, a3, *one, *two],
        [((count, D), BF16)] * 4 + [((count, D), F32), ((count, D), BF16), ((count, E), BF16), ((rows3, 128), F32),
                                    ((128, 128), BF16), ((1, D), F32)],
        [*weights, rows_scratch],
    )
    if plan.fast:
        laters = [later] + [send(later, mask) for mask in CHUNK_MASKS[1:]]
    else:
        laters = [lax.all_gather(later, "ctx", axis=0, tiled=True)]
    blocks = [len(masks_of) for masks_of in plan.grad_masks]
    outs = run(
        functools.partial(weights_kernel, plan, no, nb, masks),
        [att, gq, gk, gv, mix, gated, middle, gain_two, cot, *two],
        [((count, D), BF16)] + [((n * 48, D), BF16) for n in blocks] * 2,
        [pltpu.VMEM((D, D), BF16), pltpu.VMEM((D, D), F32), pltpu.VMEM((E, D), F32)],
    )
    result, one_grads, two_grads = outs[0], outs[1 : 1 + no], outs[1 + no :]
    z_grads = run(
        functools.partial(gate_weights_kernel, plan, no), [normed, gz], [((n * 16, E), BF16) for n in blocks],
        [pltpu.VMEM((D, E), F32)],
    )
    outs = run(
        functools.partial(back_kernel, plan, ns, no),
        [dt3, au3, gy3, a3, proj, pm, all_states, sig, act, conv, u_pre, normed, *states, *laters],
        [((n * 16, E), BF16) for n in blocks] + [((SMALL_ROWS, E), F32), ((HALO + count, E), BF16)],
        [pltpu.VMEM((144 * chunks, 128), F32), pltpu.VMEM((128 * chunks, 128), F32), rows_scratch, rows_scratch,
         pltpu.VMEM((count * 128, 128), F32), pltpu.VMEM((rows3, 128), F32), pltpu.VMEM((rows3, 128), F32),
         pltpu.VMEM((128, 128), F32), pltpu.VMEM((8, 128), F32), pltpu.VMEM((count, 128), F32),
         pltpu.VMEM((count + 2 * HALO, E), F32), pltpu.VMEM((D, E), F32)],
        limit=56,
    )
    u_grads, small_grads, gu = outs[:no], outs[no], outs[no + 1]
    own, before, gain_grad_one = run(
        functools.partial(last_kernel, plan, nu, nz, masks),
        [tok, halo, gain_one, gu, gz, grad_middle, *u_pieces, *z_pieces],
        [((count, D), BF16), ((HALO, D), BF16), ((1, D), F32)],
        [pltpu.VMEM((D, 2 * E), BF16)],
    )
    wide = lambda row: jnp.pad(row.reshape(devices, width), ((0, 0), (0, share - width))).reshape(1, E)
    small_grads = jnp.concatenate(
        [small_grads[:ROW_G1], wide(gain_grad_one), wide(gain_grad_two), small_grads[ROW_G2 + 1 :]], axis=0)
    if plan.fast:
        away = [(b, a) for a, b in home]
        result = lax.ppermute(result, ALL, away)
        grad_tok = lax.ppermute(own, ALL, away)
        tail = lax.ppermute(
            before, ALL, [(plan.place(s, c + 1), s * 8 + c) for s in range(4) for c in range(7)])
        ordered = small_grads.reshape(4, 32, BLOCKS, share).transpose(2, 1, 0, 3)
        ordered = ordered.reshape((2, 2, 2, 2, 2) + (32, 128))
        mine = reduce_small(ordered).reshape(32, 4, share).transpose(1, 0, 2).reshape(SMALL_ROWS, share)
        one_sum = reduce_blocks(*one_grads, F32)
        two_sum = reduce_blocks(*two_grads, F32)
        in_sum = jnp.concatenate([reduce_blocks(*u_grads, F32), reduce_blocks(*z_grads, F32)], axis=1)
        out_g, q_g = one_sum[:32], one_sum[32:]
        k_g, v_g, o_g = two_sum[:16], two_sum[16:32], two_sum[32:]
    else:
        grad_tok = own
        tail = lax.ppermute(before, "ctx", [(c + 1, c) for c in range(chunks - 1)])
        scatter = lambda value, dim=0: lax.psum_scatter(value, ALL, scatter_dimension=dim, tiled=True)
        mine = scatter(small_grads, 1)
        parts_of = lambda value, first, rows: value.reshape(BLOCKS, 48, D)[:, first : first + rows].reshape(-1, D).astype(F32)
        out_g, q_g = scatter(parts_of(one_grads[0], 0, 32)), scatter(parts_of(one_grads[0], 32, 16))
        k_g, v_g, o_g = (scatter(parts_of(two_grads[0], first, 16)) for first in (0, 16, 32))
        in_sum = scatter(jnp.concatenate([u_grads[0], z_grads[0]], axis=1).astype(F32))
    last = (grad_tok[count - HALO :].astype(F32) + tail.astype(F32)).astype(BF16)
    grad_tok = jnp.concatenate([grad_tok[: count - HALO], last], axis=0)
    return (
        result[None], grad_tok[None], mine[ROW_G1, :width], in_sum, mine[ROW_CW : ROW_CW + KW].T, mine[ROW_CB],
        mine[ROW_X : ROW_X + 64].T, mine[ROW_DT : ROW_DT + RANK], mine[ROW_DB], mine[ROW_A : ROW_A + NS].T,
        mine[ROW_SK], out_g, mine[ROW_G2, :width], q_g, k_g, v_g, o_g,
    )


def attend(plan, pay, count):
    if plan.chunks == HEADS:
        if plan.fast:
            groups = [[plan.place(s, c) for c in range(8)] for s in range(4)]
            swap = lambda value: lax.all_to_all(value, ALL, 0, 0, tiled=True, axis_index_groups=groups)
        else:
            swap = lambda value: lax.all_to_all(value, "ctx", 0, 0, tiled=True)
        held = swap(pay)
        length = held.shape[0]
        half = pltpu.VMEM((length, HDIM), BF16)
        flat = pltpu.VMEM((HDIM, length), BF16)
        wide = pltpu.VMEM((length, HDIM), F32)
        (back,) = run(
            attention_kernel, [held], [((length, 4 * HDIM), BF16)], [half] * 4 + [flat] * 2 + [wide] * 2
        )
        return swap(back)
    parts = pay.reshape(HEADS, count, 4, HDIM)
    query, key, value, grad = (parts[:, :, i] for i in range(4))
    key, value = (lax.all_gather(part, "ctx", axis=1, tiled=True) for part in (key, value))
    query_at = lax.axis_index("ctx") * count + jnp.arange(count)
    allowed = jnp.arange(key.shape[1])[None, :] <= query_at[:, None]
    scale = HDIM**-0.5
    dots = functools.partial(jnp.einsum, preferred_element_type=F32)
    scores = jnp.where(allowed, dots("hqd,hkd->hqk", query, key) * scale, -1e30)
    soft = jax.nn.softmax(scores, axis=-1)
    soft_low = soft.astype(BF16)
    grad_p = dots("hqd,hkd->hqk", grad, value)
    grad_s = (soft * (grad_p - jnp.sum(soft * grad_p, axis=-1, keepdims=True))).astype(BF16)
    raw = dots("hqk,hkd->hqd", soft_low, value).astype(BF16)
    grad_q = (dots("hqk,hkd->hqd", grad_s, key) * scale).astype(BF16)
    grads = (dots("hqk,hqd->hkd", grad_s, query) * scale, dots("hqk,hqd->hkd", soft_low, grad))
    grad_k, grad_v = (
        lax.psum_scatter(part.astype(BF16), "ctx", scatter_dimension=1, tiled=True) for part in grads
    )
    return jnp.concatenate([raw, grad_q, grad_k, grad_v], axis=-1).reshape(HEADS * count, 4 * HDIM)


def solution(mesh):
    plan = Plan(mesh)
    split, rows, cols = P(ALL), P(ALL, None), P(None, ALL)
    acts = P("dp", "ctx", None)
    return jax.shard_map(
        functools.partial(body, plan),
        mesh=mesh,
        in_specs=(acts, split, rows, rows, split, rows, cols, split, rows, split, rows, split, rows, rows, rows, rows, acts),
        out_specs=(acts, acts, split, rows, rows, split, rows, cols, split, rows, split, rows, split, rows, rows, rows, rows),
        check_vma=False,
    )
```

```python
import functools

import jax
import jax.numpy as jnp
from jax import lax
from jax.experimental import pallas as pl
from jax.experimental.pallas import tpu as pltpu
from jax.sharding import PartitionSpec as P

D = 512
E = 1024
NS = 16
RANK = 32
KW = 4
HEADS = 8
HDIM = 64
LG = 8
HALO = 16
BLOCKS = 32
ALL = ("dp", "ctx")
EPS = 1e-05
LOG2E = 1.4426950408889634
LN2 = 0.6931471805599453
F32 = jnp.float32
BF16 = jnp.bfloat16
VM = pl.BlockSpec(memory_space=pltpu.VMEM)

Z_MASKS = (0, 4, 2, 6)
XY_MASKS = (0, 1, 16, 17)
CORE = 8
HALF_MASKS = tuple(xy | zz for xy in XY_MASKS for zz in Z_MASKS)
FULL_MASKS = HALF_MASKS + tuple(mask | CORE for mask in HALF_MASKS)
CHUNK_MASKS = tuple((16 if c & 1 else 0) | (1 if c & 2 else 0) | (8 if c & 4 else 0) for c in range(8))

ROW_X = 0
ROW_DT = 64
ROW_A = 96
ROW_CW = 112
ROW_CB = 116
ROW_DB = 117
ROW_SK = 118
ROW_G1 = 119
ROW_G2 = 120
SMALL_ROWS = 128


ANY = pl.BlockSpec(memory_space=pl.ANY)
FAR = pl.BlockSpec(memory_space=pltpu.HBM)
WHOLE = pl.BlockSpec()


def run(kernel, ins, outs, scratch=(), limit=12, raw=(), far=(), after=(), final=False, us=2):
    first, count = len(ins) + len(raw) + len(far), len(after)

    def inner(*refs):
        kernel(*refs[:first], *refs[first + count :])

    return pl.pallas_call(
        inner,
        out_shape=[jax.ShapeDtypeStruct(shape, dtype) for shape, dtype in outs],
        in_specs=[VM] * len(ins) + [ANY] * len(raw) + [FAR] * len(far) + [ANY] * count,
        out_specs=[WHOLE if final else VM] * len(outs),
        scratch_shapes=list(scratch),
        compiler_params=pltpu.CompilerParams(vmem_limit_bytes=limit * 2**20),
        cost_estimate=pl.CostEstimate(flops=int(us * 1e3), bytes_accessed=int(us * 3e3), transcendentals=0),
    )(*ins, *raw, *far, *after)


def nn(left, right):
    return lax.dot_general(left, right, (((1,), (0,)), ((), ())), preferred_element_type=F32)


def nt(left, right):
    return lax.dot_general(left, right, (((1,), (1,)), ((), ())), preferred_element_type=F32)


def tn(left, right):
    return lax.dot_general(left, right, (((0,), (0,)), ((), ())), preferred_element_type=F32)


def sigmoid(value):
    return 1.0 / (1.0 + jnp.exp(-value))


class Plan:
    def __init__(self, mesh):
        self.dp, self.ctx = mesh.shape["dp"], mesh.shape["ctx"]
        self.fast = (self.dp, self.ctx) == (4, 8)
        self.chunks = self.ctx
        if self.fast:
            self.grad_masks = (FULL_MASKS[:16], FULL_MASKS[16:])
        else:
            self.grad_masks = (tuple(range(BLOCKS)),)

    def place(self, seq, chunk):
        return CHUNK_MASKS[chunk] | ((0, 2, 1, 3)[seq] << 1)

    def me(self):
        if self.fast:
            return lax.axis_index("dp") * 8 + lax.axis_index("ctx")
        return 0

    def chunk(self):
        if self.fast:
            lin = lax.axis_index("dp") * 8 + lax.axis_index("ctx")
            return ((lin >> 4) & 1) + (lin & 1) * 2 + ((lin >> 3) & 1) * 4
        return lax.axis_index("ctx")

    def swap(self, value):
        if self.fast:
            groups = [[self.place(s, c) for c in range(8)] for s in range(4)]
            return lax.all_to_all(value, ALL, 0, 0, tiled=True, axis_index_groups=groups)
        return lax.all_to_all(value, "ctx", 0, 0, tiled=True)


def send(value, mask):
    return lax.ppermute(value, ALL, [(i, i ^ mask) for i in range(32)])


def start_blocks(target, pieces, masks, me, sem, row_in, rows, first, cols):
    per_piece = len(masks) // len(pieces)
    height = pieces[0].shape[0] // per_piece
    for i, piece in enumerate(pieces):
        for k in range(per_piece):
            block = me ^ masks[i * per_piece + k]
            pltpu.make_async_copy(
                piece.at[pl.ds(k * height + row_in, rows), pl.ds(first, cols)],
                target.at[pl.ds(pl.multiple_of(block * rows, 16), rows), :],
                sem,
            ).start()


def wait_whole(target, sem):
    pltpu.make_async_copy(target, target, sem).wait()


def swap_blocks(value, me):
    rows, lanes = value.shape
    for bit in (16, 8, 4):
        half = bit * 32
        parts = [value[:, i : i + half] for i in range(0, lanes, half)]
        other = jnp.concatenate([parts[i ^ 1] for i in range(len(parts))], axis=1)
        value = jnp.where((me & bit) != 0, other, value)
    groups = []
    odd = (lax.broadcasted_iota(jnp.int32, (rows, 128), 1) & 32) != 0
    for i in range(0, lanes, 128):
        part = value[:, i : i + 128]
        part = jnp.where((me & 2) != 0, pltpu.roll(part, 64, 1), part)
        other = jnp.where(odd, pltpu.roll(part, 32, 1), pltpu.roll(part, 96, 1))
        groups.append(jnp.where((me & 1) != 0, other, part))
    return jnp.concatenate(groups, axis=1)


def pack_kernel(in_proj, x_proj, dt_proj, a_log, conv_w, conv_b, dt_bias, d_skip, gain_one, gain_two,
                out_proj, w_q, w_k, w_v, w_o, one, two, rows, *rest):
    (b_in, b_x, b_dt, b_a, b_cw, b_cb, b_db, b_sk, b_g1, b_g2, b_out, b_q, b_k, b_v, b_o, sems) = rest
    copies = [
        pltpu.make_async_copy(src, dst, sems.at[i])
        for i, (src, dst) in enumerate(
            zip((in_proj, x_proj, dt_proj, a_log, conv_w, conv_b, dt_bias, d_skip, gain_one, gain_two, out_proj, w_q,
                 w_k, w_v, w_o),
                (b_in, b_x, b_dt, b_a, b_cw, b_cb, b_db, b_sk, b_g1, b_g2, b_out, b_q, b_k, b_v, b_o))
        )
    ]
    for copy in copies:
        copy.start()
    for copy in copies:
        copy.wait()
    one[:, : 2 * E] = b_in[...].astype(BF16)
    two[:, :D] = b_out[...].astype(BF16)
    two[:16, D : 2 * D] = b_q[...].astype(BF16)
    two[:16, 2 * D :] = b_k[...].astype(BF16)
    two[16:, D : 2 * D] = b_v[...].astype(BF16)
    two[16:, 2 * D :] = b_o[...].astype(BF16)
    rows[...] = jnp.zeros_like(rows)
    rows[ROW_X : ROW_X + 64, :] = b_x[...].T
    rows[ROW_DT : ROW_DT + RANK, :] = b_dt[...]
    rows[ROW_A : ROW_A + NS, :] = b_a[...]
    rows[ROW_CW : ROW_CW + KW, :] = b_cw[...]
    rows[ROW_CB : ROW_CB + 1, :] = b_cb[...]
    rows[ROW_DB : ROW_DB + 1, :] = b_db[...]
    rows[ROW_SK : ROW_SK + 1, :] = b_sk[...]
    rows[ROW_G1 : ROW_G1 + 1, :16] = b_g1[...]
    rows[ROW_G2 : ROW_G2 + 1, :16] = b_g2[...]
    one[:, 2 * E :] = jnp.concatenate([rows[16 * q : 16 * q + 16, :] for q in range(8)], axis=1).astype(BF16)


def join_smalls(target, smalls, masks, me):
    place = {mask: p for p, mask in enumerate(masks)}
    for q in range(8):
        for g in range(LG):
            target[16 * q : 16 * q + 16, 128 * g : 128 * g + 128] = jnp.concatenate(
                [smalls[16 * place[m] : 16 * place[m] + 16, 32 * q : 32 * q + 32].astype(F32) for m in range(4 * g, 4 * g + 4)],
                axis=1,
            )
    target[...] = swap_blocks(target[...], me)


def gain_row(pm, row):
    return jnp.concatenate([pm[row : row + 1, 32 * s : 32 * s + 16] for s in range(BLOCKS)], axis=1)


def spread(target, source):
    count = source.shape[0]
    for s in range(LG):
        target[pl.ds(s, count, stride=LG), :] = source[:, s * 128 : (s + 1) * 128]


def gathered(source, count):
    return jnp.concatenate([source[pl.ds(s, count, stride=LG), :] for s in range(LG)], axis=1)


def broadcast_rows(target, proj, first):
    for n in range(NS):
        target[n] = jnp.broadcast_to(proj[:, first + n : first + n + 1], target.shape[1:])


def at8(ref, index):
    return ref[pl.ds(pl.multiple_of(index * 8, 8), 8), :]


def front_kernel(plan, np_, masks, tok, halo, *refs):
    pieces = refs[:np_]
    (normed, u_out, z_out, conv_out, act_out, proj_out, sig_out, dt3, au3, a3, state, weight, pm, gains, bx, smalls, sems) = refs[np_:]
    me = plan.me()
    start_blocks(weight, pieces, masks, me, sems.at[0], 0, 16, 0, 2 * E)
    height = smalls.shape[0] // np_
    for i, piece in enumerate(pieces):
        pltpu.make_async_copy(
            piece.at[:, pl.ds(2 * E, 256)], smalls.at[pl.ds(i * height, height), :], sems.at[1]).start()
    wait_whole(smalls, sems.at[1])
    join_smalls(pm, smalls, masks, me)
    gain = gain_row(pm, ROW_G1)
    gains[0:1, :] = gain
    gains[1:2, :] = gain_row(pm, ROW_G2)
    tokens = tok.shape[0]
    x = jnp.concatenate([halo[...].astype(F32), tok[...].astype(F32)], axis=0)
    r = lax.rsqrt(jnp.mean(x * x, axis=-1, keepdims=True) + EPS)
    low = (x * r * gain).astype(BF16)
    normed[...] = low
    wait_whole(weight, sems.at[0])
    u_out[...] = nn(low, weight[:, :E])
    z_out[...] = nn(low[HALO:], weight[:, E:])
    conv = pm[ROW_CB : ROW_CB + 1, :]
    for k in range(KW):
        conv = conv + pm[ROW_CW + k : ROW_CW + k + 1, :] * u_out[HALO - 3 + k : HALO - 3 + k + tokens, :]
    conv_out[...] = conv
    act = (conv * sigmoid(conv)).astype(BF16)
    act_out[...] = act
    proj = nt(act, pm[ROW_X : ROW_X + 64, :].astype(BF16))
    proj_out[:, :64] = proj
    proj_out[:, 64:] = jnp.zeros((tokens, 64), F32)
    pre = nn(proj[:, :RANK].astype(BF16), pm[ROW_DT : ROW_DT + RANK, :].astype(BF16)) + pm[ROW_DB : ROW_DB + 1, :]
    sig_out[...] = sigmoid(pre)
    step = jnp.maximum(pre, 0.0) + jnp.log1p(jnp.exp(-jnp.abs(pre)))
    spread(dt3, step)
    spread(au3, act.astype(F32))
    spread(a3, -LOG2E * jnp.exp(pm[ROW_A : ROW_A + NS, :]))
    broadcast_rows(bx, proj, RANK)
    decay = [a3[8 * n : 8 * n + 8, :] for n in range(NS)]

    def advance(t, carried):
        held, total = carried
        size = at8(dt3, t)
        drive = size * at8(au3, t)
        held = tuple(
            jnp.exp2(size * decay[n]) * held[n] + drive * bx[n, pl.ds(t, 1), :] for n in range(NS)
        )
        return held, total + size

    zero = jnp.zeros((8, 128), F32)
    held, total = lax.fori_loop(0, tokens, advance, ((zero,) * NS, zero), unroll=4)
    state[...] = jnp.concatenate([*held, total, zero], axis=0).astype(BF16)


def combine_kernel(plan, forward, states, a3, entry, states_f):
    states_f[...] = states[...].astype(F32)
    decay = [a3[8 * n : 8 * n + 8, :] for n in range(NS)]
    zero = jnp.zeros((8, 128), F32)

    def combine(i, held):
        base = (i if forward else plan.chunks - 1 - i) * 144
        total = states_f[pl.ds(pl.multiple_of(base + 128, 8), 8), :]
        return tuple(
            jnp.exp2(total * decay[n]) * held[n] + states_f[pl.ds(pl.multiple_of(base + 8 * n, 8), 8), :]
            for n in range(NS)
        )

    count = plan.chunk() if forward else plan.chunks - 1 - plan.chunk()
    held = lax.fori_loop(0, count, combine, (zero,) * NS)
    entry[...] = jnp.concatenate([*held, zero, zero], axis=0)


def merge_kernel(plan, step, forward, own, other, before, a3, group, entry):
    later = ((plan.chunk() >> step) & 1) == (1 if forward else 0)
    mine, theirs = own[...].astype(F32), other[...].astype(F32)
    first, second = jnp.where(later, theirs, mine), jnp.where(later, mine, theirs)
    decay = a3[...]
    spread_total = lambda value: jnp.concatenate([value[128:136, :]] * NS, axis=0)
    joint = jnp.exp2(spread_total(second) * decay) * first[:128, :] + second[:128, :]
    group[:128, :] = joint.astype(BF16)
    group[128:, :] = (first[128:, :] + second[128:, :]).astype(BF16)
    held = before[...]
    inner = held[:128, :] + jnp.exp2(spread_total(held) * decay) * theirs[:128, :]
    entry[:128, :] = jnp.where(later, inner, held[:128, :])
    entry[128:, :] = jnp.where(later, held[128:, :] + theirs[128:, :], held[128:, :])


def exchange(plan, state, a3, forward):
    if plan.fast:
        group, entry = state, jnp.zeros((144, 128), F32)
        for step in range(3):
            group, entry = run(
                functools.partial(merge_kernel, plan, step, forward),
                [group, send(group, CHUNK_MASKS[1 << step]), entry, a3], [((144, 128), BF16), ((144, 128), F32)])
        return entry
    states = lax.all_gather(state, "ctx", axis=0, tiled=True)
    return run(
        functools.partial(combine_kernel, plan, forward), [states, a3], [((144, 128), F32)],
        [pltpu.VMEM((144 * plan.chunks, 128), F32)])[0]


def mid_kernel(plan, nb, masks, *refs):
    tok, dt3, au3, proj, a3, z_in, pm, gains, cot, entry = refs[:10]
    pieces = refs[10 : 10 + nb]
    pay, mamba, gated_out, middle_out, all_states, w_out, w_qk, w_vo, y3, bx, cx, sems = refs[10 + nb :]
    tokens = tok.shape[0]
    me = plan.me()
    start_blocks(w_out, pieces, masks, me, sems.at[0], 0, 32, 0, D)
    start_blocks(w_qk, pieces, masks, me, sems.at[1], 0, 16, D, 2 * D)
    start_blocks(w_vo, pieces, masks, me, sems.at[2], 16, 16, D, 2 * D)
    broadcast_rows(bx, proj, RANK)
    broadcast_rows(cx, proj, RANK + NS)
    decay = [a3[8 * n : 8 * n + 8, :] for n in range(NS)]
    held = tuple(entry[8 * n : 8 * n + 8, :] for n in range(NS))
    all_states[:128, :] = entry[:128, :]

    def advance(t, held):
        size = at8(dt3, t)
        drive = size * at8(au3, t)
        base = pl.multiple_of(t * 128 + 128, 128)
        held = tuple(
            jnp.exp2(size * decay[n]) * held[n] + drive * bx[n, pl.ds(t, 1), :] for n in range(NS)
        )
        for n in range(NS):
            all_states[pl.ds(base + 8 * n, 8), :] = held[n]
        y = held[0] * cx[0, pl.ds(t, 1), :]
        for n in range(1, NS):
            y = y + held[n] * cx[n, pl.ds(t, 1), :]
        y3[pl.ds(pl.multiple_of(t * 8, 8), 8), :] = y
        return held

    lax.fori_loop(0, tokens, advance, held, unroll=4)
    act = gathered(au3, tokens)
    y = gathered(y3, tokens) + pm[ROW_SK : ROW_SK + 1, :] * act
    mamba[...] = y
    z = z_in[...]
    gated = (y * (z * sigmoid(z))).astype(BF16)
    gated_out[...] = gated
    wait_whole(w_out, sems.at[0])
    wait_whole(w_qk, sems.at[1])
    wait_whole(w_vo, sems.at[2])
    middle = tok[...].astype(F32) + nn(gated, w_out[...])
    middle_out[...] = middle
    r = lax.rsqrt(jnp.mean(middle * middle, axis=-1, keepdims=True) + EPS)
    low = (middle * r * gains[1:2, :]).astype(BF16)
    quads = (
        nn(low, w_qk[:, :D]).astype(BF16),
        nn(low, w_qk[:, D:]).astype(BF16),
        nn(low, w_vo[:, :D]).astype(BF16),
        nt(cot[...], w_vo[:, D:]).astype(BF16),
    )
    for h in range(HEADS):
        for i, part in enumerate(quads):
            pay[h * tokens : (h + 1) * tokens, i * HDIM : (i + 1) * HDIM] = part[:, h * HDIM : (h + 1) * HDIM]


def attention_kernel(pay, back, q_s, k_s, v_s, g_s, kt, vt, dk, dv):
    length = pay.shape[0]
    rows = 256
    q_s[...] = pay[:, :HDIM]
    k_s[...] = pay[:, HDIM : 2 * HDIM]
    v_s[...] = pay[:, 2 * HDIM : 3 * HDIM]
    g_s[...] = pay[:, 3 * HDIM :]
    kt[...] = k_s[...].T
    vt[...] = v_s[...].T
    dk[...] = jnp.zeros_like(dk)
    dv[...] = jnp.zeros_like(dv)
    scale = HDIM**-0.5
    key_at = lax.broadcasted_iota(jnp.int32, (rows, rows), 0)
    query_at = lax.broadcasted_iota(jnp.int32, (rows, rows), 1)
    for i in range(length // rows):
        first, last = i * rows, (i + 1) * rows
        query = q_s[first:last, :]
        grad = g_s[first:last, :]
        scores = nt(k_s[:last, :], query) * scale
        diagonal = jnp.where(key_at <= query_at, scores[first:, :], -1e30)
        scores = diagonal if i == 0 else jnp.concatenate([scores[:first, :], diagonal], axis=0)
        expo = jnp.exp(scores - jnp.max(scores, axis=0, keepdims=True))
        soft = expo * (1.0 / jnp.sum(expo, axis=0, keepdims=True))
        soft_low = soft.astype(BF16)
        grad_p = nt(v_s[:last, :], grad)
        dot = jnp.sum(soft * grad_p, axis=0, keepdims=True)
        grad_s = (soft * (grad_p - dot)).astype(BF16)
        raw = nn(vt[:, :last], soft_low)
        grad_q = nn(kt[:, :last], grad_s) * scale
        back[first:last, :HDIM] = raw.T.astype(BF16)
        back[first:last, HDIM : 2 * HDIM] = grad_q.T.astype(BF16)
        dk[:last, :] += nn(grad_s, query)
        dv[:last, :] += nn(soft_low, grad)
    back[:, 2 * HDIM : 3 * HDIM] = (dk[...] * scale).astype(BF16)
    back[:, 3 * HDIM :] = dv[...].astype(BF16)


def turn_kernel(plan, got, middle, cot, gains, z_in, mamba, dt3, proj, a3, w_out, w_qk, w_vo, first,
                att, gq, gk, gv, grad_middle, mix, gz, gy3, state, gain_grad, cx):
    tokens = middle.shape[0]
    broadcast_rows(cx, proj, RANK + NS)
    for h in range(HEADS):
        for i, part in enumerate((att, gq, gk, gv)):
            part[:, h * HDIM : (h + 1) * HDIM] = got[h * tokens : (h + 1) * tokens, i * HDIM : (i + 1) * HDIM]
    grad_n = nt(gq[...], w_qk[:, :D]) + nt(gk[...], w_qk[:, D:]) + nt(gv[...], w_vo[:, :D])
    mid = middle[...]
    r = lax.rsqrt(jnp.mean(mid * mid, axis=-1, keepdims=True) + EPS)
    gain_grad[...] = jnp.sum(grad_n * mid * r, axis=0, keepdims=True)
    q = grad_n * gains[1:2, :]
    gm = cot[...].astype(F32) + r * q - mid * (r * r * r) * jnp.mean(q * mid, axis=-1, keepdims=True)
    grad_middle[...] = gm
    low = gm.astype(BF16)
    mix[...] = low
    grad_gated = nt(low, w_out[...])
    z = z_in[...]
    s = sigmoid(z)
    spread(gy3, grad_gated * (z * s))
    gz[...] = (grad_gated * mamba[...] * (s * (1.0 + z * (1.0 - s)))).astype(BF16)
    decay = [a3[8 * n : 8 * n + 8, :] for n in range(NS)]

    def retreat(i, carried):
        t = tokens - 1 - i
        size = at8(dt3, t)
        grad = at8(gy3, t)
        return tuple(
            jnp.exp2(size * decay[n]) * (carried[n] + grad * cx[n, pl.ds(t, 1), :]) for n in range(NS)
        )

    zero = jnp.zeros((8, 128), F32)
    carried = lax.fori_loop(0, tokens, retreat, (zero,) * NS, unroll=4)
    state[:128, :] = jnp.concatenate(carried, axis=0).astype(BF16)
    state[128:, :] = first[128:, :]


def pack_blocks(plan, outs, source, rows, height, row, first, col=0, cols=None):
    me = plan.me()
    cols = source.shape[1] if cols is None else cols
    for out, masks in zip(outs, plan.grad_masks):
        for k, mask in enumerate(masks):
            block = me ^ mask
            out[k * height + row : k * height + row + rows, first : first + cols] = source[
                pl.ds(pl.multiple_of(block * rows, 16), rows), col : col + cols
            ].astype(BF16)


def weights_kernel(plan, no, att, gq, gk, gv, mix, gated, middle, gains, cot, w_vo, normed, gz, *refs):
    result, outs = refs[0], refs[1 : 1 + no]
    small, large, wide = refs[1 + no :]
    mid = middle[...]
    result[...] = (mid + nn(att[...], w_vo[:, D:])).astype(BF16)
    r = lax.rsqrt(jnp.mean(mid * mid, axis=-1, keepdims=True) + EPS)
    low = (mid * r * gains[1:2, :]).astype(BF16)
    large[...] = tn(gated[...], mix[...])
    pack_blocks(plan, outs, large, 32, 32, 0, 0)
    small[...] = tn(low, gq[...])
    pack_blocks(plan, outs, small, 16, 32, 0, D)
    small[...] = tn(low, gk[...])
    pack_blocks(plan, outs, small, 16, 32, 0, 2 * D)
    small[...] = tn(low, gv[...])
    pack_blocks(plan, outs, small, 16, 32, 16, D)
    small[...] = tn(att[...], cot[...])
    pack_blocks(plan, outs, small, 16, 32, 16, 2 * D)
    wide[...] = tn(normed[HALO:, :], gz[...])
    pack_blocks(plan, outs, wide, 16, 32, 0, 3 * D, 0, D)
    pack_blocks(plan, outs, wide, 16, 32, 16, 3 * D, D, D)


def back_kernel(plan, dt3, au3, gy3, a3, proj, pm, all_states, sig, act, conv_in, u_in, leaving,
                small_grads, gu_out, bx, cx, grads, gs3, ga3, gal, skip3, low_rank, padded):
    tokens = dt3.shape[0] // LG
    broadcast_rows(bx, proj, RANK)
    broadcast_rows(cx, proj, RANK + NS)
    decay = [a3[8 * n : 8 * n + 8, :] for n in range(NS)]
    zero = jnp.zeros((8, 128), F32)
    spread(skip3, pm[ROW_SK : ROW_SK + 1, :])
    skip = skip3[...]

    carried = tuple(leaving[8 * n : 8 * n + 8, :] for n in range(NS))
    gal[...] = jnp.zeros_like(gal)

    def retreat(i, state):
        carried, skipped = state
        t = tokens - 1 - i
        size, value, grad = at8(dt3, t), at8(au3, t), at8(gy3, t)
        base = pl.multiple_of(t * 128, 128)
        from_b = zero
        from_a = zero
        fresh = []
        for n in range(NS):
            g = carried[n] + grad * cx[n, pl.ds(t, 1), :]
            grads[pl.ds(base + 8 * n, 8), :] = g
            w = jnp.exp2(size * decay[n]) * g
            q = w * all_states[pl.ds(base + 8 * n, 8), :]
            from_a = from_a + decay[n] * q
            from_b = from_b + g * bx[n, pl.ds(t, 1), :]
            gal[8 * n : 8 * n + 8, :] += size * q
            fresh.append(w)
        at = pl.ds(pl.multiple_of(t * 8, 8), 8)
        gs3[at, :] = from_a * LN2 + from_b * value
        ga3[at, :] = from_b * size + skip * grad
        return tuple(fresh), skipped + grad * value

    _, skipped = lax.fori_loop(0, tokens, retreat, (carried, zero), unroll=2)

    span = 16
    row_t = lax.broadcasted_iota(jnp.int32, (span, span * NS), 0)
    col_t = lax.broadcasted_iota(jnp.int32, (span, span * NS), 1) // NS
    pick = (
        lax.broadcasted_iota(jnp.int32, (span * NS, NS), 0) % NS
        == lax.broadcasted_iota(jnp.int32, (span * NS, NS), 1)
    ).astype(BF16)
    for block in range(tokens // span):
        total_b = jnp.zeros((span, span * NS), F32)
        total_c = jnp.zeros((span, span * NS), F32)
        for s in range(LG):
            rows = pl.ds(block * span * 8 + s, span, stride=LG)
            grad_rows = grads[pl.ds(block * span * 128 + s, span * NS, stride=LG), :].astype(BF16)
            held_rows = all_states[pl.ds((block * span + 1) * 128 + s, span * NS, stride=LG), :].astype(BF16)
            total_b = total_b + nt((dt3[rows, :] * au3[rows, :]).astype(BF16), grad_rows)
            total_c = total_c + nt(gy3[rows, :].astype(BF16), held_rows)
        own_b = jnp.where(row_t == col_t, total_b, 0.0).astype(BF16)
        own_c = jnp.where(row_t == col_t, total_c, 0.0).astype(BF16)
        low_rank[block * span : (block + 1) * span, RANK : RANK + NS] = nn(own_b, pick)
        low_rank[block * span : (block + 1) * span, RANK + NS : RANK + 2 * NS] = nn(own_c, pick)

    grad_pre = gathered(gs3, tokens) * sig[...]
    grad_pre_low = grad_pre.astype(BF16)
    low_rank[:, :RANK] = nt(grad_pre_low, pm[ROW_DT : ROW_DT + RANK, :].astype(BF16))
    projected = low_rank[:, :64].astype(BF16)
    small_grads[ROW_X : ROW_X + 64, :] = tn(projected, act[...])
    small_grads[ROW_DT : ROW_DT + RANK, :] = tn(proj[:, :RANK].astype(BF16), grad_pre_low)
    true_a = -jnp.exp(pm[ROW_A : ROW_A + NS, :])
    small_grads[ROW_A : ROW_A + NS, :] = gathered(gal, NS) * true_a
    small_grads[ROW_DB : ROW_DB + 1, :] = jnp.sum(grad_pre, axis=0, keepdims=True)
    skip3[...] = skipped
    small_grads[ROW_SK : ROW_SK + 1, :] = gathered(skip3, 1)
    small_grads[ROW_G1:, :] = jnp.zeros((SMALL_ROWS - ROW_G1, E), F32)
    conv = conv_in[...]
    s = sigmoid(conv)
    grad_act = gathered(ga3, tokens) + nn(projected, pm[ROW_X : ROW_X + 64, :].astype(BF16))
    grad_conv = grad_act * (s * (1.0 + conv * (1.0 - s)))
    small_grads[ROW_CB : ROW_CB + 1, :] = jnp.sum(grad_conv, axis=0, keepdims=True)
    for k in range(KW):
        small_grads[ROW_CW + k : ROW_CW + k + 1, :] = jnp.sum(
            grad_conv * u_in[HALO - 3 + k : HALO - 3 + k + tokens, :], axis=0, keepdims=True
        )
    padded[:HALO, :] = jnp.zeros((HALO, E), F32)
    padded[HALO : HALO + tokens, :] = grad_conv
    padded[HALO + tokens :, :] = jnp.zeros((HALO, E), F32)
    gu = jnp.zeros((HALO + tokens, E), F32)
    for k in range(KW):
        gu = gu + pm[ROW_CW + k : ROW_CW + k + 1, :] * padded[3 - k : 3 - k + HALO + tokens, :]
    gu_out[...] = gu.astype(BF16)


def last_kernel(plan, no, tok, halo, gains, gu, gz, grad_middle, weight, normed, small_grads, gain_two, *refs):
    outs = refs[:no]
    own, before, large, spaced = refs[no:]
    me = plan.me()
    large[...] = tn(normed[...], gu[...])
    pack_blocks(plan, outs, large, 16, 16, 0, 0)
    x = jnp.concatenate([halo[...].astype(F32), tok[...].astype(F32)], axis=0)
    r = lax.rsqrt(jnp.mean(x * x, axis=-1, keepdims=True) + EPS)
    from_z = nt(gz[...], weight[:, E:])
    grad_n = nt(gu[...], weight[:, :E]) + jnp.concatenate([jnp.zeros((HALO, D), F32), from_z], axis=0)
    gain_one = jnp.sum(grad_n * x * r, axis=0, keepdims=True)
    q = grad_n * gains[0:1, :]
    base = r * q - x * (r * r * r) * jnp.mean(q * x, axis=-1, keepdims=True)
    own[...] = (grad_middle[...] + base[HALO:, :]).astype(BF16)
    before[...] = base[:HALO, :].astype(BF16)
    spaced[...] = small_grads[...]
    blank = jnp.zeros((1, 16), F32)
    for row, grad in ((ROW_G1, gain_one), (ROW_G2, gain_two[...])):
        spaced[row : row + 1, :] = jnp.concatenate(
            [part for s in range(BLOCKS) for part in (grad[:, 16 * s : 16 * s + 16], blank)], axis=1)
    spaced[...] = swap_blocks(spaced[...], me)
    for out, masks in zip(outs, plan.grad_masks):
        for k, m in enumerate(masks):
            out[16 * k : 16 * k + 16, E:] = jnp.concatenate(
                [spaced[16 * q : 16 * q + 16, 32 * m : 32 * m + 32] for q in range(8)], axis=1).astype(BF16)


def total_of(ins):
    total = ins[0][...].astype(F32)
    for other in ins[1:]:
        total = total + other[...].astype(F32)
    return total


def finish_kernel(*refs):
    u_ins, ins = refs[:4], refs[4:6]
    out_g, q_g, k_g, v_g, o_g, in_g, x_g, dt_g, a_g, cw_g, cb_g, db_g, sk_g, g1_g, g2_g, rows = refs[6:]
    total = total_of(ins)
    out_g[...] = total[:, :D]
    q_g[...] = total[:16, D : 2 * D]
    k_g[...] = total[:16, 2 * D : 3 * D]
    v_g[...] = total[16:, D : 2 * D]
    o_g[...] = total[16:, 2 * D : 3 * D]
    in_g[:, E : E + D] = total[:16, 3 * D :]
    in_g[:, E + D :] = total[16:, 3 * D :]
    total = total_of(u_ins)
    in_g[:, :E] = total[:, :E]
    for q in range(8):
        rows[16 * q : 16 * q + 16, :] = total[:, E + 32 * q : E + 32 * q + 32]
    x_g[...] = rows[ROW_X : ROW_X + 64, :].T
    dt_g[...] = rows[ROW_DT : ROW_DT + RANK, :]
    a_g[...] = rows[ROW_A : ROW_A + NS, :]
    cw_g[...] = rows[ROW_CW : ROW_CW + KW, :]
    cb_g[...] = rows[ROW_CB : ROW_CB + 1, :]
    db_g[...] = rows[ROW_DB : ROW_DB + 1, :]
    sk_g[...] = rows[ROW_SK : ROW_SK + 1, :]
    g1_g[...] = rows[ROW_G1 : ROW_G1 + 1, :16]
    g2_g[...] = rows[ROW_G2 : ROW_G2 + 1, :16]


def join_kernel(counts, *refs):
    ins, outs, sems = refs[: sum(counts)], refs[sum(counts) : -1], refs[-1]
    at = 0
    for i, count in enumerate(counts):
        rows = outs[i].shape[0] // count
        for k in range(count):
            pltpu.make_async_copy(ins[at + k], outs[i].at[pl.ds(k * rows, rows), :], sems.at[i]).start()
        at += count
    for i, out in enumerate(outs):
        wait_whole(out, sems.at[i])


def join(groups, after=()):
    counts = [len(group) for group in groups]
    outs = [((group[0].shape[0] * len(group), group[0].shape[1]), group[0].dtype) for group in groups]
    return run(
        functools.partial(join_kernel, counts), [], outs, [pltpu.SemaphoreType.DMA((len(groups),))],
        raw=[part for group in groups for part in group], after=after)


def spread_out(value, stage):
    return [value] + [send(value, mask) for mask in stage[1:]]


def cut_one_kernel(keep, got, a_keep, a_give, b_keep, b_give):
    half, quarter, cols = keep.shape[0] // 2, keep.shape[0] // 4, keep.shape[1] // 2
    add = lambda rows, lanes: (keep[rows, lanes].astype(F32) + got[rows, lanes].astype(F32)).astype(BF16)
    left, right = slice(0, cols), slice(cols, 2 * cols)
    a_keep[...] = add(slice(0, half), left)
    a_give[...] = add(slice(half, 2 * half), left)
    for i in range(2):
        b_keep[i * quarter : (i + 1) * quarter, :] = add(slice(2 * i * quarter, (2 * i + 1) * quarter), right)
        b_give[i * quarter : (i + 1) * quarter, :] = add(slice((2 * i + 1) * quarter, (2 * i + 2) * quarter), right)


def cut_two_kernel(a_own, a_got, b_own, b_got, a_keep, a_give, b_keep, b_give):
    rows = a_own.shape[0] // 2
    for own, got, keep, give in ((a_own, a_got, a_keep, a_give), (b_own, b_got, b_keep, b_give)):
        for out, part in ((keep, slice(0, rows)), (give, slice(rows, 2 * rows))):
            out[...] = (own[part, :].astype(F32) + got[part, :].astype(F32)).astype(BF16)


def add_rows(out, rows, ins, cols=slice(None), to=slice(None)):
    total = ins[0][rows, cols].astype(F32)
    for other in ins[1:]:
        total = total + other[rows, cols].astype(F32)
    out[:, to] = total.astype(out.dtype)


def cut_three_kernel(u_own, u_got, a_own, a_got, b_own, b_got, u_0, u_1, u_2, u_3, keep, give):
    rows = u_0.shape[0]
    for i, out in enumerate((u_0, u_1, u_2, u_3)):
        add_rows(out, slice(i * rows, (i + 1) * rows), (u_own, u_got))
    rows, cols = keep.shape[0], a_own.shape[1]
    for i, out in enumerate((keep, give)):
        part = slice(i * rows, (i + 1) * rows)
        add_rows(out, part, (a_own, a_got), to=slice(0, cols))
        add_rows(out, part, (b_own, b_got), to=slice(cols, 2 * cols))


def cut_four_kernel(u_own, u_a, u_b, u_c, own, got, u_0, u_1, u_2, u_3, keep, give):
    rows = u_0.shape[0]
    for i, out in enumerate((u_0, u_1, u_2, u_3)):
        add_rows(out, slice(i * rows, (i + 1) * rows), (u_own, u_a, u_b, u_c))
    rows = keep.shape[0]
    for i, out in enumerate((keep, give)):
        add_rows(out, slice(i * rows, (i + 1) * rows), (own, got))


def body(plan, *args):
    (tokens, mixer_gain, in_proj, conv_weight, conv_bias, x_proj, dt_proj, dt_bias, a_log, d_skip, out_proj,
     attn_gain, w_query, w_key, w_value, w_output, cotangent) = args
    count = tokens.shape[1]
    tok0, cot0 = tokens.reshape(count, D), cotangent.reshape(count, D)
    chunks = plan.chunks
    devices = plan.dp * plan.ctx
    share, width = E // devices, D // devices
    if plan.fast:
        masks = FULL_MASKS
        home = [(s * 8 + c, plan.place(s, c)) for s in range(4) for c in range(8)]
        tok = lax.ppermute(tok0, ALL, home)
        halo = lax.ppermute(
            tok0[count - HALO :], ALL, [(s * 8 + c, plan.place(s, c + 1)) for s in range(4) for c in range(7)]
        )
        raw = [in_proj, x_proj, dt_proj, a_log.T, conv_weight.T, conv_bias[None], dt_bias[None], d_skip[None],
               mixer_gain[None], attn_gain[None], out_proj, w_query, w_key, w_value, w_output]
        pack_one, pack_two = run(
            pack_kernel, [], [((16, 2 * E + 256), BF16), ((32, 3 * D), BF16)],
            [pltpu.VMEM((SMALL_ROWS, 32), F32)] + [pltpu.VMEM(value.shape, F32) for value in raw]
            + [pltpu.SemaphoreType.DMA((len(raw),))], far=raw, limit=60)
        one, two, cot = join([[pack_one, send(pack_one, 4)], [pack_two], [cot0]], [tok, halo])
        two_far = send(two, 4)
        cot = lax.ppermute(cot, ALL, home)
        one, two = join([[one, send(one, 2)], [two, two_far]], [cot])
        two_far = send(two, 2)
        one, two = join([spread_out(one, XY_MASKS), [two, two_far]])
        one = [one, send(one, CORE)]
        near_two = spread_out(two, XY_MASKS)
    else:
        masks = tuple(range(BLOCKS))
        tok, cot = tok0, cot0
        halo = lax.ppermute(tok0[count - HALO :], "ctx", [(c, c + 1) for c in range(chunks - 1)])
        smalls = jnp.concatenate(
            [x_proj.T, dt_proj, a_log.T, conv_weight.T, conv_bias[None], dt_bias[None], d_skip[None],
             jnp.pad(mixer_gain, (0, share - width))[None], jnp.pad(attn_gain, (0, share - width))[None],
             jnp.zeros((SMALL_ROWS - ROW_G2 - 1, share), F32)], axis=0).astype(BF16)
        small_all = lax.all_gather(smalls, ALL, axis=1, tiled=True)
        apart = lambda row: jnp.pad(
            small_all[row].reshape(devices, share)[:, :width].reshape(BLOCKS, 16), ((0, 0), (0, 16))).reshape(1, E)
        small_all = jnp.concatenate(
            [small_all[:ROW_G1], apart(ROW_G1), apart(ROW_G2), small_all[ROW_G2 + 1 :]], axis=0)
        small_all = small_all.reshape(8, 16, BLOCKS, 32).transpose(2, 1, 0, 3).reshape(BLOCKS * 16, 256)
        whole = lambda value: lax.all_gather(value.astype(BF16), ALL, axis=0, tiled=True)
        one = [jnp.concatenate([whole(in_proj), small_all], axis=1)]
        out_all, q_all, k_all, v_all, o_all = (whole(w) for w in (out_proj, w_query, w_key, w_value, w_output))
        cut = lambda value: value.reshape(BLOCKS, 16, D)
        side = jnp.concatenate(
            [jnp.concatenate([cut(q_all), cut(k_all)], axis=2), jnp.concatenate([cut(v_all), cut(o_all)], axis=2)], axis=1)
        two = [jnp.concatenate([out_all.reshape(BLOCKS, 32, D), side], axis=2).reshape(BLOCKS * 32, 3 * D)]

    no = len(plan.grad_masks)
    rows3 = count * LG
    (normed, u_pre, z, conv, act, proj, sig, dt3, au3, a3, state, w_in, pm, gains) = run(
        functools.partial(front_kernel, plan, len(one), masks),
        [tok, halo],
        [((HALO + count, D), BF16), ((HALO + count, E), F32), ((count, E), F32), ((count, E), F32),
         ((count, E), BF16), ((count, 128), F32), ((count, E), F32), ((rows3, 128), F32), ((rows3, 128), F32),
         ((128, 128), F32), ((144, 128), BF16), ((D, 2 * E), BF16), ((SMALL_ROWS, E), F32), ((8, D), F32)],
        [pltpu.VMEM((NS, count, 128), F32), pltpu.VMEM((BLOCKS * 16, 256), BF16), pltpu.SemaphoreType.DMA((2,))],
        raw=one, us=6,
    )
    entry = exchange(plan, state, a3, True)
    if plan.fast:
        (held,) = join([near_two], [entry])
        two = [held, send(held, CORE)]
    rows_scratch = pltpu.VMEM((NS, count, 128), F32)
    pay, mamba, gated, middle, all_states, w_out, w_qk, w_vo = run(
        functools.partial(mid_kernel, plan, len(two), masks),
        [tok, dt3, au3, proj, a3, z, pm, gains, cot, entry],
        [((HEADS * count, 4 * HDIM), BF16), ((count, E), F32), ((count, E), BF16), ((count, D), F32),
         (((count + 1) * 128, 128), F32), ((E, D), BF16), ((D, 2 * D), BF16), ((D, 2 * D), BF16)],
        [pltpu.VMEM((rows3, 128), F32), rows_scratch, rows_scratch, pltpu.SemaphoreType.DMA((3,))],
        raw=two, us=6,
    )
    got = attend(plan, pay, count)
    (att, gq, gk, gv, grad_middle, mix, gz, gy3, later, gain_grad_two) = run(
        functools.partial(turn_kernel, plan),
        [got, middle, cot, gains, z, mamba, dt3, proj, a3, w_out, w_qk, w_vo, state],
        [((count, D), BF16)] * 4 + [((count, D), F32), ((count, D), BF16), ((count, E), BF16), ((rows3, 128), F32),
                                    ((144, 128), BF16), ((1, D), F32)],
        [rows_scratch],
    )
    blocks = [len(masks_of) for masks_of in plan.grad_masks]
    result, *one_grads = run(
        functools.partial(weights_kernel, plan, no),
        [att, gq, gk, gv, mix, gated, middle, gains, cot, w_vo, normed, gz],
        [((count, D), BF16)] + [((n * 32, 4 * D), BF16) for n in blocks],
        [pltpu.VMEM((D, D), F32), pltpu.VMEM((E, D), F32), pltpu.VMEM((D, E), F32)],
    )
    leaving = exchange(plan, later, a3, False)
    one_parts = []
    if plan.fast:
        result = lax.ppermute(result, ALL, [(b, a) for a, b in home])
        rows = blocks[0] * 32
        one_parts = run(
            cut_one_kernel, [one_grads[0], send(one_grads[1], CORE)], [((rows // 2, 2 * D), BF16)] * 4, after=[leaving, result])
    small_grads, gu = run(
        functools.partial(back_kernel, plan),
        [dt3, au3, gy3, a3, proj, pm, all_states, sig, act, conv, u_pre, leaving],
        [((SMALL_ROWS, E), F32), ((HALO + count, E), BF16)],
        [rows_scratch, rows_scratch,
         pltpu.VMEM((count * 128, 128), F32), pltpu.VMEM((rows3, 128), F32), pltpu.VMEM((rows3, 128), F32),
         pltpu.VMEM((128, 128), F32), pltpu.VMEM((8, 128), F32), pltpu.VMEM((count, 128), F32),
         pltpu.VMEM((count + 2 * HALO, E), F32)],
        limit=32, after=one_parts[:1], us=11,
    )
    if plan.fast:
        a_keep, a_give, b_keep, b_give = one_parts
        one_parts = run(
            cut_two_kernel, [a_keep, send(a_give, 16), b_keep, send(b_give, 1)], [((rows // 4, 2 * D), BF16)] * 4,
            after=[gu])
    *two_grads, own, before = run(
        functools.partial(last_kernel, plan, no),
        [tok, halo, gains, gu, gz, grad_middle, w_in, normed, small_grads, gain_grad_two],
        [((n * 16, E + 256), BF16) for n in blocks] + [((count, D), BF16), ((HALO, D), BF16)],
        [pltpu.VMEM((D, E), F32), pltpu.VMEM((SMALL_ROWS, E), F32)], after=one_parts[:1],
    )
    if plan.fast:
        away = [(b, a) for a, b in home]
        grad_tok = lax.ppermute(own, ALL, away)
        tail = lax.ppermute(
            before, ALL, [(plan.place(s, c + 1), s * 8 + c) for s in range(4) for c in range(7)])
        a_keep, a_give, b_keep, b_give = one_parts
        sends = lambda parts, stage: [parts[0]] + [send(part, mask) for part, mask in zip(parts[1:], stage[1:])]
        n = blocks[0]
        *u_parts, keep, give = run(
            cut_three_kernel, [two_grads[0], send(two_grads[1], CORE), a_keep, send(a_give, 1), b_keep, send(b_give, 16)],
            [((n * 4, E + 256), BF16)] * 4 + [((n * 4, 4 * D), BF16)] * 2, after=[grad_tok])
        *u_parts, keep, give = run(
            cut_four_kernel, [*sends(u_parts, XY_MASKS), keep, send(give, 2)],
            [((n, E + 256), BF16)] * 4 + [((n * 2, 4 * D), BF16)] * 2, after=[tail])
        out_g, q_g, k_g, v_g, o_g, in_g, x_g, dt_g, a_g, cw_g, cb_g, db_g, sk_g, g1_g, g2_g = run(
            finish_kernel, [*sends(u_parts, Z_MASKS), keep, send(give, 4)],
            [((32, D), F32)] + [((16, D), F32)] * 4
            + [((16, 2 * E), F32), ((32, 64), F32), ((32, 32), F32), ((NS, 32), F32), ((KW, 32), F32)]
            + [((1, 32), F32)] * 3 + [((1, 16), F32)] * 2,
            [pltpu.VMEM((SMALL_ROWS, 32), F32)], final=True)
        a_g, cw_g = a_g.T, cw_g.T
        vectors = [value[0] for value in (cb_g, db_g, sk_g, g1_g, g2_g)]
    else:
        grad_tok = own
        tail = lax.ppermute(before, "ctx", [(c + 1, c) for c in range(chunks - 1)])
        scatter = lambda value, dim=0: lax.psum_scatter(value.astype(F32), ALL, scatter_dimension=dim, tiled=True)
        blocks_one = one_grads[0].reshape(BLOCKS, 32, 4 * D)
        part = lambda row, rows, col: scatter(blocks_one[:, row : row + rows, col * D : (col + 1) * D].reshape(-1, D))
        out_g, q_g, k_g, v_g, o_g = part(0, 32, 0), part(0, 16, 1), part(0, 16, 2), part(16, 16, 1), part(16, 16, 2)
        in_g = jnp.concatenate([scatter(two_grads[0][:, :E]), part(0, 16, 3), part(16, 16, 3)], axis=1)
        small = two_grads[0][:, E:].reshape(BLOCKS, 16, 8, 32).transpose(2, 1, 0, 3).reshape(SMALL_ROWS, E)
        close = lambda row: scatter(small[row].reshape(BLOCKS, 32)[:, :16].reshape(D))
        g1, g2 = close(ROW_G1), close(ROW_G2)
        mine = scatter(small, 1)
        x_g, dt_g, a_g, cw_g = (
            mine[ROW_X : ROW_X + 64].T, mine[ROW_DT : ROW_DT + RANK], mine[ROW_A : ROW_A + NS].T, mine[ROW_CW : ROW_CW + KW].T)
        vectors = [mine[ROW_CB], mine[ROW_DB], mine[ROW_SK], g1, g2]
    last = (grad_tok[count - HALO :].astype(F32) + tail.astype(F32)).astype(BF16)
    grad_tok = jnp.concatenate([grad_tok[: count - HALO], last], axis=0)
    cb_v, db_v, sk_v, g1_v, g2_v = vectors
    return (
        result[None], grad_tok[None], g1_v, in_g, cw_g, cb_v, x_g, dt_g, db_v, a_g, sk_v, out_g, g2_v, q_g, k_g, v_g, o_g,
    )


def attend(plan, pay, count):
    if plan.chunks == HEADS:
        held = plan.swap(pay)
        length = held.shape[0]
        half = pltpu.VMEM((length, HDIM), BF16)
        flat = pltpu.VMEM((HDIM, length), BF16)
        wide = pltpu.VMEM((length, HDIM), F32)
        (back,) = run(
            attention_kernel, [held], [((length, 4 * HDIM), BF16)], [half] * 4 + [flat] * 2 + [wide] * 2, us=4
        )
        return plan.swap(back)
    parts = pay.reshape(HEADS, count, 4, HDIM)
    query, key, value, grad = (parts[:, :, i] for i in range(4))
    key, value = (lax.all_gather(part, "ctx", axis=1, tiled=True) for part in (key, value))
    query_at = lax.axis_index("ctx") * count + jnp.arange(count)
    allowed = jnp.arange(key.shape[1])[None, :] <= query_at[:, None]
    scale = HDIM**-0.5
    dots = functools.partial(jnp.einsum, preferred_element_type=F32)
    scores = jnp.where(allowed, dots("hqd,hkd->hqk", query, key) * scale, -1e30)
    soft = jax.nn.softmax(scores, axis=-1)
    soft_low = soft.astype(BF16)
    grad_p = dots("hqd,hkd->hqk", grad, value)
    grad_s = (soft * (grad_p - jnp.sum(soft * grad_p, axis=-1, keepdims=True))).astype(BF16)
    raw = dots("hqk,hkd->hqd", soft_low, value).astype(BF16)
    grad_q = (dots("hqk,hkd->hqd", grad_s, key) * scale).astype(BF16)
    grads = (dots("hqk,hqd->hkd", grad_s, query) * scale, dots("hqk,hqd->hkd", soft_low, grad))
    grad_k, grad_v = (
        lax.psum_scatter(part.astype(BF16), "ctx", scatter_dimension=1, tiled=True) for part in grads
    )
    return jnp.concatenate([raw, grad_q, grad_k, grad_v], axis=-1).reshape(HEADS * count, 4 * HDIM)


def solution(mesh):
    plan = Plan(mesh)
    split, rows, cols = P(ALL), P(ALL, None), P(None, ALL)
    acts = P("dp", "ctx", None)
    return jax.shard_map(
        functools.partial(body, plan),
        mesh=mesh,
        in_specs=(acts, split, rows, rows, split, rows, cols, split, rows, split, rows, split, rows, rows, rows, rows, acts),
        out_specs=(acts, acts, split, rows, rows, split, rows, cols, split, rows, split, rows, split, rows, rows, rows, rows),
        check_vma=False,
    )
```

```python
import functools

import jax
import jax.numpy as jnp
from jax import lax
from jax.experimental import pallas as pl
from jax.experimental.pallas import tpu as pltpu
from jax.sharding import PartitionSpec as P

D = 512
E = 1024
NS = 16
RANK = 32
KW = 4
HEADS = 8
HDIM = 64
LG = 8
HALO = 16
BLOCKS = 32
ALL = ("dp", "ctx")
EPS = 1e-05
LOG2E = 1.4426950408889634
LN2 = 0.6931471805599453
F32 = jnp.float32
BF16 = jnp.bfloat16
VM = pl.BlockSpec(memory_space=pltpu.VMEM)

Z_MASKS = (0, 4, 2, 6)
XY_MASKS = (0, 1, 16, 17)
CORE = 8
HALF_MASKS = tuple(xy | zz for xy in XY_MASKS for zz in Z_MASKS)
FULL_MASKS = HALF_MASKS + tuple(mask | CORE for mask in HALF_MASKS)
CHUNK_MASKS = tuple((16 if c & 1 else 0) | (1 if c & 2 else 0) | (8 if c & 4 else 0) for c in range(8))

ROW_X = 0
ROW_DT = 64
ROW_A = 96
ROW_CW = 112
ROW_CB = 116
ROW_DB = 117
ROW_SK = 118
ROW_G1 = 119
ROW_G2 = 120
SMALL_ROWS = 128


ANY = pl.BlockSpec(memory_space=pl.ANY)
FAR = pl.BlockSpec(memory_space=pltpu.HBM)
WHOLE = pl.BlockSpec()


def run(kernel, ins, outs, scratch=(), limit=12, raw=(), far=(), after=(), final=False, us=2):
    first, count = len(ins) + len(raw) + len(far), len(after)

    def inner(*refs):
        kernel(*refs[:first], *refs[first + count :])

    return pl.pallas_call(
        inner,
        out_shape=[jax.ShapeDtypeStruct(shape, dtype) for shape, dtype in outs],
        in_specs=[VM] * len(ins) + [ANY] * len(raw) + [FAR] * len(far) + [ANY] * count,
        out_specs=[WHOLE if final else VM] * len(outs),
        scratch_shapes=list(scratch),
        compiler_params=pltpu.CompilerParams(vmem_limit_bytes=limit * 2**20),
        cost_estimate=pl.CostEstimate(flops=int(us * 1e3), bytes_accessed=int(us * 3e3), transcendentals=0),
    )(*ins, *raw, *far, *after)


def nn(left, right):
    return lax.dot_general(left, right, (((1,), (0,)), ((), ())), preferred_element_type=F32)


def nt(left, right):
    return lax.dot_general(left, right, (((1,), (1,)), ((), ())), preferred_element_type=F32)


def tn(left, right):
    return lax.dot_general(left, right, (((0,), (0,)), ((), ())), preferred_element_type=F32)


def sigmoid(value):
    return 1.0 / (1.0 + jnp.exp(-value))


class Plan:
    def __init__(self, mesh):
        self.dp, self.ctx = mesh.shape["dp"], mesh.shape["ctx"]
        self.fast = (self.dp, self.ctx) == (4, 8)
        self.chunks = self.ctx
        if self.fast:
            self.grad_masks = (FULL_MASKS[:16], FULL_MASKS[16:])
        else:
            self.grad_masks = (tuple(range(BLOCKS)),)

    def place(self, seq, chunk):
        return CHUNK_MASKS[chunk] | ((0, 2, 1, 3)[seq] << 1)

    def me(self):
        if self.fast:
            return lax.axis_index("dp") * 8 + lax.axis_index("ctx")
        return 0

    def chunk(self):
        if self.fast:
            lin = lax.axis_index("dp") * 8 + lax.axis_index("ctx")
            return ((lin >> 4) & 1) + (lin & 1) * 2 + ((lin >> 3) & 1) * 4
        return lax.axis_index("ctx")

    def swap(self, value):
        if self.fast:
            groups = [[self.place(s, c) for c in range(8)] for s in range(4)]
            return lax.all_to_all(value, ALL, 0, 0, tiled=True, axis_index_groups=groups)
        return lax.all_to_all(value, "ctx", 0, 0, tiled=True)


def send(value, mask):
    return lax.ppermute(value, ALL, [(i, i ^ mask) for i in range(32)])


def start_blocks(target, pieces, masks, me, sem, row_in, rows, first, cols, to=0):
    per_piece = len(masks) // len(pieces)
    height = pieces[0].shape[0] // per_piece
    for i, piece in enumerate(pieces):
        for k in range(per_piece):
            block = me ^ masks[i * per_piece + k]
            pltpu.make_async_copy(
                piece.at[pl.ds(k * height + row_in, rows), pl.ds(first, cols)],
                target.at[pl.ds(pl.multiple_of(block * rows, 16), rows), pl.ds(to, cols)],
                sem,
            ).start()


def wait_whole(target, sem):
    pltpu.make_async_copy(target, target, sem).wait()


def swap_blocks(value, me):
    rows, lanes = value.shape
    for bit in (16, 8, 4):
        half = bit * 32
        parts = [value[:, i : i + half] for i in range(0, lanes, half)]
        other = jnp.concatenate([parts[i ^ 1] for i in range(len(parts))], axis=1)
        value = jnp.where((me & bit) != 0, other, value)
    groups = []
    odd = (lax.broadcasted_iota(jnp.int32, (rows, 128), 1) & 32) != 0
    for i in range(0, lanes, 128):
        part = value[:, i : i + 128]
        part = jnp.where((me & 2) != 0, pltpu.roll(part, 64, 1), part)
        other = jnp.where(odd, pltpu.roll(part, 32, 1), pltpu.roll(part, 96, 1))
        groups.append(jnp.where((me & 1) != 0, other, part))
    return jnp.concatenate(groups, axis=1)


def pack_kernel(in_proj, x_proj, dt_proj, a_log, conv_w, conv_b, dt_bias, d_skip, gain_one, gain_two,
                out_proj, w_q, w_k, w_v, w_o, one, two, rows, *rest):
    (b_in, b_x, b_dt, b_a, b_cw, b_cb, b_db, b_sk, b_g1, b_g2, b_out, b_q, b_k, b_v, b_o, sems) = rest
    copies = [
        pltpu.make_async_copy(src, dst, sems.at[i])
        for i, (src, dst) in enumerate(
            zip((in_proj, x_proj, dt_proj, a_log, conv_w, conv_b, dt_bias, d_skip, gain_one, gain_two, out_proj, w_q,
                 w_k, w_v, w_o),
                (b_in, b_x, b_dt, b_a, b_cw, b_cb, b_db, b_sk, b_g1, b_g2, b_out, b_q, b_k, b_v, b_o))
        )
    ]
    for copy in copies:
        copy.start()
    for copy in copies:
        copy.wait()
    one[:, :E] = b_in[:, :E].astype(BF16)
    two[:16, 3 * D :] = b_in[:, E : E + D].astype(BF16)
    two[16:, 3 * D :] = b_in[:, E + D :].astype(BF16)
    two[:, :D] = b_out[...].astype(BF16)
    two[:16, D : 2 * D] = b_q[...].astype(BF16)
    two[:16, 2 * D : 3 * D] = b_k[...].astype(BF16)
    two[16:, D : 2 * D] = b_v[...].astype(BF16)
    two[16:, 2 * D : 3 * D] = b_o[...].astype(BF16)
    rows[...] = jnp.zeros_like(rows)
    rows[ROW_X : ROW_X + 64, :] = b_x[...].T
    rows[ROW_DT : ROW_DT + RANK, :] = b_dt[...]
    rows[ROW_A : ROW_A + NS, :] = b_a[...]
    rows[ROW_CW : ROW_CW + KW, :] = b_cw[...]
    rows[ROW_CB : ROW_CB + 1, :] = b_cb[...]
    rows[ROW_DB : ROW_DB + 1, :] = b_db[...]
    rows[ROW_SK : ROW_SK + 1, :] = b_sk[...]
    rows[ROW_G1 : ROW_G1 + 1, :16] = b_g1[...]
    rows[ROW_G2 : ROW_G2 + 1, :16] = b_g2[...]
    one[:, E:] = jnp.concatenate([rows[16 * q : 16 * q + 16, :] for q in range(8)], axis=1).astype(BF16)


def join_smalls(target, smalls, masks, me):
    place = {mask: p for p, mask in enumerate(masks)}
    for q in range(8):
        for g in range(LG):
            target[16 * q : 16 * q + 16, 128 * g : 128 * g + 128] = jnp.concatenate(
                [smalls[16 * place[m] : 16 * place[m] + 16, 32 * q : 32 * q + 32].astype(F32) for m in range(4 * g, 4 * g + 4)],
                axis=1,
            )
    target[...] = swap_blocks(target[...], me)


def gain_row(pm, row):
    return jnp.concatenate([pm[row : row + 1, 32 * s : 32 * s + 16] for s in range(BLOCKS)], axis=1)


def spread(target, source):
    count = source.shape[0]
    for s in range(LG):
        target[pl.ds(s, count, stride=LG), :] = source[:, s * 128 : (s + 1) * 128]


def gathered(source, count):
    return jnp.concatenate([source[pl.ds(s, count, stride=LG), :] for s in range(LG)], axis=1)


def broadcast_rows(target, proj, first):
    for n in range(NS):
        target[n] = jnp.broadcast_to(proj[:, first + n : first + n + 1], target.shape[1:])


def at8(ref, index):
    return ref[pl.ds(pl.multiple_of(index * 8, 8), 8), :]


def front_kernel(plan, np_, masks, tok, halo, *refs):
    pieces = refs[:np_]
    (normed, u_out, conv_out, act_out, proj_out, sig_out, dt3, au3, a3, state, weight, pm, gains, bx, cx, smalls, sems) = refs[np_:]
    me = plan.me()
    start_blocks(weight, pieces, masks, me, sems.at[0], 0, 16, 0, E)
    height = smalls.shape[0] // np_
    for i, piece in enumerate(pieces):
        pltpu.make_async_copy(
            piece.at[:, pl.ds(E, 256)], smalls.at[pl.ds(i * height, height), :], sems.at[1]).start()
    wait_whole(smalls, sems.at[1])
    join_smalls(pm, smalls, masks, me)
    gain = gain_row(pm, ROW_G1)
    gains[0:1, :] = gain
    gains[1:2, :] = gain_row(pm, ROW_G2)
    tokens = tok.shape[0]
    x = jnp.concatenate([halo[...].astype(F32), tok[...].astype(F32)], axis=0)
    r = lax.rsqrt(jnp.mean(x * x, axis=-1, keepdims=True) + EPS)
    low = (x * r * gain).astype(BF16)
    normed[...] = low
    wait_whole(weight, sems.at[0])
    u_out[...] = nn(low, weight[...])
    conv = pm[ROW_CB : ROW_CB + 1, :]
    for k in range(KW):
        conv = conv + pm[ROW_CW + k : ROW_CW + k + 1, :] * u_out[HALO - 3 + k : HALO - 3 + k + tokens, :]
    conv_out[...] = conv
    act = (conv * sigmoid(conv)).astype(BF16)
    act_out[...] = act
    proj = nt(act, pm[ROW_X : ROW_X + 64, :].astype(BF16))
    proj_out[:, :64] = proj
    proj_out[:, 64:] = jnp.zeros((tokens, 64), F32)
    pre = nn(proj[:, :RANK].astype(BF16), pm[ROW_DT : ROW_DT + RANK, :].astype(BF16)) + pm[ROW_DB : ROW_DB + 1, :]
    sig_out[...] = sigmoid(pre)
    step = jnp.maximum(pre, 0.0) + jnp.log1p(jnp.exp(-jnp.abs(pre)))
    spread(dt3, step)
    spread(au3, act.astype(F32))
    spread(a3, -LOG2E * jnp.exp(pm[ROW_A : ROW_A + NS, :]))
    broadcast_rows(bx, proj, RANK)
    broadcast_rows(cx, proj, RANK + NS)
    decay = [a3[8 * n : 8 * n + 8, :] for n in range(NS)]

    def advance(t, carried):
        held, total = carried
        size = at8(dt3, t)
        drive = size * at8(au3, t)
        held = tuple(
            jnp.exp2(size * decay[n]) * held[n] + drive * bx[n, pl.ds(t, 1), :] for n in range(NS)
        )
        return held, total + size

    zero = jnp.zeros((8, 128), F32)
    held, total = lax.fori_loop(0, tokens, advance, ((zero,) * NS, zero), unroll=4)
    state[...] = jnp.concatenate([*held, total, zero], axis=0).astype(BF16)


def combine_kernel(plan, forward, states, a3, entry, states_f):
    states_f[...] = states[...].astype(F32)
    decay = [a3[8 * n : 8 * n + 8, :] for n in range(NS)]
    zero = jnp.zeros((8, 128), F32)

    def combine(i, held):
        base = (i if forward else plan.chunks - 1 - i) * 144
        total = states_f[pl.ds(pl.multiple_of(base + 128, 8), 8), :]
        return tuple(
            jnp.exp2(total * decay[n]) * held[n] + states_f[pl.ds(pl.multiple_of(base + 8 * n, 8), 8), :]
            for n in range(NS)
        )

    count = plan.chunk() if forward else plan.chunks - 1 - plan.chunk()
    held = lax.fori_loop(0, count, combine, (zero,) * NS)
    entry[...] = jnp.concatenate([*held, zero, zero], axis=0)


def merge_kernel(plan, step, forward, own, other, before, a3, group, entry):
    later = ((plan.chunk() >> step) & 1) == (1 if forward else 0)
    mine, theirs = own[...].astype(F32), other[...].astype(F32)
    first, second = jnp.where(later, theirs, mine), jnp.where(later, mine, theirs)
    decay = a3[...]
    spread_total = lambda value: jnp.concatenate([value[128:136, :]] * NS, axis=0)
    joint = jnp.exp2(spread_total(second) * decay) * first[:128, :] + second[:128, :]
    group[:128, :] = joint.astype(BF16)
    group[128:, :] = (first[128:, :] + second[128:, :]).astype(BF16)
    held = before[...]
    inner = held[:128, :] + jnp.exp2(spread_total(held) * decay) * theirs[:128, :]
    entry[:128, :] = jnp.where(later, inner, held[:128, :])
    entry[128:, :] = jnp.where(later, held[128:, :] + theirs[128:, :], held[128:, :])


def exchange(plan, state, a3, forward, beside=lambda step, entry: []):
    if plan.fast:
        group, entry, firsts = state, jnp.zeros((144, 128), F32), []
        for step in range(3):
            other = send(group, CHUNK_MASKS[1 << step])
            group, entry = run(
                functools.partial(merge_kernel, plan, step, forward), [group, other, entry, a3],
                [((144, 128), BF16), ((144, 128), F32)], after=beside(step, entry if step else group))
            firsts.append(entry)
        return entry, firsts
    states = lax.all_gather(state, "ctx", axis=0, tiled=True)
    return run(
        functools.partial(combine_kernel, plan, forward), [states, a3], [((144, 128), F32)],
        [pltpu.VMEM((144 * plan.chunks, 128), F32)])[0], []


def mid_kernel(plan, nb, masks, *refs):
    tok, dt3, au3, a3, normed, pm, gains, cot, entry, bx, cx = refs[:11]
    pieces = refs[11 : 11 + nb]
    pay, mamba, gated_out, middle_out, all_states, w_out, w_qk, w_vo, w_z, z_out, y3, sems = refs[11 + nb :]
    tokens = tok.shape[0]
    me = plan.me()
    start_blocks(w_z, pieces, masks, me, sems.at[3], 0, 16, 3 * D, D)
    start_blocks(w_z, pieces, masks, me, sems.at[3], 16, 16, 3 * D, D, D)
    start_blocks(w_out, pieces, masks, me, sems.at[0], 0, 32, 0, D)
    start_blocks(w_qk, pieces, masks, me, sems.at[1], 0, 16, D, 2 * D)
    start_blocks(w_vo, pieces, masks, me, sems.at[2], 16, 16, D, 2 * D)
    decay = [a3[8 * n : 8 * n + 8, :] for n in range(NS)]
    held = tuple(entry[8 * n : 8 * n + 8, :] for n in range(NS))
    all_states[:128, :] = entry[:128, :]

    def advance(t, held):
        size = at8(dt3, t)
        drive = size * at8(au3, t)
        base = pl.multiple_of(t * 128 + 128, 128)
        held = tuple(
            jnp.exp2(size * decay[n]) * held[n] + drive * bx[n, pl.ds(t, 1), :] for n in range(NS)
        )
        for n in range(NS):
            all_states[pl.ds(base + 8 * n, 8), :] = held[n]
        y = held[0] * cx[0, pl.ds(t, 1), :]
        for n in range(1, NS):
            y = y + held[n] * cx[n, pl.ds(t, 1), :]
        y3[pl.ds(pl.multiple_of(t * 8, 8), 8), :] = y
        return held

    lax.fori_loop(0, tokens, advance, held, unroll=4)
    act = gathered(au3, tokens)
    y = gathered(y3, tokens) + pm[ROW_SK : ROW_SK + 1, :] * act
    mamba[...] = y
    wait_whole(w_z, sems.at[3])
    z = nn(normed[HALO:, :], w_z[...])
    z_out[...] = z
    gated = (y * (z * sigmoid(z))).astype(BF16)
    gated_out[...] = gated
    wait_whole(w_out, sems.at[0])
    wait_whole(w_qk, sems.at[1])
    wait_whole(w_vo, sems.at[2])
    middle = tok[...].astype(F32) + nn(gated, w_out[...])
    middle_out[...] = middle
    r = lax.rsqrt(jnp.mean(middle * middle, axis=-1, keepdims=True) + EPS)
    low = (middle * r * gains[1:2, :]).astype(BF16)
    quads = (
        nn(low, w_qk[:, :D]).astype(BF16),
        nn(low, w_qk[:, D:]).astype(BF16),
        nn(low, w_vo[:, :D]).astype(BF16),
        nt(cot[...], w_vo[:, D:]).astype(BF16),
    )
    for h in range(HEADS):
        for i, part in enumerate(quads):
            pay[h * tokens : (h + 1) * tokens, i * HDIM : (i + 1) * HDIM] = part[:, h * HDIM : (h + 1) * HDIM]


def attention_kernel(pay, back, q_s, k_s, v_s, g_s, kt, vt, dk, dv):
    length = pay.shape[0]
    rows = 256
    q_s[...] = pay[:, :HDIM]
    k_s[...] = pay[:, HDIM : 2 * HDIM]
    v_s[...] = pay[:, 2 * HDIM : 3 * HDIM]
    g_s[...] = pay[:, 3 * HDIM :]
    kt[...] = k_s[...].T
    vt[...] = v_s[...].T
    dk[...] = jnp.zeros_like(dk)
    dv[...] = jnp.zeros_like(dv)
    scale = HDIM**-0.5
    key_at = lax.broadcasted_iota(jnp.int32, (rows, rows), 0)
    query_at = lax.broadcasted_iota(jnp.int32, (rows, rows), 1)
    for i in range(length // rows):
        first, last = i * rows, (i + 1) * rows
        query = q_s[first:last, :]
        grad = g_s[first:last, :]
        scores = nt(k_s[:last, :], query) * scale
        diagonal = jnp.where(key_at <= query_at, scores[first:, :], -1e30)
        scores = diagonal if i == 0 else jnp.concatenate([scores[:first, :], diagonal], axis=0)
        expo = jnp.exp(scores - jnp.max(scores, axis=0, keepdims=True))
        soft = expo * (1.0 / jnp.sum(expo, axis=0, keepdims=True))
        soft_low = soft.astype(BF16)
        grad_p = nt(v_s[:last, :], grad)
        dot = jnp.sum(soft * grad_p, axis=0, keepdims=True)
        grad_s = (soft * (grad_p - dot)).astype(BF16)
        raw = nn(vt[:, :last], soft_low)
        grad_q = nn(kt[:, :last], grad_s) * scale
        back[first:last, :HDIM] = raw.T.astype(BF16)
        back[first:last, HDIM : 2 * HDIM] = grad_q.T.astype(BF16)
        dk[:last, :] += nn(grad_s, query)
        dv[:last, :] += nn(soft_low, grad)
    back[:, 2 * HDIM : 3 * HDIM] = (dk[...] * scale).astype(BF16)
    back[:, 3 * HDIM :] = dv[...].astype(BF16)


def turn_kernel(plan, got, middle, cot, gains, z_in, mamba, dt3, cx, a3, w_out, w_qk, w_vo, first,
                att, gq, gk, gv, grad_middle, mix, gz, gy3, state, gain_grad):
    tokens = middle.shape[0]
    for h in range(HEADS):
        for i, part in enumerate((att, gq, gk, gv)):
            part[:, h * HDIM : (h + 1) * HDIM] = got[h * tokens : (h + 1) * tokens, i * HDIM : (i + 1) * HDIM]
    grad_n = nt(gq[...], w_qk[:, :D]) + nt(gk[...], w_qk[:, D:]) + nt(gv[...], w_vo[:, :D])
    mid = middle[...]
    r = lax.rsqrt(jnp.mean(mid * mid, axis=-1, keepdims=True) + EPS)
    gain_grad[...] = jnp.sum(grad_n * mid * r, axis=0, keepdims=True)
    q = grad_n * gains[1:2, :]
    gm = cot[...].astype(F32) + r * q - mid * (r * r * r) * jnp.mean(q * mid, axis=-1, keepdims=True)
    grad_middle[...] = gm
    low = gm.astype(BF16)
    mix[...] = low
    grad_gated = nt(low, w_out[...])
    z = z_in[...]
    s = sigmoid(z)
    spread(gy3, grad_gated * (z * s))
    gz[...] = (grad_gated * mamba[...] * (s * (1.0 + z * (1.0 - s)))).astype(BF16)
    decay = [a3[8 * n : 8 * n + 8, :] for n in range(NS)]

    def retreat(i, carried):
        t = tokens - 1 - i
        size = at8(dt3, t)
        grad = at8(gy3, t)
        return tuple(
            jnp.exp2(size * decay[n]) * (carried[n] + grad * cx[n, pl.ds(t, 1), :]) for n in range(NS)
        )

    zero = jnp.zeros((8, 128), F32)
    carried = lax.fori_loop(0, tokens, retreat, (zero,) * NS, unroll=4)
    state[:128, :] = jnp.concatenate(carried, axis=0).astype(BF16)
    state[128:, :] = first[128:, :]


def pack_blocks(plan, outs, source, rows, height, row, first, col=0, cols=None):
    me = plan.me()
    cols = source.shape[1] if cols is None else cols
    for out, masks in zip(outs, plan.grad_masks):
        for k, mask in enumerate(masks):
            block = me ^ mask
            out[k * height + row : k * height + row + rows, first : first + cols] = source[
                pl.ds(pl.multiple_of(block * rows, 16), rows), col : col + cols
            ].astype(BF16)


def grad_c_kernel(gy3, all_states, grad_c):
    diagonal_sums(grad_c, 0, lambda rows: gy3[rows, :], all_states, 1)


def weights_kernel(plan, no, att, gq, gk, gv, mix, gated, middle, gains, cot, w_vo, normed, gz, *refs):
    result, outs = refs[0], refs[1 : 1 + no]
    small, large, wide = refs[1 + no :]
    mid = middle[...]
    result[...] = (mid + nn(att[...], w_vo[:, D:])).astype(BF16)
    r = lax.rsqrt(jnp.mean(mid * mid, axis=-1, keepdims=True) + EPS)
    low = (mid * r * gains[1:2, :]).astype(BF16)
    large[...] = tn(gated[...], mix[...])
    pack_blocks(plan, outs, large, 32, 32, 0, 0)
    small[...] = tn(low, gq[...])
    pack_blocks(plan, outs, small, 16, 32, 0, D)
    small[...] = tn(low, gk[...])
    pack_blocks(plan, outs, small, 16, 32, 0, 2 * D)
    small[...] = tn(low, gv[...])
    pack_blocks(plan, outs, small, 16, 32, 16, D)
    small[...] = tn(att[...], cot[...])
    pack_blocks(plan, outs, small, 16, 32, 16, 2 * D)
    wide[...] = tn(normed[HALO:, :], gz[...])
    pack_blocks(plan, outs, wide, 16, 32, 0, 3 * D, 0, D)
    pack_blocks(plan, outs, wide, 16, 32, 16, 3 * D, D, D)


def diagonal_sums(out, col, channels, held, offset, span=16):
    row_t = lax.broadcasted_iota(jnp.int32, (span, span * NS), 0)
    col_t = lax.broadcasted_iota(jnp.int32, (span, span * NS), 1) // NS
    pick = (
        lax.broadcasted_iota(jnp.int32, (span * NS, NS), 0) % NS
        == lax.broadcasted_iota(jnp.int32, (span * NS, NS), 1)
    ).astype(BF16)
    for block in range(out.shape[0] // span):
        total = jnp.zeros((span, span * NS), F32)
        for s in range(LG):
            held_rows = held[pl.ds((block * span + offset) * 128 + s, span * NS, stride=LG), :].astype(BF16)
            total = total + nt(channels(pl.ds(block * span * 8 + s, span, stride=LG)).astype(BF16), held_rows)
        own = jnp.where(row_t == col_t, total, 0.0).astype(BF16)
        out[block * span : (block + 1) * span, col : col + NS] = nn(own, pick)


def back_kernel(plan, dt3, au3, gy3, a3, proj, pm, all_states, sig, act, conv_in, u_in, leaving, bx, cx, grad_c,
                small_grads, gu_out, grads, gs3, ga3, gal, skip3, low_rank, padded):
    tokens = dt3.shape[0] // LG
    decay = [a3[8 * n : 8 * n + 8, :] for n in range(NS)]
    zero = jnp.zeros((8, 128), F32)
    spread(skip3, pm[ROW_SK : ROW_SK + 1, :])
    skip = skip3[...]

    carried = tuple(leaving[8 * n : 8 * n + 8, :] for n in range(NS))
    gal[...] = jnp.zeros_like(gal)

    def retreat(i, state):
        carried, skipped = state
        t = tokens - 1 - i
        size, value, grad = at8(dt3, t), at8(au3, t), at8(gy3, t)
        base = pl.multiple_of(t * 128, 128)
        from_b = zero
        from_a = zero
        fresh = []
        for n in range(NS):
            g = carried[n] + grad * cx[n, pl.ds(t, 1), :]
            grads[pl.ds(base + 8 * n, 8), :] = g
            w = jnp.exp2(size * decay[n]) * g
            q = w * all_states[pl.ds(base + 8 * n, 8), :]
            from_a = from_a + decay[n] * q
            from_b = from_b + g * bx[n, pl.ds(t, 1), :]
            gal[8 * n : 8 * n + 8, :] += size * q
            fresh.append(w)
        at = pl.ds(pl.multiple_of(t * 8, 8), 8)
        gs3[at, :] = from_a * LN2 + from_b * value
        ga3[at, :] = from_b * size + skip * grad
        return tuple(fresh), skipped + grad * value

    _, skipped = lax.fori_loop(0, tokens, retreat, (carried, zero), unroll=4)

    diagonal_sums(low_rank, RANK, lambda rows: dt3[rows, :] * au3[rows, :], grads, 0)
    low_rank[:, RANK + NS : RANK + 2 * NS] = grad_c[:, :NS]

    grad_pre = gathered(gs3, tokens) * sig[...]
    grad_pre_low = grad_pre.astype(BF16)
    low_rank[:, :RANK] = nt(grad_pre_low, pm[ROW_DT : ROW_DT + RANK, :].astype(BF16))
    projected = low_rank[:, :64].astype(BF16)
    small_grads[ROW_X : ROW_X + 64, :] = tn(projected, act[...])
    small_grads[ROW_DT : ROW_DT + RANK, :] = tn(proj[:, :RANK].astype(BF16), grad_pre_low)
    true_a = -jnp.exp(pm[ROW_A : ROW_A + NS, :])
    small_grads[ROW_A : ROW_A + NS, :] = gathered(gal, NS) * true_a
    small_grads[ROW_DB : ROW_DB + 1, :] = jnp.sum(grad_pre, axis=0, keepdims=True)
    skip3[...] = skipped
    small_grads[ROW_SK : ROW_SK + 1, :] = gathered(skip3, 1)
    small_grads[ROW_G1:, :] = jnp.zeros((SMALL_ROWS - ROW_G1, E), F32)
    conv = conv_in[...]
    s = sigmoid(conv)
    grad_act = gathered(ga3, tokens) + nn(projected, pm[ROW_X : ROW_X + 64, :].astype(BF16))
    grad_conv = grad_act * (s * (1.0 + conv * (1.0 - s)))
    small_grads[ROW_CB : ROW_CB + 1, :] = jnp.sum(grad_conv, axis=0, keepdims=True)
    for k in range(KW):
        small_grads[ROW_CW + k : ROW_CW + k + 1, :] = jnp.sum(
            grad_conv * u_in[HALO - 3 + k : HALO - 3 + k + tokens, :], axis=0, keepdims=True
        )
    padded[:HALO, :] = jnp.zeros((HALO, E), F32)
    padded[HALO : HALO + tokens, :] = grad_conv
    padded[HALO + tokens :, :] = jnp.zeros((HALO, E), F32)
    gu = jnp.zeros((HALO + tokens, E), F32)
    for k in range(KW):
        gu = gu + pm[ROW_CW + k : ROW_CW + k + 1, :] * padded[3 - k : 3 - k + HALO + tokens, :]
    gu_out[...] = gu.astype(BF16)


def last_kernel(plan, no, tok, halo, gains, gu, gz, grad_middle, w_u, w_z, normed, small_grads, gain_two, *refs):
    outs = refs[:no]
    own, before, large, spaced = refs[no:]
    me = plan.me()
    large[...] = tn(normed[...], gu[...])
    pack_blocks(plan, outs, large, 16, 16, 0, 0)
    x = jnp.concatenate([halo[...].astype(F32), tok[...].astype(F32)], axis=0)
    r = lax.rsqrt(jnp.mean(x * x, axis=-1, keepdims=True) + EPS)
    from_z = nt(gz[...], w_z[...])
    grad_n = nt(gu[...], w_u[...]) + jnp.concatenate([jnp.zeros((HALO, D), F32), from_z], axis=0)
    gain_one = jnp.sum(grad_n * x * r, axis=0, keepdims=True)
    q = grad_n * gains[0:1, :]
    base = r * q - x * (r * r * r) * jnp.mean(q * x, axis=-1, keepdims=True)
    own[...] = grad_middle[...] + base[HALO:, :]
    before[...] = base[:HALO, :]
    spaced[...] = small_grads[...]
    blank = jnp.zeros((1, 16), F32)
    for row, grad in ((ROW_G1, gain_one), (ROW_G2, gain_two[...])):
        spaced[row : row + 1, :] = jnp.concatenate(
            [part for s in range(BLOCKS) for part in (grad[:, 16 * s : 16 * s + 16], blank)], axis=1)
    spaced[...] = swap_blocks(spaced[...], me)
    for out, masks in zip(outs, plan.grad_masks):
        for k, m in enumerate(masks):
            out[16 * k : 16 * k + 16, E:] = jnp.concatenate(
                [spaced[16 * q : 16 * q + 16, 32 * m : 32 * m + 32] for q in range(8)], axis=1).astype(BF16)


def total_of(ins):
    total = ins[0][...].astype(F32)
    for other in ins[1:]:
        total = total + other[...].astype(F32)
    return total


def finish_kernel(*refs):
    (own, result), refs = refs[:2], refs[2:]
    u_ins, ins, (own_out, result_out), refs = refs[:4], refs[4:6], refs[6:8], refs[2:]
    own_out[...] = own[...]
    result_out[...] = result[...]
    out_g, q_g, k_g, v_g, o_g, in_g, x_g, dt_g, a_g, cw_g, cb_g, db_g, sk_g, g1_g, g2_g, rows = refs[6:]
    total = total_of(ins)
    out_g[...] = total[:, :D]
    q_g[...] = total[:16, D : 2 * D]
    k_g[...] = total[:16, 2 * D : 3 * D]
    v_g[...] = total[16:, D : 2 * D]
    o_g[...] = total[16:, 2 * D : 3 * D]
    in_g[:, E : E + D] = total[:16, 3 * D :]
    in_g[:, E + D :] = total[16:, 3 * D :]
    total = total_of(u_ins)
    in_g[:, :E] = total[:, :E]
    for q in range(8):
        rows[16 * q : 16 * q + 16, :] = total[:, E + 32 * q : E + 32 * q + 32]
    x_g[...] = rows[ROW_X : ROW_X + 64, :].T
    dt_g[...] = rows[ROW_DT : ROW_DT + RANK, :]
    a_g[...] = rows[ROW_A : ROW_A + NS, :]
    cw_g[...] = rows[ROW_CW : ROW_CW + KW, :]
    cb_g[...] = rows[ROW_CB : ROW_CB + 1, :]
    db_g[...] = rows[ROW_DB : ROW_DB + 1, :]
    sk_g[...] = rows[ROW_SK : ROW_SK + 1, :]
    g1_g[...] = rows[ROW_G1 : ROW_G1 + 1, :16]
    g2_g[...] = rows[ROW_G2 : ROW_G2 + 1, :16]


def join_kernel(counts, *refs):
    ins, outs, sems = refs[: sum(counts)], refs[sum(counts) : -1], refs[-1]
    at = 0
    for i, count in enumerate(counts):
        rows = outs[i].shape[0] // count
        for k in range(count):
            pltpu.make_async_copy(ins[at + k], outs[i].at[pl.ds(k * rows, rows), :], sems.at[i]).start()
        at += count
    for i, out in enumerate(outs):
        wait_whole(out, sems.at[i])


def join(groups, after=(), limit=12):
    counts = [len(group) for group in groups]
    outs = [((group[0].shape[0] * len(group), group[0].shape[1]), group[0].dtype) for group in groups]
    return run(
        functools.partial(join_kernel, counts), [], outs, [pltpu.SemaphoreType.DMA((len(groups),))],
        raw=[part for group in groups for part in group], after=after, limit=limit)


def spread_out(value, stage):
    return [value] + [send(value, mask) for mask in stage[1:]]


def cut_one_kernel(keep, got, a_keep, a_give, b_keep, b_give):
    half, quarter, cols = keep.shape[0] // 2, keep.shape[0] // 4, keep.shape[1] // 2
    add = lambda rows, lanes: (keep[rows, lanes].astype(F32) + got[rows, lanes].astype(F32)).astype(BF16)
    left, right = slice(0, cols), slice(cols, 2 * cols)
    a_keep[...] = add(slice(0, half), left)
    a_give[...] = add(slice(half, 2 * half), left)
    for i in range(2):
        b_keep[i * quarter : (i + 1) * quarter, :] = add(slice(2 * i * quarter, (2 * i + 1) * quarter), right)
        b_give[i * quarter : (i + 1) * quarter, :] = add(slice((2 * i + 1) * quarter, (2 * i + 2) * quarter), right)


def cut_two_kernel(a_own, a_got, b_own, b_got, a_keep, a_give, b_keep, b_give):
    rows = a_own.shape[0] // 2
    for own, got, keep, give in ((a_own, a_got, a_keep, a_give), (b_own, b_got, b_keep, b_give)):
        for out, part in ((keep, slice(0, rows)), (give, slice(rows, 2 * rows))):
            out[...] = (own[part, :].astype(F32) + got[part, :].astype(F32)).astype(BF16)


def add_rows(out, rows, ins, cols=slice(None), to=slice(None)):
    total = ins[0][rows, cols].astype(F32)
    for other in ins[1:]:
        total = total + other[rows, cols].astype(F32)
    out[:, to] = total.astype(out.dtype)


def add_tail(out, own, tail):
    rows = own.shape[0] - HALO
    out[:rows, :] = own[:rows, :].astype(BF16)
    out[rows:, :] = (own[rows:, :] + tail[...]).astype(BF16)


def cut_three_kernel(u_own, u_got, a_own, a_got, b_own, b_got, own, tail, own_out, u_0, u_1, u_2, u_3, keep, give):
    add_tail(own_out, own, tail)
    rows = u_0.shape[0]
    for i, out in enumerate((u_0, u_1, u_2, u_3)):
        add_rows(out, slice(i * rows, (i + 1) * rows), (u_own, u_got))
    rows, cols = keep.shape[0], a_own.shape[1]
    for i, out in enumerate((keep, give)):
        part = slice(i * rows, (i + 1) * rows)
        add_rows(out, part, (a_own, a_got), to=slice(0, cols))
        add_rows(out, part, (b_own, b_got), to=slice(cols, 2 * cols))


def cut_four_kernel(u_own, u_a, u_b, u_c, own, got, u_0, u_1, u_2, u_3, keep, give):
    rows = u_0.shape[0]
    for i, out in enumerate((u_0, u_1, u_2, u_3)):
        add_rows(out, slice(i * rows, (i + 1) * rows), (u_own, u_a, u_b, u_c))
    rows = keep.shape[0]
    for i, out in enumerate((keep, give)):
        add_rows(out, slice(i * rows, (i + 1) * rows), (own, got))


def body(plan, *args):
    (tokens, mixer_gain, in_proj, conv_weight, conv_bias, x_proj, dt_proj, dt_bias, a_log, d_skip, out_proj,
     attn_gain, w_query, w_key, w_value, w_output, cotangent) = args
    count = tokens.shape[1]
    tok0, cot0 = tokens.reshape(count, D), cotangent.reshape(count, D)
    chunks = plan.chunks
    devices = plan.dp * plan.ctx
    share, width = E // devices, D // devices
    if plan.fast:
        masks = FULL_MASKS
        home = [(s * 8 + c, plan.place(s, c)) for s in range(4) for c in range(8)]
        tok = lax.ppermute(tok0, ALL, home)
        halo = lax.ppermute(
            tok0[count - HALO :], ALL, [(s * 8 + c, plan.place(s, c + 1)) for s in range(4) for c in range(7)]
        )
        raw = [in_proj, x_proj, dt_proj, a_log.T, conv_weight.T, conv_bias[None], dt_bias[None], d_skip[None],
               mixer_gain[None], attn_gain[None], out_proj, w_query, w_key, w_value, w_output]
        pack_one, pack_two = run(
            pack_kernel, [], [((16, E + 256), BF16), ((32, 4 * D), BF16)],
            [pltpu.VMEM((SMALL_ROWS, 32), F32)] + [pltpu.VMEM(value.shape, F32) for value in raw]
            + [pltpu.SemaphoreType.DMA((len(raw),))], far=raw, limit=60)
        two_far = send(pack_two, 4)
        (one,) = join([[pack_one, send(pack_one, 4)]])
        cot = lax.ppermute(cot0, ALL, home)
        one, two = join([[one, send(one, 2)], [pack_two, two_far]], [tok, halo])
        two_far = send(two, 2)
        one, two = join([spread_out(one, XY_MASKS), [two, two_far]], [cot])
        one = [one, send(one, CORE)]
        near_two = spread_out(two, XY_MASKS)
    else:
        masks = tuple(range(BLOCKS))
        tok, cot = tok0, cot0
        halo = lax.ppermute(tok0[count - HALO :], "ctx", [(c, c + 1) for c in range(chunks - 1)])
        smalls = jnp.concatenate(
            [x_proj.T, dt_proj, a_log.T, conv_weight.T, conv_bias[None], dt_bias[None], d_skip[None],
             jnp.pad(mixer_gain, (0, share - width))[None], jnp.pad(attn_gain, (0, share - width))[None],
             jnp.zeros((SMALL_ROWS - ROW_G2 - 1, share), F32)], axis=0).astype(BF16)
        small_all = lax.all_gather(smalls, ALL, axis=1, tiled=True)
        apart = lambda row: jnp.pad(
            small_all[row].reshape(devices, share)[:, :width].reshape(BLOCKS, 16), ((0, 0), (0, 16))).reshape(1, E)
        small_all = jnp.concatenate(
            [small_all[:ROW_G1], apart(ROW_G1), apart(ROW_G2), small_all[ROW_G2 + 1 :]], axis=0)
        small_all = small_all.reshape(8, 16, BLOCKS, 32).transpose(2, 1, 0, 3).reshape(BLOCKS * 16, 256)
        whole = lambda value: lax.all_gather(value.astype(BF16), ALL, axis=0, tiled=True)
        in_all = whole(in_proj)
        one = [jnp.concatenate([in_all[:, :E], small_all], axis=1)]
        out_all, q_all, k_all, v_all, o_all = (whole(w) for w in (out_proj, w_query, w_key, w_value, w_output))
        cut = lambda value: value.reshape(BLOCKS, 16, D)
        side = jnp.concatenate(
            [jnp.concatenate([cut(q_all), cut(k_all)], axis=2), jnp.concatenate([cut(v_all), cut(o_all)], axis=2)], axis=1)
        gate = jnp.concatenate([cut(in_all[:, E : E + D]), cut(in_all[:, E + D :])], axis=1)
        two = [jnp.concatenate([out_all.reshape(BLOCKS, 32, D), side, gate], axis=2).reshape(BLOCKS * 32, 4 * D)]

    no = len(plan.grad_masks)
    rows3 = count * LG
    (normed, u_pre, conv, act, proj, sig, dt3, au3, a3, state, w_in, pm, gains, bx, cx) = run(
        functools.partial(front_kernel, plan, len(one), masks),
        [tok, halo],
        [((HALO + count, D), BF16), ((HALO + count, E), F32), ((count, E), F32),
         ((count, E), BF16), ((count, 128), F32), ((count, E), F32), ((rows3, 128), F32), ((rows3, 128), F32),
         ((128, 128), F32), ((144, 128), BF16), ((D, E), BF16), ((SMALL_ROWS, E), F32), ((8, D), F32),
         ((NS, count, 128), F32), ((NS, count, 128), F32)],
        [pltpu.VMEM((BLOCKS * 16, 256), BF16), pltpu.SemaphoreType.DMA((2,))],
        raw=one, us=6,
    )
    entry, firsts = exchange(plan, state, a3, True)
    if plan.fast:
        (held,) = join([near_two], firsts[:1], 12)
        two = [held, send(held, CORE)]
    pay, mamba, gated, middle, all_states, w_out, w_qk, w_vo, w_z, z = run(
        functools.partial(mid_kernel, plan, len(two), masks),
        [tok, dt3, au3, a3, normed, pm, gains, cot, entry, bx, cx],
        [((HEADS * count, 4 * HDIM), BF16), ((count, E), F32), ((count, E), BF16), ((count, D), F32),
         (((count + 1) * 128, 128), F32), ((E, D), BF16), ((D, 2 * D), BF16), ((D, 2 * D), BF16), ((D, E), BF16), ((count, E), F32)],
        [pltpu.VMEM((rows3, 128), F32), pltpu.SemaphoreType.DMA((4,))],
        raw=two, us=6,
    )
    got = attend(plan, pay, count)
    (att, gq, gk, gv, grad_middle, mix, gz, gy3, later, gain_grad_two) = run(
        functools.partial(turn_kernel, plan),
        [got, middle, cot, gains, z, mamba, dt3, cx, a3, w_out, w_qk, w_vo, state],
        [((count, D), BF16)] * 4 + [((count, D), F32), ((count, D), BF16), ((count, E), BF16), ((rows3, 128), F32),
                                    ((144, 128), BF16), ((1, D), F32)],
    )
    blocks = [len(masks_of) for masks_of in plan.grad_masks]
    (grad_c,) = run(grad_c_kernel, [gy3, all_states], [((count, 128), F32)])
    blocks = [len(masks_of) for masks_of in plan.grad_masks]

    def weight_grads(after):
        return run(
            functools.partial(weights_kernel, plan, no),
            [att, gq, gk, gv, mix, gated, middle, gains, cot, w_vo, normed, gz],
            [((count, D), BF16)] + [((n * 32, 4 * D), BF16) for n in blocks],
            [pltpu.VMEM((D, D), F32), pltpu.VMEM((E, D), F32), pltpu.VMEM((D, E), F32)], after=after)

    done = []

    def beside(step, entry):
        if step == 0:
            return [grad_c]
        if step == 1:
            done.extend(weight_grads([entry]))
            return done[:1]
        return []

    leaving, _ = exchange(plan, later, a3, False, beside)
    result, *one_grads = done or weight_grads([])
    one_parts = []
    if plan.fast:
        result = lax.ppermute(result, ALL, [(b, a) for a, b in home])
        rows = blocks[0] * 32
        one_parts = run(
            cut_one_kernel, [one_grads[0], send(one_grads[1], CORE)], [((rows // 2, 2 * D), BF16)] * 4, after=[leaving])
    small_grads, gu = run(
        functools.partial(back_kernel, plan),
        [dt3, au3, gy3, a3, proj, pm, all_states, sig, act, conv, u_pre, leaving, bx, cx, grad_c],
        [((SMALL_ROWS, E), F32), ((HALO + count, E), BF16)],
        [pltpu.VMEM((count * 128, 128), F32), pltpu.VMEM((rows3, 128), F32), pltpu.VMEM((rows3, 128), F32),
         pltpu.VMEM((128, 128), F32), pltpu.VMEM((8, 128), F32), pltpu.VMEM((count, 128), F32),
         pltpu.VMEM((count + 2 * HALO, E), F32)],
        limit=32, after=one_parts[:1], us=11,
    )
    *two_grads, own, before = run(
        functools.partial(last_kernel, plan, no),
        [tok, halo, gains, gu, gz, grad_middle, w_in, w_z, normed, small_grads, gain_grad_two],
        [((n * 16, E + 256), BF16) for n in blocks] + [((count, D), F32), ((HALO, D), F32)],
        [pltpu.VMEM((D, E), F32), pltpu.VMEM((SMALL_ROWS, E), F32)], after=[result],
    )
    if plan.fast:
        a_keep, a_give, b_keep, b_give = one_parts
        one_parts = run(
            cut_two_kernel, [a_keep, send(a_give, 16), b_keep, send(b_give, 1)], [((rows // 4, 2 * D), BF16)] * 4,
            after=[two_grads[0]])
    if plan.fast:
        tail = lax.ppermute(
            before, ALL, [(plan.place(s, c + 1), plan.place(s, c)) for s in range(4) for c in range(7)])
        a_keep, a_give, b_keep, b_give = one_parts
        sends = lambda parts, stage: [parts[0]] + [send(part, mask) for part, mask in zip(parts[1:], stage[1:])]
        n = blocks[0]
        whole, *u_parts, keep, give = run(
            cut_three_kernel,
            [two_grads[0], send(two_grads[1], CORE), a_keep, send(a_give, 1), b_keep, send(b_give, 16), own, tail],
            [((count, D), BF16)] + [((n * 4, E + 256), BF16)] * 4 + [((n * 4, 4 * D), BF16)] * 2)
        grad_tok = lax.ppermute(whole, ALL, [(b, a) for a, b in home])
        *u_parts, keep, give = run(
            cut_four_kernel, [*sends(u_parts, XY_MASKS), keep, send(give, 2)],
            [((n, E + 256), BF16)] * 4 + [((n * 2, 4 * D), BF16)] * 2, after=[grad_tok])
        grad_tok, result, out_g, q_g, k_g, v_g, o_g, in_g, x_g, dt_g, a_g, cw_g, cb_g, db_g, sk_g, g1_g, g2_g = run(
            finish_kernel, [grad_tok, result, *sends(u_parts, Z_MASKS), keep, send(give, 4)],
            [((count, D), BF16)] * 2 + [((32, D), F32)] + [((16, D), F32)] * 4
            + [((16, 2 * E), F32), ((32, 64), F32), ((32, 32), F32), ((NS, 32), F32), ((KW, 32), F32)]
            + [((1, 32), F32)] * 3 + [((1, 16), F32)] * 2,
            [pltpu.VMEM((SMALL_ROWS, 32), F32)], final=True)
        a_g, cw_g = a_g.T, cw_g.T
        vectors = [value[0] for value in (cb_g, db_g, sk_g, g1_g, g2_g)]
    else:
        tail = lax.ppermute(before, "ctx", [(c + 1, c) for c in range(chunks - 1)])
        grad_tok = jnp.concatenate([own[: count - HALO], own[count - HALO :] + tail], axis=0).astype(BF16)
        scatter = lambda value, dim=0: lax.psum_scatter(value.astype(F32), ALL, scatter_dimension=dim, tiled=True)
        blocks_one = one_grads[0].reshape(BLOCKS, 32, 4 * D)
        part = lambda row, rows, col: scatter(blocks_one[:, row : row + rows, col * D : (col + 1) * D].reshape(-1, D))
        out_g, q_g, k_g, v_g, o_g = part(0, 32, 0), part(0, 16, 1), part(0, 16, 2), part(16, 16, 1), part(16, 16, 2)
        in_g = jnp.concatenate([scatter(two_grads[0][:, :E]), part(0, 16, 3), part(16, 16, 3)], axis=1)
        small = two_grads[0][:, E:].reshape(BLOCKS, 16, 8, 32).transpose(2, 1, 0, 3).reshape(SMALL_ROWS, E)
        close = lambda row: scatter(small[row].reshape(BLOCKS, 32)[:, :16].reshape(D))
        g1, g2 = close(ROW_G1), close(ROW_G2)
        mine = scatter(small, 1)
        x_g, dt_g, a_g, cw_g = (
            mine[ROW_X : ROW_X + 64].T, mine[ROW_DT : ROW_DT + RANK], mine[ROW_A : ROW_A + NS].T, mine[ROW_CW : ROW_CW + KW].T)
        vectors = [mine[ROW_CB], mine[ROW_DB], mine[ROW_SK], g1, g2]
    cb_v, db_v, sk_v, g1_v, g2_v = vectors
    return (
        result[None], grad_tok[None], g1_v, in_g, cw_g, cb_v, x_g, dt_g, db_v, a_g, sk_v, out_g, g2_v, q_g, k_g, v_g, o_g,
    )


def attend(plan, pay, count):
    if plan.chunks == HEADS:
        held = plan.swap(pay)
        length = held.shape[0]
        half = pltpu.VMEM((length, HDIM), BF16)
        flat = pltpu.VMEM((HDIM, length), BF16)
        wide = pltpu.VMEM((length, HDIM), F32)
        (back,) = run(
            attention_kernel, [held], [((length, 4 * HDIM), BF16)], [half] * 4 + [flat] * 2 + [wide] * 2, us=4
        )
        return plan.swap(back)
    parts = pay.reshape(HEADS, count, 4, HDIM)
    query, key, value, grad = (parts[:, :, i] for i in range(4))
    key, value = (lax.all_gather(part, "ctx", axis=1, tiled=True) for part in (key, value))
    query_at = lax.axis_index("ctx") * count + jnp.arange(count)
    allowed = jnp.arange(key.shape[1])[None, :] <= query_at[:, None]
    scale = HDIM**-0.5
    dots = functools.partial(jnp.einsum, preferred_element_type=F32)
    scores = jnp.where(allowed, dots("hqd,hkd->hqk", query, key) * scale, -1e30)
    soft = jax.nn.softmax(scores, axis=-1)
    soft_low = soft.astype(BF16)
    grad_p = dots("hqd,hkd->hqk", grad, value)
    grad_s = (soft * (grad_p - jnp.sum(soft * grad_p, axis=-1, keepdims=True))).astype(BF16)
    raw = dots("hqk,hkd->hqd", soft_low, value).astype(BF16)
    grad_q = (dots("hqk,hkd->hqd", grad_s, key) * scale).astype(BF16)
    grads = (dots("hqk,hqd->hkd", grad_s, query) * scale, dots("hqk,hqd->hkd", soft_low, grad))
    grad_k, grad_v = (
        lax.psum_scatter(part.astype(BF16), "ctx", scatter_dimension=1, tiled=True) for part in grads
    )
    return jnp.concatenate([raw, grad_q, grad_k, grad_v], axis=-1).reshape(HEADS * count, 4 * HDIM)


def solution(mesh):
    plan = Plan(mesh)
    split, rows, cols = P(ALL), P(ALL, None), P(None, ALL)
    acts = P("dp", "ctx", None)
    return jax.shard_map(
        functools.partial(body, plan),
        mesh=mesh,
        in_specs=(acts, split, rows, rows, split, rows, cols, split, rows, split, rows, split, rows, rows, rows, rows, acts),
        out_specs=(acts, acts, split, rows, rows, split, rows, cols, split, rows, split, rows, split, rows, rows, rows, rows),
        check_vma=False,
    )
```

```python
import functools

import jax
import jax.numpy as jnp
from jax import lax
from jax.experimental import pallas as pl
from jax.experimental.pallas import tpu as pltpu
from jax.sharding import PartitionSpec as P

D = 512
E = 1024
NS = 16
RANK = 32
KW = 4
HEADS = 8
HDIM = 64
LG = 8
HALO = 16
BLOCKS = 32
ALL = ("dp", "ctx")
EPS = 1e-05
LOG2E = 1.4426950408889634
LN2 = 0.6931471805599453
F32 = jnp.float32
BF16 = jnp.bfloat16
VM = pl.BlockSpec(memory_space=pltpu.VMEM)

Z_MASKS = (0, 4, 2, 6)
XY_MASKS = (0, 1, 16, 17)
CORE = 8
HALF_MASKS = tuple(xy | zz for xy in XY_MASKS for zz in Z_MASKS)
FULL_MASKS = HALF_MASKS + tuple(mask | CORE for mask in HALF_MASKS)
CHUNK_MASKS = tuple((8 if c & 1 else 0) | (16 if c & 2 else 0) | (1 if c & 4 else 0) for c in range(8))

ROW_X = 0
ROW_DT = 64
ROW_A = 96
ROW_CW = 112
ROW_CB = 116
ROW_DB = 117
ROW_SK = 118
ROW_G1 = 119
ROW_G2 = 120
SMALL_ROWS = 128


ANY = pl.BlockSpec(memory_space=pl.ANY)
FAR = pl.BlockSpec(memory_space=pltpu.HBM)
WHOLE = pl.BlockSpec()


def run(kernel, ins, outs, scratch=(), limit=12, raw=(), far=(), after=(), final=False, us=2):
    first, count = len(ins) + len(raw) + len(far), len(after)

    def inner(*refs):
        kernel(*refs[:first], *refs[first + count :])

    return pl.pallas_call(
        inner,
        out_shape=[jax.ShapeDtypeStruct(shape, dtype) for shape, dtype in outs],
        in_specs=[VM] * len(ins) + [ANY] * len(raw) + [FAR] * len(far) + [ANY] * count,
        out_specs=[WHOLE if final else VM] * len(outs),
        scratch_shapes=list(scratch),
        compiler_params=pltpu.CompilerParams(vmem_limit_bytes=limit * 2**20),
        cost_estimate=pl.CostEstimate(flops=int(us * 1e3), bytes_accessed=int(us * 3e3), transcendentals=0),
    )(*ins, *raw, *far, *after)


def nn(left, right):
    return lax.dot_general(left, right, (((1,), (0,)), ((), ())), preferred_element_type=F32)


def nt(left, right):
    return lax.dot_general(left, right, (((1,), (1,)), ((), ())), preferred_element_type=F32)


def tn(left, right):
    return lax.dot_general(left, right, (((0,), (0,)), ((), ())), preferred_element_type=F32)


def sigmoid(value):
    return 1.0 / (1.0 + jnp.exp(-value))


class Plan:
    def __init__(self, mesh):
        self.dp, self.ctx = mesh.shape["dp"], mesh.shape["ctx"]
        self.fast = (self.dp, self.ctx) == (4, 8)
        self.chunks = self.ctx
        if self.fast:
            self.grad_masks = (FULL_MASKS[:16], FULL_MASKS[16:])
        else:
            self.grad_masks = (tuple(range(BLOCKS)),)

    def place(self, seq, chunk):
        return CHUNK_MASKS[chunk] | ((0, 2, 1, 3)[seq] << 1)

    def me(self):
        if self.fast:
            return lax.axis_index("dp") * 8 + lax.axis_index("ctx")
        return 0

    def chunk(self):
        if self.fast:
            lin = lax.axis_index("dp") * 8 + lax.axis_index("ctx")
            return ((lin >> 3) & 1) + ((lin >> 4) & 1) * 2 + (lin & 1) * 4
        return lax.axis_index("ctx")

    def side(self):
        return ((lax.axis_index("ctx") + lax.axis_index("dp") * 8) & CORE) != 0 if self.fast else False

    def swap(self, value):
        if self.fast:
            groups = [[self.place(s, c) for c in range(8)] for s in range(4)]
            return lax.all_to_all(value, ALL, 0, 0, tiled=True, axis_index_groups=groups)
        return lax.all_to_all(value, "ctx", 0, 0, tiled=True)


def send(value, mask):
    return lax.ppermute(value, ALL, [(i, i ^ mask) for i in range(32)])


def own_first(value, side, width):
    groups = [value[:, i * width : (i + 1) * width] for i in range(4)]
    pick = lambda x, own: jnp.where(side, groups[2 * x + own], groups[2 * x + 1 - own])
    return jnp.concatenate([pick(0, 1), pick(1, 1), pick(0, 0), pick(1, 0)], axis=1)


def in_order(value, side, width):
    own_a, own_b, far_a, far_b = (value[:, i * width : (i + 1) * width] for i in range(4))
    return jnp.concatenate(
        [jnp.where(side, far_a, own_a), jnp.where(side, own_a, far_a),
         jnp.where(side, far_b, own_b), jnp.where(side, own_b, far_b)], axis=1)


def rows_of(ref, half, first, cols):
    return jnp.concatenate(
        [ref[k * 32 + half * 16 : k * 32 + half * 16 + 16, first : first + cols] for k in range(ref.shape[0] // 32)], axis=0)


def wait_whole(target, sem):
    pltpu.make_async_copy(target, target, sem).wait()


def swap_blocks(value, me):
    rows, lanes = value.shape
    for bit in (16, 8, 4):
        half = bit * 32
        parts = [value[:, i : i + half] for i in range(0, lanes, half)]
        other = jnp.concatenate([parts[i ^ 1] for i in range(len(parts))], axis=1)
        value = jnp.where((me & bit) != 0, other, value)
    groups = []
    odd = (lax.broadcasted_iota(jnp.int32, (rows, 128), 1) & 32) != 0
    for i in range(0, lanes, 128):
        part = value[:, i : i + 128]
        part = jnp.where((me & 2) != 0, pltpu.roll(part, 64, 1), part)
        other = jnp.where(odd, pltpu.roll(part, 32, 1), pltpu.roll(part, 96, 1))
        groups.append(jnp.where((me & 1) != 0, other, part))
    return jnp.concatenate(groups, axis=1)


def pack_kernel(in_proj, x_proj, dt_proj, a_log, conv_w, conv_b, dt_bias, d_skip, gain_one, gain_two,
                out_proj, w_q, w_k, w_v, w_o, one, two, rows, *rest):
    (b_in, b_x, b_dt, b_a, b_cw, b_cb, b_db, b_sk, b_g1, b_g2, b_out, b_q, b_k, b_v, b_o, sems) = rest
    copies = [
        pltpu.make_async_copy(src, dst, sems.at[i])
        for i, (src, dst) in enumerate(
            zip((in_proj, x_proj, dt_proj, a_log, conv_w, conv_b, dt_bias, d_skip, gain_one, gain_two, out_proj, w_q,
                 w_k, w_v, w_o),
                (b_in, b_x, b_dt, b_a, b_cw, b_cb, b_db, b_sk, b_g1, b_g2, b_out, b_q, b_k, b_v, b_o))
        )
    ]
    for copy in copies:
        copy.start()
    for copy in copies:
        copy.wait()
    one[:, :E] = b_in[:, :E].astype(BF16)
    two[:16, 3 * D :] = b_in[:, E : E + D].astype(BF16)
    two[16:, 3 * D :] = b_in[:, E + D :].astype(BF16)
    two[:, :D] = b_out[...].astype(BF16)
    two[:16, D : 2 * D] = b_q[...].astype(BF16)
    two[:16, 2 * D : 3 * D] = b_k[...].astype(BF16)
    two[16:, D : 2 * D] = b_v[...].astype(BF16)
    two[16:, 2 * D : 3 * D] = b_o[...].astype(BF16)
    rows[...] = jnp.zeros_like(rows)
    rows[ROW_X : ROW_X + 64, :] = b_x[...].T
    rows[ROW_DT : ROW_DT + RANK, :] = b_dt[...]
    rows[ROW_A : ROW_A + NS, :] = b_a[...]
    rows[ROW_CW : ROW_CW + KW, :] = b_cw[...]
    rows[ROW_CB : ROW_CB + 1, :] = b_cb[...]
    rows[ROW_DB : ROW_DB + 1, :] = b_db[...]
    rows[ROW_SK : ROW_SK + 1, :] = b_sk[...]
    rows[ROW_G1 : ROW_G1 + 1, :16] = b_g1[...]
    rows[ROW_G2 : ROW_G2 + 1, :16] = b_g2[...]
    one[:, E:] = jnp.concatenate([rows[16 * q : 16 * q + 16, :] for q in range(8)], axis=1).astype(BF16)


def join_smalls(target, own, far, side):
    for q in range(8):
        rows = jnp.concatenate(
            [ref[16 * k : 16 * k + 16, E + 32 * q : E + 32 * q + 32].astype(F32) for ref in (own, far) for k in range(16)], axis=1)
        target[16 * q : 16 * q + 16, :] = in_order(rows, side, 256)


def gain_row(pm, row):
    return jnp.concatenate([pm[row : row + 1, 32 * s : 32 * s + 16] for s in range(BLOCKS)], axis=1)


def spread(target, source):
    count = source.shape[0]
    for s in range(LG):
        target[pl.ds(s, count, stride=LG), :] = source[:, s * 128 : (s + 1) * 128]


def gathered(source, count):
    return jnp.concatenate([source[pl.ds(s, count, stride=LG), :] for s in range(LG)], axis=1)


def broadcast_rows(target, proj, first):
    for n in range(NS):
        target[n] = jnp.broadcast_to(proj[:, first + n : first + n + 1], target.shape[1:])


def at8(ref, index):
    return ref[pl.ds(pl.multiple_of(index * 8, 8), 8), :]


def front_kernel(plan, tok, halo, own, far, normed, turned, u_out, conv_out, act_out, proj_out, sig_out, dt3, au3, a3,
                 state, pm, gains, bx, cx):
    side = plan.side()
    join_smalls(pm, own, far, side)
    gain = gain_row(pm, ROW_G1)
    gains[0:1, :] = gain
    gains[1:2, :] = gain_row(pm, ROW_G2)
    tokens = tok.shape[0]
    x = jnp.concatenate([halo[...].astype(F32), tok[...].astype(F32)], axis=0)
    r = lax.rsqrt(jnp.mean(x * x, axis=-1, keepdims=True) + EPS)
    low = x * r * gain
    normed[...] = low.astype(BF16)
    low = own_first(low, side, 128).astype(BF16)
    turned[...] = low
    u_out[...] = nn(low[:, : D // 2], own[:, :E]) + nn(low[:, D // 2 :], far[:, :E])
    conv = pm[ROW_CB : ROW_CB + 1, :]
    for k in range(KW):
        conv = conv + pm[ROW_CW + k : ROW_CW + k + 1, :] * u_out[HALO - 3 + k : HALO - 3 + k + tokens, :]
    conv_out[...] = conv
    act = (conv * sigmoid(conv)).astype(BF16)
    act_out[...] = act
    proj = nt(act, pm[ROW_X : ROW_X + 64, :].astype(BF16))
    proj_out[:, :64] = proj
    proj_out[:, 64:] = jnp.zeros((tokens, 64), F32)
    pre = nn(proj[:, :RANK].astype(BF16), pm[ROW_DT : ROW_DT + RANK, :].astype(BF16)) + pm[ROW_DB : ROW_DB + 1, :]
    sig_out[...] = sigmoid(pre)
    step = jnp.maximum(pre, 0.0) + jnp.log1p(jnp.exp(-jnp.abs(pre)))
    spread(dt3, step)
    spread(au3, act.astype(F32))
    spread(a3, -LOG2E * jnp.exp(pm[ROW_A : ROW_A + NS, :]))
    broadcast_rows(bx, proj, RANK)
    broadcast_rows(cx, proj, RANK + NS)
    decay = [a3[8 * n : 8 * n + 8, :] for n in range(NS)]

    def advance(t, carried):
        held, total = carried
        size = at8(dt3, t)
        drive = size * at8(au3, t)
        held = tuple(
            jnp.exp2(size * decay[n]) * held[n] + drive * bx[n, pl.ds(t, 1), :] for n in range(NS)
        )
        return held, total + size

    zero = jnp.zeros((8, 128), F32)
    held, total = lax.fori_loop(0, tokens, advance, ((zero,) * NS, zero), unroll=4)
    state[...] = jnp.concatenate([*held, total, zero], axis=0).astype(BF16)


def combine_kernel(plan, forward, states, a3, entry, states_f):
    states_f[...] = states[...].astype(F32)
    decay = [a3[8 * n : 8 * n + 8, :] for n in range(NS)]
    zero = jnp.zeros((8, 128), F32)

    def combine(i, held):
        base = (i if forward else plan.chunks - 1 - i) * 144
        total = states_f[pl.ds(pl.multiple_of(base + 128, 8), 8), :]
        return tuple(
            jnp.exp2(total * decay[n]) * held[n] + states_f[pl.ds(pl.multiple_of(base + 8 * n, 8), 8), :]
            for n in range(NS)
        )

    count = plan.chunk() if forward else plan.chunks - 1 - plan.chunk()
    held = lax.fori_loop(0, count, combine, (zero,) * NS)
    entry[...] = jnp.concatenate([*held, zero, zero], axis=0)


def merge_kernel(plan, step, forward, own, other, before, a3, group, entry):
    later = ((plan.chunk() >> step) & 1) == (1 if forward else 0)
    mine, theirs = own[...].astype(F32), other[...].astype(F32)
    first, second = jnp.where(later, theirs, mine), jnp.where(later, mine, theirs)
    decay = a3[...]
    spread_total = lambda value: jnp.concatenate([value[128:136, :]] * NS, axis=0)
    joint = jnp.exp2(spread_total(second) * decay) * first[:128, :] + second[:128, :]
    group[:128, :] = joint.astype(BF16)
    group[128:, :] = (first[128:, :] + second[128:, :]).astype(BF16)
    held = before[...]
    inner = held[:128, :] + jnp.exp2(spread_total(held) * decay) * theirs[:128, :]
    entry[:128, :] = jnp.where(later, inner, held[:128, :])
    entry[128:, :] = jnp.where(later, held[128:, :] + theirs[128:, :], held[128:, :])


def exchange(plan, state, a3, forward, beside=lambda step, entry: []):
    if plan.fast:
        group, entry, firsts = state, jnp.zeros((144, 128), F32), []
        for step in range(3):
            other = send(group, CHUNK_MASKS[1 << step])
            group, entry = run(
                functools.partial(merge_kernel, plan, step, forward), [group, other, entry, a3],
                [((144, 128), BF16), ((144, 128), F32)], after=beside(step, entry if step else group))
            firsts.append(entry)
        return entry, firsts
    states = lax.all_gather(state, "ctx", axis=0, tiled=True)
    return run(
        functools.partial(combine_kernel, plan, forward), [states, a3], [((144, 128), F32)],
        [pltpu.VMEM((144 * plan.chunks, 128), F32)])[0], []


def mid_kernel(plan, tok, dt3, au3, a3, turned, pm, gains, cot, entry, bx, cx, own, far,
               pay, mamba, gated_out, middle_out, all_states, z_out, y3):
    tokens = tok.shape[0]
    side = plan.side()
    both = lambda left, half, first, cols: nn(left[:, : D // 2], rows_of(own, half, first, cols)) + nn(
        left[:, D // 2 :], rows_of(far, half, first, cols))
    decay = [a3[8 * n : 8 * n + 8, :] for n in range(NS)]
    held = tuple(entry[8 * n : 8 * n + 8, :] for n in range(NS))
    all_states[:128, :] = entry[:128, :]

    def advance(t, held):
        size = at8(dt3, t)
        drive = size * at8(au3, t)
        base = pl.multiple_of(t * 128 + 128, 128)
        held = tuple(
            jnp.exp2(size * decay[n]) * held[n] + drive * bx[n, pl.ds(t, 1), :] for n in range(NS)
        )
        for n in range(NS):
            all_states[pl.ds(base + 8 * n, 8), :] = held[n]
        y = held[0] * cx[0, pl.ds(t, 1), :]
        for n in range(1, NS):
            y = y + held[n] * cx[n, pl.ds(t, 1), :]
        y3[pl.ds(pl.multiple_of(t * 8, 8), 8), :] = y
        return held

    lax.fori_loop(0, tokens, advance, held, unroll=4)
    act = gathered(au3, tokens)
    y = gathered(y3, tokens) + pm[ROW_SK : ROW_SK + 1, :] * act
    mamba[...] = y
    low = turned[HALO:, :]
    z = jnp.concatenate([both(low, 0, 3 * D, D), both(low, 1, 3 * D, D)], axis=1)
    z_out[...] = z
    gated = y * (z * sigmoid(z))
    gated_out[...] = gated.astype(BF16)
    gated = own_first(gated, side, 256).astype(BF16)
    middle = tok[...].astype(F32) + nn(gated[:, : E // 2], own[:, :D]) + nn(gated[:, E // 2 :], far[:, :D])
    middle_out[...] = middle
    r = lax.rsqrt(jnp.mean(middle * middle, axis=-1, keepdims=True) + EPS)
    low = own_first(middle * r * gains[1:2, :], side, 128).astype(BF16)
    query_key, value = both(low, 0, D, 2 * D), both(low, 1, D, D)
    grad = jnp.concatenate([nt(cot[...], rows_of(ref, 1, 2 * D, D)) for ref in (own, far)], axis=1)
    quads = tuple(part.astype(BF16) for part in (query_key[:, :D], query_key[:, D:], value, in_order(grad, side, 128)))
    for h in range(HEADS):
        for i, part in enumerate(quads):
            pay[h * tokens : (h + 1) * tokens, i * HDIM : (i + 1) * HDIM] = part[:, h * HDIM : (h + 1) * HDIM]


def attention_kernel(pay, back, q_s, k_s, v_s, g_s, kt, vt, dk, dv):
    length = pay.shape[0]
    rows = 256
    q_s[...] = pay[:, :HDIM]
    k_s[...] = pay[:, HDIM : 2 * HDIM]
    v_s[...] = pay[:, 2 * HDIM : 3 * HDIM]
    g_s[...] = pay[:, 3 * HDIM :]
    kt[...] = k_s[...].T
    vt[...] = v_s[...].T
    dk[...] = jnp.zeros_like(dk)
    dv[...] = jnp.zeros_like(dv)
    scale = HDIM**-0.5
    key_at = lax.broadcasted_iota(jnp.int32, (rows, rows), 0)
    query_at = lax.broadcasted_iota(jnp.int32, (rows, rows), 1)
    for i in range(length // rows):
        first, last = i * rows, (i + 1) * rows
        query = q_s[first:last, :]
        grad = g_s[first:last, :]
        scores = nt(k_s[:last, :], query) * scale
        diagonal = jnp.where(key_at <= query_at, scores[first:, :], -1e30)
        scores = diagonal if i == 0 else jnp.concatenate([scores[:first, :], diagonal], axis=0)
        expo = jnp.exp(scores - jnp.max(scores, axis=0, keepdims=True))
        soft = expo * (1.0 / jnp.sum(expo, axis=0, keepdims=True))
        soft_low = soft.astype(BF16)
        grad_p = nt(v_s[:last, :], grad)
        dot = jnp.sum(soft * grad_p, axis=0, keepdims=True)
        grad_s = (soft * (grad_p - dot)).astype(BF16)
        raw = nn(vt[:, :last], soft_low)
        grad_q = nn(kt[:, :last], grad_s) * scale
        back[first:last, :HDIM] = raw.T.astype(BF16)
        back[first:last, HDIM : 2 * HDIM] = grad_q.T.astype(BF16)
        dk[:last, :] += nn(grad_s, query)
        dv[:last, :] += nn(soft_low, grad)
    back[:, 2 * HDIM : 3 * HDIM] = (dk[...] * scale).astype(BF16)
    back[:, 3 * HDIM :] = dv[...].astype(BF16)


def turn_kernel(plan, got, middle, cot, gains, z_in, mamba, dt3, cx, a3, own, far, first,
                att, gq, gk, gv, grad_middle, mix, gz, gy3, state, gain_grad):
    tokens = middle.shape[0]
    for h in range(HEADS):
        for i, part in enumerate((att, gq, gk, gv)):
            part[:, h * HDIM : (h + 1) * HDIM] = got[h * tokens : (h + 1) * tokens, i * HDIM : (i + 1) * HDIM]
    side = plan.side()
    grad_n = in_order(jnp.concatenate(
        [nt(gq[...], rows_of(ref, 0, D, D)) + nt(gk[...], rows_of(ref, 0, 2 * D, D)) + nt(gv[...], rows_of(ref, 1, D, D))
         for ref in (own, far)], axis=1), side, 128)
    mid = middle[...]
    r = lax.rsqrt(jnp.mean(mid * mid, axis=-1, keepdims=True) + EPS)
    gain_grad[...] = jnp.sum(grad_n * mid * r, axis=0, keepdims=True)
    q = grad_n * gains[1:2, :]
    gm = cot[...].astype(F32) + r * q - mid * (r * r * r) * jnp.mean(q * mid, axis=-1, keepdims=True)
    grad_middle[...] = gm
    low = gm.astype(BF16)
    mix[...] = low
    grad_gated = in_order(jnp.concatenate([nt(low, ref[:, :D]) for ref in (own, far)], axis=1), side, 256)
    z = z_in[...]
    s = sigmoid(z)
    spread(gy3, grad_gated * (z * s))
    gz[...] = (grad_gated * mamba[...] * (s * (1.0 + z * (1.0 - s)))).astype(BF16)
    decay = [a3[8 * n : 8 * n + 8, :] for n in range(NS)]

    def retreat(i, carried):
        t = tokens - 1 - i
        size = at8(dt3, t)
        grad = at8(gy3, t)
        return tuple(
            jnp.exp2(size * decay[n]) * (carried[n] + grad * cx[n, pl.ds(t, 1), :]) for n in range(NS)
        )

    zero = jnp.zeros((8, 128), F32)
    carried = lax.fori_loop(0, tokens, retreat, (zero,) * NS, unroll=4)
    state[:128, :] = jnp.concatenate(carried, axis=0).astype(BF16)
    state[128:, :] = first[128:, :]


def pack_blocks(plan, outs, source, rows, height, row, first, col=0, cols=None):
    me = plan.me()
    cols = source.shape[1] if cols is None else cols
    for out, masks in zip(outs, plan.grad_masks):
        for k, mask in enumerate(masks):
            block = me ^ mask
            out[k * height + row : k * height + row + rows, first : first + cols] = source[
                pl.ds(pl.multiple_of(block * rows, 16), rows), col : col + cols
            ].astype(BF16)


def grad_c_kernel(gy3, all_states, grad_c):
    diagonal_sums(grad_c, 0, lambda rows: gy3[rows, :], all_states, 1)


def weights_kernel(plan, no, att, gq, gk, gv, mix, gated, middle, gains, cot, own, far, normed, gz, *refs):
    result, outs = refs[0], refs[1 : 1 + no]
    small, large, wide = refs[1 + no :]
    mid = middle[...]
    held = own_first(att[...], plan.side(), 128)
    result[...] = (
        mid + nn(held[:, : D // 2], rows_of(own, 1, 2 * D, D)) + nn(held[:, D // 2 :], rows_of(far, 1, 2 * D, D))
    ).astype(BF16)
    r = lax.rsqrt(jnp.mean(mid * mid, axis=-1, keepdims=True) + EPS)
    low = (mid * r * gains[1:2, :]).astype(BF16)
    large[...] = tn(gated[...], mix[...])
    pack_blocks(plan, outs, large, 32, 32, 0, 0)
    small[...] = tn(low, gq[...])
    pack_blocks(plan, outs, small, 16, 32, 0, D)
    small[...] = tn(low, gk[...])
    pack_blocks(plan, outs, small, 16, 32, 0, 2 * D)
    small[...] = tn(low, gv[...])
    pack_blocks(plan, outs, small, 16, 32, 16, D)
    small[...] = tn(att[...], cot[...])
    pack_blocks(plan, outs, small, 16, 32, 16, 2 * D)
    wide[...] = tn(normed[HALO:, :], gz[...])
    pack_blocks(plan, outs, wide, 16, 32, 0, 3 * D, 0, D)
    pack_blocks(plan, outs, wide, 16, 32, 16, 3 * D, D, D)


def diagonal_sums(out, col, channels, held, offset, span=16):
    row_t = lax.broadcasted_iota(jnp.int32, (span, span * NS), 0)
    col_t = lax.broadcasted_iota(jnp.int32, (span, span * NS), 1) // NS
    pick = (
        lax.broadcasted_iota(jnp.int32, (span * NS, NS), 0) % NS
        == lax.broadcasted_iota(jnp.int32, (span * NS, NS), 1)
    ).astype(BF16)
    for block in range(out.shape[0] // span):
        total = jnp.zeros((span, span * NS), F32)
        for s in range(LG):
            held_rows = held[pl.ds((block * span + offset) * 128 + s, span * NS, stride=LG), :].astype(BF16)
            total = total + nt(channels(pl.ds(block * span * 8 + s, span, stride=LG)).astype(BF16), held_rows)
        own = jnp.where(row_t == col_t, total, 0.0).astype(BF16)
        out[block * span : (block + 1) * span, col : col + NS] = nn(own, pick)


def back_kernel(plan, dt3, au3, gy3, a3, proj, pm, all_states, sig, act, conv_in, u_in, leaving, bx, cx, grad_c,
                small_grads, gu_out, grads, gs3, ga3, gal, skip3, low_rank, padded):
    tokens = dt3.shape[0] // LG
    decay = [a3[8 * n : 8 * n + 8, :] for n in range(NS)]
    zero = jnp.zeros((8, 128), F32)
    spread(skip3, pm[ROW_SK : ROW_SK + 1, :])
    skip = skip3[...]

    carried = tuple(leaving[8 * n : 8 * n + 8, :] for n in range(NS))
    gal[...] = jnp.zeros_like(gal)

    def retreat(i, state):
        carried, skipped = state
        t = tokens - 1 - i
        size, value, grad = at8(dt3, t), at8(au3, t), at8(gy3, t)
        base = pl.multiple_of(t * 128, 128)
        from_b = zero
        from_a = zero
        fresh = []
        for n in range(NS):
            g = carried[n] + grad * cx[n, pl.ds(t, 1), :]
            grads[pl.ds(base + 8 * n, 8), :] = g
            w = jnp.exp2(size * decay[n]) * g
            q = w * all_states[pl.ds(base + 8 * n, 8), :]
            from_a = from_a + decay[n] * q
            from_b = from_b + g * bx[n, pl.ds(t, 1), :]
            gal[8 * n : 8 * n + 8, :] += size * q
            fresh.append(w)
        at = pl.ds(pl.multiple_of(t * 8, 8), 8)
        gs3[at, :] = from_a * LN2 + from_b * value
        ga3[at, :] = from_b * size + skip * grad
        return tuple(fresh), skipped + grad * value

    _, skipped = lax.fori_loop(0, tokens, retreat, (carried, zero), unroll=4)

    diagonal_sums(low_rank, RANK, lambda rows: dt3[rows, :] * au3[rows, :], grads, 0)
    low_rank[:, RANK + NS : RANK + 2 * NS] = grad_c[:, :NS]

    grad_pre = gathered(gs3, tokens) * sig[...]
    grad_pre_low = grad_pre.astype(BF16)
    low_rank[:, :RANK] = nt(grad_pre_low, pm[ROW_DT : ROW_DT + RANK, :].astype(BF16))
    projected = low_rank[:, :64].astype(BF16)
    small_grads[ROW_X : ROW_X + 64, :] = tn(projected, act[...])
    small_grads[ROW_DT : ROW_DT + RANK, :] = tn(proj[:, :RANK].astype(BF16), grad_pre_low)
    true_a = -jnp.exp(pm[ROW_A : ROW_A + NS, :])
    small_grads[ROW_A : ROW_A + NS, :] = gathered(gal, NS) * true_a
    small_grads[ROW_DB : ROW_DB + 1, :] = jnp.sum(grad_pre, axis=0, keepdims=True)
    skip3[...] = skipped
    small_grads[ROW_SK : ROW_SK + 1, :] = gathered(skip3, 1)
    small_grads[ROW_G1:, :] = jnp.zeros((SMALL_ROWS - ROW_G1, E), F32)
    conv = conv_in[...]
    s = sigmoid(conv)
    grad_act = gathered(ga3, tokens) + nn(projected, pm[ROW_X : ROW_X + 64, :].astype(BF16))
    grad_conv = grad_act * (s * (1.0 + conv * (1.0 - s)))
    small_grads[ROW_CB : ROW_CB + 1, :] = jnp.sum(grad_conv, axis=0, keepdims=True)
    for k in range(KW):
        small_grads[ROW_CW + k : ROW_CW + k + 1, :] = jnp.sum(
            grad_conv * u_in[HALO - 3 + k : HALO - 3 + k + tokens, :], axis=0, keepdims=True
        )
    padded[:HALO, :] = jnp.zeros((HALO, E), F32)
    padded[HALO : HALO + tokens, :] = grad_conv
    padded[HALO + tokens :, :] = jnp.zeros((HALO, E), F32)
    gu = jnp.zeros((HALO + tokens, E), F32)
    for k in range(KW):
        gu = gu + pm[ROW_CW + k : ROW_CW + k + 1, :] * padded[3 - k : 3 - k + HALO + tokens, :]
    gu_out[...] = gu.astype(BF16)


def last_kernel(plan, no, tok, halo, gains, gu, gz, grad_middle, own_u, far_u, own_z, far_z, normed, small_grads, gain_two, *refs):
    outs = refs[:no]
    own, before, large, spaced = refs[no:]
    me = plan.me()
    large[...] = tn(normed[...], gu[...])
    pack_blocks(plan, outs, large, 16, 16, 0, 0)
    x = jnp.concatenate([halo[...].astype(F32), tok[...].astype(F32)], axis=0)
    r = lax.rsqrt(jnp.mean(x * x, axis=-1, keepdims=True) + EPS)
    from_z = jnp.concatenate(
        [nt(gz[:, :D], rows_of(ref, 0, 3 * D, D)) + nt(gz[:, D:], rows_of(ref, 1, 3 * D, D)) for ref in (own_z, far_z)], axis=1)
    from_u = jnp.concatenate([nt(gu[...], ref[:, :E]) for ref in (own_u, far_u)], axis=1)
    grad_n = in_order(from_u + jnp.concatenate([jnp.zeros((HALO, D), F32), from_z], axis=0), plan.side(), 128)
    gain_one = jnp.sum(grad_n * x * r, axis=0, keepdims=True)
    q = grad_n * gains[0:1, :]
    base = r * q - x * (r * r * r) * jnp.mean(q * x, axis=-1, keepdims=True)
    own[...] = (grad_middle[...] + base[HALO:, :]).astype(BF16)
    before[...] = base[:HALO, :].astype(BF16)
    spaced[...] = small_grads[...]
    blank = jnp.zeros((1, 16), F32)
    for row, grad in ((ROW_G1, gain_one), (ROW_G2, gain_two[...])):
        spaced[row : row + 1, :] = jnp.concatenate(
            [part for s in range(BLOCKS) for part in (grad[:, 16 * s : 16 * s + 16], blank)], axis=1)
    spaced[...] = swap_blocks(spaced[...], me)
    for out, masks in zip(outs, plan.grad_masks):
        for k, m in enumerate(masks):
            out[16 * k : 16 * k + 16, E:] = jnp.concatenate(
                [spaced[16 * q : 16 * q + 16, 32 * m : 32 * m + 32] for q in range(8)], axis=1).astype(BF16)


def total_of(ins):
    total = ins[0][...].astype(F32)
    for other in ins[1:]:
        total = total + other[...].astype(F32)
    return total


def finish_kernel(*refs):
    (own, tail, result), refs = refs[:3], refs[3:]
    u_ins, ins, (own_out, result_out), refs = refs[:4], refs[4:6], refs[6:8], refs[2:]
    rows = own.shape[0] - HALO
    own_out[:rows, :] = own[:rows, :]
    own_out[rows:, :] = (own[rows:, :].astype(F32) + tail[...].astype(F32)).astype(BF16)
    result_out[...] = result[...]
    out_g, q_g, k_g, v_g, o_g, in_g, x_g, dt_g, a_g, cw_g, cb_g, db_g, sk_g, g1_g, g2_g, rows = refs[6:]
    total = total_of(ins)
    out_g[...] = total[:, :D]
    q_g[...] = total[:16, D : 2 * D]
    k_g[...] = total[:16, 2 * D : 3 * D]
    v_g[...] = total[16:, D : 2 * D]
    o_g[...] = total[16:, 2 * D : 3 * D]
    in_g[:, E : E + D] = total[:16, 3 * D :]
    in_g[:, E + D :] = total[16:, 3 * D :]
    total = total_of(u_ins)
    in_g[:, :E] = total[:, :E]
    for q in range(8):
        rows[16 * q : 16 * q + 16, :] = total[:, E + 32 * q : E + 32 * q + 32]
    x_g[...] = rows[ROW_X : ROW_X + 64, :].T
    dt_g[...] = rows[ROW_DT : ROW_DT + RANK, :]
    a_g[...] = rows[ROW_A : ROW_A + NS, :]
    cw_g[...] = rows[ROW_CW : ROW_CW + KW, :]
    cb_g[...] = rows[ROW_CB : ROW_CB + 1, :]
    db_g[...] = rows[ROW_DB : ROW_DB + 1, :]
    sk_g[...] = rows[ROW_SK : ROW_SK + 1, :]
    g1_g[...] = rows[ROW_G1 : ROW_G1 + 1, :16]
    g2_g[...] = rows[ROW_G2 : ROW_G2 + 1, :16]


def join_kernel(plan, counts, placed, *refs):
    ins, outs = refs[: sum(counts)], refs[sum(counts) :]
    at = 0
    for i, count in enumerate(counts):
        rows = outs[i].shape[0] // count
        for k in range(count):
            part = ins[at + k]
            if not placed[i]:
                outs[i][k * rows : (k + 1) * rows, :] = part[...]
                continue
            height = rows // len(Z_MASKS)
            for j, zz in enumerate(Z_MASKS):
                owner = plan.me() ^ (XY_MASKS[k] | zz)
                to = (((owner >> 4) & 1) * 8 + (owner & 7)) * height
                outs[i][pl.ds(pl.multiple_of(to, 16), height), :] = part[j * height : (j + 1) * height, :]
        at += count


def join(plan, groups, after=(), placed=()):
    counts = [len(group) for group in groups]
    outs = [((group[0].shape[0] * len(group), group[0].shape[1]), group[0].dtype) for group in groups]
    return run(
        functools.partial(join_kernel, plan, counts, [i in placed for i in range(len(groups))]),
        [part for group in groups for part in group], outs, after=after, us=1)


def spread_out(value, stage):
    return [value] + [send(value, mask) for mask in stage[1:]]


def cut_one_kernel(keep, got, a_keep, a_give, b_keep, b_give):
    half, quarter, cols = keep.shape[0] // 2, keep.shape[0] // 4, keep.shape[1] // 2
    add = lambda rows, lanes: (keep[rows, lanes].astype(F32) + got[rows, lanes].astype(F32)).astype(BF16)
    left, right = slice(0, cols), slice(cols, 2 * cols)
    a_keep[...] = add(slice(0, half), left)
    a_give[...] = add(slice(half, 2 * half), left)
    for i in range(2):
        b_keep[i * quarter : (i + 1) * quarter, :] = add(slice(2 * i * quarter, (2 * i + 1) * quarter), right)
        b_give[i * quarter : (i + 1) * quarter, :] = add(slice((2 * i + 1) * quarter, (2 * i + 2) * quarter), right)


def cut_two_kernel(a_own, a_got, b_own, b_got, a_keep, a_give, b_keep, b_give):
    rows = a_own.shape[0] // 2
    for own, got, keep, give in ((a_own, a_got, a_keep, a_give), (b_own, b_got, b_keep, b_give)):
        for out, part in ((keep, slice(0, rows)), (give, slice(rows, 2 * rows))):
            out[...] = (own[part, :].astype(F32) + got[part, :].astype(F32)).astype(BF16)


def add_rows(out, rows, ins, cols=slice(None), to=slice(None)):
    total = ins[0][rows, cols].astype(F32)
    for other in ins[1:]:
        total = total + other[rows, cols].astype(F32)
    out[:, to] = total.astype(out.dtype)


def cut_three_kernel(u_own, u_got, a_own, a_got, b_own, b_got, u_0, u_1, u_2, u_3, keep, give):
    rows = u_0.shape[0]
    for i, out in enumerate((u_0, u_1, u_2, u_3)):
        add_rows(out, slice(i * rows, (i + 1) * rows), (u_own, u_got))
    rows, cols = keep.shape[0], a_own.shape[1]
    for i, out in enumerate((keep, give)):
        part = slice(i * rows, (i + 1) * rows)
        add_rows(out, part, (a_own, a_got), to=slice(0, cols))
        add_rows(out, part, (b_own, b_got), to=slice(cols, 2 * cols))


def cut_four_kernel(u_own, u_a, u_b, u_c, own, got, u_0, u_1, u_2, u_3, keep, give):
    rows = u_0.shape[0]
    for i, out in enumerate((u_0, u_1, u_2, u_3)):
        add_rows(out, slice(i * rows, (i + 1) * rows), (u_own, u_a, u_b, u_c))
    rows = keep.shape[0]
    for i, out in enumerate((keep, give)):
        add_rows(out, slice(i * rows, (i + 1) * rows), (own, got))


def body(plan, *args):
    (tokens, mixer_gain, in_proj, conv_weight, conv_bias, x_proj, dt_proj, dt_bias, a_log, d_skip, out_proj,
     attn_gain, w_query, w_key, w_value, w_output, cotangent) = args
    count = tokens.shape[1]
    tok0, cot0 = tokens.reshape(count, D), cotangent.reshape(count, D)
    chunks = plan.chunks
    devices = plan.dp * plan.ctx
    share, width = E // devices, D // devices
    if plan.fast:
        home = [(s * 8 + c, plan.place(s, c)) for s in range(4) for c in range(8)]
        tok = lax.ppermute(tok0, ALL, home)
        halo = lax.ppermute(
            tok0[count - HALO :], ALL, [(s * 8 + c, plan.place(s, c + 1)) for s in range(4) for c in range(7)]
        )
        raw = [in_proj, x_proj, dt_proj, a_log.T, conv_weight.T, conv_bias[None], dt_bias[None], d_skip[None],
               mixer_gain[None], attn_gain[None], out_proj, w_query, w_key, w_value, w_output]
        pack_one, pack_two = run(
            pack_kernel, [], [((16, E + 256), BF16), ((32, 4 * D), BF16)],
            [pltpu.VMEM((SMALL_ROWS, 32), F32)] + [pltpu.VMEM(value.shape, F32) for value in raw]
            + [pltpu.SemaphoreType.DMA((len(raw),))], far=raw, limit=60)
        two_far = send(pack_two, 4)
        (one,) = join(plan, [[pack_one, send(pack_one, 4)]])
        cot = lax.ppermute(cot0, ALL, home)
        one, two = join(plan, [[one, send(one, 2)], [pack_two, two_far]], [tok, halo])
        two_far = send(two, 2)
        one, two = join(plan, [spread_out(one, XY_MASKS), [two, two_far]], [cot], (0,))
        one = [one, send(one, CORE)]
        near_two = spread_out(two, XY_MASKS)
    else:
        tok, cot = tok0, cot0
        halo = lax.ppermute(tok0[count - HALO :], "ctx", [(c, c + 1) for c in range(chunks - 1)])
        smalls = jnp.concatenate(
            [x_proj.T, dt_proj, a_log.T, conv_weight.T, conv_bias[None], dt_bias[None], d_skip[None],
             jnp.pad(mixer_gain, (0, share - width))[None], jnp.pad(attn_gain, (0, share - width))[None],
             jnp.zeros((SMALL_ROWS - ROW_G2 - 1, share), F32)], axis=0).astype(BF16)
        small_all = lax.all_gather(smalls, ALL, axis=1, tiled=True)
        apart = lambda row: jnp.pad(
            small_all[row].reshape(devices, share)[:, :width].reshape(BLOCKS, 16), ((0, 0), (0, 16))).reshape(1, E)
        small_all = jnp.concatenate(
            [small_all[:ROW_G1], apart(ROW_G1), apart(ROW_G2), small_all[ROW_G2 + 1 :]], axis=0)
        small_all = small_all.reshape(8, 16, BLOCKS, 32).transpose(2, 1, 0, 3).reshape(BLOCKS * 16, 256)
        whole = lambda value: lax.all_gather(value.astype(BF16), ALL, axis=0, tiled=True)
        in_all = whole(in_proj)
        halves = lambda value: [value.reshape(2, 2, -1, value.shape[1])[:, i].reshape(-1, value.shape[1]) for i in range(2)]
        one = halves(jnp.concatenate([in_all[:, :E], small_all], axis=1))
        out_all, q_all, k_all, v_all, o_all = (whole(w) for w in (out_proj, w_query, w_key, w_value, w_output))
        cut = lambda value: value.reshape(BLOCKS, 16, D)
        side = jnp.concatenate(
            [jnp.concatenate([cut(q_all), cut(k_all)], axis=2), jnp.concatenate([cut(v_all), cut(o_all)], axis=2)], axis=1)
        gate = jnp.concatenate([cut(in_all[:, E : E + D]), cut(in_all[:, E + D :])], axis=1)
        two = halves(jnp.concatenate([out_all.reshape(BLOCKS, 32, D), side, gate], axis=2).reshape(BLOCKS * 32, 4 * D))

    no = len(plan.grad_masks)
    rows3 = count * LG
    (normed, turned, u_pre, conv, act, proj, sig, dt3, au3, a3, state, pm, gains, bx, cx) = run(
        functools.partial(front_kernel, plan),
        [tok, halo, *one],
        [((HALO + count, D), BF16), ((HALO + count, D), BF16), ((HALO + count, E), F32), ((count, E), F32),
         ((count, E), BF16), ((count, 128), F32), ((count, E), F32), ((rows3, 128), F32), ((rows3, 128), F32),
         ((128, 128), F32), ((144, 128), BF16), ((SMALL_ROWS, E), F32), ((8, D), F32),
         ((NS, count, 128), F32), ((NS, count, 128), F32)], us=6,
    )
    entry, firsts = exchange(plan, state, a3, True)
    if plan.fast:
        (held,) = join(plan, [near_two], firsts[1:2], (0,))
        two = [held, send(held, CORE)]
    pay, mamba, gated, middle, all_states, z = run(
        functools.partial(mid_kernel, plan),
        [tok, dt3, au3, a3, turned, pm, gains, cot, entry, bx, cx, *two],
        [((HEADS * count, 4 * HDIM), BF16), ((count, E), F32), ((count, E), BF16), ((count, D), F32),
         (((count + 1) * 128, 128), F32), ((count, E), F32)],
        [pltpu.VMEM((rows3, 128), F32)], us=6,
    )
    got = attend(plan, pay, count)
    (att, gq, gk, gv, grad_middle, mix, gz, gy3, later, gain_grad_two) = run(
        functools.partial(turn_kernel, plan),
        [got, middle, cot, gains, z, mamba, dt3, cx, a3, *two, state],
        [((count, D), BF16)] * 4 + [((count, D), F32), ((count, D), BF16), ((count, E), BF16), ((rows3, 128), F32),
                                    ((144, 128), BF16), ((1, D), F32)],
    )
    blocks = [len(masks_of) for masks_of in plan.grad_masks]

    def weight_grads(after):
        return run(
            functools.partial(weights_kernel, plan, no),
            [att, gq, gk, gv, mix, gated, middle, gains, cot, *two, normed, gz],
            [((count, D), BF16)] + [((n * 32, 4 * D), BF16) for n in blocks],
            [pltpu.VMEM((D, D), F32), pltpu.VMEM((E, D), F32), pltpu.VMEM((D, E), F32)], after=after)

    def c_grads(after):
        return run(grad_c_kernel, [gy3, all_states], [((count, 128), F32)], after=after)

    done, extra = [], []

    def beside(step, entry):
        if step == 1:
            done.extend(weight_grads([entry]))
            return done[:1]
        if step == 2:
            extra.extend(c_grads([entry]))
        return list(extra)

    leaving, _ = exchange(plan, later, a3, False, beside)
    result, *one_grads = done or weight_grads([])
    (grad_c,) = extra or c_grads([])
    one_parts = []
    if plan.fast:
        result = lax.ppermute(result, ALL, [(b, a) for a, b in home])
        rows = blocks[0] * 32
        one_parts = run(
            cut_one_kernel, [one_grads[0], send(one_grads[1], CORE)], [((rows // 2, 2 * D), BF16)] * 4, after=[leaving])
    small_grads, gu = run(
        functools.partial(back_kernel, plan),
        [dt3, au3, gy3, a3, proj, pm, all_states, sig, act, conv, u_pre, leaving, bx, cx, grad_c],
        [((SMALL_ROWS, E), F32), ((HALO + count, E), BF16)],
        [pltpu.VMEM((count * 128, 128), F32), pltpu.VMEM((rows3, 128), F32), pltpu.VMEM((rows3, 128), F32),
         pltpu.VMEM((128, 128), F32), pltpu.VMEM((8, 128), F32), pltpu.VMEM((count, 128), F32),
         pltpu.VMEM((count + 2 * HALO, E), F32)],
        limit=32, after=one_parts[:1], us=11,
    )
    *two_grads, own, before = run(
        functools.partial(last_kernel, plan, no),
        [tok, halo, gains, gu, gz, grad_middle, *one, *two, normed, small_grads, gain_grad_two],
        [((n * 16, E + 256), BF16) for n in blocks] + [((count, D), BF16), ((HALO, D), BF16)],
        [pltpu.VMEM((D, E), F32), pltpu.VMEM((SMALL_ROWS, E), F32)], after=[result],
    )
    if plan.fast:
        a_keep, a_give, b_keep, b_give = one_parts
        one_parts = run(
            cut_two_kernel, [a_keep, send(a_give, 16), b_keep, send(b_give, 1)], [((rows // 4, 2 * D), BF16)] * 4,
            after=[two_grads[0]])
    if plan.fast:
        back = [(b, a) for a, b in home]
        grad_tok = lax.ppermute(own, ALL, back)
        tail = lax.ppermute(
            before, ALL, [(plan.place(s, c + 1), s * 8 + c) for s in range(4) for c in range(7)])
        a_keep, a_give, b_keep, b_give = one_parts
        sends = lambda parts, stage: [parts[0]] + [send(part, mask) for part, mask in zip(parts[1:], stage[1:])]
        n = blocks[0]
        *u_parts, keep, give = run(
            cut_three_kernel,
            [two_grads[0], send(two_grads[1], CORE), a_keep, send(a_give, 1), b_keep, send(b_give, 16)],
            [((n * 4, E + 256), BF16)] * 4 + [((n * 4, 4 * D), BF16)] * 2)
        *u_parts, keep, give = run(
            cut_four_kernel, [*sends(u_parts, XY_MASKS), keep, send(give, 2)],
            [((n, E + 256), BF16)] * 4 + [((n * 2, 4 * D), BF16)] * 2, after=[grad_tok])
        grad_tok, result, out_g, q_g, k_g, v_g, o_g, in_g, x_g, dt_g, a_g, cw_g, cb_g, db_g, sk_g, g1_g, g2_g = run(
            finish_kernel, [grad_tok, tail, result, *sends(u_parts, Z_MASKS), keep, send(give, 4)],
            [((count, D), BF16)] * 2 + [((32, D), F32)] + [((16, D), F32)] * 4
            + [((16, 2 * E), F32), ((32, 64), F32), ((32, 32), F32), ((NS, 32), F32), ((KW, 32), F32)]
            + [((1, 32), F32)] * 3 + [((1, 16), F32)] * 2,
            [pltpu.VMEM((SMALL_ROWS, 32), F32)], final=True)
        a_g, cw_g = a_g.T, cw_g.T
        vectors = [value[0] for value in (cb_g, db_g, sk_g, g1_g, g2_g)]
    else:
        tail = lax.ppermute(before, "ctx", [(c + 1, c) for c in range(chunks - 1)])
        end = (own[count - HALO :].astype(F32) + tail.astype(F32)).astype(BF16)
        grad_tok = jnp.concatenate([own[: count - HALO], end], axis=0)
        scatter = lambda value, dim=0: lax.psum_scatter(value.astype(F32), ALL, scatter_dimension=dim, tiled=True)
        blocks_one = one_grads[0].reshape(BLOCKS, 32, 4 * D)
        part = lambda row, rows, col: scatter(blocks_one[:, row : row + rows, col * D : (col + 1) * D].reshape(-1, D))
        out_g, q_g, k_g, v_g, o_g = part(0, 32, 0), part(0, 16, 1), part(0, 16, 2), part(16, 16, 1), part(16, 16, 2)
        in_g = jnp.concatenate([scatter(two_grads[0][:, :E]), part(0, 16, 3), part(16, 16, 3)], axis=1)
        small = two_grads[0][:, E:].reshape(BLOCKS, 16, 8, 32).transpose(2, 1, 0, 3).reshape(SMALL_ROWS, E)
        close = lambda row: scatter(small[row].reshape(BLOCKS, 32)[:, :16].reshape(D))
        g1, g2 = close(ROW_G1), close(ROW_G2)
        mine = scatter(small, 1)
        x_g, dt_g, a_g, cw_g = (
            mine[ROW_X : ROW_X + 64].T, mine[ROW_DT : ROW_DT + RANK], mine[ROW_A : ROW_A + NS].T, mine[ROW_CW : ROW_CW + KW].T)
        vectors = [mine[ROW_CB], mine[ROW_DB], mine[ROW_SK], g1, g2]
    cb_v, db_v, sk_v, g1_v, g2_v = vectors
    return (
        result[None], grad_tok[None], g1_v, in_g, cw_g, cb_v, x_g, dt_g, db_v, a_g, sk_v, out_g, g2_v, q_g, k_g, v_g, o_g,
    )


def attend(plan, pay, count):
    if plan.chunks == HEADS:
        held = plan.swap(pay)
        length = held.shape[0]
        half = pltpu.VMEM((length, HDIM), BF16)
        flat = pltpu.VMEM((HDIM, length), BF16)
        wide = pltpu.VMEM((length, HDIM), F32)
        (back,) = run(
            attention_kernel, [held], [((length, 4 * HDIM), BF16)], [half] * 4 + [flat] * 2 + [wide] * 2, us=4
        )
        return plan.swap(back)
    parts = pay.reshape(HEADS, count, 4, HDIM)
    query, key, value, grad = (parts[:, :, i] for i in range(4))
    key, value = (lax.all_gather(part, "ctx", axis=1, tiled=True) for part in (key, value))
    query_at = lax.axis_index("ctx") * count + jnp.arange(count)
    allowed = jnp.arange(key.shape[1])[None, :] <= query_at[:, None]
    scale = HDIM**-0.5
    dots = functools.partial(jnp.einsum, preferred_element_type=F32)
    scores = jnp.where(allowed, dots("hqd,hkd->hqk", query, key) * scale, -1e30)
    soft = jax.nn.softmax(scores, axis=-1)
    soft_low = soft.astype(BF16)
    grad_p = dots("hqd,hkd->hqk", grad, value)
    grad_s = (soft * (grad_p - jnp.sum(soft * grad_p, axis=-1, keepdims=True))).astype(BF16)
    raw = dots("hqk,hkd->hqd", soft_low, value).astype(BF16)
    grad_q = (dots("hqk,hkd->hqd", grad_s, key) * scale).astype(BF16)
    grads = (dots("hqk,hqd->hkd", grad_s, query) * scale, dots("hqk,hqd->hkd", soft_low, grad))
    grad_k, grad_v = (
        lax.psum_scatter(part.astype(BF16), "ctx", scatter_dimension=1, tiled=True) for part in grads
    )
    return jnp.concatenate([raw, grad_q, grad_k, grad_v], axis=-1).reshape(HEADS * count, 4 * HDIM)


def solution(mesh):
    plan = Plan(mesh)
    split, rows, cols = P(ALL), P(ALL, None), P(None, ALL)
    acts = P("dp", "ctx", None)
    return jax.shard_map(
        functools.partial(body, plan),
        mesh=mesh,
        in_specs=(acts, split, rows, rows, split, rows, cols, split, rows, split, rows, split, rows, rows, rows, rows, acts),
        out_specs=(acts, acts, split, rows, rows, split, rows, cols, split, rows, split, rows, split, rows, rows, rows, rows),
        check_vma=False,
    )
```

```python
import functools
import math

import jax
import jax.numpy as jnp
from jax import lax
from jax.experimental import pallas as pl
from jax.experimental.pallas import tpu as pltpu
from jax.sharding import PartitionSpec as P

D = 512
E = 1024
NS = 16
RANK = 32
KW = 4
HEADS = 8
HDIM = 64
LG = 8
HALO = 16
BLOCKS = 32
ALL = ("dp", "ctx")
EPS = 1e-05
LOG2E = 1.4426950408889634
LN2 = 0.6931471805599453
F32 = jnp.float32
BF16 = jnp.bfloat16
VM = pl.BlockSpec(memory_space=pltpu.VMEM)

Z_MASKS = (0, 4, 2, 6)
XY_MASKS = (0, 1, 16, 17)
CORE = 8
HALF_MASKS = tuple(xy | zz for xy in XY_MASKS for zz in Z_MASKS)
FULL_MASKS = HALF_MASKS + tuple(mask | CORE for mask in HALF_MASKS)
CHUNK_MASKS = tuple((8 if c & 1 else 0) | (2 if c & 2 else 0) | (1 if c & 4 else 0) for c in range(8))

ROW_X = 0
ROW_DT = 64
ROW_A = 96
ROW_CW = 112
ROW_CB = 116
ROW_DB = 117
ROW_SK = 118
ROW_G1 = 119
ROW_G2 = 120
SMALL_ROWS = 128


ANY = pl.BlockSpec(memory_space=pl.ANY)
FAR = pl.BlockSpec(memory_space=pltpu.HBM)
WHOLE = pl.BlockSpec()


def run(kernel, ins, outs, scratch=(), limit=12, raw=(), far=(), after=(), final=False, us=2):
    first, count = len(ins) + len(raw) + len(far), len(after)

    def inner(*refs):
        kernel(*refs[:first], *refs[first + count :])

    return pl.pallas_call(
        inner,
        out_shape=[jax.ShapeDtypeStruct(shape, dtype) for shape, dtype in outs],
        in_specs=[VM] * len(ins) + [ANY] * len(raw) + [FAR] * len(far) + [ANY] * count,
        out_specs=[WHOLE if final else VM] * len(outs),
        scratch_shapes=list(scratch),
        compiler_params=pltpu.CompilerParams(vmem_limit_bytes=limit * 2**20),
        cost_estimate=pl.CostEstimate(flops=int(us * 1e3), bytes_accessed=int(us * 3e3), transcendentals=0),
    )(*ins, *raw, *far, *after)


def nn(left, right):
    return lax.dot_general(left, right, (((1,), (0,)), ((), ())), preferred_element_type=F32)


def nt(left, right):
    return lax.dot_general(left, right, (((1,), (1,)), ((), ())), preferred_element_type=F32)


def tn(left, right):
    return lax.dot_general(left, right, (((0,), (0,)), ((), ())), preferred_element_type=F32)


def sigmoid(value):
    return 1.0 / (1.0 + jnp.exp(-value))


class Plan:
    def __init__(self, mesh):
        self.dp, self.ctx = mesh.shape["dp"], mesh.shape["ctx"]
        self.fast = (self.dp, self.ctx) == (4, 8)
        self.chunks = self.ctx
        if self.fast:
            self.grad_masks = (FULL_MASKS[:16], FULL_MASKS[16:])
        else:
            self.grad_masks = (tuple(range(BLOCKS)),)

    def place(self, seq, chunk):
        return CHUNK_MASKS[chunk] | ((seq >> 1) << 4) | ((seq & 1) << 2)

    def me(self):
        if self.fast:
            return lax.axis_index("dp") * 8 + lax.axis_index("ctx")
        return 0

    def chunk(self):
        if self.fast:
            lin = lax.axis_index("dp") * 8 + lax.axis_index("ctx")
            return ((lin >> 3) & 1) + ((lin >> 1) & 1) * 2 + (lin & 1) * 4
        return lax.axis_index("ctx")

    def side(self):
        return ((lax.axis_index("ctx") + lax.axis_index("dp") * 8) & CORE) != 0 if self.fast else False

    def swap(self, value):
        if self.fast:
            groups = [[self.place(s, c) for c in range(8)] for s in range(4)]
            return lax.all_to_all(value, ALL, 0, 0, tiled=True, axis_index_groups=groups)
        return lax.all_to_all(value, "ctx", 0, 0, tiled=True)


def send(value, mask):
    return lax.ppermute(value, ALL, [(i, i ^ mask) for i in range(32)])


def own_first(value, side, width):
    groups = [value[:, i * width : (i + 1) * width] for i in range(4)]
    pick = lambda x, own: jnp.where(side, groups[2 * x + own], groups[2 * x + 1 - own])
    return jnp.concatenate([pick(0, 1), pick(1, 1), pick(0, 0), pick(1, 0)], axis=1)


def in_order(value, side, width):
    own_a, own_b, far_a, far_b = (value[:, i * width : (i + 1) * width] for i in range(4))
    return jnp.concatenate(
        [jnp.where(side, far_a, own_a), jnp.where(side, own_a, far_a),
         jnp.where(side, far_b, own_b), jnp.where(side, own_b, far_b)], axis=1)


def rows_of(ref, half, first, cols):
    return jnp.concatenate(
        [ref[k * 32 + half * 16 : k * 32 + half * 16 + 16, first : first + cols] for k in range(ref.shape[0] // 32)], axis=0)


def wait_whole(target, sem):
    pltpu.make_async_copy(target, target, sem).wait()


def swap_blocks(value, me):
    rows, lanes = value.shape
    for bit in (16, 8, 4):
        half = bit * 32
        parts = [value[:, i : i + half] for i in range(0, lanes, half)]
        other = jnp.concatenate([parts[i ^ 1] for i in range(len(parts))], axis=1)
        value = jnp.where((me & bit) != 0, other, value)
    groups = []
    odd = (lax.broadcasted_iota(jnp.int32, (rows, 128), 1) & 32) != 0
    for i in range(0, lanes, 128):
        part = value[:, i : i + 128]
        part = jnp.where((me & 2) != 0, pltpu.roll(part, 64, 1), part)
        other = jnp.where(odd, pltpu.roll(part, 32, 1), pltpu.roll(part, 96, 1))
        groups.append(jnp.where((me & 1) != 0, other, part))
    return jnp.concatenate(groups, axis=1)


def pack_kernel(in_proj, x_proj, dt_proj, a_log, conv_w, conv_b, dt_bias, d_skip, gain_one, gain_two,
                out_proj, w_q, w_k, w_v, w_o, one, two, rows, *rest):
    (b_in, b_x, b_dt, b_a, b_cw, b_cb, b_db, b_sk, b_g1, b_g2, b_out, b_q, b_k, b_v, b_o, sems) = rest
    copies = [
        pltpu.make_async_copy(src, dst, sems.at[i])
        for i, (src, dst) in enumerate(
            zip((in_proj, x_proj, dt_proj, a_log, conv_w, conv_b, dt_bias, d_skip, gain_one, gain_two, out_proj, w_q,
                 w_k, w_v, w_o),
                (b_in, b_x, b_dt, b_a, b_cw, b_cb, b_db, b_sk, b_g1, b_g2, b_out, b_q, b_k, b_v, b_o))
        )
    ]
    for copy in copies:
        copy.start()
    for copy in copies:
        copy.wait()
    one[:, :E] = b_in[:, :E].astype(BF16)
    two[:16, 3 * D :] = b_in[:, E : E + D].astype(BF16)
    two[16:, 3 * D :] = b_in[:, E + D :].astype(BF16)
    two[:, :D] = b_out[...].astype(BF16)
    two[:16, D : 2 * D] = b_q[...].astype(BF16)
    two[:16, 2 * D : 3 * D] = b_k[...].astype(BF16)
    two[16:, D : 2 * D] = b_v[...].astype(BF16)
    two[16:, 2 * D : 3 * D] = b_o[...].astype(BF16)
    rows[...] = jnp.zeros_like(rows)
    rows[ROW_X : ROW_X + 64, :] = b_x[...].T
    rows[ROW_DT : ROW_DT + RANK, :] = b_dt[...]
    rows[ROW_A : ROW_A + NS, :] = b_a[...]
    rows[ROW_CW : ROW_CW + KW, :] = b_cw[...]
    rows[ROW_CB : ROW_CB + 1, :] = b_cb[...]
    rows[ROW_DB : ROW_DB + 1, :] = b_db[...]
    rows[ROW_SK : ROW_SK + 1, :] = b_sk[...]
    rows[ROW_G1 : ROW_G1 + 1, :16] = b_g1[...]
    rows[ROW_G2 : ROW_G2 + 1, :16] = b_g2[...]
    one[:, E:] = jnp.concatenate([rows[16 * q : 16 * q + 16, :] for q in range(8)], axis=1).astype(BF16)


def join_smalls(target, own, far, side):
    for q in range(8):
        rows = jnp.concatenate(
            [ref[16 * k : 16 * k + 16, E + 32 * q : E + 32 * q + 32].astype(F32) for ref in (own, far) for k in range(16)], axis=1)
        target[16 * q : 16 * q + 16, :] = in_order(rows, side, 256)


def gain_row(pm, row):
    return jnp.concatenate([pm[row : row + 1, 32 * s : 32 * s + 16] for s in range(BLOCKS)], axis=1)


def spread(target, source):
    count = source.shape[0]
    for s in range(LG):
        target[pl.ds(s, count, stride=LG), :] = source[:, s * 128 : (s + 1) * 128]


def gathered(source, count):
    return jnp.concatenate([source[pl.ds(s, count, stride=LG), :] for s in range(LG)], axis=1)


def broadcast_rows(target, proj, first):
    for n in range(NS):
        target[n] = jnp.broadcast_to(proj[:, first + n : first + n + 1], target.shape[1:])


def at8(ref, index):
    return ref[pl.ds(pl.multiple_of(index * 8, 8), 8), :]


def front_kernel(plan, tok, halo, own, far, normed, turned, u_out, conv_out, act_out, proj_out, sig_out, dt3, au3, a3,
                 state, pm, gains, bx, cx):
    side = plan.side()
    join_smalls(pm, own, far, side)
    gain = gain_row(pm, ROW_G1)
    gains[0:1, :] = gain
    gains[1:2, :] = gain_row(pm, ROW_G2)
    tokens = tok.shape[0]
    x = jnp.concatenate([halo[...].astype(F32), tok[...].astype(F32)], axis=0)
    r = lax.rsqrt(jnp.mean(x * x, axis=-1, keepdims=True) + EPS)
    low = x * r * gain
    normed[...] = low.astype(BF16)
    low = own_first(low, side, 128).astype(BF16)
    turned[...] = low
    u_out[...] = nn(low[:, : D // 2], own[:, :E]) + nn(low[:, D // 2 :], far[:, :E])
    conv = pm[ROW_CB : ROW_CB + 1, :]
    for k in range(KW):
        conv = conv + pm[ROW_CW + k : ROW_CW + k + 1, :] * u_out[HALO - 3 + k : HALO - 3 + k + tokens, :]
    conv_out[...] = conv
    act = (conv * sigmoid(conv)).astype(BF16)
    act_out[...] = act
    proj = nt(act, pm[ROW_X : ROW_X + 64, :].astype(BF16))
    proj_out[:, :64] = proj
    proj_out[:, 64:] = jnp.zeros((tokens, 64), F32)
    pre = nn(proj[:, :RANK].astype(BF16), pm[ROW_DT : ROW_DT + RANK, :].astype(BF16)) + pm[ROW_DB : ROW_DB + 1, :]
    sig_out[...] = sigmoid(pre)
    step = jnp.maximum(pre, 0.0) + jnp.log1p(jnp.exp(-jnp.abs(pre)))
    spread(dt3, step)
    spread(au3, act.astype(F32))
    spread(a3, -LOG2E * jnp.exp(pm[ROW_A : ROW_A + NS, :]))
    broadcast_rows(bx, proj, RANK)
    broadcast_rows(cx, proj, RANK + NS)
    decay = [a3[8 * n : 8 * n + 8, :] for n in range(NS)]

    def advance(t, carried):
        held, total = carried
        size = at8(dt3, t)
        drive = size * at8(au3, t)
        held = tuple(
            jnp.exp2(size * decay[n]) * held[n] + drive * bx[n, pl.ds(t, 1), :] for n in range(NS)
        )
        return held, total + size

    zero = jnp.zeros((8, 128), F32)
    held, total = lax.fori_loop(0, tokens, advance, ((zero,) * NS, zero), unroll=4)
    state[...] = jnp.concatenate([*held, total, zero], axis=0).astype(BF16)


def combine_kernel(plan, forward, states, a3, entry, states_f):
    states_f[...] = states[...].astype(F32)
    decay = [a3[8 * n : 8 * n + 8, :] for n in range(NS)]
    zero = jnp.zeros((8, 128), F32)

    def combine(i, held):
        base = (i if forward else plan.chunks - 1 - i) * 144
        total = states_f[pl.ds(pl.multiple_of(base + 128, 8), 8), :]
        return tuple(
            jnp.exp2(total * decay[n]) * held[n] + states_f[pl.ds(pl.multiple_of(base + 8 * n, 8), 8), :]
            for n in range(NS)
        )

    count = plan.chunk() if forward else plan.chunks - 1 - plan.chunk()
    held = lax.fori_loop(0, count, combine, (zero,) * NS)
    entry[...] = jnp.concatenate([*held, zero, zero], axis=0)


def merge_kernel(plan, step, forward, own, other, before, a3, group, entry):
    later = ((plan.chunk() >> step) & 1) == (1 if forward else 0)
    mine, theirs = own[...].astype(F32), other[...].astype(F32)
    first, second = jnp.where(later, theirs, mine), jnp.where(later, mine, theirs)
    decay = a3[...]
    spread_total = lambda value: jnp.concatenate([value[128:136, :]] * NS, axis=0)
    joint = jnp.exp2(spread_total(second) * decay) * first[:128, :] + second[:128, :]
    group[:128, :] = joint.astype(BF16)
    group[128:, :] = (first[128:, :] + second[128:, :]).astype(BF16)
    held = before[...]
    inner = held[:128, :] + jnp.exp2(spread_total(held) * decay) * theirs[:128, :]
    entry[:128, :] = jnp.where(later, inner, held[:128, :])
    entry[128:, :] = jnp.where(later, held[128:, :] + theirs[128:, :], held[128:, :])


def exchange(plan, state, a3, forward, beside=lambda step, entry: []):
    if plan.fast:
        group, entry, firsts = state, jnp.zeros((144, 128), F32), []
        for step in range(3):
            other = send(group, CHUNK_MASKS[1 << step])
            group, entry = run(
                functools.partial(merge_kernel, plan, step, forward), [group, other, entry, a3],
                [((144, 128), BF16), ((144, 128), F32)], after=beside(step, entry if step else group))
            firsts.append(entry)
        return entry, firsts
    states = lax.all_gather(state, "ctx", axis=0, tiled=True)
    return run(
        functools.partial(combine_kernel, plan, forward), [states, a3], [((144, 128), F32)],
        [pltpu.VMEM((144 * plan.chunks, 128), F32)])[0], []


def mid_kernel(plan, tok, dt3, au3, a3, turned, pm, gains, cot, entry, bx, cx, own, far,
               pay, mamba, gated_out, middle_out, all_states, z_out, y3):
    tokens = tok.shape[0]
    side = plan.side()
    both = lambda left, half, first, cols: nn(left[:, : D // 2], rows_of(own, half, first, cols)) + nn(
        left[:, D // 2 :], rows_of(far, half, first, cols))
    decay = [a3[8 * n : 8 * n + 8, :] for n in range(NS)]
    held = tuple(entry[8 * n : 8 * n + 8, :] for n in range(NS))
    all_states[:128, :] = entry[:128, :]

    def advance(t, held):
        size = at8(dt3, t)
        drive = size * at8(au3, t)
        base = pl.multiple_of(t * 128 + 128, 128)
        held = tuple(
            jnp.exp2(size * decay[n]) * held[n] + drive * bx[n, pl.ds(t, 1), :] for n in range(NS)
        )
        for n in range(NS):
            all_states[pl.ds(base + 8 * n, 8), :] = held[n]
        y = held[0] * cx[0, pl.ds(t, 1), :]
        for n in range(1, NS):
            y = y + held[n] * cx[n, pl.ds(t, 1), :]
        y3[pl.ds(pl.multiple_of(t * 8, 8), 8), :] = y
        return held

    lax.fori_loop(0, tokens, advance, held, unroll=4)
    act = gathered(au3, tokens)
    y = gathered(y3, tokens) + pm[ROW_SK : ROW_SK + 1, :] * act
    mamba[...] = y
    low = turned[HALO:, :]
    z = jnp.concatenate([both(low, 0, 3 * D, D), both(low, 1, 3 * D, D)], axis=1)
    z_out[...] = z
    gated = y * (z * sigmoid(z))
    gated_out[...] = gated.astype(BF16)
    gated = own_first(gated, side, 256).astype(BF16)
    middle = tok[...].astype(F32) + nn(gated[:, : E // 2], own[:, :D]) + nn(gated[:, E // 2 :], far[:, :D])
    middle_out[...] = middle
    r = lax.rsqrt(jnp.mean(middle * middle, axis=-1, keepdims=True) + EPS)
    low = own_first(middle * r * gains[1:2, :], side, 128).astype(BF16)
    query_key, value = both(low, 0, D, 2 * D), both(low, 1, D, D)
    grad = jnp.concatenate([nt(cot[...], rows_of(ref, 1, 2 * D, D)) for ref in (own, far)], axis=1)
    quads = tuple(part.astype(BF16) for part in (query_key[:, :D], query_key[:, D:], value, in_order(grad, side, 128)))
    for h in range(HEADS):
        for i, part in enumerate(quads):
            pay[h * tokens : (h + 1) * tokens, i * HDIM : (i + 1) * HDIM] = part[:, h * HDIM : (h + 1) * HDIM]


def attention_kernel(pay, back, q_s, k_s, v_s, g_s, kt, vt, dk, dv):
    length = pay.shape[0]
    rows = math.gcd(length, 512)
    q_s[...] = pay[:, :HDIM]
    k_s[...] = pay[:, HDIM : 2 * HDIM]
    v_s[...] = pay[:, 2 * HDIM : 3 * HDIM]
    g_s[...] = pay[:, 3 * HDIM :]
    kt[...] = k_s[...].T
    vt[...] = v_s[...].T
    dk[...] = jnp.zeros_like(dk)
    dv[...] = jnp.zeros_like(dv)
    scale = HDIM**-0.5
    key_at = lax.broadcasted_iota(jnp.int32, (rows, rows), 0)
    query_at = lax.broadcasted_iota(jnp.int32, (rows, rows), 1)
    for i in range(length // rows):
        first, last = i * rows, (i + 1) * rows
        query = q_s[first:last, :]
        grad = g_s[first:last, :]
        scores = nt(k_s[:last, :], query) * scale
        diagonal = jnp.where(key_at <= query_at, scores[first:, :], -1e30)
        scores = diagonal if i == 0 else jnp.concatenate([scores[:first, :], diagonal], axis=0)
        expo = jnp.exp(scores - jnp.max(scores, axis=0, keepdims=True))
        soft = expo * (1.0 / jnp.sum(expo, axis=0, keepdims=True))
        soft_low = soft.astype(BF16)
        grad_p = nt(v_s[:last, :], grad)
        dot = jnp.sum(soft * grad_p, axis=0, keepdims=True)
        grad_s = (soft * (grad_p - dot)).astype(BF16)
        raw = nn(vt[:, :last], soft_low)
        grad_q = nn(kt[:, :last], grad_s) * scale
        back[first:last, :HDIM] = raw.T.astype(BF16)
        back[first:last, HDIM : 2 * HDIM] = grad_q.T.astype(BF16)
        dk[:last, :] += nn(grad_s, query)
        dv[:last, :] += nn(soft_low, grad)
    back[:, 2 * HDIM : 3 * HDIM] = (dk[...] * scale).astype(BF16)
    back[:, 3 * HDIM :] = dv[...].astype(BF16)


def turn_kernel(plan, got, middle, cot, gains, z_in, mamba, dt3, cx, a3, own, far, first,
                att, gq, gk, gv, grad_middle, mix, gz, gy3, state, gain_grad):
    tokens = middle.shape[0]
    for h in range(HEADS):
        for i, part in enumerate((att, gq, gk, gv)):
            part[:, h * HDIM : (h + 1) * HDIM] = got[h * tokens : (h + 1) * tokens, i * HDIM : (i + 1) * HDIM]
    side = plan.side()
    grad_n = in_order(jnp.concatenate(
        [nt(gq[...], rows_of(ref, 0, D, D)) + nt(gk[...], rows_of(ref, 0, 2 * D, D)) + nt(gv[...], rows_of(ref, 1, D, D))
         for ref in (own, far)], axis=1), side, 128)
    mid = middle[...]
    r = lax.rsqrt(jnp.mean(mid * mid, axis=-1, keepdims=True) + EPS)
    gain_grad[...] = jnp.sum(grad_n * mid * r, axis=0, keepdims=True)
    q = grad_n * gains[1:2, :]
    gm = cot[...].astype(F32) + r * q - mid * (r * r * r) * jnp.mean(q * mid, axis=-1, keepdims=True)
    grad_middle[...] = gm
    low = gm.astype(BF16)
    mix[...] = low
    grad_gated = in_order(jnp.concatenate([nt(low, ref[:, :D]) for ref in (own, far)], axis=1), side, 256)
    z = z_in[...]
    s = sigmoid(z)
    spread(gy3, grad_gated * (z * s))
    gz[...] = (grad_gated * mamba[...] * (s * (1.0 + z * (1.0 - s)))).astype(BF16)
    decay = [a3[8 * n : 8 * n + 8, :] for n in range(NS)]

    def retreat(i, carried):
        t = tokens - 1 - i
        size = at8(dt3, t)
        grad = at8(gy3, t)
        return tuple(
            jnp.exp2(size * decay[n]) * (carried[n] + grad * cx[n, pl.ds(t, 1), :]) for n in range(NS)
        )

    zero = jnp.zeros((8, 128), F32)
    carried = lax.fori_loop(0, tokens, retreat, (zero,) * NS, unroll=4)
    state[:128, :] = jnp.concatenate(carried, axis=0).astype(BF16)
    state[128:, :] = first[128:, :]


def pack_blocks(plan, outs, source, rows, height, row, first, col=0, cols=None):
    me = plan.me()
    cols = source.shape[1] if cols is None else cols
    for out, masks in zip(outs, plan.grad_masks):
        for k, mask in enumerate(masks):
            block = me ^ mask
            out[k * height + row : k * height + row + rows, first : first + cols] = source[
                pl.ds(pl.multiple_of(block * rows, 16), rows), col : col + cols
            ].astype(BF16)


def grad_c_kernel(gy3, all_states, grad_c):
    diagonal_sums(grad_c, 0, lambda rows: gy3[rows, :], all_states, 1)


def weights_kernel(plan, no, att, gq, gk, gv, mix, gated, middle, gains, cot, own, far, normed, gz, *refs):
    result, outs = refs[0], refs[1 : 1 + no]
    small, large, wide = refs[1 + no :]
    mid = middle[...]
    held = own_first(att[...], plan.side(), 128)
    result[...] = (
        mid + nn(held[:, : D // 2], rows_of(own, 1, 2 * D, D)) + nn(held[:, D // 2 :], rows_of(far, 1, 2 * D, D))
    ).astype(BF16)
    r = lax.rsqrt(jnp.mean(mid * mid, axis=-1, keepdims=True) + EPS)
    low = (mid * r * gains[1:2, :]).astype(BF16)
    large[...] = tn(gated[...], mix[...])
    pack_blocks(plan, outs, large, 32, 32, 0, 0)
    small[...] = tn(low, gq[...])
    pack_blocks(plan, outs, small, 16, 32, 0, D)
    small[...] = tn(low, gk[...])
    pack_blocks(plan, outs, small, 16, 32, 0, 2 * D)
    small[...] = tn(low, gv[...])
    pack_blocks(plan, outs, small, 16, 32, 16, D)
    small[...] = tn(att[...], cot[...])
    pack_blocks(plan, outs, small, 16, 32, 16, 2 * D)
    wide[...] = tn(normed[HALO:, :], gz[...])
    pack_blocks(plan, outs, wide, 16, 32, 0, 3 * D, 0, D)
    pack_blocks(plan, outs, wide, 16, 32, 16, 3 * D, D, D)


def diagonal_sums(out, col, channels, held, offset, span=16):
    row_t = lax.broadcasted_iota(jnp.int32, (span, span * NS), 0)
    col_t = lax.broadcasted_iota(jnp.int32, (span, span * NS), 1) // NS
    pick = (
        lax.broadcasted_iota(jnp.int32, (span * NS, NS), 0) % NS
        == lax.broadcasted_iota(jnp.int32, (span * NS, NS), 1)
    ).astype(BF16)
    for block in range(out.shape[0] // span):
        total = jnp.zeros((span, span * NS), F32)
        for s in range(LG):
            held_rows = held[pl.ds((block * span + offset) * 128 + s, span * NS, stride=LG), :].astype(BF16)
            total = total + nt(channels(pl.ds(block * span * 8 + s, span, stride=LG)).astype(BF16), held_rows)
        own = jnp.where(row_t == col_t, total, 0.0).astype(BF16)
        out[block * span : (block + 1) * span, col : col + NS] = nn(own, pick)


def back_kernel(plan, dt3, au3, gy3, a3, proj, pm, all_states, sig, act, conv_in, u_in, leaving, bx, cx, grad_c,
                small_grads, gu_out, grads, gs3, ga3, gal, skip3, low_rank, padded):
    tokens = dt3.shape[0] // LG
    decay = [a3[8 * n : 8 * n + 8, :] for n in range(NS)]
    zero = jnp.zeros((8, 128), F32)
    spread(skip3, pm[ROW_SK : ROW_SK + 1, :])
    skip = skip3[...]

    carried = tuple(leaving[8 * n : 8 * n + 8, :] for n in range(NS))
    gal[...] = jnp.zeros_like(gal)

    def retreat(i, state):
        carried, skipped = state
        t = tokens - 1 - i
        size, value, grad = at8(dt3, t), at8(au3, t), at8(gy3, t)
        base = pl.multiple_of(t * 128, 128)
        from_b = zero
        from_a = zero
        fresh = []
        for n in range(NS):
            g = carried[n] + grad * cx[n, pl.ds(t, 1), :]
            grads[pl.ds(base + 8 * n, 8), :] = g
            w = jnp.exp2(size * decay[n]) * g
            q = w * all_states[pl.ds(base + 8 * n, 8), :]
            from_a = from_a + decay[n] * q
            from_b = from_b + g * bx[n, pl.ds(t, 1), :]
            gal[8 * n : 8 * n + 8, :] += size * q
            fresh.append(w)
        at = pl.ds(pl.multiple_of(t * 8, 8), 8)
        gs3[at, :] = from_a * LN2 + from_b * value
        ga3[at, :] = from_b * size + skip * grad
        return tuple(fresh), skipped + grad * value

    _, skipped = lax.fori_loop(0, tokens, retreat, (carried, zero), unroll=4)

    diagonal_sums(low_rank, RANK, lambda rows: dt3[rows, :] * au3[rows, :], grads, 0)
    low_rank[:, RANK + NS : RANK + 2 * NS] = grad_c[:, :NS]

    grad_pre = gathered(gs3, tokens) * sig[...]
    grad_pre_low = grad_pre.astype(BF16)
    low_rank[:, :RANK] = nt(grad_pre_low, pm[ROW_DT : ROW_DT + RANK, :].astype(BF16))
    projected = low_rank[:, :64].astype(BF16)
    small_grads[ROW_X : ROW_X + 64, :] = tn(projected, act[...])
    small_grads[ROW_DT : ROW_DT + RANK, :] = tn(proj[:, :RANK].astype(BF16), grad_pre_low)
    true_a = -jnp.exp(pm[ROW_A : ROW_A + NS, :])
    small_grads[ROW_A : ROW_A + NS, :] = gathered(gal, NS) * true_a
    small_grads[ROW_DB : ROW_DB + 1, :] = jnp.sum(grad_pre, axis=0, keepdims=True)
    skip3[...] = skipped
    small_grads[ROW_SK : ROW_SK + 1, :] = gathered(skip3, 1)
    small_grads[ROW_G1:, :] = jnp.zeros((SMALL_ROWS - ROW_G1, E), F32)
    conv = conv_in[...]
    s = sigmoid(conv)
    grad_act = gathered(ga3, tokens) + nn(projected, pm[ROW_X : ROW_X + 64, :].astype(BF16))
    grad_conv = grad_act * (s * (1.0 + conv * (1.0 - s)))
    small_grads[ROW_CB : ROW_CB + 1, :] = jnp.sum(grad_conv, axis=0, keepdims=True)
    for k in range(KW):
        small_grads[ROW_CW + k : ROW_CW + k + 1, :] = jnp.sum(
            grad_conv * u_in[HALO - 3 + k : HALO - 3 + k + tokens, :], axis=0, keepdims=True
        )
    padded[:HALO, :] = jnp.zeros((HALO, E), F32)
    padded[HALO : HALO + tokens, :] = grad_conv
    padded[HALO + tokens :, :] = jnp.zeros((HALO, E), F32)
    gu = jnp.zeros((HALO + tokens, E), F32)
    for k in range(KW):
        gu = gu + pm[ROW_CW + k : ROW_CW + k + 1, :] * padded[3 - k : 3 - k + HALO + tokens, :]
    gu_out[...] = gu.astype(BF16)


def last_kernel(plan, no, tok, halo, gains, gu, gz, grad_middle, own_u, far_u, own_z, far_z, normed, small_grads, gain_two, *refs):
    outs = refs[:no]
    own, before, large, spaced = refs[no:]
    me = plan.me()
    large[...] = tn(normed[...], gu[...])
    pack_blocks(plan, outs, large, 16, 16, 0, 0)
    x = jnp.concatenate([halo[...].astype(F32), tok[...].astype(F32)], axis=0)
    r = lax.rsqrt(jnp.mean(x * x, axis=-1, keepdims=True) + EPS)
    from_z = jnp.concatenate(
        [nt(gz[:, :D], rows_of(ref, 0, 3 * D, D)) + nt(gz[:, D:], rows_of(ref, 1, 3 * D, D)) for ref in (own_z, far_z)], axis=1)
    from_u = jnp.concatenate([nt(gu[...], ref[:, :E]) for ref in (own_u, far_u)], axis=1)
    grad_n = in_order(from_u + jnp.concatenate([jnp.zeros((HALO, D), F32), from_z], axis=0), plan.side(), 128)
    gain_one = jnp.sum(grad_n * x * r, axis=0, keepdims=True)
    q = grad_n * gains[0:1, :]
    base = r * q - x * (r * r * r) * jnp.mean(q * x, axis=-1, keepdims=True)
    own[...] = (grad_middle[...] + base[HALO:, :]).astype(BF16)
    before[...] = base[:HALO, :].astype(BF16)
    spaced[...] = small_grads[...]
    blank = jnp.zeros((1, 16), F32)
    for row, grad in ((ROW_G1, gain_one), (ROW_G2, gain_two[...])):
        spaced[row : row + 1, :] = jnp.concatenate(
            [part for s in range(BLOCKS) for part in (grad[:, 16 * s : 16 * s + 16], blank)], axis=1)
    spaced[...] = swap_blocks(spaced[...], me)
    for out, masks in zip(outs, plan.grad_masks):
        for k, m in enumerate(masks):
            out[16 * k : 16 * k + 16, E:] = jnp.concatenate(
                [spaced[16 * q : 16 * q + 16, 32 * m : 32 * m + 32] for q in range(8)], axis=1).astype(BF16)


def total_of(ins):
    total = ins[0][...].astype(F32)
    for other in ins[1:]:
        total = total + other[...].astype(F32)
    return total


def finish_kernel(*refs):
    (own, tail, result), refs = refs[:3], refs[3:]
    u_ins, ins, (own_out, result_out), refs = refs[:4], refs[4:6], refs[6:8], refs[2:]
    rows = own.shape[0] - HALO
    own_out[:rows, :] = own[:rows, :]
    own_out[rows:, :] = (own[rows:, :].astype(F32) + tail[...].astype(F32)).astype(BF16)
    result_out[...] = result[...]
    out_g, q_g, k_g, v_g, o_g, in_g, x_g, dt_g, a_g, cw_g, cb_g, db_g, sk_g, g1_g, g2_g, rows = refs[6:]
    total = total_of(ins)
    out_g[...] = total[:, :D]
    q_g[...] = total[:16, D : 2 * D]
    k_g[...] = total[:16, 2 * D : 3 * D]
    v_g[...] = total[16:, D : 2 * D]
    o_g[...] = total[16:, 2 * D : 3 * D]
    in_g[:, E : E + D] = total[:16, 3 * D :]
    in_g[:, E + D :] = total[16:, 3 * D :]
    total = total_of(u_ins)
    in_g[:, :E] = total[:, :E]
    for q in range(8):
        rows[16 * q : 16 * q + 16, :] = total[:, E + 32 * q : E + 32 * q + 32]
    x_g[...] = rows[ROW_X : ROW_X + 64, :].T
    dt_g[...] = rows[ROW_DT : ROW_DT + RANK, :]
    a_g[...] = rows[ROW_A : ROW_A + NS, :]
    cw_g[...] = rows[ROW_CW : ROW_CW + KW, :]
    cb_g[...] = rows[ROW_CB : ROW_CB + 1, :]
    db_g[...] = rows[ROW_DB : ROW_DB + 1, :]
    sk_g[...] = rows[ROW_SK : ROW_SK + 1, :]
    g1_g[...] = rows[ROW_G1 : ROW_G1 + 1, :16]
    g2_g[...] = rows[ROW_G2 : ROW_G2 + 1, :16]


def join_kernel(plan, counts, placed, *refs):
    ins, outs = refs[: sum(counts)], refs[sum(counts) :]
    at = 0
    for i, count in enumerate(counts):
        rows = outs[i].shape[0] // count
        for k in range(count):
            part = ins[at + k]
            if not placed[i]:
                outs[i][k * rows : (k + 1) * rows, :] = part[...]
                continue
            height = rows // len(Z_MASKS)
            for j, zz in enumerate(Z_MASKS):
                owner = plan.me() ^ (XY_MASKS[k] | zz)
                to = (((owner >> 4) & 1) * 8 + (owner & 7)) * height
                outs[i][pl.ds(pl.multiple_of(to, 16), height), :] = part[j * height : (j + 1) * height, :]
        at += count


def join(plan, groups, after=(), placed=()):
    counts = [len(group) for group in groups]
    outs = [((group[0].shape[0] * len(group), group[0].shape[1]), group[0].dtype) for group in groups]
    return run(
        functools.partial(join_kernel, plan, counts, [i in placed for i in range(len(groups))]),
        [part for group in groups for part in group], outs, after=after, us=1)


def spread_out(value, stage):
    return [value] + [send(value, mask) for mask in stage[1:]]


def cut_one_kernel(keep, got, a_keep, a_give, b_keep, b_give):
    half, quarter, cols = keep.shape[0] // 2, keep.shape[0] // 4, keep.shape[1] // 2
    add = lambda rows, lanes: (keep[rows, lanes].astype(F32) + got[rows, lanes].astype(F32)).astype(BF16)
    left, right = slice(0, cols), slice(cols, 2 * cols)
    a_keep[...] = add(slice(0, half), left)
    a_give[...] = add(slice(half, 2 * half), left)
    for i in range(2):
        b_keep[i * quarter : (i + 1) * quarter, :] = add(slice(2 * i * quarter, (2 * i + 1) * quarter), right)
        b_give[i * quarter : (i + 1) * quarter, :] = add(slice((2 * i + 1) * quarter, (2 * i + 2) * quarter), right)


def cut_two_kernel(a_own, a_got, b_own, b_got, a_keep, a_give, b_keep, b_give):
    rows = a_own.shape[0] // 2
    for own, got, keep, give in ((a_own, a_got, a_keep, a_give), (b_own, b_got, b_keep, b_give)):
        for out, part in ((keep, slice(0, rows)), (give, slice(rows, 2 * rows))):
            out[...] = (own[part, :].astype(F32) + got[part, :].astype(F32)).astype(BF16)


def add_rows(out, rows, ins, cols=slice(None), to=slice(None)):
    total = ins[0][rows, cols].astype(F32)
    for other in ins[1:]:
        total = total + other[rows, cols].astype(F32)
    out[:, to] = total.astype(out.dtype)


def cut_three_kernel(u_own, u_got, a_own, a_got, b_own, b_got, u_0, u_1, u_2, u_3, keep, give):
    rows = u_0.shape[0]
    for i, out in enumerate((u_0, u_1, u_2, u_3)):
        add_rows(out, slice(i * rows, (i + 1) * rows), (u_own, u_got))
    rows, cols = keep.shape[0], a_own.shape[1]
    for i, out in enumerate((keep, give)):
        part = slice(i * rows, (i + 1) * rows)
        add_rows(out, part, (a_own, a_got), to=slice(0, cols))
        add_rows(out, part, (b_own, b_got), to=slice(cols, 2 * cols))


def cut_four_kernel(u_own, u_a, u_b, u_c, own, got, u_0, u_1, u_2, u_3, keep, give):
    rows = u_0.shape[0]
    for i, out in enumerate((u_0, u_1, u_2, u_3)):
        add_rows(out, slice(i * rows, (i + 1) * rows), (u_own, u_a, u_b, u_c))
    rows = keep.shape[0]
    for i, out in enumerate((keep, give)):
        add_rows(out, slice(i * rows, (i + 1) * rows), (own, got))


def body(plan, *args):
    (tokens, mixer_gain, in_proj, conv_weight, conv_bias, x_proj, dt_proj, dt_bias, a_log, d_skip, out_proj,
     attn_gain, w_query, w_key, w_value, w_output, cotangent) = args
    count = tokens.shape[1]
    tok0, cot0 = tokens.reshape(count, D), cotangent.reshape(count, D)
    chunks = plan.chunks
    devices = plan.dp * plan.ctx
    share, width = E // devices, D // devices
    if plan.fast:
        home = [(s * 8 + c, plan.place(s, c)) for s in range(4) for c in range(8)]
        tok = lax.ppermute(tok0, ALL, home)
        halo = lax.ppermute(
            tok0[count - HALO :], ALL, [(s * 8 + c, plan.place(s, c + 1)) for s in range(4) for c in range(7)]
        )
        raw = [in_proj, x_proj, dt_proj, a_log.T, conv_weight.T, conv_bias[None], dt_bias[None], d_skip[None],
               mixer_gain[None], attn_gain[None], out_proj, w_query, w_key, w_value, w_output]
        pack_one, pack_two = run(
            pack_kernel, [], [((16, E + 256), BF16), ((32, 4 * D), BF16)],
            [pltpu.VMEM((SMALL_ROWS, 32), F32)] + [pltpu.VMEM(value.shape, F32) for value in raw]
            + [pltpu.SemaphoreType.DMA((len(raw),))], far=raw, limit=60)
        two_far = send(pack_two, 4)
        (one,) = join(plan, [[pack_one, send(pack_one, 4)]])
        cot = lax.ppermute(cot0, ALL, home)
        one, two = join(plan, [[one, send(one, 2)], [pack_two, two_far]], [tok, halo])
        two_far = send(two, 2)
        one, two = join(plan, [spread_out(one, XY_MASKS), [two, two_far]], [cot], (0,))
        one = [one, send(one, CORE)]
        near_two = spread_out(two, XY_MASKS)
    else:
        tok, cot = tok0, cot0
        halo = lax.ppermute(tok0[count - HALO :], "ctx", [(c, c + 1) for c in range(chunks - 1)])
        smalls = jnp.concatenate(
            [x_proj.T, dt_proj, a_log.T, conv_weight.T, conv_bias[None], dt_bias[None], d_skip[None],
             jnp.pad(mixer_gain, (0, share - width))[None], jnp.pad(attn_gain, (0, share - width))[None],
             jnp.zeros((SMALL_ROWS - ROW_G2 - 1, share), F32)], axis=0).astype(BF16)
        small_all = lax.all_gather(smalls, ALL, axis=1, tiled=True)
        apart = lambda row: jnp.pad(
            small_all[row].reshape(devices, share)[:, :width].reshape(BLOCKS, 16), ((0, 0), (0, 16))).reshape(1, E)
        small_all = jnp.concatenate(
            [small_all[:ROW_G1], apart(ROW_G1), apart(ROW_G2), small_all[ROW_G2 + 1 :]], axis=0)
        small_all = small_all.reshape(8, 16, BLOCKS, 32).transpose(2, 1, 0, 3).reshape(BLOCKS * 16, 256)
        whole = lambda value: lax.all_gather(value.astype(BF16), ALL, axis=0, tiled=True)
        in_all = whole(in_proj)
        halves = lambda value: [value.reshape(2, 2, -1, value.shape[1])[:, i].reshape(-1, value.shape[1]) for i in range(2)]
        one = halves(jnp.concatenate([in_all[:, :E], small_all], axis=1))
        out_all, q_all, k_all, v_all, o_all = (whole(w) for w in (out_proj, w_query, w_key, w_value, w_output))
        cut = lambda value: value.reshape(BLOCKS, 16, D)
        side = jnp.concatenate(
            [jnp.concatenate([cut(q_all), cut(k_all)], axis=2), jnp.concatenate([cut(v_all), cut(o_all)], axis=2)], axis=1)
        gate = jnp.concatenate([cut(in_all[:, E : E + D]), cut(in_all[:, E + D :])], axis=1)
        two = halves(jnp.concatenate([out_all.reshape(BLOCKS, 32, D), side, gate], axis=2).reshape(BLOCKS * 32, 4 * D))

    no = len(plan.grad_masks)
    rows3 = count * LG
    (normed, turned, u_pre, conv, act, proj, sig, dt3, au3, a3, state, pm, gains, bx, cx) = run(
        functools.partial(front_kernel, plan),
        [tok, halo, *one],
        [((HALO + count, D), BF16), ((HALO + count, D), BF16), ((HALO + count, E), F32), ((count, E), F32),
         ((count, E), BF16), ((count, 128), F32), ((count, E), F32), ((rows3, 128), F32), ((rows3, 128), F32),
         ((128, 128), F32), ((144, 128), BF16), ((SMALL_ROWS, E), F32), ((8, D), F32),
         ((NS, count, 128), F32), ((NS, count, 128), F32)], us=6,
    )
    entry, firsts = exchange(plan, state, a3, True)
    if plan.fast:
        (held,) = join(plan, [near_two], firsts[1:2], (0,))
        two = [held, send(held, CORE)]
    pay, mamba, gated, middle, all_states, z = run(
        functools.partial(mid_kernel, plan),
        [tok, dt3, au3, a3, turned, pm, gains, cot, entry, bx, cx, *two],
        [((HEADS * count, 4 * HDIM), BF16), ((count, E), F32), ((count, E), BF16), ((count, D), F32),
         (((count + 1) * 128, 128), F32), ((count, E), F32)],
        [pltpu.VMEM((rows3, 128), F32)], us=6,
    )
    got = attend(plan, pay, count)
    (att, gq, gk, gv, grad_middle, mix, gz, gy3, later, gain_grad_two) = run(
        functools.partial(turn_kernel, plan),
        [got, middle, cot, gains, z, mamba, dt3, cx, a3, *two, state],
        [((count, D), BF16)] * 4 + [((count, D), F32), ((count, D), BF16), ((count, E), BF16), ((rows3, 128), F32),
                                    ((144, 128), BF16), ((1, D), F32)],
    )
    blocks = [len(masks_of) for masks_of in plan.grad_masks]

    def weight_grads(after):
        return run(
            functools.partial(weights_kernel, plan, no),
            [att, gq, gk, gv, mix, gated, middle, gains, cot, *two, normed, gz],
            [((count, D), BF16)] + [((n * 32, 4 * D), BF16) for n in blocks],
            [pltpu.VMEM((D, D), F32), pltpu.VMEM((E, D), F32), pltpu.VMEM((D, E), F32)], after=after)

    def c_grads(after):
        return run(grad_c_kernel, [gy3, all_states], [((count, 128), F32)], after=after)

    done, extra = [], []

    def beside(step, entry):
        if step == 1:
            done.extend(weight_grads([entry]))
            return done[:1]
        if step == 2:
            extra.extend(c_grads([entry]))
        return list(extra)

    leaving, _ = exchange(plan, later, a3, False, beside)
    result, *one_grads = done or weight_grads([])
    (grad_c,) = extra or c_grads([])
    one_parts = []
    if plan.fast:
        result = lax.ppermute(result, ALL, [(b, a) for a, b in home])
        rows = blocks[0] * 32
        one_parts = run(
            cut_one_kernel, [one_grads[0], send(one_grads[1], CORE)], [((rows // 2, 2 * D), BF16)] * 4, after=[leaving])
    small_grads, gu = run(
        functools.partial(back_kernel, plan),
        [dt3, au3, gy3, a3, proj, pm, all_states, sig, act, conv, u_pre, leaving, bx, cx, grad_c],
        [((SMALL_ROWS, E), F32), ((HALO + count, E), BF16)],
        [pltpu.VMEM((count * 128, 128), F32), pltpu.VMEM((rows3, 128), F32), pltpu.VMEM((rows3, 128), F32),
         pltpu.VMEM((128, 128), F32), pltpu.VMEM((8, 128), F32), pltpu.VMEM((count, 128), F32),
         pltpu.VMEM((count + 2 * HALO, E), F32)],
        limit=32, after=one_parts[:1], us=11,
    )
    *two_grads, own, before = run(
        functools.partial(last_kernel, plan, no),
        [tok, halo, gains, gu, gz, grad_middle, *one, *two, normed, small_grads, gain_grad_two],
        [((n * 16, E + 256), BF16) for n in blocks] + [((count, D), BF16), ((HALO, D), BF16)],
        [pltpu.VMEM((D, E), F32), pltpu.VMEM((SMALL_ROWS, E), F32)], after=[result],
    )
    if plan.fast:
        a_keep, a_give, b_keep, b_give = one_parts
        one_parts = run(
            cut_two_kernel, [a_keep, send(a_give, 16), b_keep, send(b_give, 1)], [((rows // 4, 2 * D), BF16)] * 4,
            after=[two_grads[0]])
    if plan.fast:
        back = [(b, a) for a, b in home]
        grad_tok = lax.ppermute(own, ALL, back)
        tail = lax.ppermute(
            before, ALL, [(plan.place(s, c + 1), s * 8 + c) for s in range(4) for c in range(7)])
        a_keep, a_give, b_keep, b_give = one_parts
        sends = lambda parts, stage: [parts[0]] + [send(part, mask) for part, mask in zip(parts[1:], stage[1:])]
        n = blocks[0]
        *u_parts, keep, give = run(
            cut_three_kernel,
            [two_grads[0], send(two_grads[1], CORE), a_keep, send(a_give, 1), b_keep, send(b_give, 16)],
            [((n * 4, E + 256), BF16)] * 4 + [((n * 4, 4 * D), BF16)] * 2, after=[tail])
        *u_parts, keep, give = run(
            cut_four_kernel, [*sends(u_parts, XY_MASKS), keep, send(give, 2)],
            [((n, E + 256), BF16)] * 4 + [((n * 2, 4 * D), BF16)] * 2, after=[grad_tok])
        grad_tok, result, out_g, q_g, k_g, v_g, o_g, in_g, x_g, dt_g, a_g, cw_g, cb_g, db_g, sk_g, g1_g, g2_g = run(
            finish_kernel, [grad_tok, tail, result, *sends(u_parts, Z_MASKS), keep, send(give, 4)],
            [((count, D), BF16)] * 2 + [((32, D), F32)] + [((16, D), F32)] * 4
            + [((16, 2 * E), F32), ((32, 64), F32), ((32, 32), F32), ((NS, 32), F32), ((KW, 32), F32)]
            + [((1, 32), F32)] * 3 + [((1, 16), F32)] * 2,
            [pltpu.VMEM((SMALL_ROWS, 32), F32)], final=True)
        a_g, cw_g = a_g.T, cw_g.T
        vectors = [value[0] for value in (cb_g, db_g, sk_g, g1_g, g2_g)]
    else:
        tail = lax.ppermute(before, "ctx", [(c + 1, c) for c in range(chunks - 1)])
        end = (own[count - HALO :].astype(F32) + tail.astype(F32)).astype(BF16)
        grad_tok = jnp.concatenate([own[: count - HALO], end], axis=0)
        scatter = lambda value, dim=0: lax.psum_scatter(value.astype(F32), ALL, scatter_dimension=dim, tiled=True)
        blocks_one = one_grads[0].reshape(BLOCKS, 32, 4 * D)
        part = lambda row, rows, col: scatter(blocks_one[:, row : row + rows, col * D : (col + 1) * D].reshape(-1, D))
        out_g, q_g, k_g, v_g, o_g = part(0, 32, 0), part(0, 16, 1), part(0, 16, 2), part(16, 16, 1), part(16, 16, 2)
        in_g = jnp.concatenate([scatter(two_grads[0][:, :E]), part(0, 16, 3), part(16, 16, 3)], axis=1)
        small = two_grads[0][:, E:].reshape(BLOCKS, 16, 8, 32).transpose(2, 1, 0, 3).reshape(SMALL_ROWS, E)
        close = lambda row: scatter(small[row].reshape(BLOCKS, 32)[:, :16].reshape(D))
        g1, g2 = close(ROW_G1), close(ROW_G2)
        mine = scatter(small, 1)
        x_g, dt_g, a_g, cw_g = (
            mine[ROW_X : ROW_X + 64].T, mine[ROW_DT : ROW_DT + RANK], mine[ROW_A : ROW_A + NS].T, mine[ROW_CW : ROW_CW + KW].T)
        vectors = [mine[ROW_CB], mine[ROW_DB], mine[ROW_SK], g1, g2]
    cb_v, db_v, sk_v, g1_v, g2_v = vectors
    return (
        result[None], grad_tok[None], g1_v, in_g, cw_g, cb_v, x_g, dt_g, db_v, a_g, sk_v, out_g, g2_v, q_g, k_g, v_g, o_g,
    )


def attend(plan, pay, count):
    if plan.chunks == HEADS:
        held = plan.swap(pay)
        length = held.shape[0]
        half = pltpu.VMEM((length, HDIM), BF16)
        flat = pltpu.VMEM((HDIM, length), BF16)
        wide = pltpu.VMEM((length, HDIM), F32)
        (back,) = run(
            attention_kernel, [held], [((length, 4 * HDIM), BF16)], [half] * 4 + [flat] * 2 + [wide] * 2, us=4
        )
        return plan.swap(back)
    parts = pay.reshape(HEADS, count, 4, HDIM)
    query, key, value, grad = (parts[:, :, i] for i in range(4))
    key, value = (lax.all_gather(part, "ctx", axis=1, tiled=True) for part in (key, value))
    query_at = lax.axis_index("ctx") * count + jnp.arange(count)
    allowed = jnp.arange(key.shape[1])[None, :] <= query_at[:, None]
    scale = HDIM**-0.5
    dots = functools.partial(jnp.einsum, preferred_element_type=F32)
    scores = jnp.where(allowed, dots("hqd,hkd->hqk", query, key) * scale, -1e30)
    soft = jax.nn.softmax(scores, axis=-1)
    soft_low = soft.astype(BF16)
    grad_p = dots("hqd,hkd->hqk", grad, value)
    grad_s = (soft * (grad_p - jnp.sum(soft * grad_p, axis=-1, keepdims=True))).astype(BF16)
    raw = dots("hqk,hkd->hqd", soft_low, value).astype(BF16)
    grad_q = (dots("hqk,hkd->hqd", grad_s, key) * scale).astype(BF16)
    grads = (dots("hqk,hqd->hkd", grad_s, query) * scale, dots("hqk,hqd->hkd", soft_low, grad))
    grad_k, grad_v = (
        lax.psum_scatter(part.astype(BF16), "ctx", scatter_dimension=1, tiled=True) for part in grads
    )
    return jnp.concatenate([raw, grad_q, grad_k, grad_v], axis=-1).reshape(HEADS * count, 4 * HDIM)


def solution(mesh):
    plan = Plan(mesh)
    split, rows, cols = P(ALL), P(ALL, None), P(None, ALL)
    acts = P("dp", "ctx", None)
    return jax.shard_map(
        functools.partial(body, plan),
        mesh=mesh,
        in_specs=(acts, split, rows, rows, split, rows, cols, split, rows, split, rows, split, rows, rows, rows, rows, acts),
        out_specs=(acts, acts, split, rows, rows, split, rows, cols, split, rows, split, rows, split, rows, rows, rows, rows),
        check_vma=False,
    )
```

```python
import functools
import math

import jax
import jax.numpy as jnp
from jax import lax
from jax.experimental import pallas as pl
from jax.experimental.pallas import tpu as pltpu
from jax.sharding import PartitionSpec as P

D = 512
E = 1024
NS = 16
RANK = 32
KW = 4
HEADS = 8
HDIM = 64
LG = 8
HALO = 16
BLOCKS = 32
ALL = ("dp", "ctx")
EPS = 1e-05
LOG2E = 1.4426950408889634
LN2 = 0.6931471805599453
F32 = jnp.float32
BF16 = jnp.bfloat16
VM = pl.BlockSpec(memory_space=pltpu.VMEM)

Z_MASKS = (0, 4, 2, 6)
XY_MASKS = (0, 1, 16, 17)
CORE = 8
HALF_MASKS = tuple(xy | zz for xy in XY_MASKS for zz in Z_MASKS)
FULL_MASKS = HALF_MASKS + tuple(mask | CORE for mask in HALF_MASKS)
CHUNK_MASKS = tuple((8 if c & 1 else 0) | (2 if c & 2 else 0) | (1 if c & 4 else 0) for c in range(8))

ROW_X = 0
ROW_DT = 64
ROW_A = 96
ROW_CW = 112
ROW_CB = 116
ROW_DB = 117
ROW_SK = 118
ROW_G1 = 119
ROW_G2 = 120
SMALL_ROWS = 128


ANY = pl.BlockSpec(memory_space=pl.ANY)
FAR = pl.BlockSpec(memory_space=pltpu.HBM)
WHOLE = pl.BlockSpec()


def run(kernel, ins, outs, scratch=(), limit=12, raw=(), far=(), after=(), final=False, us=2):
    first, count = len(ins) + len(raw) + len(far), len(after)

    def inner(*refs):
        kernel(*refs[:first], *refs[first + count :])

    return pl.pallas_call(
        inner,
        out_shape=[jax.ShapeDtypeStruct(shape, dtype) for shape, dtype in outs],
        in_specs=[VM] * len(ins) + [ANY] * len(raw) + [FAR] * len(far) + [ANY] * count,
        out_specs=[WHOLE if final else VM] * len(outs),
        scratch_shapes=list(scratch),
        compiler_params=pltpu.CompilerParams(vmem_limit_bytes=limit * 2**20),
        cost_estimate=pl.CostEstimate(flops=int(us * 1e3), bytes_accessed=int(us * 3e3), transcendentals=0),
    )(*ins, *raw, *far, *after)


def nn(left, right):
    return lax.dot_general(left, right, (((1,), (0,)), ((), ())), preferred_element_type=F32)


def nt(left, right):
    return lax.dot_general(left, right, (((1,), (1,)), ((), ())), preferred_element_type=F32)


def tn(left, right):
    return lax.dot_general(left, right, (((0,), (0,)), ((), ())), preferred_element_type=F32)


def sigmoid(value):
    return 1.0 / (1.0 + jnp.exp(-value))


class Plan:
    def __init__(self, mesh):
        self.dp, self.ctx = mesh.shape["dp"], mesh.shape["ctx"]
        self.fast = (self.dp, self.ctx) == (4, 8)
        self.chunks = self.ctx
        if self.fast:
            self.grad_masks = (FULL_MASKS[:16], FULL_MASKS[16:])
        else:
            self.grad_masks = (tuple(range(BLOCKS)),)

    def place(self, seq, chunk):
        return CHUNK_MASKS[chunk] | ((seq >> 1) << 4) | ((seq & 1) << 2)

    def me(self):
        if self.fast:
            return lax.axis_index("dp") * 8 + lax.axis_index("ctx")
        return 0

    def chunk(self):
        if self.fast:
            lin = lax.axis_index("dp") * 8 + lax.axis_index("ctx")
            return ((lin >> 3) & 1) + ((lin >> 1) & 1) * 2 + (lin & 1) * 4
        return lax.axis_index("ctx")

    def side(self):
        return ((lax.axis_index("ctx") + lax.axis_index("dp") * 8) & CORE) != 0 if self.fast else False

    def swap(self, value):
        if self.fast:
            groups = [[self.place(s, c) for c in range(8)] for s in range(4)]
            return lax.all_to_all(value, ALL, 0, 0, tiled=True, axis_index_groups=groups)
        return lax.all_to_all(value, "ctx", 0, 0, tiled=True)


def send(value, mask):
    return lax.ppermute(value, ALL, [(i, i ^ mask) for i in range(32)])


def own_first(value, side, width):
    groups = [value[:, i * width : (i + 1) * width] for i in range(4)]
    pick = lambda x, own: jnp.where(side, groups[2 * x + own], groups[2 * x + 1 - own])
    return jnp.concatenate([pick(0, 1), pick(1, 1), pick(0, 0), pick(1, 0)], axis=1)


def in_order(value, side, width):
    own_a, own_b, far_a, far_b = (value[:, i * width : (i + 1) * width] for i in range(4))
    return jnp.concatenate(
        [jnp.where(side, far_a, own_a), jnp.where(side, own_a, far_a),
         jnp.where(side, far_b, own_b), jnp.where(side, own_b, far_b)], axis=1)


def rows_of(ref, half, first, cols):
    return jnp.concatenate(
        [ref[k * 32 + half * 16 : k * 32 + half * 16 + 16, first : first + cols] for k in range(ref.shape[0] // 32)], axis=0)


def wait_whole(target, sem):
    pltpu.make_async_copy(target, target, sem).wait()


def swap_blocks(value, me):
    rows, lanes = value.shape
    for bit in (16, 8, 4):
        half = bit * 32
        parts = [value[:, i : i + half] for i in range(0, lanes, half)]
        other = jnp.concatenate([parts[i ^ 1] for i in range(len(parts))], axis=1)
        value = jnp.where((me & bit) != 0, other, value)
    groups = []
    odd = (lax.broadcasted_iota(jnp.int32, (rows, 128), 1) & 32) != 0
    for i in range(0, lanes, 128):
        part = value[:, i : i + 128]
        part = jnp.where((me & 2) != 0, pltpu.roll(part, 64, 1), part)
        other = jnp.where(odd, pltpu.roll(part, 32, 1), pltpu.roll(part, 96, 1))
        groups.append(jnp.where((me & 1) != 0, other, part))
    return jnp.concatenate(groups, axis=1)


def pack_kernel(in_proj, x_proj, dt_proj, a_log, conv_w, conv_b, dt_bias, d_skip, gain_one, gain_two,
                out_proj, w_q, w_k, w_v, w_o, one, two, rows, *rest):
    (b_in, b_x, b_dt, b_a, b_cw, b_cb, b_db, b_sk, b_g1, b_g2, b_out, b_q, b_k, b_v, b_o, sems) = rest
    copies = [
        pltpu.make_async_copy(src, dst, sems.at[i])
        for i, (src, dst) in enumerate(
            zip((in_proj, x_proj, dt_proj, a_log, conv_w, conv_b, dt_bias, d_skip, gain_one, gain_two, out_proj, w_q,
                 w_k, w_v, w_o),
                (b_in, b_x, b_dt, b_a, b_cw, b_cb, b_db, b_sk, b_g1, b_g2, b_out, b_q, b_k, b_v, b_o))
        )
    ]
    for copy in copies:
        copy.start()
    for copy in copies:
        copy.wait()
    one[:, :E] = b_in[:, :E].astype(BF16)
    two[:16, 3 * D :] = b_in[:, E : E + D].astype(BF16)
    two[16:, 3 * D :] = b_in[:, E + D :].astype(BF16)
    two[:, :D] = b_out[...].astype(BF16)
    two[:16, D : 2 * D] = b_q[...].astype(BF16)
    two[:16, 2 * D : 3 * D] = b_k[...].astype(BF16)
    two[16:, D : 2 * D] = b_v[...].astype(BF16)
    two[16:, 2 * D : 3 * D] = b_o[...].astype(BF16)
    rows[...] = jnp.zeros_like(rows)
    rows[ROW_X : ROW_X + 64, :] = b_x[...].T
    rows[ROW_DT : ROW_DT + RANK, :] = b_dt[...]
    rows[ROW_A : ROW_A + NS, :] = b_a[...]
    rows[ROW_CW : ROW_CW + KW, :] = b_cw[...]
    rows[ROW_CB : ROW_CB + 1, :] = b_cb[...]
    rows[ROW_DB : ROW_DB + 1, :] = b_db[...]
    rows[ROW_SK : ROW_SK + 1, :] = b_sk[...]
    rows[ROW_G1 : ROW_G1 + 1, :16] = b_g1[...]
    rows[ROW_G2 : ROW_G2 + 1, :16] = b_g2[...]
    one[:, E:] = jnp.concatenate([rows[16 * q : 16 * q + 16, :] for q in range(8)], axis=1).astype(BF16)


def join_smalls(target, own, far, side):
    for q in range(8):
        rows = jnp.concatenate(
            [ref[16 * k : 16 * k + 16, E + 32 * q : E + 32 * q + 32].astype(F32) for ref in (own, far) for k in range(16)], axis=1)
        target[16 * q : 16 * q + 16, :] = in_order(rows, side, 256)


def gain_row(pm, row):
    return jnp.concatenate([pm[row : row + 1, 32 * s : 32 * s + 16] for s in range(BLOCKS)], axis=1)


def spread(target, source):
    count = source.shape[0]
    for s in range(LG):
        target[pl.ds(s, count, stride=LG), :] = source[:, s * 128 : (s + 1) * 128]


def gathered(source, count):
    return jnp.concatenate([source[pl.ds(s, count, stride=LG), :] for s in range(LG)], axis=1)


def broadcast_rows(target, proj, first):
    for n in range(NS):
        target[n] = jnp.broadcast_to(proj[:, first + n : first + n + 1], target.shape[1:])


def at8(ref, index):
    return ref[pl.ds(pl.multiple_of(index * 8, 8), 8), :]


def front_kernel(plan, tok, halo, own, far, normed, turned, u_out, conv_out, act_out, proj_out, sig_out, dt3, au3, a3,
                 state, pm, gains, bx, cx):
    side = plan.side()
    join_smalls(pm, own, far, side)
    gain = gain_row(pm, ROW_G1)
    gains[0:1, :] = gain
    gains[1:2, :] = gain_row(pm, ROW_G2)
    tokens = tok.shape[0]
    x = jnp.concatenate([halo[...].astype(F32), tok[...].astype(F32)], axis=0)
    r = lax.rsqrt(jnp.mean(x * x, axis=-1, keepdims=True) + EPS)
    low = x * r * gain
    normed[...] = low.astype(BF16)
    low = own_first(low, side, 128).astype(BF16)
    turned[...] = low
    u_out[...] = nn(low[:, : D // 2], own[:, :E]) + nn(low[:, D // 2 :], far[:, :E])
    conv = pm[ROW_CB : ROW_CB + 1, :]
    for k in range(KW):
        conv = conv + pm[ROW_CW + k : ROW_CW + k + 1, :] * u_out[HALO - 3 + k : HALO - 3 + k + tokens, :]
    conv_out[...] = conv
    act = (conv * sigmoid(conv)).astype(BF16)
    act_out[...] = act
    proj = nt(act, pm[ROW_X : ROW_X + 64, :].astype(BF16))
    proj_out[:, :64] = proj
    proj_out[:, 64:] = jnp.zeros((tokens, 64), F32)
    pre = nn(proj[:, :RANK].astype(BF16), pm[ROW_DT : ROW_DT + RANK, :].astype(BF16)) + pm[ROW_DB : ROW_DB + 1, :]
    sig_out[...] = sigmoid(pre)
    step = jnp.maximum(pre, 0.0) + jnp.log1p(jnp.exp(-jnp.abs(pre)))
    spread(dt3, step)
    spread(au3, act.astype(F32))
    spread(a3, -LOG2E * jnp.exp(pm[ROW_A : ROW_A + NS, :]))
    broadcast_rows(bx, proj, RANK)
    broadcast_rows(cx, proj, RANK + NS)
    decay = [a3[8 * n : 8 * n + 8, :] for n in range(NS)]

    def advance(t, carried):
        held, total = carried
        size = at8(dt3, t)
        drive = size * at8(au3, t)
        held = tuple(
            jnp.exp2(size * decay[n]) * held[n] + drive * bx[n, pl.ds(t, 1), :] for n in range(NS)
        )
        return held, total + size

    zero = jnp.zeros((8, 128), F32)
    held, total = lax.fori_loop(0, tokens, advance, ((zero,) * NS, zero), unroll=4)
    state[...] = jnp.concatenate([*held, total, zero], axis=0).astype(BF16)


def combine_kernel(plan, forward, states, a3, entry, states_f):
    states_f[...] = states[...].astype(F32)
    decay = [a3[8 * n : 8 * n + 8, :] for n in range(NS)]
    zero = jnp.zeros((8, 128), F32)

    def combine(i, held):
        base = (i if forward else plan.chunks - 1 - i) * 144
        total = states_f[pl.ds(pl.multiple_of(base + 128, 8), 8), :]
        return tuple(
            jnp.exp2(total * decay[n]) * held[n] + states_f[pl.ds(pl.multiple_of(base + 8 * n, 8), 8), :]
            for n in range(NS)
        )

    count = plan.chunk() if forward else plan.chunks - 1 - plan.chunk()
    held = lax.fori_loop(0, count, combine, (zero,) * NS)
    entry[...] = jnp.concatenate([*held, zero, zero], axis=0)


def merge_kernel(plan, step, forward, own, other, before, a3, group, entry):
    later = ((plan.chunk() >> step) & 1) == (1 if forward else 0)
    mine, theirs = own[...].astype(F32), other[...].astype(F32)
    first, second = jnp.where(later, theirs, mine), jnp.where(later, mine, theirs)
    decay = a3[...]
    spread_total = lambda value: jnp.concatenate([value[128:136, :]] * NS, axis=0)
    joint = jnp.exp2(spread_total(second) * decay) * first[:128, :] + second[:128, :]
    group[:128, :] = joint.astype(BF16)
    group[128:, :] = (first[128:, :] + second[128:, :]).astype(BF16)
    held = before[...]
    inner = held[:128, :] + jnp.exp2(spread_total(held) * decay) * theirs[:128, :]
    entry[:128, :] = jnp.where(later, inner, held[:128, :])
    entry[128:, :] = jnp.where(later, held[128:, :] + theirs[128:, :], held[128:, :])


def exchange(plan, state, a3, forward, beside=lambda step, entry: []):
    if plan.fast:
        group, entry, firsts = state, jnp.zeros((144, 128), F32), []
        for step in range(3):
            other = send(group, CHUNK_MASKS[1 << step])
            group, entry = run(
                functools.partial(merge_kernel, plan, step, forward), [group, other, entry, a3],
                [((144, 128), BF16), ((144, 128), F32)], after=beside(step, entry if step else group))
            firsts.append(entry)
        return entry, firsts
    states = lax.all_gather(state, "ctx", axis=0, tiled=True)
    return run(
        functools.partial(combine_kernel, plan, forward), [states, a3], [((144, 128), F32)],
        [pltpu.VMEM((144 * plan.chunks, 128), F32)])[0], []


def mid_kernel(plan, tok, dt3, au3, a3, turned, pm, gains, cot, entry, bx, cx, own, far,
               pay, mamba, gated_out, middle_out, all_states, z_out, y3):
    tokens = tok.shape[0]
    side = plan.side()
    both = lambda left, half, first, cols: nn(left[:, : D // 2], rows_of(own, half, first, cols)) + nn(
        left[:, D // 2 :], rows_of(far, half, first, cols))
    decay = [a3[8 * n : 8 * n + 8, :] for n in range(NS)]
    held = tuple(entry[8 * n : 8 * n + 8, :] for n in range(NS))
    all_states[:128, :] = entry[:128, :]

    def advance(t, held):
        size = at8(dt3, t)
        drive = size * at8(au3, t)
        base = pl.multiple_of(t * 128 + 128, 128)
        held = tuple(
            jnp.exp2(size * decay[n]) * held[n] + drive * bx[n, pl.ds(t, 1), :] for n in range(NS)
        )
        for n in range(NS):
            all_states[pl.ds(base + 8 * n, 8), :] = held[n]
        y = held[0] * cx[0, pl.ds(t, 1), :]
        for n in range(1, NS):
            y = y + held[n] * cx[n, pl.ds(t, 1), :]
        y3[pl.ds(pl.multiple_of(t * 8, 8), 8), :] = y
        return held

    lax.fori_loop(0, tokens, advance, held, unroll=4)
    act = gathered(au3, tokens)
    y = gathered(y3, tokens) + pm[ROW_SK : ROW_SK + 1, :] * act
    mamba[...] = y
    low = turned[HALO:, :]
    z = jnp.concatenate([both(low, 0, 3 * D, D), both(low, 1, 3 * D, D)], axis=1)
    z_out[...] = z
    gated = y * (z * sigmoid(z))
    gated_out[...] = gated.astype(BF16)
    gated = own_first(gated, side, 256).astype(BF16)
    middle = tok[...].astype(F32) + nn(gated[:, : E // 2], own[:, :D]) + nn(gated[:, E // 2 :], far[:, :D])
    middle_out[...] = middle
    r = lax.rsqrt(jnp.mean(middle * middle, axis=-1, keepdims=True) + EPS)
    low = own_first(middle * r * gains[1:2, :], side, 128).astype(BF16)
    query_key, value = both(low, 0, D, 2 * D), both(low, 1, D, D)
    grad = jnp.concatenate([nt(cot[...], rows_of(ref, 1, 2 * D, D)) for ref in (own, far)], axis=1)
    quads = tuple(part.astype(BF16) for part in (query_key[:, :D], query_key[:, D:], value, in_order(grad, side, 128)))
    for h in range(HEADS):
        for i, part in enumerate(quads):
            pay[h * tokens : (h + 1) * tokens, i * HDIM : (i + 1) * HDIM] = part[:, h * HDIM : (h + 1) * HDIM]


def attention_kernel(pay, back, q_s, k_s, v_s, g_s, kt, vt, dk, dv):
    length = pay.shape[0]
    rows = math.gcd(length, 512)
    q_s[...] = pay[:, :HDIM]
    k_s[...] = pay[:, HDIM : 2 * HDIM]
    v_s[...] = pay[:, 2 * HDIM : 3 * HDIM]
    g_s[...] = pay[:, 3 * HDIM :]
    kt[...] = k_s[...].T
    vt[...] = v_s[...].T
    dk[...] = jnp.zeros_like(dk)
    dv[...] = jnp.zeros_like(dv)
    scale = HDIM**-0.5
    key_at = lax.broadcasted_iota(jnp.int32, (rows, rows), 0)
    query_at = lax.broadcasted_iota(jnp.int32, (rows, rows), 1)
    for i in range(length // rows):
        first, last = i * rows, (i + 1) * rows
        query = q_s[first:last, :]
        grad = g_s[first:last, :]
        scores = nt(k_s[:last, :], query) * scale
        diagonal = jnp.where(key_at <= query_at, scores[first:, :], -1e30)
        scores = diagonal if i == 0 else jnp.concatenate([scores[:first, :], diagonal], axis=0)
        expo = jnp.exp(scores - jnp.max(scores, axis=0, keepdims=True))
        soft = expo * (1.0 / jnp.sum(expo, axis=0, keepdims=True))
        soft_low = soft.astype(BF16)
        grad_p = nt(v_s[:last, :], grad)
        dot = jnp.sum(soft * grad_p, axis=0, keepdims=True)
        grad_s = (soft * (grad_p - dot)).astype(BF16)
        raw = nn(vt[:, :last], soft_low)
        grad_q = nn(kt[:, :last], grad_s) * scale
        back[first:last, :HDIM] = raw.T.astype(BF16)
        back[first:last, HDIM : 2 * HDIM] = grad_q.T.astype(BF16)
        dk[:last, :] += nn(grad_s, query)
        dv[:last, :] += nn(soft_low, grad)
    back[:, 2 * HDIM : 3 * HDIM] = (dk[...] * scale).astype(BF16)
    back[:, 3 * HDIM :] = dv[...].astype(BF16)


def turn_kernel(plan, got, middle, cot, gains, z_in, mamba, dt3, cx, a3, own, far, first,
                att, gq, gk, gv, grad_middle, mix, gz, gy3, state, gain_grad):
    tokens = middle.shape[0]
    for h in range(HEADS):
        for i, part in enumerate((att, gq, gk, gv)):
            part[:, h * HDIM : (h + 1) * HDIM] = got[h * tokens : (h + 1) * tokens, i * HDIM : (i + 1) * HDIM]
    side = plan.side()
    grad_n = in_order(jnp.concatenate(
        [nt(gq[...], rows_of(ref, 0, D, D)) + nt(gk[...], rows_of(ref, 0, 2 * D, D)) + nt(gv[...], rows_of(ref, 1, D, D))
         for ref in (own, far)], axis=1), side, 128)
    mid = middle[...]
    r = lax.rsqrt(jnp.mean(mid * mid, axis=-1, keepdims=True) + EPS)
    gain_grad[...] = jnp.sum(grad_n * mid * r, axis=0, keepdims=True)
    q = grad_n * gains[1:2, :]
    gm = cot[...].astype(F32) + r * q - mid * (r * r * r) * jnp.mean(q * mid, axis=-1, keepdims=True)
    grad_middle[...] = gm
    low = gm.astype(BF16)
    mix[...] = low
    grad_gated = in_order(jnp.concatenate([nt(low, ref[:, :D]) for ref in (own, far)], axis=1), side, 256)
    z = z_in[...]
    s = sigmoid(z)
    spread(gy3, grad_gated * (z * s))
    gz[...] = (grad_gated * mamba[...] * (s * (1.0 + z * (1.0 - s)))).astype(BF16)
    decay = [a3[8 * n : 8 * n + 8, :] for n in range(NS)]

    def retreat(i, carried):
        t = tokens - 1 - i
        size = at8(dt3, t)
        grad = at8(gy3, t)
        return tuple(
            jnp.exp2(size * decay[n]) * (carried[n] + grad * cx[n, pl.ds(t, 1), :]) for n in range(NS)
        )

    zero = jnp.zeros((8, 128), F32)
    carried = lax.fori_loop(0, tokens, retreat, (zero,) * NS, unroll=4)
    state[:128, :] = jnp.concatenate(carried, axis=0).astype(BF16)
    state[128:, :] = first[128:, :]


def pack_blocks(plan, outs, source, rows, height, row, first, col=0, cols=None):
    me = plan.me()
    cols = source.shape[1] if cols is None else cols
    for out, masks in zip(outs, plan.grad_masks):
        for k, mask in enumerate(masks):
            block = me ^ mask
            out[k * height + row : k * height + row + rows, first : first + cols] = source[
                pl.ds(pl.multiple_of(block * rows, 16), rows), col : col + cols
            ].astype(BF16)


def grad_c_kernel(gy3, all_states, grad_c):
    diagonal_sums(grad_c, 0, lambda rows: gy3[rows, :], all_states, 1)


def weights_kernel(plan, no, att, gq, gk, gv, mix, gated, middle, gains, cot, own, far, normed, gz, *refs):
    result, outs = refs[0], refs[1 : 1 + no]
    small, large, wide = refs[1 + no :]
    mid = middle[...]
    held = own_first(att[...], plan.side(), 128)
    result[...] = (
        mid + nn(held[:, : D // 2], rows_of(own, 1, 2 * D, D)) + nn(held[:, D // 2 :], rows_of(far, 1, 2 * D, D))
    ).astype(BF16)
    r = lax.rsqrt(jnp.mean(mid * mid, axis=-1, keepdims=True) + EPS)
    low = (mid * r * gains[1:2, :]).astype(BF16)
    large[...] = tn(gated[...], mix[...])
    pack_blocks(plan, outs, large, 32, 32, 0, 0)
    small[...] = tn(low, gq[...])
    pack_blocks(plan, outs, small, 16, 32, 0, D)
    small[...] = tn(low, gk[...])
    pack_blocks(plan, outs, small, 16, 32, 0, 2 * D)
    small[...] = tn(low, gv[...])
    pack_blocks(plan, outs, small, 16, 32, 16, D)
    small[...] = tn(att[...], cot[...])
    pack_blocks(plan, outs, small, 16, 32, 16, 2 * D)
    wide[...] = tn(normed[HALO:, :], gz[...])
    pack_blocks(plan, outs, wide, 16, 32, 0, 3 * D, 0, D)
    pack_blocks(plan, outs, wide, 16, 32, 16, 3 * D, D, D)


def diagonal_sums(out, col, channels, held, offset, span=16):
    row_t = lax.broadcasted_iota(jnp.int32, (span, span * NS), 0)
    col_t = lax.broadcasted_iota(jnp.int32, (span, span * NS), 1) // NS
    pick = (
        lax.broadcasted_iota(jnp.int32, (span * NS, NS), 0) % NS
        == lax.broadcasted_iota(jnp.int32, (span * NS, NS), 1)
    ).astype(BF16)
    for block in range(out.shape[0] // span):
        total = jnp.zeros((span, span * NS), F32)
        for s in range(LG):
            held_rows = held[pl.ds((block * span + offset) * 128 + s, span * NS, stride=LG), :].astype(BF16)
            total = total + nt(channels(pl.ds(block * span * 8 + s, span, stride=LG)).astype(BF16), held_rows)
        own = jnp.where(row_t == col_t, total, 0.0).astype(BF16)
        out[block * span : (block + 1) * span, col : col + NS] = nn(own, pick)


def back_kernel(plan, dt3, au3, gy3, a3, proj, pm, all_states, sig, act, conv_in, u_in, leaving, bx, cx, grad_c,
                small_grads, gu_out, grads, gs3, ga3, gal, skip3, low_rank, padded):
    tokens = dt3.shape[0] // LG
    decay = [a3[8 * n : 8 * n + 8, :] for n in range(NS)]
    zero = jnp.zeros((8, 128), F32)
    spread(skip3, pm[ROW_SK : ROW_SK + 1, :])
    skip = skip3[...]

    carried = tuple(leaving[8 * n : 8 * n + 8, :] for n in range(NS))
    gal[...] = jnp.zeros_like(gal)

    def retreat(i, state):
        carried, skipped = state
        t = tokens - 1 - i
        size, value, grad = at8(dt3, t), at8(au3, t), at8(gy3, t)
        base = pl.multiple_of(t * 128, 128)
        from_b = zero
        from_a = zero
        fresh = []
        for n in range(NS):
            g = carried[n] + grad * cx[n, pl.ds(t, 1), :]
            grads[pl.ds(base + 8 * n, 8), :] = g
            w = jnp.exp2(size * decay[n]) * g
            q = w * all_states[pl.ds(base + 8 * n, 8), :]
            from_a = from_a + decay[n] * q
            from_b = from_b + g * bx[n, pl.ds(t, 1), :]
            gal[8 * n : 8 * n + 8, :] += size * q
            fresh.append(w)
        at = pl.ds(pl.multiple_of(t * 8, 8), 8)
        gs3[at, :] = from_a * LN2 + from_b * value
        ga3[at, :] = from_b * size + skip * grad
        return tuple(fresh), skipped + grad * value

    _, skipped = lax.fori_loop(0, tokens, retreat, (carried, zero), unroll=4)

    diagonal_sums(low_rank, RANK, lambda rows: dt3[rows, :] * au3[rows, :], grads, 0)
    low_rank[:, RANK + NS : RANK + 2 * NS] = grad_c[:, :NS]

    grad_pre = gathered(gs3, tokens) * sig[...]
    grad_pre_low = grad_pre.astype(BF16)
    low_rank[:, :RANK] = nt(grad_pre_low, pm[ROW_DT : ROW_DT + RANK, :].astype(BF16))
    projected = low_rank[:, :64].astype(BF16)
    small_grads[ROW_X : ROW_X + 64, :] = tn(projected, act[...])
    small_grads[ROW_DT : ROW_DT + RANK, :] = tn(proj[:, :RANK].astype(BF16), grad_pre_low)
    true_a = -jnp.exp(pm[ROW_A : ROW_A + NS, :])
    small_grads[ROW_A : ROW_A + NS, :] = gathered(gal, NS) * true_a
    small_grads[ROW_DB : ROW_DB + 1, :] = jnp.sum(grad_pre, axis=0, keepdims=True)
    skip3[...] = skipped
    small_grads[ROW_SK : ROW_SK + 1, :] = gathered(skip3, 1)
    small_grads[ROW_G1:, :] = jnp.zeros((SMALL_ROWS - ROW_G1, E), F32)
    conv = conv_in[...]
    s = sigmoid(conv)
    grad_act = gathered(ga3, tokens) + nn(projected, pm[ROW_X : ROW_X + 64, :].astype(BF16))
    grad_conv = grad_act * (s * (1.0 + conv * (1.0 - s)))
    small_grads[ROW_CB : ROW_CB + 1, :] = jnp.sum(grad_conv, axis=0, keepdims=True)
    for k in range(KW):
        small_grads[ROW_CW + k : ROW_CW + k + 1, :] = jnp.sum(
            grad_conv * u_in[HALO - 3 + k : HALO - 3 + k + tokens, :], axis=0, keepdims=True
        )
    padded[:HALO, :] = jnp.zeros((HALO, E), F32)
    padded[HALO : HALO + tokens, :] = grad_conv
    padded[HALO + tokens :, :] = jnp.zeros((HALO, E), F32)
    gu = jnp.zeros((HALO + tokens, E), F32)
    for k in range(KW):
        gu = gu + pm[ROW_CW + k : ROW_CW + k + 1, :] * padded[3 - k : 3 - k + HALO + tokens, :]
    gu_out[...] = gu.astype(BF16)


def last_kernel(plan, no, tok, halo, gains, gu, gz, grad_middle, own_u, far_u, own_z, far_z, normed, small_grads, gain_two, result, *refs):
    outs = refs[:no]
    both, before, large, spaced = refs[no:]
    tokens = tok.shape[0]
    both[tokens:, :] = result[...]
    me = plan.me()
    large[...] = tn(normed[...], gu[...])
    pack_blocks(plan, outs, large, 16, 16, 0, 0)
    x = jnp.concatenate([halo[...].astype(F32), tok[...].astype(F32)], axis=0)
    r = lax.rsqrt(jnp.mean(x * x, axis=-1, keepdims=True) + EPS)
    from_z = jnp.concatenate(
        [nt(gz[:, :D], rows_of(ref, 0, 3 * D, D)) + nt(gz[:, D:], rows_of(ref, 1, 3 * D, D)) for ref in (own_z, far_z)], axis=1)
    from_u = jnp.concatenate([nt(gu[...], ref[:, :E]) for ref in (own_u, far_u)], axis=1)
    grad_n = in_order(from_u + jnp.concatenate([jnp.zeros((HALO, D), F32), from_z], axis=0), plan.side(), 128)
    gain_one = jnp.sum(grad_n * x * r, axis=0, keepdims=True)
    q = grad_n * gains[0:1, :]
    base = r * q - x * (r * r * r) * jnp.mean(q * x, axis=-1, keepdims=True)
    both[:tokens, :] = (grad_middle[...] + base[HALO:, :]).astype(BF16)
    before[...] = base[:HALO, :].astype(BF16)
    spaced[...] = small_grads[...]
    blank = jnp.zeros((1, 16), F32)
    for row, grad in ((ROW_G1, gain_one), (ROW_G2, gain_two[...])):
        spaced[row : row + 1, :] = jnp.concatenate(
            [part for s in range(BLOCKS) for part in (grad[:, 16 * s : 16 * s + 16], blank)], axis=1)
    spaced[...] = swap_blocks(spaced[...], me)
    for out, masks in zip(outs, plan.grad_masks):
        for k, m in enumerate(masks):
            out[16 * k : 16 * k + 16, E:] = jnp.concatenate(
                [spaced[16 * q : 16 * q + 16, 32 * m : 32 * m + 32] for q in range(8)], axis=1).astype(BF16)


def total_of(ins):
    total = ins[0][...].astype(F32)
    for other in ins[1:]:
        total = total + other[...].astype(F32)
    return total


def finish_kernel(*refs):
    (both, tail), refs = refs[:2], refs[2:]
    u_ins, ins, (own_out, result_out), refs = refs[:4], refs[4:6], refs[6:8], refs[2:]
    count = own_out.shape[0]
    rows = count - HALO
    own_out[:rows, :] = both[:rows, :]
    own_out[rows:, :] = (both[rows:count, :].astype(F32) + tail[...].astype(F32)).astype(BF16)
    result_out[...] = both[count:, :]
    out_g, q_g, k_g, v_g, o_g, in_g, x_g, dt_g, a_g, cw_g, cb_g, db_g, sk_g, g1_g, g2_g, rows = refs[6:]
    total = total_of(ins)
    out_g[...] = total[:, :D]
    q_g[...] = total[:16, D : 2 * D]
    k_g[...] = total[:16, 2 * D : 3 * D]
    v_g[...] = total[16:, D : 2 * D]
    o_g[...] = total[16:, 2 * D : 3 * D]
    in_g[:, E : E + D] = total[:16, 3 * D :]
    in_g[:, E + D :] = total[16:, 3 * D :]
    total = total_of(u_ins)
    in_g[:, :E] = total[:, :E]
    for q in range(8):
        rows[16 * q : 16 * q + 16, :] = total[:, E + 32 * q : E + 32 * q + 32]
    x_g[...] = rows[ROW_X : ROW_X + 64, :].T
    dt_g[...] = rows[ROW_DT : ROW_DT + RANK, :]
    a_g[...] = rows[ROW_A : ROW_A + NS, :]
    cw_g[...] = rows[ROW_CW : ROW_CW + KW, :]
    cb_g[...] = rows[ROW_CB : ROW_CB + 1, :]
    db_g[...] = rows[ROW_DB : ROW_DB + 1, :]
    sk_g[...] = rows[ROW_SK : ROW_SK + 1, :]
    g1_g[...] = rows[ROW_G1 : ROW_G1 + 1, :16]
    g2_g[...] = rows[ROW_G2 : ROW_G2 + 1, :16]


def join_kernel(plan, counts, placed, *refs):
    ins, outs = refs[: sum(counts)], refs[sum(counts) :]
    at = 0
    for i, count in enumerate(counts):
        rows = outs[i].shape[0] // count
        for k in range(count):
            part = ins[at + k]
            if not placed[i]:
                outs[i][k * rows : (k + 1) * rows, :] = part[...]
                continue
            height = rows // len(Z_MASKS)
            for j, zz in enumerate(Z_MASKS):
                owner = plan.me() ^ (XY_MASKS[k] | zz)
                to = (((owner >> 4) & 1) * 8 + (owner & 7)) * height
                outs[i][pl.ds(pl.multiple_of(to, 16), height), :] = part[j * height : (j + 1) * height, :]
        at += count


def join(plan, groups, after=(), placed=()):
    counts = [len(group) for group in groups]
    outs = [((group[0].shape[0] * len(group), group[0].shape[1]), group[0].dtype) for group in groups]
    return run(
        functools.partial(join_kernel, plan, counts, [i in placed for i in range(len(groups))]),
        [part for group in groups for part in group], outs, after=after, us=1)


def spread_out(value, stage):
    return [value] + [send(value, mask) for mask in stage[1:]]


def cut_one_kernel(keep, got, a_keep, a_give, b_keep, b_give):
    half, quarter, cols = keep.shape[0] // 2, keep.shape[0] // 4, keep.shape[1] // 2
    add = lambda rows, lanes: (keep[rows, lanes].astype(F32) + got[rows, lanes].astype(F32)).astype(BF16)
    left, right = slice(0, cols), slice(cols, 2 * cols)
    a_keep[...] = add(slice(0, half), left)
    a_give[...] = add(slice(half, 2 * half), left)
    for i in range(2):
        b_keep[i * quarter : (i + 1) * quarter, :] = add(slice(2 * i * quarter, (2 * i + 1) * quarter), right)
        b_give[i * quarter : (i + 1) * quarter, :] = add(slice((2 * i + 1) * quarter, (2 * i + 2) * quarter), right)


def cut_two_kernel(a_own, a_got, b_own, b_got, a_keep, a_give, b_keep, b_give):
    rows = a_own.shape[0] // 2
    for own, got, keep, give in ((a_own, a_got, a_keep, a_give), (b_own, b_got, b_keep, b_give)):
        for out, part in ((keep, slice(0, rows)), (give, slice(rows, 2 * rows))):
            out[...] = (own[part, :].astype(F32) + got[part, :].astype(F32)).astype(BF16)


def add_rows(out, rows, ins, cols=slice(None), to=slice(None)):
    total = ins[0][rows, cols].astype(F32)
    for other in ins[1:]:
        total = total + other[rows, cols].astype(F32)
    out[:, to] = total.astype(out.dtype)


def cut_three_kernel(u_own, u_got, a_own, a_got, b_own, b_got, u_0, u_1, u_2, u_3, keep, give):
    rows = u_0.shape[0]
    for i, out in enumerate((u_0, u_1, u_2, u_3)):
        add_rows(out, slice(i * rows, (i + 1) * rows), (u_own, u_got))
    rows, cols = keep.shape[0], a_own.shape[1]
    for i, out in enumerate((keep, give)):
        part = slice(i * rows, (i + 1) * rows)
        add_rows(out, part, (a_own, a_got), to=slice(0, cols))
        add_rows(out, part, (b_own, b_got), to=slice(cols, 2 * cols))


def cut_four_kernel(u_own, u_a, u_b, u_c, own, got, u_0, u_1, u_2, u_3, keep, give):
    rows = u_0.shape[0]
    for i, out in enumerate((u_0, u_1, u_2, u_3)):
        add_rows(out, slice(i * rows, (i + 1) * rows), (u_own, u_a, u_b, u_c))
    rows = keep.shape[0]
    for i, out in enumerate((keep, give)):
        add_rows(out, slice(i * rows, (i + 1) * rows), (own, got))


def body(plan, *args):
    (tokens, mixer_gain, in_proj, conv_weight, conv_bias, x_proj, dt_proj, dt_bias, a_log, d_skip, out_proj,
     attn_gain, w_query, w_key, w_value, w_output, cotangent) = args
    count = tokens.shape[1]
    tok0, cot0 = tokens.reshape(count, D), cotangent.reshape(count, D)
    chunks = plan.chunks
    devices = plan.dp * plan.ctx
    share, width = E // devices, D // devices
    if plan.fast:
        home = [(s * 8 + c, plan.place(s, c)) for s in range(4) for c in range(8)]
        tok = lax.ppermute(tok0, ALL, home)
        halo = lax.ppermute(
            tok0[count - HALO :], ALL, [(s * 8 + c, plan.place(s, c + 1)) for s in range(4) for c in range(7)]
        )
        raw = [in_proj, x_proj, dt_proj, a_log.T, conv_weight.T, conv_bias[None], dt_bias[None], d_skip[None],
               mixer_gain[None], attn_gain[None], out_proj, w_query, w_key, w_value, w_output]
        pack_one, pack_two = run(
            pack_kernel, [], [((16, E + 256), BF16), ((32, 4 * D), BF16)],
            [pltpu.VMEM((SMALL_ROWS, 32), F32)] + [pltpu.VMEM(value.shape, F32) for value in raw]
            + [pltpu.SemaphoreType.DMA((len(raw),))], far=raw, limit=60)
        (one,) = join(plan, [spread_out(pack_one, Z_MASKS)])
        near_one = spread_out(one, XY_MASKS)
        (two,) = join(plan, [[pack_two, send(pack_two, 4)]], [one, tok])
        cot = lax.ppermute(cot0, ALL, home)
        one, two = join(plan, [near_one, [two, send(two, 2)]], [halo], (0,))
        one = [one, send(one, CORE)]
        near_two = spread_out(two, XY_MASKS)
    else:
        tok, cot = tok0, cot0
        halo = lax.ppermute(tok0[count - HALO :], "ctx", [(c, c + 1) for c in range(chunks - 1)])
        smalls = jnp.concatenate(
            [x_proj.T, dt_proj, a_log.T, conv_weight.T, conv_bias[None], dt_bias[None], d_skip[None],
             jnp.pad(mixer_gain, (0, share - width))[None], jnp.pad(attn_gain, (0, share - width))[None],
             jnp.zeros((SMALL_ROWS - ROW_G2 - 1, share), F32)], axis=0).astype(BF16)
        small_all = lax.all_gather(smalls, ALL, axis=1, tiled=True)
        apart = lambda row: jnp.pad(
            small_all[row].reshape(devices, share)[:, :width].reshape(BLOCKS, 16), ((0, 0), (0, 16))).reshape(1, E)
        small_all = jnp.concatenate(
            [small_all[:ROW_G1], apart(ROW_G1), apart(ROW_G2), small_all[ROW_G2 + 1 :]], axis=0)
        small_all = small_all.reshape(8, 16, BLOCKS, 32).transpose(2, 1, 0, 3).reshape(BLOCKS * 16, 256)
        whole = lambda value: lax.all_gather(value.astype(BF16), ALL, axis=0, tiled=True)
        in_all = whole(in_proj)
        halves = lambda value: [value.reshape(2, 2, -1, value.shape[1])[:, i].reshape(-1, value.shape[1]) for i in range(2)]
        one = halves(jnp.concatenate([in_all[:, :E], small_all], axis=1))
        out_all, q_all, k_all, v_all, o_all = (whole(w) for w in (out_proj, w_query, w_key, w_value, w_output))
        cut = lambda value: value.reshape(BLOCKS, 16, D)
        side = jnp.concatenate(
            [jnp.concatenate([cut(q_all), cut(k_all)], axis=2), jnp.concatenate([cut(v_all), cut(o_all)], axis=2)], axis=1)
        gate = jnp.concatenate([cut(in_all[:, E : E + D]), cut(in_all[:, E + D :])], axis=1)
        two = halves(jnp.concatenate([out_all.reshape(BLOCKS, 32, D), side, gate], axis=2).reshape(BLOCKS * 32, 4 * D))

    no = len(plan.grad_masks)
    rows3 = count * LG
    (normed, turned, u_pre, conv, act, proj, sig, dt3, au3, a3, state, pm, gains, bx, cx) = run(
        functools.partial(front_kernel, plan),
        [tok, halo, *one],
        [((HALO + count, D), BF16), ((HALO + count, D), BF16), ((HALO + count, E), F32), ((count, E), F32),
         ((count, E), BF16), ((count, 128), F32), ((count, E), F32), ((rows3, 128), F32), ((rows3, 128), F32),
         ((128, 128), F32), ((144, 128), BF16), ((SMALL_ROWS, E), F32), ((8, D), F32),
         ((NS, count, 128), F32), ((NS, count, 128), F32)], us=6,
    )
    entry, firsts = exchange(plan, state, a3, True)
    if plan.fast:
        (held,) = join(plan, [near_two], [*firsts[1:2], cot], (0,))
        two = [held, send(held, CORE)]
    pay, mamba, gated, middle, all_states, z = run(
        functools.partial(mid_kernel, plan),
        [tok, dt3, au3, a3, turned, pm, gains, cot, entry, bx, cx, *two],
        [((HEADS * count, 4 * HDIM), BF16), ((count, E), F32), ((count, E), BF16), ((count, D), F32),
         (((count + 1) * 128, 128), F32), ((count, E), F32)],
        [pltpu.VMEM((rows3, 128), F32)], us=6,
    )
    got = attend(plan, pay, count)
    (att, gq, gk, gv, grad_middle, mix, gz, gy3, later, gain_grad_two) = run(
        functools.partial(turn_kernel, plan),
        [got, middle, cot, gains, z, mamba, dt3, cx, a3, *two, state],
        [((count, D), BF16)] * 4 + [((count, D), F32), ((count, D), BF16), ((count, E), BF16), ((rows3, 128), F32),
                                    ((144, 128), BF16), ((1, D), F32)],
    )
    blocks = [len(masks_of) for masks_of in plan.grad_masks]

    def weight_grads(after):
        return run(
            functools.partial(weights_kernel, plan, no),
            [att, gq, gk, gv, mix, gated, middle, gains, cot, *two, normed, gz],
            [((count, D), BF16)] + [((n * 32, 4 * D), BF16) for n in blocks],
            [pltpu.VMEM((D, D), F32), pltpu.VMEM((E, D), F32), pltpu.VMEM((D, E), F32)], after=after)

    def c_grads(after):
        return run(grad_c_kernel, [gy3, all_states], [((count, 128), F32)], after=after)

    done, extra = [], []

    def beside(step, entry):
        if step == 1:
            done.extend(weight_grads([entry]))
            return done[:1]
        if step == 2:
            extra.extend(c_grads([entry]))
        return list(extra)

    leaving, _ = exchange(plan, later, a3, False, beside)
    result, *one_grads = done or weight_grads([])
    (grad_c,) = extra or c_grads([])
    one_parts = []
    if plan.fast:
        rows = blocks[0] * 32
        one_parts = run(
            cut_one_kernel, [one_grads[0], send(one_grads[1], CORE)], [((rows // 2, 2 * D), BF16)] * 4, after=[leaving])
    small_grads, gu = run(
        functools.partial(back_kernel, plan),
        [dt3, au3, gy3, a3, proj, pm, all_states, sig, act, conv, u_pre, leaving, bx, cx, grad_c],
        [((SMALL_ROWS, E), F32), ((HALO + count, E), BF16)],
        [pltpu.VMEM((count * 128, 128), F32), pltpu.VMEM((rows3, 128), F32), pltpu.VMEM((rows3, 128), F32),
         pltpu.VMEM((128, 128), F32), pltpu.VMEM((8, 128), F32), pltpu.VMEM((count, 128), F32),
         pltpu.VMEM((count + 2 * HALO, E), F32)],
        limit=32, after=one_parts[:1], us=11,
    )
    *two_grads, both, before = run(
        functools.partial(last_kernel, plan, no),
        [tok, halo, gains, gu, gz, grad_middle, *one, *two, normed, small_grads, gain_grad_two, result],
        [((n * 16, E + 256), BF16) for n in blocks] + [((2 * count, D), BF16), ((HALO, D), BF16)],
        [pltpu.VMEM((D, E), F32), pltpu.VMEM((SMALL_ROWS, E), F32)],     )
    if plan.fast:
        a_keep, a_give, b_keep, b_give = one_parts
        one_parts = run(
            cut_two_kernel, [a_keep, send(a_give, 16), b_keep, send(b_give, 1)], [((rows // 4, 2 * D), BF16)] * 4,
            after=[two_grads[0]])
    if plan.fast:
        back = [(b, a) for a, b in home]
        both = lax.ppermute(both, ALL, back)
        tail = lax.ppermute(
            before, ALL, [(plan.place(s, c + 1), s * 8 + c) for s in range(4) for c in range(7)])
        a_keep, a_give, b_keep, b_give = one_parts
        sends = lambda parts, stage: [parts[0]] + [send(part, mask) for part, mask in zip(parts[1:], stage[1:])]
        n = blocks[0]
        *u_parts, keep, give = run(
            cut_three_kernel,
            [two_grads[0], send(two_grads[1], CORE), a_keep, send(a_give, 1), b_keep, send(b_give, 16)],
            [((n * 4, E + 256), BF16)] * 4 + [((n * 4, 4 * D), BF16)] * 2, after=[tail])
        *u_parts, keep, give = run(
            cut_four_kernel, [*sends(u_parts, XY_MASKS), keep, send(give, 2)],
            [((n, E + 256), BF16)] * 4 + [((n * 2, 4 * D), BF16)] * 2, after=[both])
        grad_tok, result, out_g, q_g, k_g, v_g, o_g, in_g, x_g, dt_g, a_g, cw_g, cb_g, db_g, sk_g, g1_g, g2_g = run(
            finish_kernel, [both, tail, *sends(u_parts, Z_MASKS), keep, send(give, 4)],
            [((count, D), BF16)] * 2 + [((32, D), F32)] + [((16, D), F32)] * 4
            + [((16, 2 * E), F32), ((32, 64), F32), ((32, 32), F32), ((NS, 32), F32), ((KW, 32), F32)]
            + [((1, 32), F32)] * 3 + [((1, 16), F32)] * 2,
            [pltpu.VMEM((SMALL_ROWS, 32), F32)], final=True)
        a_g, cw_g = a_g.T, cw_g.T
        vectors = [value[0] for value in (cb_g, db_g, sk_g, g1_g, g2_g)]
    else:
        tail = lax.ppermute(before, "ctx", [(c + 1, c) for c in range(chunks - 1)])
        own, result = both[:count], both[count:]
        end = (own[count - HALO :].astype(F32) + tail.astype(F32)).astype(BF16)
        grad_tok = jnp.concatenate([own[: count - HALO], end], axis=0)
        scatter = lambda value, dim=0: lax.psum_scatter(value.astype(F32), ALL, scatter_dimension=dim, tiled=True)
        blocks_one = one_grads[0].reshape(BLOCKS, 32, 4 * D)
        part = lambda row, rows, col: scatter(blocks_one[:, row : row + rows, col * D : (col + 1) * D].reshape(-1, D))
        out_g, q_g, k_g, v_g, o_g = part(0, 32, 0), part(0, 16, 1), part(0, 16, 2), part(16, 16, 1), part(16, 16, 2)
        in_g = jnp.concatenate([scatter(two_grads[0][:, :E]), part(0, 16, 3), part(16, 16, 3)], axis=1)
        small = two_grads[0][:, E:].reshape(BLOCKS, 16, 8, 32).transpose(2, 1, 0, 3).reshape(SMALL_ROWS, E)
        close = lambda row: scatter(small[row].reshape(BLOCKS, 32)[:, :16].reshape(D))
        g1, g2 = close(ROW_G1), close(ROW_G2)
        mine = scatter(small, 1)
        x_g, dt_g, a_g, cw_g = (
            mine[ROW_X : ROW_X + 64].T, mine[ROW_DT : ROW_DT + RANK], mine[ROW_A : ROW_A + NS].T, mine[ROW_CW : ROW_CW + KW].T)
        vectors = [mine[ROW_CB], mine[ROW_DB], mine[ROW_SK], g1, g2]
    cb_v, db_v, sk_v, g1_v, g2_v = vectors
    return (
        result[None], grad_tok[None], g1_v, in_g, cw_g, cb_v, x_g, dt_g, db_v, a_g, sk_v, out_g, g2_v, q_g, k_g, v_g, o_g,
    )


def attend(plan, pay, count):
    if plan.chunks == HEADS:
        held = plan.swap(pay)
        length = held.shape[0]
        half = pltpu.VMEM((length, HDIM), BF16)
        flat = pltpu.VMEM((HDIM, length), BF16)
        wide = pltpu.VMEM((length, HDIM), F32)
        (back,) = run(
            attention_kernel, [held], [((length, 4 * HDIM), BF16)], [half] * 4 + [flat] * 2 + [wide] * 2, us=4
        )
        return plan.swap(back)
    parts = pay.reshape(HEADS, count, 4, HDIM)
    query, key, value, grad = (parts[:, :, i] for i in range(4))
    key, value = (lax.all_gather(part, "ctx", axis=1, tiled=True) for part in (key, value))
    query_at = lax.axis_index("ctx") * count + jnp.arange(count)
    allowed = jnp.arange(key.shape[1])[None, :] <= query_at[:, None]
    scale = HDIM**-0.5
    dots = functools.partial(jnp.einsum, preferred_element_type=F32)
    scores = jnp.where(allowed, dots("hqd,hkd->hqk", query, key) * scale, -1e30)
    soft = jax.nn.softmax(scores, axis=-1)
    soft_low = soft.astype(BF16)
    grad_p = dots("hqd,hkd->hqk", grad, value)
    grad_s = (soft * (grad_p - jnp.sum(soft * grad_p, axis=-1, keepdims=True))).astype(BF16)
    raw = dots("hqk,hkd->hqd", soft_low, value).astype(BF16)
    grad_q = (dots("hqk,hkd->hqd", grad_s, key) * scale).astype(BF16)
    grads = (dots("hqk,hqd->hkd", grad_s, query) * scale, dots("hqk,hqd->hkd", soft_low, grad))
    grad_k, grad_v = (
        lax.psum_scatter(part.astype(BF16), "ctx", scatter_dimension=1, tiled=True) for part in grads
    )
    return jnp.concatenate([raw, grad_q, grad_k, grad_v], axis=-1).reshape(HEADS * count, 4 * HDIM)


def solution(mesh):
    plan = Plan(mesh)
    split, rows, cols = P(ALL), P(ALL, None), P(None, ALL)
    acts = P("dp", "ctx", None)
    return jax.shard_map(
        functools.partial(body, plan),
        mesh=mesh,
        in_specs=(acts, split, rows, rows, split, rows, cols, split, rows, split, rows, split, rows, rows, rows, rows, acts),
        out_specs=(acts, acts, split, rows, rows, split, rows, cols, split, rows, split, rows, split, rows, rows, rows, rows),
        check_vma=False,
    )
```

```python
import functools
import math

import jax
import jax.numpy as jnp
from jax import lax
from jax.experimental import pallas as pl
from jax.experimental.pallas import tpu as pltpu
from jax.sharding import PartitionSpec as P

D = 512
E = 1024
NS = 16
RANK = 32
KW = 4
HEADS = 8
HDIM = 64
LG = 8
HALO = 16
BLOCKS = 32
ALL = ("dp", "ctx")
EPS = 1e-05
LOG2E = 1.4426950408889634
LN2 = 0.6931471805599453
F32 = jnp.float32
BF16 = jnp.bfloat16
VM = pl.BlockSpec(memory_space=pltpu.VMEM)

Z_MASKS = (0, 4, 2, 6)
XY_MASKS = (0, 1, 16, 17)
CORE = 8
HALF_MASKS = tuple(xy | zz for xy in XY_MASKS for zz in Z_MASKS)
FULL_MASKS = HALF_MASKS + tuple(mask | CORE for mask in HALF_MASKS)
CHUNK_MASKS = tuple((8 if c & 1 else 0) | (2 if c & 2 else 0) | (1 if c & 4 else 0) for c in range(8))

ROW_X = 0
ROW_DT = 64
ROW_A = 96
ROW_CW = 112
ROW_CB = 116
ROW_DB = 117
ROW_SK = 118
ROW_G1 = 119
ROW_G2 = 120
SMALL_ROWS = 128


ANY = pl.BlockSpec(memory_space=pl.ANY)
FAR = pl.BlockSpec(memory_space=pltpu.HBM)
WHOLE = pl.BlockSpec()


def run(kernel, ins, outs, scratch=(), limit=12, raw=(), far=(), after=(), final=False, us=2):
    first, count = len(ins) + len(raw) + len(far), len(after)

    def inner(*refs):
        kernel(*refs[:first], *refs[first + count :])

    return pl.pallas_call(
        inner,
        out_shape=[jax.ShapeDtypeStruct(shape, dtype) for shape, dtype in outs],
        in_specs=[VM] * len(ins) + [ANY] * len(raw) + [FAR] * len(far) + [ANY] * count,
        out_specs=[WHOLE if final else VM] * len(outs),
        scratch_shapes=list(scratch),
        compiler_params=pltpu.CompilerParams(vmem_limit_bytes=limit * 2**20),
        cost_estimate=pl.CostEstimate(flops=int(us * 1e3), bytes_accessed=int(us * 3e3), transcendentals=0),
    )(*ins, *raw, *far, *after)


def nn(left, right):
    return lax.dot_general(left, right, (((1,), (0,)), ((), ())), preferred_element_type=F32)


def nt(left, right):
    return lax.dot_general(left, right, (((1,), (1,)), ((), ())), preferred_element_type=F32)


def tn(left, right):
    return lax.dot_general(left, right, (((0,), (0,)), ((), ())), preferred_element_type=F32)


def sigmoid(value):
    return 1.0 / (1.0 + jnp.exp(-value))


class Plan:
    def __init__(self, mesh):
        self.dp, self.ctx = mesh.shape["dp"], mesh.shape["ctx"]
        self.fast = (self.dp, self.ctx) == (4, 8)
        self.chunks = self.ctx
        if self.fast:
            self.grad_masks = (FULL_MASKS[:16], FULL_MASKS[16:])
        else:
            self.grad_masks = (tuple(range(BLOCKS)),)

    def place(self, seq, chunk):
        return CHUNK_MASKS[chunk] | ((seq >> 1) << 4) | ((seq & 1) << 2)

    def me(self):
        if self.fast:
            return lax.axis_index("dp") * 8 + lax.axis_index("ctx")
        return 0

    def chunk(self):
        if self.fast:
            lin = lax.axis_index("dp") * 8 + lax.axis_index("ctx")
            return ((lin >> 3) & 1) + ((lin >> 1) & 1) * 2 + (lin & 1) * 4
        return lax.axis_index("ctx")

    def side(self):
        return ((lax.axis_index("ctx") + lax.axis_index("dp") * 8) & CORE) != 0 if self.fast else False

    def swap(self, value):
        if self.fast:
            groups = [[self.place(s, c) for c in range(8)] for s in range(4)]
            return lax.all_to_all(value, ALL, 0, 0, tiled=True, axis_index_groups=groups)
        return lax.all_to_all(value, "ctx", 0, 0, tiled=True)


def send(value, mask):
    return lax.ppermute(value, ALL, [(i, i ^ mask) for i in range(32)])


def own_first(value, side, width):
    groups = [value[:, i * width : (i + 1) * width] for i in range(4)]
    pick = lambda x, own: jnp.where(side, groups[2 * x + own], groups[2 * x + 1 - own])
    return jnp.concatenate([pick(0, 1), pick(1, 1), pick(0, 0), pick(1, 0)], axis=1)


def in_order(value, side, width):
    own_a, own_b, far_a, far_b = (value[:, i * width : (i + 1) * width] for i in range(4))
    return jnp.concatenate(
        [jnp.where(side, far_a, own_a), jnp.where(side, own_a, far_a),
         jnp.where(side, far_b, own_b), jnp.where(side, own_b, far_b)], axis=1)


def rows_of(ref, half, first, cols):
    return jnp.concatenate(
        [ref[k * 32 + half * 16 : k * 32 + half * 16 + 16, first : first + cols] for k in range(ref.shape[0] // 32)], axis=0)


def wait_whole(target, sem):
    pltpu.make_async_copy(target, target, sem).wait()


def swap_blocks(value, me):
    rows, lanes = value.shape
    for bit in (16, 8, 4):
        half = bit * 32
        parts = [value[:, i : i + half] for i in range(0, lanes, half)]
        other = jnp.concatenate([parts[i ^ 1] for i in range(len(parts))], axis=1)
        value = jnp.where((me & bit) != 0, other, value)
    groups = []
    odd = (lax.broadcasted_iota(jnp.int32, (rows, 128), 1) & 32) != 0
    for i in range(0, lanes, 128):
        part = value[:, i : i + 128]
        part = jnp.where((me & 2) != 0, pltpu.roll(part, 64, 1), part)
        other = jnp.where(odd, pltpu.roll(part, 32, 1), pltpu.roll(part, 96, 1))
        groups.append(jnp.where((me & 1) != 0, other, part))
    return jnp.concatenate(groups, axis=1)


def pack_kernel(in_proj, x_proj, dt_proj, a_log, conv_w, conv_b, dt_bias, d_skip, gain_one, gain_two,
                out_proj, w_q, w_k, w_v, w_o, one, two, rows, *rest):
    (b_in, b_x, b_dt, b_a, b_cw, b_cb, b_db, b_sk, b_g1, b_g2, b_out, b_q, b_k, b_v, b_o, sems) = rest
    copies = [
        pltpu.make_async_copy(src, dst, sems.at[i])
        for i, (src, dst) in enumerate(
            zip((in_proj, x_proj, dt_proj, a_log, conv_w, conv_b, dt_bias, d_skip, gain_one, gain_two, out_proj, w_q,
                 w_k, w_v, w_o),
                (b_in, b_x, b_dt, b_a, b_cw, b_cb, b_db, b_sk, b_g1, b_g2, b_out, b_q, b_k, b_v, b_o))
        )
    ]
    for copy in copies:
        copy.start()
    for copy in copies:
        copy.wait()
    one[:, :E] = b_in[:, :E].astype(BF16)
    two[:16, 3 * D :] = b_in[:, E : E + D].astype(BF16)
    two[16:, 3 * D :] = b_in[:, E + D :].astype(BF16)
    two[:, :D] = b_out[...].astype(BF16)
    two[:16, D : 2 * D] = b_q[...].astype(BF16)
    two[:16, 2 * D : 3 * D] = b_k[...].astype(BF16)
    two[16:, D : 2 * D] = b_v[...].astype(BF16)
    two[16:, 2 * D : 3 * D] = b_o[...].astype(BF16)
    rows[...] = jnp.zeros_like(rows)
    rows[ROW_X : ROW_X + 64, :] = b_x[...].T
    rows[ROW_DT : ROW_DT + RANK, :] = b_dt[...]
    rows[ROW_A : ROW_A + NS, :] = b_a[...]
    rows[ROW_CW : ROW_CW + KW, :] = b_cw[...]
    rows[ROW_CB : ROW_CB + 1, :] = b_cb[...]
    rows[ROW_DB : ROW_DB + 1, :] = b_db[...]
    rows[ROW_SK : ROW_SK + 1, :] = b_sk[...]
    rows[ROW_G1 : ROW_G1 + 1, :16] = b_g1[...]
    rows[ROW_G2 : ROW_G2 + 1, :16] = b_g2[...]
    one[:, E:] = jnp.concatenate([rows[16 * q : 16 * q + 16, :] for q in range(8)], axis=1).astype(BF16)


def join_smalls(target, own, far, side):
    for q in range(8):
        rows = jnp.concatenate(
            [ref[16 * k : 16 * k + 16, E + 32 * q : E + 32 * q + 32].astype(F32) for ref in (own, far) for k in range(16)], axis=1)
        target[16 * q : 16 * q + 16, :] = in_order(rows, side, 256)


def gain_row(pm, row):
    return jnp.concatenate([pm[row : row + 1, 32 * s : 32 * s + 16] for s in range(BLOCKS)], axis=1)


def spread(target, source):
    count = source.shape[0]
    for s in range(LG):
        target[pl.ds(s, count, stride=LG), :] = source[:, s * 128 : (s + 1) * 128]


def gathered(source, count):
    return jnp.concatenate([source[pl.ds(s, count, stride=LG), :] for s in range(LG)], axis=1)


def broadcast_rows(target, proj, first):
    for n in range(NS):
        target[n] = jnp.broadcast_to(proj[:, first + n : first + n + 1], target.shape[1:])


def at8(ref, index):
    return ref[pl.ds(pl.multiple_of(index * 8, 8), 8), :]


def front_kernel(plan, tok, halo, own, far, normed, turned, u_out, conv_out, act_out, proj_out, sig_out, dt3, au3, a3,
                 state, pm, gains, bx, cx):
    side = plan.side()
    join_smalls(pm, own, far, side)
    gain = gain_row(pm, ROW_G1)
    gains[0:1, :] = gain
    gains[1:2, :] = gain_row(pm, ROW_G2)
    tokens = tok.shape[0]
    x = jnp.concatenate([halo[...].astype(F32), tok[...].astype(F32)], axis=0)
    r = lax.rsqrt(jnp.mean(x * x, axis=-1, keepdims=True) + EPS)
    low = x * r * gain
    normed[...] = low.astype(BF16)
    low = own_first(low, side, 128).astype(BF16)
    turned[...] = low
    u_out[...] = nn(low[:, : D // 2], own[:, :E]) + nn(low[:, D // 2 :], far[:, :E])
    conv = pm[ROW_CB : ROW_CB + 1, :]
    for k in range(KW):
        conv = conv + pm[ROW_CW + k : ROW_CW + k + 1, :] * u_out[HALO - 3 + k : HALO - 3 + k + tokens, :]
    conv_out[...] = conv
    act = (conv * sigmoid(conv)).astype(BF16)
    act_out[...] = act
    proj = nt(act, pm[ROW_X : ROW_X + 64, :].astype(BF16))
    proj_out[:, :64] = proj
    proj_out[:, 64:] = jnp.zeros((tokens, 64), F32)
    pre = nn(proj[:, :RANK].astype(BF16), pm[ROW_DT : ROW_DT + RANK, :].astype(BF16)) + pm[ROW_DB : ROW_DB + 1, :]
    sig_out[...] = sigmoid(pre)
    step = jnp.maximum(pre, 0.0) + jnp.log1p(jnp.exp(-jnp.abs(pre)))
    spread(dt3, step)
    spread(au3, act.astype(F32))
    spread(a3, -LOG2E * jnp.exp(pm[ROW_A : ROW_A + NS, :]))
    broadcast_rows(bx, proj, RANK)
    broadcast_rows(cx, proj, RANK + NS)
    decay = [a3[8 * n : 8 * n + 8, :] for n in range(NS)]

    def advance(t, carried):
        held, total = carried
        size = at8(dt3, t)
        drive = size * at8(au3, t)
        held = tuple(
            jnp.exp2(size * decay[n]) * held[n] + drive * bx[n, pl.ds(t, 1), :] for n in range(NS)
        )
        return held, total + size

    zero = jnp.zeros((8, 128), F32)
    held, total = lax.fori_loop(0, tokens, advance, ((zero,) * NS, zero), unroll=4)
    state[...] = jnp.concatenate([*held, total, zero], axis=0).astype(BF16)


def combine_kernel(plan, forward, states, a3, entry, states_f):
    states_f[...] = states[...].astype(F32)
    decay = [a3[8 * n : 8 * n + 8, :] for n in range(NS)]
    zero = jnp.zeros((8, 128), F32)

    def combine(i, held):
        base = (i if forward else plan.chunks - 1 - i) * 144
        total = states_f[pl.ds(pl.multiple_of(base + 128, 8), 8), :]
        return tuple(
            jnp.exp2(total * decay[n]) * held[n] + states_f[pl.ds(pl.multiple_of(base + 8 * n, 8), 8), :]
            for n in range(NS)
        )

    count = plan.chunk() if forward else plan.chunks - 1 - plan.chunk()
    held = lax.fori_loop(0, count, combine, (zero,) * NS)
    entry[...] = jnp.concatenate([*held, zero, zero], axis=0)


def merge_kernel(plan, step, forward, own, other, before, a3, group, entry):
    later = ((plan.chunk() >> step) & 1) == (1 if forward else 0)
    mine, theirs = own[...].astype(F32), other[...].astype(F32)
    first, second = jnp.where(later, theirs, mine), jnp.where(later, mine, theirs)
    decay = a3[...]
    spread_total = lambda value: jnp.concatenate([value[128:136, :]] * NS, axis=0)
    joint = jnp.exp2(spread_total(second) * decay) * first[:128, :] + second[:128, :]
    group[:128, :] = joint.astype(BF16)
    group[128:, :] = (first[128:, :] + second[128:, :]).astype(BF16)
    held = before[...]
    inner = held[:128, :] + jnp.exp2(spread_total(held) * decay) * theirs[:128, :]
    entry[:128, :] = jnp.where(later, inner, held[:128, :])
    entry[128:, :] = jnp.where(later, held[128:, :] + theirs[128:, :], held[128:, :])


def exchange(plan, state, a3, forward, beside=lambda step, entry: []):
    if plan.fast:
        group, entry, firsts = state, jnp.zeros((144, 128), F32), []
        for step in range(3):
            other = send(group, CHUNK_MASKS[1 << step])
            group, entry = run(
                functools.partial(merge_kernel, plan, step, forward), [group, other, entry, a3],
                [((144, 128), BF16), ((144, 128), F32)], after=beside(step, entry if step else group))
            firsts.append(entry)
        return entry, firsts
    states = lax.all_gather(state, "ctx", axis=0, tiled=True)
    return run(
        functools.partial(combine_kernel, plan, forward), [states, a3], [((144, 128), F32)],
        [pltpu.VMEM((144 * plan.chunks, 128), F32)])[0], []


def mid_kernel(plan, tok, dt3, au3, a3, turned, pm, gains, cot, entry, bx, cx, own, far,
               pay, mamba, gated_out, middle_out, all_states, z_out, y3):
    tokens = tok.shape[0]
    side = plan.side()
    both = lambda left, half, first, cols: nn(left[:, : D // 2], rows_of(own, half, first, cols)) + nn(
        left[:, D // 2 :], rows_of(far, half, first, cols))
    decay = [a3[8 * n : 8 * n + 8, :] for n in range(NS)]
    held = tuple(entry[8 * n : 8 * n + 8, :] for n in range(NS))
    all_states[:128, :] = entry[:128, :]

    def advance(t, held):
        size = at8(dt3, t)
        drive = size * at8(au3, t)
        base = pl.multiple_of(t * 128 + 128, 128)
        held = tuple(
            jnp.exp2(size * decay[n]) * held[n] + drive * bx[n, pl.ds(t, 1), :] for n in range(NS)
        )
        for n in range(NS):
            all_states[pl.ds(base + 8 * n, 8), :] = held[n]
        y = held[0] * cx[0, pl.ds(t, 1), :]
        for n in range(1, NS):
            y = y + held[n] * cx[n, pl.ds(t, 1), :]
        y3[pl.ds(pl.multiple_of(t * 8, 8), 8), :] = y
        return held

    lax.fori_loop(0, tokens, advance, held, unroll=4)
    act = gathered(au3, tokens)
    y = gathered(y3, tokens) + pm[ROW_SK : ROW_SK + 1, :] * act
    mamba[...] = y
    low = turned[HALO:, :]
    z = jnp.concatenate([both(low, 0, 3 * D, D), both(low, 1, 3 * D, D)], axis=1)
    z_out[...] = z
    gated = y * (z * sigmoid(z))
    gated_out[...] = gated.astype(BF16)
    gated = own_first(gated, side, 256).astype(BF16)
    middle = tok[...].astype(F32) + nn(gated[:, : E // 2], own[:, :D]) + nn(gated[:, E // 2 :], far[:, :D])
    middle_out[...] = middle
    r = lax.rsqrt(jnp.mean(middle * middle, axis=-1, keepdims=True) + EPS)
    low = own_first(middle * r * gains[1:2, :], side, 128).astype(BF16)
    query_key, value = both(low, 0, D, 2 * D), both(low, 1, D, D)
    grad = jnp.concatenate([nt(cot[...], rows_of(ref, 1, 2 * D, D)) for ref in (own, far)], axis=1)
    quads = tuple(part.astype(BF16) for part in (query_key[:, :D], query_key[:, D:], value, in_order(grad, side, 128)))
    for h in range(HEADS):
        for i, part in enumerate(quads):
            pay[h * tokens : (h + 1) * tokens, i * HDIM : (i + 1) * HDIM] = part[:, h * HDIM : (h + 1) * HDIM]


def attention_kernel(pay, back, q_s, k_s, v_s, g_s, kt, vt, dk, dv):
    length = pay.shape[0]
    rows = math.gcd(length, 512)
    q_s[...] = pay[:, :HDIM]
    k_s[...] = pay[:, HDIM : 2 * HDIM]
    v_s[...] = pay[:, 2 * HDIM : 3 * HDIM]
    g_s[...] = pay[:, 3 * HDIM :]
    kt[...] = k_s[...].T
    vt[...] = v_s[...].T
    dk[...] = jnp.zeros_like(dk)
    dv[...] = jnp.zeros_like(dv)
    scale = HDIM**-0.5
    key_at = lax.broadcasted_iota(jnp.int32, (rows, rows), 0)
    query_at = lax.broadcasted_iota(jnp.int32, (rows, rows), 1)
    for i in range(length // rows):
        first, last = i * rows, (i + 1) * rows
        query = q_s[first:last, :]
        grad = g_s[first:last, :]
        scores = nt(k_s[:last, :], query) * scale
        diagonal = jnp.where(key_at <= query_at, scores[first:, :], -1e30)
        scores = diagonal if i == 0 else jnp.concatenate([scores[:first, :], diagonal], axis=0)
        expo = jnp.exp(scores - jnp.max(scores, axis=0, keepdims=True))
        soft = expo * (1.0 / jnp.sum(expo, axis=0, keepdims=True))
        soft_low = soft.astype(BF16)
        grad_p = nt(v_s[:last, :], grad)
        dot = jnp.sum(soft * grad_p, axis=0, keepdims=True)
        grad_s = (soft * (grad_p - dot)).astype(BF16)
        raw = nn(vt[:, :last], soft_low)
        grad_q = nn(kt[:, :last], grad_s) * scale
        back[first:last, :HDIM] = raw.T.astype(BF16)
        back[first:last, HDIM : 2 * HDIM] = grad_q.T.astype(BF16)
        dk[:last, :] += nn(grad_s, query)
        dv[:last, :] += nn(soft_low, grad)
    back[:, 2 * HDIM : 3 * HDIM] = (dk[...] * scale).astype(BF16)
    back[:, 3 * HDIM :] = dv[...].astype(BF16)


def turn_kernel(plan, got, middle, cot, gains, z_in, mamba, dt3, cx, a3, own, far, first,
                att, gq, gk, gv, grad_middle, mix, gz, gy3, state, gain_grad):
    tokens = middle.shape[0]
    for h in range(HEADS):
        for i, part in enumerate((att, gq, gk, gv)):
            part[:, h * HDIM : (h + 1) * HDIM] = got[h * tokens : (h + 1) * tokens, i * HDIM : (i + 1) * HDIM]
    side = plan.side()
    grad_n = in_order(jnp.concatenate(
        [nt(gq[...], rows_of(ref, 0, D, D)) + nt(gk[...], rows_of(ref, 0, 2 * D, D)) + nt(gv[...], rows_of(ref, 1, D, D))
         for ref in (own, far)], axis=1), side, 128)
    mid = middle[...]
    r = lax.rsqrt(jnp.mean(mid * mid, axis=-1, keepdims=True) + EPS)
    gain_grad[...] = jnp.sum(grad_n * mid * r, axis=0, keepdims=True)
    q = grad_n * gains[1:2, :]
    gm = cot[...].astype(F32) + r * q - mid * (r * r * r) * jnp.mean(q * mid, axis=-1, keepdims=True)
    grad_middle[...] = gm
    low = gm.astype(BF16)
    mix[...] = low
    grad_gated = in_order(jnp.concatenate([nt(low, ref[:, :D]) for ref in (own, far)], axis=1), side, 256)
    z = z_in[...]
    s = sigmoid(z)
    spread(gy3, grad_gated * (z * s))
    gz[...] = (grad_gated * mamba[...] * (s * (1.0 + z * (1.0 - s)))).astype(BF16)
    decay = [a3[8 * n : 8 * n + 8, :] for n in range(NS)]

    def retreat(i, carried):
        t = tokens - 1 - i
        size = at8(dt3, t)
        grad = at8(gy3, t)
        return tuple(
            jnp.exp2(size * decay[n]) * (carried[n] + grad * cx[n, pl.ds(t, 1), :]) for n in range(NS)
        )

    zero = jnp.zeros((8, 128), F32)
    carried = lax.fori_loop(0, tokens, retreat, (zero,) * NS, unroll=4)
    state[:128, :] = jnp.concatenate(carried, axis=0).astype(BF16)
    state[128:, :] = first[128:, :]


def pack_blocks(plan, outs, source, rows, height, row, first, col=0, cols=None):
    me = plan.me()
    cols = source.shape[1] if cols is None else cols
    for out, masks in zip(outs, plan.grad_masks):
        for k, mask in enumerate(masks):
            block = me ^ mask
            out[k * height + row : k * height + row + rows, first : first + cols] = source[
                pl.ds(pl.multiple_of(block * rows, 16), rows), col : col + cols
            ].astype(BF16)


def grad_c_kernel(gy3, all_states, grad_c):
    diagonal_sums(grad_c, 0, lambda rows: gy3[rows, :], all_states, 1)


def weights_kernel(plan, no, att, gq, gk, gv, mix, gated, middle, gains, cot, own, far, normed, gz, *refs):
    result, outs = refs[0], refs[1 : 1 + no]
    small, large, wide = refs[1 + no :]
    mid = middle[...]
    held = own_first(att[...], plan.side(), 128)
    result[...] = (
        mid + nn(held[:, : D // 2], rows_of(own, 1, 2 * D, D)) + nn(held[:, D // 2 :], rows_of(far, 1, 2 * D, D))
    ).astype(BF16)
    r = lax.rsqrt(jnp.mean(mid * mid, axis=-1, keepdims=True) + EPS)
    low = (mid * r * gains[1:2, :]).astype(BF16)
    large[...] = tn(gated[...], mix[...])
    pack_blocks(plan, outs, large, 32, 32, 0, 0)
    small[...] = tn(low, gq[...])
    pack_blocks(plan, outs, small, 16, 32, 0, D)
    small[...] = tn(low, gk[...])
    pack_blocks(plan, outs, small, 16, 32, 0, 2 * D)
    small[...] = tn(low, gv[...])
    pack_blocks(plan, outs, small, 16, 32, 16, D)
    small[...] = tn(att[...], cot[...])
    pack_blocks(plan, outs, small, 16, 32, 16, 2 * D)
    wide[...] = tn(normed[HALO:, :], gz[...])
    pack_blocks(plan, outs, wide, 16, 32, 0, 3 * D, 0, D)
    pack_blocks(plan, outs, wide, 16, 32, 16, 3 * D, D, D)


def diagonal_sums(out, col, channels, held, offset, span=16):
    row_t = lax.broadcasted_iota(jnp.int32, (span, span * NS), 0)
    col_t = lax.broadcasted_iota(jnp.int32, (span, span * NS), 1) // NS
    pick = (
        lax.broadcasted_iota(jnp.int32, (span * NS, NS), 0) % NS
        == lax.broadcasted_iota(jnp.int32, (span * NS, NS), 1)
    ).astype(BF16)
    for block in range(out.shape[0] // span):
        total = jnp.zeros((span, span * NS), F32)
        for s in range(LG):
            held_rows = held[pl.ds((block * span + offset) * 128 + s, span * NS, stride=LG), :].astype(BF16)
            total = total + nt(channels(pl.ds(block * span * 8 + s, span, stride=LG)).astype(BF16), held_rows)
        own = jnp.where(row_t == col_t, total, 0.0).astype(BF16)
        out[block * span : (block + 1) * span, col : col + NS] = nn(own, pick)


def back_kernel(plan, dt3, au3, gy3, a3, proj, pm, all_states, sig, act, conv_in, u_in, leaving, bx, cx, grad_c,
                small_grads, gu_out, grads, gs3, ga3, gal, skip3, low_rank, padded):
    tokens = dt3.shape[0] // LG
    decay = [a3[8 * n : 8 * n + 8, :] for n in range(NS)]
    zero = jnp.zeros((8, 128), F32)
    spread(skip3, pm[ROW_SK : ROW_SK + 1, :])
    skip = skip3[...]

    carried = tuple(leaving[8 * n : 8 * n + 8, :] for n in range(NS))
    gal[...] = jnp.zeros_like(gal)

    def retreat(i, state):
        carried, skipped = state
        t = tokens - 1 - i
        size, value, grad = at8(dt3, t), at8(au3, t), at8(gy3, t)
        base = pl.multiple_of(t * 128, 128)
        from_b = zero
        from_a = zero
        fresh = []
        for n in range(NS):
            g = carried[n] + grad * cx[n, pl.ds(t, 1), :]
            grads[pl.ds(base + 8 * n, 8), :] = g
            w = jnp.exp2(size * decay[n]) * g
            q = w * all_states[pl.ds(base + 8 * n, 8), :]
            from_a = from_a + decay[n] * q
            from_b = from_b + g * bx[n, pl.ds(t, 1), :]
            gal[8 * n : 8 * n + 8, :] += size * q
            fresh.append(w)
        at = pl.ds(pl.multiple_of(t * 8, 8), 8)
        gs3[at, :] = from_a * LN2 + from_b * value
        ga3[at, :] = from_b * size + skip * grad
        return tuple(fresh), skipped + grad * value

    _, skipped = lax.fori_loop(0, tokens, retreat, (carried, zero), unroll=4)

    diagonal_sums(low_rank, RANK, lambda rows: dt3[rows, :] * au3[rows, :], grads, 0)
    low_rank[:, RANK + NS : RANK + 2 * NS] = grad_c[:, :NS]

    grad_pre = gathered(gs3, tokens) * sig[...]
    grad_pre_low = grad_pre.astype(BF16)
    low_rank[:, :RANK] = nt(grad_pre_low, pm[ROW_DT : ROW_DT + RANK, :].astype(BF16))
    projected = low_rank[:, :64].astype(BF16)
    small_grads[ROW_X : ROW_X + 64, :] = tn(projected, act[...])
    small_grads[ROW_DT : ROW_DT + RANK, :] = tn(proj[:, :RANK].astype(BF16), grad_pre_low)
    true_a = -jnp.exp(pm[ROW_A : ROW_A + NS, :])
    small_grads[ROW_A : ROW_A + NS, :] = gathered(gal, NS) * true_a
    small_grads[ROW_DB : ROW_DB + 1, :] = jnp.sum(grad_pre, axis=0, keepdims=True)
    skip3[...] = skipped
    small_grads[ROW_SK : ROW_SK + 1, :] = gathered(skip3, 1)
    small_grads[ROW_G1:, :] = jnp.zeros((SMALL_ROWS - ROW_G1, E), F32)
    conv = conv_in[...]
    s = sigmoid(conv)
    grad_act = gathered(ga3, tokens) + nn(projected, pm[ROW_X : ROW_X + 64, :].astype(BF16))
    grad_conv = grad_act * (s * (1.0 + conv * (1.0 - s)))
    small_grads[ROW_CB : ROW_CB + 1, :] = jnp.sum(grad_conv, axis=0, keepdims=True)
    for k in range(KW):
        small_grads[ROW_CW + k : ROW_CW + k + 1, :] = jnp.sum(
            grad_conv * u_in[HALO - 3 + k : HALO - 3 + k + tokens, :], axis=0, keepdims=True
        )
    padded[:HALO, :] = jnp.zeros((HALO, E), F32)
    padded[HALO : HALO + tokens, :] = grad_conv
    padded[HALO + tokens :, :] = jnp.zeros((HALO, E), F32)
    gu = jnp.zeros((HALO + tokens, E), F32)
    for k in range(KW):
        gu = gu + pm[ROW_CW + k : ROW_CW + k + 1, :] * padded[3 - k : 3 - k + HALO + tokens, :]
    gu_out[...] = gu.astype(BF16)


def last_kernel(plan, no, tok, halo, gains, gu, gz, grad_middle, own_u, far_u, own_z, far_z, normed, small_grads, gain_two, result, *refs):
    outs = refs[:no]
    both, before, large, spaced = refs[no:]
    tokens = tok.shape[0]
    both[tokens:, :] = result[...]
    me = plan.me()
    large[...] = tn(normed[...], gu[...])
    pack_blocks(plan, outs, large, 16, 16, 0, 0)
    x = jnp.concatenate([halo[...].astype(F32), tok[...].astype(F32)], axis=0)
    r = lax.rsqrt(jnp.mean(x * x, axis=-1, keepdims=True) + EPS)
    from_z = jnp.concatenate(
        [nt(gz[:, :D], rows_of(ref, 0, 3 * D, D)) + nt(gz[:, D:], rows_of(ref, 1, 3 * D, D)) for ref in (own_z, far_z)], axis=1)
    from_u = jnp.concatenate([nt(gu[...], ref[:, :E]) for ref in (own_u, far_u)], axis=1)
    grad_n = in_order(from_u + jnp.concatenate([jnp.zeros((HALO, D), F32), from_z], axis=0), plan.side(), 128)
    gain_one = jnp.sum(grad_n * x * r, axis=0, keepdims=True)
    q = grad_n * gains[0:1, :]
    base = r * q - x * (r * r * r) * jnp.mean(q * x, axis=-1, keepdims=True)
    both[:tokens, :] = (grad_middle[...] + base[HALO:, :]).astype(BF16)
    before[...] = base[:HALO, :].astype(BF16)
    spaced[...] = small_grads[...]
    blank = jnp.zeros((1, 16), F32)
    for row, grad in ((ROW_G1, gain_one), (ROW_G2, gain_two[...])):
        spaced[row : row + 1, :] = jnp.concatenate(
            [part for s in range(BLOCKS) for part in (grad[:, 16 * s : 16 * s + 16], blank)], axis=1)
    spaced[...] = swap_blocks(spaced[...], me)
    for out, masks in zip(outs, plan.grad_masks):
        for k, m in enumerate(masks):
            out[16 * k : 16 * k + 16, E:] = jnp.concatenate(
                [spaced[16 * q : 16 * q + 16, 32 * m : 32 * m + 32] for q in range(8)], axis=1).astype(BF16)


def total_of(ins):
    total = ins[0][...].astype(F32)
    for other in ins[1:]:
        total = total + other[...].astype(F32)
    return total


def finish_kernel(*refs):
    (both, tail), refs = refs[:2], refs[2:]
    u_ins, ins, (own_out, result_out), refs = refs[:4], refs[4:6], refs[6:8], refs[2:]
    count = own_out.shape[0]
    rows = count - HALO
    own_out[:rows, :] = both[:rows, :]
    own_out[rows:, :] = (both[rows:count, :].astype(F32) + tail[...].astype(F32)).astype(BF16)
    result_out[...] = both[count:, :]
    out_g, q_g, k_g, v_g, o_g, in_g, x_g, dt_g, a_g, cw_g, cb_g, db_g, sk_g, g1_g, g2_g, rows = refs[6:]
    total = total_of(ins)
    out_g[...] = total[:, :D]
    q_g[...] = total[:16, D : 2 * D]
    k_g[...] = total[:16, 2 * D : 3 * D]
    v_g[...] = total[16:, D : 2 * D]
    o_g[...] = total[16:, 2 * D : 3 * D]
    in_g[:, E : E + D] = total[:16, 3 * D :]
    in_g[:, E + D :] = total[16:, 3 * D :]
    total = total_of(u_ins)
    in_g[:, :E] = total[:, :E]
    for q in range(8):
        rows[16 * q : 16 * q + 16, :] = total[:, E + 32 * q : E + 32 * q + 32]
    x_g[...] = rows[ROW_X : ROW_X + 64, :].T
    dt_g[...] = rows[ROW_DT : ROW_DT + RANK, :]
    a_g[...] = rows[ROW_A : ROW_A + NS, :]
    cw_g[...] = rows[ROW_CW : ROW_CW + KW, :]
    cb_g[...] = rows[ROW_CB : ROW_CB + 1, :]
    db_g[...] = rows[ROW_DB : ROW_DB + 1, :]
    sk_g[...] = rows[ROW_SK : ROW_SK + 1, :]
    g1_g[...] = rows[ROW_G1 : ROW_G1 + 1, :16]
    g2_g[...] = rows[ROW_G2 : ROW_G2 + 1, :16]


def join_kernel(plan, counts, placed, *refs):
    ins, outs = refs[: sum(counts)], refs[sum(counts) :]
    at = 0
    for i, count in enumerate(counts):
        rows = outs[i].shape[0] // count
        for k in range(count):
            part = ins[at + k]
            if not placed[i]:
                outs[i][k * rows : (k + 1) * rows, :] = part[...]
                continue
            height = rows // len(Z_MASKS)
            for j, zz in enumerate(Z_MASKS):
                owner = plan.me() ^ (XY_MASKS[k] | zz)
                to = (((owner >> 4) & 1) * 8 + (owner & 7)) * height
                outs[i][pl.ds(pl.multiple_of(to, 16), height), :] = part[j * height : (j + 1) * height, :]
        at += count


def join(plan, groups, after=(), placed=()):
    counts = [len(group) for group in groups]
    outs = [((group[0].shape[0] * len(group), group[0].shape[1]), group[0].dtype) for group in groups]
    return run(
        functools.partial(join_kernel, plan, counts, [i in placed for i in range(len(groups))]),
        [part for group in groups for part in group], outs, after=after, us=1)


def spread_out(value, stage):
    return [value] + [send(value, mask) for mask in stage[1:]]


def cut_one_kernel(keep, got, a_keep, a_give, b_keep, b_give):
    half, quarter, cols = keep.shape[0] // 2, keep.shape[0] // 4, keep.shape[1] // 2
    add = lambda rows, lanes: (keep[rows, lanes].astype(F32) + got[rows, lanes].astype(F32)).astype(BF16)
    left, right = slice(0, cols), slice(cols, 2 * cols)
    a_keep[...] = add(slice(0, half), left)
    a_give[...] = add(slice(half, 2 * half), left)
    for i in range(2):
        b_keep[i * quarter : (i + 1) * quarter, :] = add(slice(2 * i * quarter, (2 * i + 1) * quarter), right)
        b_give[i * quarter : (i + 1) * quarter, :] = add(slice((2 * i + 1) * quarter, (2 * i + 2) * quarter), right)


def cut_two_kernel(a_own, a_got, b_own, b_got, a_keep, a_give, b_keep, b_give):
    rows = a_own.shape[0] // 2
    for own, got, keep, give in ((a_own, a_got, a_keep, a_give), (b_own, b_got, b_keep, b_give)):
        for out, part in ((keep, slice(0, rows)), (give, slice(rows, 2 * rows))):
            out[...] = (own[part, :].astype(F32) + got[part, :].astype(F32)).astype(BF16)


def add_rows(out, rows, ins, cols=slice(None), to=slice(None)):
    total = ins[0][rows, cols].astype(F32)
    for other in ins[1:]:
        total = total + other[rows, cols].astype(F32)
    out[:, to] = total.astype(out.dtype)


def cut_three_kernel(u_own, u_got, a_own, a_got, b_own, b_got, u_0, u_1, u_2, u_3, keep, give):
    rows = u_0.shape[0]
    for i, out in enumerate((u_0, u_1, u_2, u_3)):
        add_rows(out, slice(i * rows, (i + 1) * rows), (u_own, u_got))
    rows, cols = keep.shape[0], a_own.shape[1]
    for i, out in enumerate((keep, give)):
        part = slice(i * rows, (i + 1) * rows)
        add_rows(out, part, (a_own, a_got), to=slice(0, cols))
        add_rows(out, part, (b_own, b_got), to=slice(cols, 2 * cols))


def cut_four_kernel(u_own, u_a, u_b, u_c, own, got, u_0, u_1, u_2, u_3, keep, give):
    rows = u_0.shape[0]
    for i, out in enumerate((u_0, u_1, u_2, u_3)):
        add_rows(out, slice(i * rows, (i + 1) * rows), (u_own, u_a, u_b, u_c))
    rows = keep.shape[0]
    for i, out in enumerate((keep, give)):
        add_rows(out, slice(i * rows, (i + 1) * rows), (own, got))


def body(plan, *args):
    (tokens, mixer_gain, in_proj, conv_weight, conv_bias, x_proj, dt_proj, dt_bias, a_log, d_skip, out_proj,
     attn_gain, w_query, w_key, w_value, w_output, cotangent) = args
    count = tokens.shape[1]
    tok0, cot0 = tokens.reshape(count, D), cotangent.reshape(count, D)
    chunks = plan.chunks
    devices = plan.dp * plan.ctx
    share, width = E // devices, D // devices
    if plan.fast:
        home = [(s * 8 + c, plan.place(s, c)) for s in range(4) for c in range(8)]
        halo = lax.ppermute(
            tok0[count - HALO :], ALL, [(s * 8 + c, plan.place(s, c + 1)) for s in range(4) for c in range(7)]
        )
        raw = [in_proj, x_proj, dt_proj, a_log.T, conv_weight.T, conv_bias[None], dt_bias[None], d_skip[None],
               mixer_gain[None], attn_gain[None], out_proj, w_query, w_key, w_value, w_output]
        pack_one, pack_two = run(
            pack_kernel, [], [((16, E + 256), BF16), ((32, 4 * D), BF16)],
            [pltpu.VMEM((SMALL_ROWS, 32), F32)] + [pltpu.VMEM(value.shape, F32) for value in raw]
            + [pltpu.SemaphoreType.DMA((len(raw),))], far=raw, limit=60)
        one, tok = join(plan, [spread_out(pack_one, Z_MASKS), [tok0]])
        tok = lax.ppermute(tok, ALL, home)
        near_one = spread_out(one, XY_MASKS)
        (two,) = join(plan, [[pack_two, send(pack_two, 4)]], [one, halo])
        cot = lax.ppermute(cot0, ALL, home)
        one, two = join(plan, [near_one, [two, send(two, 2)]], [tok], (0,))
        one = [one, send(one, CORE)]
        near_two = spread_out(two, XY_MASKS)
    else:
        tok, cot = tok0, cot0
        halo = lax.ppermute(tok0[count - HALO :], "ctx", [(c, c + 1) for c in range(chunks - 1)])
        smalls = jnp.concatenate(
            [x_proj.T, dt_proj, a_log.T, conv_weight.T, conv_bias[None], dt_bias[None], d_skip[None],
             jnp.pad(mixer_gain, (0, share - width))[None], jnp.pad(attn_gain, (0, share - width))[None],
             jnp.zeros((SMALL_ROWS - ROW_G2 - 1, share), F32)], axis=0).astype(BF16)
        small_all = lax.all_gather(smalls, ALL, axis=1, tiled=True)
        apart = lambda row: jnp.pad(
            small_all[row].reshape(devices, share)[:, :width].reshape(BLOCKS, 16), ((0, 0), (0, 16))).reshape(1, E)
        small_all = jnp.concatenate(
            [small_all[:ROW_G1], apart(ROW_G1), apart(ROW_G2), small_all[ROW_G2 + 1 :]], axis=0)
        small_all = small_all.reshape(8, 16, BLOCKS, 32).transpose(2, 1, 0, 3).reshape(BLOCKS * 16, 256)
        whole = lambda value: lax.all_gather(value.astype(BF16), ALL, axis=0, tiled=True)
        in_all = whole(in_proj)
        halves = lambda value: [value.reshape(2, 2, -1, value.shape[1])[:, i].reshape(-1, value.shape[1]) for i in range(2)]
        one = halves(jnp.concatenate([in_all[:, :E], small_all], axis=1))
        out_all, q_all, k_all, v_all, o_all = (whole(w) for w in (out_proj, w_query, w_key, w_value, w_output))
        cut = lambda value: value.reshape(BLOCKS, 16, D)
        side = jnp.concatenate(
            [jnp.concatenate([cut(q_all), cut(k_all)], axis=2), jnp.concatenate([cut(v_all), cut(o_all)], axis=2)], axis=1)
        gate = jnp.concatenate([cut(in_all[:, E : E + D]), cut(in_all[:, E + D :])], axis=1)
        two = halves(jnp.concatenate([out_all.reshape(BLOCKS, 32, D), side, gate], axis=2).reshape(BLOCKS * 32, 4 * D))

    no = len(plan.grad_masks)
    rows3 = count * LG
    (normed, turned, u_pre, conv, act, proj, sig, dt3, au3, a3, state, pm, gains, bx, cx) = run(
        functools.partial(front_kernel, plan),
        [tok, halo, *one],
        [((HALO + count, D), BF16), ((HALO + count, D), BF16), ((HALO + count, E), F32), ((count, E), F32),
         ((count, E), BF16), ((count, 128), F32), ((count, E), F32), ((rows3, 128), F32), ((rows3, 128), F32),
         ((128, 128), F32), ((144, 128), BF16), ((SMALL_ROWS, E), F32), ((8, D), F32),
         ((NS, count, 128), F32), ((NS, count, 128), F32)], us=6,
    )
    entry, firsts = exchange(plan, state, a3, True)
    if plan.fast:
        (held,) = join(plan, [near_two], [*firsts[1:2], cot], (0,))
        two = [held, send(held, CORE)]
    pay, mamba, gated, middle, all_states, z = run(
        functools.partial(mid_kernel, plan),
        [tok, dt3, au3, a3, turned, pm, gains, cot, entry, bx, cx, *two],
        [((HEADS * count, 4 * HDIM), BF16), ((count, E), F32), ((count, E), BF16), ((count, D), F32),
         (((count + 1) * 128, 128), F32), ((count, E), F32)],
        [pltpu.VMEM((rows3, 128), F32)], us=6,
    )
    got = attend(plan, pay, count)
    (att, gq, gk, gv, grad_middle, mix, gz, gy3, later, gain_grad_two) = run(
        functools.partial(turn_kernel, plan),
        [got, middle, cot, gains, z, mamba, dt3, cx, a3, *two, state],
        [((count, D), BF16)] * 4 + [((count, D), F32), ((count, D), BF16), ((count, E), BF16), ((rows3, 128), F32),
                                    ((144, 128), BF16), ((1, D), F32)],
    )
    blocks = [len(masks_of) for masks_of in plan.grad_masks]

    def weight_grads(after):
        return run(
            functools.partial(weights_kernel, plan, no),
            [att, gq, gk, gv, mix, gated, middle, gains, cot, *two, normed, gz],
            [((count, D), BF16)] + [((n * 32, 4 * D), BF16) for n in blocks],
            [pltpu.VMEM((D, D), F32), pltpu.VMEM((E, D), F32), pltpu.VMEM((D, E), F32)], after=after)

    def c_grads(after):
        return run(grad_c_kernel, [gy3, all_states], [((count, 128), F32)], after=after)

    done, extra = [], []

    def beside(step, entry):
        if step == 1:
            done.extend(weight_grads([entry]))
            return done[:1]
        if step == 2:
            extra.extend(c_grads([entry]))
        return list(extra)

    leaving, _ = exchange(plan, later, a3, False, beside)
    result, *one_grads = done or weight_grads([])
    (grad_c,) = extra or c_grads([])
    one_parts = []
    if plan.fast:
        rows = blocks[0] * 32
        one_parts = run(
            cut_one_kernel, [one_grads[0], send(one_grads[1], CORE)], [((rows // 2, 2 * D), BF16)] * 4, after=[leaving])
    small_grads, gu = run(
        functools.partial(back_kernel, plan),
        [dt3, au3, gy3, a3, proj, pm, all_states, sig, act, conv, u_pre, leaving, bx, cx, grad_c],
        [((SMALL_ROWS, E), F32), ((HALO + count, E), BF16)],
        [pltpu.VMEM((count * 128, 128), F32), pltpu.VMEM((rows3, 128), F32), pltpu.VMEM((rows3, 128), F32),
         pltpu.VMEM((128, 128), F32), pltpu.VMEM((8, 128), F32), pltpu.VMEM((count, 128), F32),
         pltpu.VMEM((count + 2 * HALO, E), F32)],
        limit=32, after=one_parts[:1], us=11,
    )
    *two_grads, both, before = run(
        functools.partial(last_kernel, plan, no),
        [tok, halo, gains, gu, gz, grad_middle, *one, *two, normed, small_grads, gain_grad_two, result],
        [((n * 16, E + 256), BF16) for n in blocks] + [((2 * count, D), BF16), ((HALO, D), BF16)],
        [pltpu.VMEM((D, E), F32), pltpu.VMEM((SMALL_ROWS, E), F32)],     )
    if plan.fast:
        a_keep, a_give, b_keep, b_give = one_parts
        one_parts = run(
            cut_two_kernel, [a_keep, send(a_give, 16), b_keep, send(b_give, 1)], [((rows // 4, 2 * D), BF16)] * 4,
            after=[two_grads[0]])
    if plan.fast:
        back = [(b, a) for a, b in home]
        both = lax.ppermute(both, ALL, back)
        tail = lax.ppermute(
            before, ALL, [(plan.place(s, c + 1), s * 8 + c) for s in range(4) for c in range(7)])
        a_keep, a_give, b_keep, b_give = one_parts
        sends = lambda parts, stage: [parts[0]] + [send(part, mask) for part, mask in zip(parts[1:], stage[1:])]
        n = blocks[0]
        *u_parts, keep, give = run(
            cut_three_kernel,
            [two_grads[0], send(two_grads[1], CORE), a_keep, send(a_give, 1), b_keep, send(b_give, 16)],
            [((n * 4, E + 256), BF16)] * 4 + [((n * 4, 4 * D), BF16)] * 2, after=[tail])
        *u_parts, keep, give = run(
            cut_four_kernel, [*sends(u_parts, XY_MASKS), keep, send(give, 2)],
            [((n, E + 256), BF16)] * 4 + [((n * 2, 4 * D), BF16)] * 2, after=[both])
        grad_tok, result, out_g, q_g, k_g, v_g, o_g, in_g, x_g, dt_g, a_g, cw_g, cb_g, db_g, sk_g, g1_g, g2_g = run(
            finish_kernel, [both, tail, *sends(u_parts, Z_MASKS), keep, send(give, 4)],
            [((count, D), BF16)] * 2 + [((32, D), F32)] + [((16, D), F32)] * 4
            + [((16, 2 * E), F32), ((32, 64), F32), ((32, 32), F32), ((NS, 32), F32), ((KW, 32), F32)]
            + [((1, 32), F32)] * 3 + [((1, 16), F32)] * 2,
            [pltpu.VMEM((SMALL_ROWS, 32), F32)], final=True)
        a_g, cw_g = a_g.T, cw_g.T
        vectors = [value[0] for value in (cb_g, db_g, sk_g, g1_g, g2_g)]
    else:
        tail = lax.ppermute(before, "ctx", [(c + 1, c) for c in range(chunks - 1)])
        own, result = both[:count], both[count:]
        end = (own[count - HALO :].astype(F32) + tail.astype(F32)).astype(BF16)
        grad_tok = jnp.concatenate([own[: count - HALO], end], axis=0)
        scatter = lambda value, dim=0: lax.psum_scatter(value.astype(F32), ALL, scatter_dimension=dim, tiled=True)
        blocks_one = one_grads[0].reshape(BLOCKS, 32, 4 * D)
        part = lambda row, rows, col: scatter(blocks_one[:, row : row + rows, col * D : (col + 1) * D].reshape(-1, D))
        out_g, q_g, k_g, v_g, o_g = part(0, 32, 0), part(0, 16, 1), part(0, 16, 2), part(16, 16, 1), part(16, 16, 2)
        in_g = jnp.concatenate([scatter(two_grads[0][:, :E]), part(0, 16, 3), part(16, 16, 3)], axis=1)
        small = two_grads[0][:, E:].reshape(BLOCKS, 16, 8, 32).transpose(2, 1, 0, 3).reshape(SMALL_ROWS, E)
        close = lambda row: scatter(small[row].reshape(BLOCKS, 32)[:, :16].reshape(D))
        g1, g2 = close(ROW_G1), close(ROW_G2)
        mine = scatter(small, 1)
        x_g, dt_g, a_g, cw_g = (
            mine[ROW_X : ROW_X + 64].T, mine[ROW_DT : ROW_DT + RANK], mine[ROW_A : ROW_A + NS].T, mine[ROW_CW : ROW_CW + KW].T)
        vectors = [mine[ROW_CB], mine[ROW_DB], mine[ROW_SK], g1, g2]
    cb_v, db_v, sk_v, g1_v, g2_v = vectors
    return (
        result[None], grad_tok[None], g1_v, in_g, cw_g, cb_v, x_g, dt_g, db_v, a_g, sk_v, out_g, g2_v, q_g, k_g, v_g, o_g,
    )


def attend(plan, pay, count):
    if plan.chunks == HEADS:
        held = plan.swap(pay)
        length = held.shape[0]
        half = pltpu.VMEM((length, HDIM), BF16)
        flat = pltpu.VMEM((HDIM, length), BF16)
        wide = pltpu.VMEM((length, HDIM), F32)
        (back,) = run(
            attention_kernel, [held], [((length, 4 * HDIM), BF16)], [half] * 4 + [flat] * 2 + [wide] * 2, us=4
        )
        return plan.swap(back)
    parts = pay.reshape(HEADS, count, 4, HDIM)
    query, key, value, grad = (parts[:, :, i] for i in range(4))
    key, value = (lax.all_gather(part, "ctx", axis=1, tiled=True) for part in (key, value))
    query_at = lax.axis_index("ctx") * count + jnp.arange(count)
    allowed = jnp.arange(key.shape[1])[None, :] <= query_at[:, None]
    scale = HDIM**-0.5
    dots = functools.partial(jnp.einsum, preferred_element_type=F32)
    scores = jnp.where(allowed, dots("hqd,hkd->hqk", query, key) * scale, -1e30)
    soft = jax.nn.softmax(scores, axis=-1)
    soft_low = soft.astype(BF16)
    grad_p = dots("hqd,hkd->hqk", grad, value)
    grad_s = (soft * (grad_p - jnp.sum(soft * grad_p, axis=-1, keepdims=True))).astype(BF16)
    raw = dots("hqk,hkd->hqd", soft_low, value).astype(BF16)
    grad_q = (dots("hqk,hkd->hqd", grad_s, key) * scale).astype(BF16)
    grads = (dots("hqk,hqd->hkd", grad_s, query) * scale, dots("hqk,hqd->hkd", soft_low, grad))
    grad_k, grad_v = (
        lax.psum_scatter(part.astype(BF16), "ctx", scatter_dimension=1, tiled=True) for part in grads
    )
    return jnp.concatenate([raw, grad_q, grad_k, grad_v], axis=-1).reshape(HEADS * count, 4 * HDIM)


def solution(mesh):
    plan = Plan(mesh)
    split, rows, cols = P(ALL), P(ALL, None), P(None, ALL)
    acts = P("dp", "ctx", None)
    return jax.shard_map(
        functools.partial(body, plan),
        mesh=mesh,
        in_specs=(acts, split, rows, rows, split, rows, cols, split, rows, split, rows, split, rows, rows, rows, rows, acts),
        out_specs=(acts, acts, split, rows, rows, split, rows, cols, split, rows, split, rows, split, rows, rows, rows, rows),
        check_vma=False,
    )
```

```python
import functools
import math

import jax
import jax.numpy as jnp
from jax import lax
from jax.experimental import pallas as pl
from jax.experimental.pallas import tpu as pltpu
from jax.sharding import PartitionSpec as P

D = 512
E = 1024
NS = 16
RANK = 32
KW = 4
HEADS = 8
HDIM = 64
LG = 8
HALO = 16
BLOCKS = 32
ALL = ("dp", "ctx")
EPS = 1e-05
LOG2E = 1.4426950408889634
LN2 = 0.6931471805599453
F32 = jnp.float32
BF16 = jnp.bfloat16
VM = pl.BlockSpec(memory_space=pltpu.VMEM)

Z_MASKS = (0, 4, 2, 6)
XY_MASKS = (0, 1, 16, 17)
CORE = 8
HALF_MASKS = tuple(xy | zz for xy in XY_MASKS for zz in Z_MASKS)
FULL_MASKS = HALF_MASKS + tuple(mask | CORE for mask in HALF_MASKS)
CHUNK_MASKS = tuple((8 if c & 1 else 0) | (2 if c & 2 else 0) | (1 if c & 4 else 0) for c in range(8))

ROW_X = 0
ROW_DT = 64
ROW_A = 96
ROW_CW = 112
ROW_CB = 116
ROW_DB = 117
ROW_SK = 118
ROW_G1 = 119
ROW_G2 = 120
SMALL_ROWS = 128


ANY = pl.BlockSpec(memory_space=pl.ANY)
FAR = pl.BlockSpec(memory_space=pltpu.HBM)
WHOLE = pl.BlockSpec()


def run(kernel, ins, outs, scratch=(), limit=12, raw=(), far=(), after=(), final=False, us=2):
    first, count = len(ins) + len(raw) + len(far), len(after)

    def inner(*refs):
        kernel(*refs[:first], *refs[first + count :])

    return pl.pallas_call(
        inner,
        out_shape=[jax.ShapeDtypeStruct(shape, dtype) for shape, dtype in outs],
        in_specs=[VM] * len(ins) + [ANY] * len(raw) + [FAR] * len(far) + [ANY] * count,
        out_specs=[WHOLE if final else VM] * len(outs),
        scratch_shapes=list(scratch),
        compiler_params=pltpu.CompilerParams(vmem_limit_bytes=limit * 2**20),
        cost_estimate=pl.CostEstimate(flops=int(us * 1e3), bytes_accessed=int(us * 3e3), transcendentals=0),
    )(*ins, *raw, *far, *after)


def nn(left, right):
    return lax.dot_general(left, right, (((1,), (0,)), ((), ())), preferred_element_type=F32)


def nt(left, right):
    return lax.dot_general(left, right, (((1,), (1,)), ((), ())), preferred_element_type=F32)


def tn(left, right):
    return lax.dot_general(left, right, (((0,), (0,)), ((), ())), preferred_element_type=F32)


def sigmoid(value):
    return 1.0 / (1.0 + jnp.exp(-value))


class Plan:
    def __init__(self, mesh):
        self.dp, self.ctx = mesh.shape["dp"], mesh.shape["ctx"]
        self.fast = (self.dp, self.ctx) == (4, 8)
        self.chunks = self.ctx
        if self.fast:
            self.grad_masks = (FULL_MASKS[:16], FULL_MASKS[16:])
        else:
            self.grad_masks = (tuple(range(BLOCKS)),)

    def place(self, seq, chunk):
        return CHUNK_MASKS[chunk] | ((seq >> 1) << 4) | ((seq & 1) << 2)

    def me(self):
        if self.fast:
            return lax.axis_index("dp") * 8 + lax.axis_index("ctx")
        return 0

    def chunk(self):
        if self.fast:
            lin = lax.axis_index("dp") * 8 + lax.axis_index("ctx")
            return ((lin >> 3) & 1) + ((lin >> 1) & 1) * 2 + (lin & 1) * 4
        return lax.axis_index("ctx")

    def side(self):
        return ((lax.axis_index("ctx") + lax.axis_index("dp") * 8) & CORE) != 0 if self.fast else False

    def swap(self, value):
        if self.fast:
            groups = [[self.place(s, c) for c in range(8)] for s in range(4)]
            return lax.all_to_all(value, ALL, 0, 0, tiled=True, axis_index_groups=groups)
        return lax.all_to_all(value, "ctx", 0, 0, tiled=True)


def send(value, mask):
    return lax.ppermute(value, ALL, [(i, i ^ mask) for i in range(32)])


def own_first(value, side, width):
    groups = [value[:, i * width : (i + 1) * width] for i in range(4)]
    pick = lambda x, own: jnp.where(side, groups[2 * x + own], groups[2 * x + 1 - own])
    return jnp.concatenate([pick(0, 1), pick(1, 1), pick(0, 0), pick(1, 0)], axis=1)


def in_order(value, side, width):
    own_a, own_b, far_a, far_b = (value[:, i * width : (i + 1) * width] for i in range(4))
    return jnp.concatenate(
        [jnp.where(side, far_a, own_a), jnp.where(side, own_a, far_a),
         jnp.where(side, far_b, own_b), jnp.where(side, own_b, far_b)], axis=1)


def rows_of(ref, half, first, cols):
    return jnp.concatenate(
        [ref[k * 32 + half * 16 : k * 32 + half * 16 + 16, first : first + cols] for k in range(ref.shape[0] // 32)], axis=0)


def wait_whole(target, sem):
    pltpu.make_async_copy(target, target, sem).wait()


def swap_blocks(value, me):
    rows, lanes = value.shape
    for bit in (16, 8, 4):
        half = bit * 32
        parts = [value[:, i : i + half] for i in range(0, lanes, half)]
        other = jnp.concatenate([parts[i ^ 1] for i in range(len(parts))], axis=1)
        value = jnp.where((me & bit) != 0, other, value)
    groups = []
    odd = (lax.broadcasted_iota(jnp.int32, (rows, 128), 1) & 32) != 0
    for i in range(0, lanes, 128):
        part = value[:, i : i + 128]
        part = jnp.where((me & 2) != 0, pltpu.roll(part, 64, 1), part)
        other = jnp.where(odd, pltpu.roll(part, 32, 1), pltpu.roll(part, 96, 1))
        groups.append(jnp.where((me & 1) != 0, other, part))
    return jnp.concatenate(groups, axis=1)


def pack_kernel(in_proj, x_proj, dt_proj, a_log, conv_w, conv_b, dt_bias, d_skip, gain_one, gain_two,
                out_proj, w_q, w_k, w_v, w_o, one, two, rows, *rest):
    (b_in, b_x, b_dt, b_a, b_cw, b_cb, b_db, b_sk, b_g1, b_g2, b_out, b_q, b_k, b_v, b_o, sems) = rest
    copies = [
        pltpu.make_async_copy(src, dst, sems.at[i])
        for i, (src, dst) in enumerate(
            zip((in_proj, x_proj, dt_proj, a_log, conv_w, conv_b, dt_bias, d_skip, gain_one, gain_two, out_proj, w_q,
                 w_k, w_v, w_o),
                (b_in, b_x, b_dt, b_a, b_cw, b_cb, b_db, b_sk, b_g1, b_g2, b_out, b_q, b_k, b_v, b_o))
        )
    ]
    for copy in copies:
        copy.start()
    for copy in copies:
        copy.wait()
    one[:, :E] = b_in[:, :E].astype(BF16)
    two[:16, 3 * D :] = b_in[:, E : E + D].astype(BF16)
    two[16:, 3 * D :] = b_in[:, E + D :].astype(BF16)
    two[:, :D] = b_out[...].astype(BF16)
    two[:16, D : 2 * D] = b_q[...].astype(BF16)
    two[:16, 2 * D : 3 * D] = b_k[...].astype(BF16)
    two[16:, D : 2 * D] = b_v[...].astype(BF16)
    two[16:, 2 * D : 3 * D] = b_o[...].astype(BF16)
    rows[...] = jnp.zeros_like(rows)
    rows[ROW_X : ROW_X + 64, :] = b_x[...].T
    rows[ROW_DT : ROW_DT + RANK, :] = b_dt[...]
    rows[ROW_A : ROW_A + NS, :] = b_a[...]
    rows[ROW_CW : ROW_CW + KW, :] = b_cw[...]
    rows[ROW_CB : ROW_CB + 1, :] = b_cb[...]
    rows[ROW_DB : ROW_DB + 1, :] = b_db[...]
    rows[ROW_SK : ROW_SK + 1, :] = b_sk[...]
    rows[ROW_G1 : ROW_G1 + 1, :16] = b_g1[...]
    rows[ROW_G2 : ROW_G2 + 1, :16] = b_g2[...]
    one[:, E:] = jnp.concatenate([rows[16 * q : 16 * q + 16, :] for q in range(8)], axis=1).astype(BF16)


def join_smalls(target, own, far, side):
    for q in range(8):
        rows = jnp.concatenate(
            [ref[16 * k : 16 * k + 16, E + 32 * q : E + 32 * q + 32].astype(F32) for ref in (own, far) for k in range(16)], axis=1)
        target[16 * q : 16 * q + 16, :] = in_order(rows, side, 256)


def gain_row(pm, row):
    return jnp.concatenate([pm[row : row + 1, 32 * s : 32 * s + 16] for s in range(BLOCKS)], axis=1)


def spread(target, source):
    count = source.shape[0]
    for s in range(LG):
        target[pl.ds(s, count, stride=LG), :] = source[:, s * 128 : (s + 1) * 128]


def gathered(source, count):
    return jnp.concatenate([source[pl.ds(s, count, stride=LG), :] for s in range(LG)], axis=1)


def broadcast_rows(target, proj, first):
    for n in range(NS):
        target[n] = jnp.broadcast_to(proj[:, first + n : first + n + 1], target.shape[1:])


def at8(ref, index):
    return ref[pl.ds(pl.multiple_of(index * 8, 8), 8), :]


def front_kernel(plan, tok, halo, own, far, normed, turned, u_out, conv_out, act_out, proj_out, sig_out, dt3, au3, a3,
                 state, pm, gains, bx, cx):
    side = plan.side()
    join_smalls(pm, own, far, side)
    gain = gain_row(pm, ROW_G1)
    gains[0:1, :] = gain
    gains[1:2, :] = gain_row(pm, ROW_G2)
    tokens = tok.shape[0]
    x = jnp.concatenate([halo[...].astype(F32), tok[...].astype(F32)], axis=0)
    r = lax.rsqrt(jnp.mean(x * x, axis=-1, keepdims=True) + EPS)
    low = x * r * gain
    normed[...] = low.astype(BF16)
    low = own_first(low, side, 128).astype(BF16)
    turned[...] = low
    u_out[...] = nn(low[:, : D // 2], own[:, :E]) + nn(low[:, D // 2 :], far[:, :E])
    conv = pm[ROW_CB : ROW_CB + 1, :]
    for k in range(KW):
        conv = conv + pm[ROW_CW + k : ROW_CW + k + 1, :] * u_out[HALO - 3 + k : HALO - 3 + k + tokens, :]
    conv_out[...] = conv
    act = (conv * sigmoid(conv)).astype(BF16)
    act_out[...] = act
    proj = nt(act, pm[ROW_X : ROW_X + 64, :].astype(BF16))
    proj_out[:, :64] = proj
    proj_out[:, 64:] = jnp.zeros((tokens, 64), F32)
    pre = nn(proj[:, :RANK].astype(BF16), pm[ROW_DT : ROW_DT + RANK, :].astype(BF16)) + pm[ROW_DB : ROW_DB + 1, :]
    sig_out[...] = sigmoid(pre)
    step = jnp.maximum(pre, 0.0) + jnp.log1p(jnp.exp(-jnp.abs(pre)))
    spread(dt3, step)
    spread(au3, act.astype(F32))
    spread(a3, -LOG2E * jnp.exp(pm[ROW_A : ROW_A + NS, :]))
    broadcast_rows(bx, proj, RANK)
    broadcast_rows(cx, proj, RANK + NS)
    decay = [a3[8 * n : 8 * n + 8, :] for n in range(NS)]

    def advance(t, carried):
        held, total = carried
        size = at8(dt3, t)
        drive = size * at8(au3, t)
        held = tuple(
            jnp.exp2(size * decay[n]) * held[n] + drive * bx[n, pl.ds(t, 1), :] for n in range(NS)
        )
        return held, total + size

    zero = jnp.zeros((8, 128), F32)
    held, total = lax.fori_loop(0, tokens, advance, ((zero,) * NS, zero), unroll=8)
    state[...] = jnp.concatenate([*held, total, zero], axis=0).astype(BF16)


def combine_kernel(plan, forward, states, a3, entry, states_f):
    states_f[...] = states[...].astype(F32)
    decay = [a3[8 * n : 8 * n + 8, :] for n in range(NS)]
    zero = jnp.zeros((8, 128), F32)

    def combine(i, held):
        base = (i if forward else plan.chunks - 1 - i) * 144
        total = states_f[pl.ds(pl.multiple_of(base + 128, 8), 8), :]
        return tuple(
            jnp.exp2(total * decay[n]) * held[n] + states_f[pl.ds(pl.multiple_of(base + 8 * n, 8), 8), :]
            for n in range(NS)
        )

    count = plan.chunk() if forward else plan.chunks - 1 - plan.chunk()
    held = lax.fori_loop(0, count, combine, (zero,) * NS)
    entry[...] = jnp.concatenate([*held, zero, zero], axis=0)


def merge_kernel(plan, step, forward, own, other, before, a3, *outs):
    later = ((plan.chunk() >> step) & 1) == (1 if forward else 0)
    mine, theirs = own[...].astype(F32), other[...].astype(F32)
    first, second = jnp.where(later, theirs, mine), jnp.where(later, mine, theirs)
    decay = a3[...]
    spread_total = lambda value: jnp.concatenate([value[128:136, :]] * NS, axis=0)
    entry = outs[0]
    for group in outs[1:]:
        joint = jnp.exp2(spread_total(second) * decay) * first[:128, :] + second[:128, :]
        group[:128, :] = joint.astype(BF16)
        group[128:, :] = (first[128:, :] + second[128:, :]).astype(BF16)
    held = before[...]
    inner = held[:128, :] + jnp.exp2(spread_total(held) * decay) * theirs[:128, :]
    entry[:128, :] = jnp.where(later, inner, held[:128, :])
    entry[128:, :] = jnp.where(later, held[128:, :] + theirs[128:, :], held[128:, :])


def exchange(plan, state, a3, forward, beside=lambda step, entry: []):
    if plan.fast:
        group, entry, firsts = state, jnp.zeros((144, 128), F32), []
        for step in range(3):
            other = send(group, CHUNK_MASKS[1 << step])
            entry, *more = run(
                functools.partial(merge_kernel, plan, step, forward), [group, other, entry, a3],
                [((144, 128), F32)] + [((144, 128), BF16)] * (step < 2), after=beside(step, entry if step else group))
            group = more[0] if more else None
            firsts.append(entry)
        return entry, firsts
    states = lax.all_gather(state, "ctx", axis=0, tiled=True)
    return run(
        functools.partial(combine_kernel, plan, forward), [states, a3], [((144, 128), F32)],
        [pltpu.VMEM((144 * plan.chunks, 128), F32)])[0], []


def mid_kernel(plan, tok, dt3, au3, a3, turned, pm, gains, cot, entry, bx, cx, own, far,
               pay, mamba, gated_out, middle_out, all_states, z_out, y3):
    tokens = tok.shape[0]
    side = plan.side()
    both = lambda left, half, first, cols: nn(left[:, : D // 2], rows_of(own, half, first, cols)) + nn(
        left[:, D // 2 :], rows_of(far, half, first, cols))
    decay = [a3[8 * n : 8 * n + 8, :] for n in range(NS)]
    held = tuple(entry[8 * n : 8 * n + 8, :] for n in range(NS))
    all_states[:128, :] = entry[:128, :]

    def advance(t, held):
        size = at8(dt3, t)
        drive = size * at8(au3, t)
        base = pl.multiple_of(t * 128 + 128, 128)
        held = tuple(
            jnp.exp2(size * decay[n]) * held[n] + drive * bx[n, pl.ds(t, 1), :] for n in range(NS)
        )
        for n in range(NS):
            all_states[pl.ds(base + 8 * n, 8), :] = held[n]
        y = held[0] * cx[0, pl.ds(t, 1), :]
        for n in range(1, NS):
            y = y + held[n] * cx[n, pl.ds(t, 1), :]
        y3[pl.ds(pl.multiple_of(t * 8, 8), 8), :] = y
        return held

    lax.fori_loop(0, tokens, advance, held, unroll=8)
    act = gathered(au3, tokens)
    y = gathered(y3, tokens) + pm[ROW_SK : ROW_SK + 1, :] * act
    mamba[...] = y
    low = turned[HALO:, :]
    z = jnp.concatenate([both(low, 0, 3 * D, D), both(low, 1, 3 * D, D)], axis=1)
    z_out[...] = z
    gated = y * (z * sigmoid(z))
    gated_out[...] = gated.astype(BF16)
    gated = own_first(gated, side, 256).astype(BF16)
    middle = tok[...].astype(F32) + nn(gated[:, : E // 2], own[:, :D]) + nn(gated[:, E // 2 :], far[:, :D])
    middle_out[...] = middle
    r = lax.rsqrt(jnp.mean(middle * middle, axis=-1, keepdims=True) + EPS)
    low = own_first(middle * r * gains[1:2, :], side, 128).astype(BF16)
    query_key, value = both(low, 0, D, 2 * D), both(low, 1, D, D)
    grad = jnp.concatenate([nt(cot[...], rows_of(ref, 1, 2 * D, D)) for ref in (own, far)], axis=1)
    quads = tuple(part.astype(BF16) for part in (query_key[:, :D], query_key[:, D:], value, in_order(grad, side, 128)))
    for h in range(HEADS):
        for i, part in enumerate(quads):
            pay[h * tokens : (h + 1) * tokens, i * HDIM : (i + 1) * HDIM] = part[:, h * HDIM : (h + 1) * HDIM]


def attention_kernel(pay, back, q_s, k_s, v_s, g_s, kt, vt, dk, dv):
    length = pay.shape[0]
    rows = math.gcd(length, 512)
    q_s[...] = pay[:, :HDIM]
    k_s[...] = pay[:, HDIM : 2 * HDIM]
    v_s[...] = pay[:, 2 * HDIM : 3 * HDIM]
    g_s[...] = pay[:, 3 * HDIM :]
    kt[...] = k_s[...].T
    vt[...] = v_s[...].T
    dk[...] = jnp.zeros_like(dk)
    dv[...] = jnp.zeros_like(dv)
    scale = HDIM**-0.5
    key_at = lax.broadcasted_iota(jnp.int32, (rows, rows), 0)
    query_at = lax.broadcasted_iota(jnp.int32, (rows, rows), 1)
    for i in range(length // rows):
        first, last = i * rows, (i + 1) * rows
        query = q_s[first:last, :]
        grad = g_s[first:last, :]
        scores = nt(k_s[:last, :], query) * scale
        diagonal = jnp.where(key_at <= query_at, scores[first:, :], -1e30)
        scores = diagonal if i == 0 else jnp.concatenate([scores[:first, :], diagonal], axis=0)
        expo = jnp.exp(scores - jnp.max(scores, axis=0, keepdims=True))
        soft = expo * (1.0 / jnp.sum(expo, axis=0, keepdims=True))
        soft_low = soft.astype(BF16)
        grad_p = nt(v_s[:last, :], grad)
        dot = jnp.sum(soft * grad_p, axis=0, keepdims=True)
        grad_s = (soft * (grad_p - dot)).astype(BF16)
        raw = nn(vt[:, :last], soft_low)
        grad_q = nn(kt[:, :last], grad_s) * scale
        back[first:last, :HDIM] = raw.T.astype(BF16)
        back[first:last, HDIM : 2 * HDIM] = grad_q.T.astype(BF16)
        dk[:last, :] += nn(grad_s, query)
        dv[:last, :] += nn(soft_low, grad)
    back[:, 2 * HDIM : 3 * HDIM] = (dk[...] * scale).astype(BF16)
    back[:, 3 * HDIM :] = dv[...].astype(BF16)


def turn_kernel(plan, got, middle, cot, gains, z_in, mamba, dt3, cx, a3, own, far, first,
                att, gq, gk, gv, grad_middle, mix, gz, gy3, state, gain_grad):
    tokens = middle.shape[0]
    for h in range(HEADS):
        for i, part in enumerate((att, gq, gk, gv)):
            part[:, h * HDIM : (h + 1) * HDIM] = got[h * tokens : (h + 1) * tokens, i * HDIM : (i + 1) * HDIM]
    side = plan.side()
    grad_n = in_order(jnp.concatenate(
        [nt(gq[...], rows_of(ref, 0, D, D)) + nt(gk[...], rows_of(ref, 0, 2 * D, D)) + nt(gv[...], rows_of(ref, 1, D, D))
         for ref in (own, far)], axis=1), side, 128)
    mid = middle[...]
    r = lax.rsqrt(jnp.mean(mid * mid, axis=-1, keepdims=True) + EPS)
    gain_grad[...] = jnp.sum(grad_n * mid * r, axis=0, keepdims=True)
    q = grad_n * gains[1:2, :]
    gm = cot[...].astype(F32) + r * q - mid * (r * r * r) * jnp.mean(q * mid, axis=-1, keepdims=True)
    grad_middle[...] = gm
    low = gm.astype(BF16)
    mix[...] = low
    grad_gated = in_order(jnp.concatenate([nt(low, ref[:, :D]) for ref in (own, far)], axis=1), side, 256)
    z = z_in[...]
    s = sigmoid(z)
    spread(gy3, grad_gated * (z * s))
    gz[...] = (grad_gated * mamba[...] * (s * (1.0 + z * (1.0 - s)))).astype(BF16)
    decay = [a3[8 * n : 8 * n + 8, :] for n in range(NS)]

    def retreat(i, carried):
        t = tokens - 1 - i
        size = at8(dt3, t)
        grad = at8(gy3, t)
        return tuple(
            jnp.exp2(size * decay[n]) * (carried[n] + grad * cx[n, pl.ds(t, 1), :]) for n in range(NS)
        )

    zero = jnp.zeros((8, 128), F32)
    carried = lax.fori_loop(0, tokens, retreat, (zero,) * NS, unroll=8)
    state[:128, :] = jnp.concatenate(carried, axis=0).astype(BF16)
    state[128:, :] = first[128:, :]


def pack_blocks(plan, outs, source, rows, height, row, first, col=0, cols=None):
    me = plan.me()
    cols = source.shape[1] if cols is None else cols
    for out, masks in zip(outs, plan.grad_masks):
        for k, mask in enumerate(masks):
            block = me ^ mask
            out[k * height + row : k * height + row + rows, first : first + cols] = source[
                pl.ds(pl.multiple_of(block * rows, 16), rows), col : col + cols
            ].astype(BF16)


def grad_c_kernel(gy3, all_states, grad_c):
    diagonal_sums(grad_c, 0, lambda rows: gy3[rows, :], all_states, 1)


def weights_kernel(plan, no, att, gq, gk, gv, mix, gated, middle, gains, cot, own, far, normed, gz, *refs):
    result, outs = refs[0], refs[1 : 1 + no]
    small, large, wide = refs[1 + no :]
    mid = middle[...]
    held = own_first(att[...], plan.side(), 128)
    result[...] = (
        mid + nn(held[:, : D // 2], rows_of(own, 1, 2 * D, D)) + nn(held[:, D // 2 :], rows_of(far, 1, 2 * D, D))
    ).astype(BF16)
    r = lax.rsqrt(jnp.mean(mid * mid, axis=-1, keepdims=True) + EPS)
    low = (mid * r * gains[1:2, :]).astype(BF16)
    large[...] = tn(gated[...], mix[...])
    pack_blocks(plan, outs, large, 32, 32, 0, 0)
    small[...] = tn(low, gq[...])
    pack_blocks(plan, outs, small, 16, 32, 0, D)
    small[...] = tn(low, gk[...])
    pack_blocks(plan, outs, small, 16, 32, 0, 2 * D)
    small[...] = tn(low, gv[...])
    pack_blocks(plan, outs, small, 16, 32, 16, D)
    small[...] = tn(att[...], cot[...])
    pack_blocks(plan, outs, small, 16, 32, 16, 2 * D)
    wide[...] = tn(normed[HALO:, :], gz[...])
    pack_blocks(plan, outs, wide, 16, 32, 0, 3 * D, 0, D)
    pack_blocks(plan, outs, wide, 16, 32, 16, 3 * D, D, D)


def diagonal_sums(out, col, channels, held, offset, span=16):
    row_t = lax.broadcasted_iota(jnp.int32, (span, span * NS), 0)
    col_t = lax.broadcasted_iota(jnp.int32, (span, span * NS), 1) // NS
    pick = (
        lax.broadcasted_iota(jnp.int32, (span * NS, NS), 0) % NS
        == lax.broadcasted_iota(jnp.int32, (span * NS, NS), 1)
    ).astype(BF16)
    for block in range(out.shape[0] // span):
        total = jnp.zeros((span, span * NS), F32)
        for s in range(LG):
            held_rows = held[pl.ds((block * span + offset) * 128 + s, span * NS, stride=LG), :].astype(BF16)
            total = total + nt(channels(pl.ds(block * span * 8 + s, span, stride=LG)).astype(BF16), held_rows)
        own = jnp.where(row_t == col_t, total, 0.0).astype(BF16)
        out[block * span : (block + 1) * span, col : col + NS] = nn(own, pick)


def back_kernel(plan, dt3, au3, gy3, a3, proj, pm, all_states, sig, act, conv_in, u_in, leaving, bx, cx, grad_c,
                small_grads, gu_out, grads, gs3, ga3, gal, skip3, low_rank, padded):
    tokens = dt3.shape[0] // LG
    decay = [a3[8 * n : 8 * n + 8, :] for n in range(NS)]
    zero = jnp.zeros((8, 128), F32)
    spread(skip3, pm[ROW_SK : ROW_SK + 1, :])
    skip = skip3[...]

    carried = tuple(leaving[8 * n : 8 * n + 8, :] for n in range(NS))
    gal[...] = jnp.zeros_like(gal)

    def retreat(i, state):
        carried, skipped = state
        t = tokens - 1 - i
        size, value, grad = at8(dt3, t), at8(au3, t), at8(gy3, t)
        base = pl.multiple_of(t * 128, 128)
        from_b = zero
        from_a = zero
        fresh = []
        for n in range(NS):
            g = carried[n] + grad * cx[n, pl.ds(t, 1), :]
            grads[pl.ds(base + 8 * n, 8), :] = g
            w = jnp.exp2(size * decay[n]) * g
            q = w * all_states[pl.ds(base + 8 * n, 8), :]
            from_a = from_a + decay[n] * q
            from_b = from_b + g * bx[n, pl.ds(t, 1), :]
            gal[8 * n : 8 * n + 8, :] += size * q
            fresh.append(w)
        at = pl.ds(pl.multiple_of(t * 8, 8), 8)
        gs3[at, :] = from_a * LN2 + from_b * value
        ga3[at, :] = from_b * size + skip * grad
        return tuple(fresh), skipped + grad * value

    _, skipped = lax.fori_loop(0, tokens, retreat, (carried, zero), unroll=8)

    diagonal_sums(low_rank, RANK, lambda rows: dt3[rows, :] * au3[rows, :], grads, 0)
    low_rank[:, RANK + NS : RANK + 2 * NS] = grad_c[:, :NS]

    grad_pre = gathered(gs3, tokens) * sig[...]
    grad_pre_low = grad_pre.astype(BF16)
    low_rank[:, :RANK] = nt(grad_pre_low, pm[ROW_DT : ROW_DT + RANK, :].astype(BF16))
    projected = low_rank[:, :64].astype(BF16)
    small_grads[ROW_X : ROW_X + 64, :] = tn(projected, act[...])
    small_grads[ROW_DT : ROW_DT + RANK, :] = tn(proj[:, :RANK].astype(BF16), grad_pre_low)
    true_a = -jnp.exp(pm[ROW_A : ROW_A + NS, :])
    small_grads[ROW_A : ROW_A + NS, :] = gathered(gal, NS) * true_a
    small_grads[ROW_DB : ROW_DB + 1, :] = jnp.sum(grad_pre, axis=0, keepdims=True)
    skip3[...] = skipped
    small_grads[ROW_SK : ROW_SK + 1, :] = gathered(skip3, 1)
    small_grads[ROW_G1:, :] = jnp.zeros((SMALL_ROWS - ROW_G1, E), F32)
    conv = conv_in[...]
    s = sigmoid(conv)
    grad_act = gathered(ga3, tokens) + nn(projected, pm[ROW_X : ROW_X + 64, :].astype(BF16))
    grad_conv = grad_act * (s * (1.0 + conv * (1.0 - s)))
    small_grads[ROW_CB : ROW_CB + 1, :] = jnp.sum(grad_conv, axis=0, keepdims=True)
    for k in range(KW):
        small_grads[ROW_CW + k : ROW_CW + k + 1, :] = jnp.sum(
            grad_conv * u_in[HALO - 3 + k : HALO - 3 + k + tokens, :], axis=0, keepdims=True
        )
    padded[:HALO, :] = jnp.zeros((HALO, E), F32)
    padded[HALO : HALO + tokens, :] = grad_conv
    padded[HALO + tokens :, :] = jnp.zeros((HALO, E), F32)
    gu = jnp.zeros((HALO + tokens, E), F32)
    for k in range(KW):
        gu = gu + pm[ROW_CW + k : ROW_CW + k + 1, :] * padded[3 - k : 3 - k + HALO + tokens, :]
    gu_out[...] = gu.astype(BF16)


def last_kernel(plan, no, tok, halo, gains, gu, gz, grad_middle, own_u, far_u, own_z, far_z, normed, small_grads, gain_two, result, *refs):
    outs = refs[:no]
    both, before, large, spaced = refs[no:]
    tokens = tok.shape[0]
    both[tokens:, :] = result[...]
    me = plan.me()
    large[...] = tn(normed[...], gu[...])
    pack_blocks(plan, outs, large, 16, 16, 0, 0)
    x = jnp.concatenate([halo[...].astype(F32), tok[...].astype(F32)], axis=0)
    r = lax.rsqrt(jnp.mean(x * x, axis=-1, keepdims=True) + EPS)
    from_z = jnp.concatenate(
        [nt(gz[:, :D], rows_of(ref, 0, 3 * D, D)) + nt(gz[:, D:], rows_of(ref, 1, 3 * D, D)) for ref in (own_z, far_z)], axis=1)
    from_u = jnp.concatenate([nt(gu[...], ref[:, :E]) for ref in (own_u, far_u)], axis=1)
    grad_n = in_order(from_u + jnp.concatenate([jnp.zeros((HALO, D), F32), from_z], axis=0), plan.side(), 128)
    gain_one = jnp.sum(grad_n * x * r, axis=0, keepdims=True)
    q = grad_n * gains[0:1, :]
    base = r * q - x * (r * r * r) * jnp.mean(q * x, axis=-1, keepdims=True)
    both[:tokens, :] = (grad_middle[...] + base[HALO:, :]).astype(BF16)
    before[...] = base[:HALO, :].astype(BF16)
    spaced[...] = small_grads[...]
    blank = jnp.zeros((1, 16), F32)
    for row, grad in ((ROW_G1, gain_one), (ROW_G2, gain_two[...])):
        spaced[row : row + 1, :] = jnp.concatenate(
            [part for s in range(BLOCKS) for part in (grad[:, 16 * s : 16 * s + 16], blank)], axis=1)
    spaced[...] = swap_blocks(spaced[...], me)
    for out, masks in zip(outs, plan.grad_masks):
        for k, m in enumerate(masks):
            out[16 * k : 16 * k + 16, E:] = jnp.concatenate(
                [spaced[16 * q : 16 * q + 16, 32 * m : 32 * m + 32] for q in range(8)], axis=1).astype(BF16)


def total_of(ins):
    total = ins[0][...].astype(F32)
    for other in ins[1:]:
        total = total + other[...].astype(F32)
    return total


def finish_kernel(*refs):
    (both, tail), refs = refs[:2], refs[2:]
    u_ins, ins, (own_out, result_out), refs = refs[:4], refs[4:6], refs[6:8], refs[2:]
    count = own_out.shape[0]
    rows = count - HALO
    own_out[:rows, :] = both[:rows, :]
    own_out[rows:, :] = (both[rows:count, :].astype(F32) + tail[...].astype(F32)).astype(BF16)
    result_out[...] = both[count:, :]
    out_g, q_g, k_g, v_g, o_g, in_g, x_g, dt_g, a_g, cw_g, cb_g, db_g, sk_g, g1_g, g2_g, rows = refs[6:]
    total = total_of(ins)
    out_g[...] = total[:, :D]
    q_g[...] = total[:16, D : 2 * D]
    k_g[...] = total[:16, 2 * D : 3 * D]
    v_g[...] = total[16:, D : 2 * D]
    o_g[...] = total[16:, 2 * D : 3 * D]
    in_g[:, E : E + D] = total[:16, 3 * D :]
    in_g[:, E + D :] = total[16:, 3 * D :]
    total = total_of(u_ins)
    in_g[:, :E] = total[:, :E]
    for q in range(8):
        rows[16 * q : 16 * q + 16, :] = total[:, E + 32 * q : E + 32 * q + 32]
    x_g[...] = rows[ROW_X : ROW_X + 64, :].T
    dt_g[...] = rows[ROW_DT : ROW_DT + RANK, :]
    a_g[...] = rows[ROW_A : ROW_A + NS, :]
    cw_g[...] = rows[ROW_CW : ROW_CW + KW, :]
    cb_g[...] = rows[ROW_CB : ROW_CB + 1, :]
    db_g[...] = rows[ROW_DB : ROW_DB + 1, :]
    sk_g[...] = rows[ROW_SK : ROW_SK + 1, :]
    g1_g[...] = rows[ROW_G1 : ROW_G1 + 1, :16]
    g2_g[...] = rows[ROW_G2 : ROW_G2 + 1, :16]


def join_kernel(plan, counts, placed, *refs):
    ins, outs = refs[: sum(counts)], refs[sum(counts) :]
    at = 0
    for i, count in enumerate(counts):
        rows = outs[i].shape[0] // count
        for k in range(count):
            part = ins[at + k]
            if not placed[i]:
                outs[i][k * rows : (k + 1) * rows, :] = part[...]
                continue
            height = rows // len(Z_MASKS)
            for j, zz in enumerate(Z_MASKS):
                owner = plan.me() ^ (XY_MASKS[k] | zz)
                to = (((owner >> 4) & 1) * 8 + (owner & 7)) * height
                outs[i][pl.ds(pl.multiple_of(to, 16), height), :] = part[j * height : (j + 1) * height, :]
        at += count


def join(plan, groups, after=(), placed=()):
    counts = [len(group) for group in groups]
    outs = [((group[0].shape[0] * len(group), group[0].shape[1]), group[0].dtype) for group in groups]
    return run(
        functools.partial(join_kernel, plan, counts, [i in placed for i in range(len(groups))]),
        [part for group in groups for part in group], outs, after=after, us=1)


def spread_out(value, stage):
    return [value] + [send(value, mask) for mask in stage[1:]]


def cut_one_kernel(keep, got, a_keep, a_give, b_keep, b_give):
    half, quarter, cols = keep.shape[0] // 2, keep.shape[0] // 4, keep.shape[1] // 2
    add = lambda rows, lanes: (keep[rows, lanes].astype(F32) + got[rows, lanes].astype(F32)).astype(BF16)
    left, right = slice(0, cols), slice(cols, 2 * cols)
    a_keep[...] = add(slice(0, half), left)
    a_give[...] = add(slice(half, 2 * half), left)
    for i in range(2):
        b_keep[i * quarter : (i + 1) * quarter, :] = add(slice(2 * i * quarter, (2 * i + 1) * quarter), right)
        b_give[i * quarter : (i + 1) * quarter, :] = add(slice((2 * i + 1) * quarter, (2 * i + 2) * quarter), right)


def cut_two_kernel(a_own, a_got, b_own, b_got, a_keep, a_give, b_keep, b_give):
    rows = a_own.shape[0] // 2
    for own, got, keep, give in ((a_own, a_got, a_keep, a_give), (b_own, b_got, b_keep, b_give)):
        for out, part in ((keep, slice(0, rows)), (give, slice(rows, 2 * rows))):
            out[...] = (own[part, :].astype(F32) + got[part, :].astype(F32)).astype(BF16)


def add_rows(out, rows, ins, cols=slice(None), to=slice(None)):
    total = ins[0][rows, cols].astype(F32)
    for other in ins[1:]:
        total = total + other[rows, cols].astype(F32)
    out[:, to] = total.astype(out.dtype)


def cut_three_kernel(u_own, u_got, a_own, a_got, b_own, b_got, u_0, u_1, u_2, u_3, keep, give):
    rows = u_0.shape[0]
    for i, out in enumerate((u_0, u_1, u_2, u_3)):
        add_rows(out, slice(i * rows, (i + 1) * rows), (u_own, u_got))
    rows, cols = keep.shape[0], a_own.shape[1]
    for i, out in enumerate((keep, give)):
        part = slice(i * rows, (i + 1) * rows)
        add_rows(out, part, (a_own, a_got), to=slice(0, cols))
        add_rows(out, part, (b_own, b_got), to=slice(cols, 2 * cols))


def cut_four_kernel(u_own, u_a, u_b, u_c, own, got, u_0, u_1, u_2, u_3, keep, give):
    rows = u_0.shape[0]
    for i, out in enumerate((u_0, u_1, u_2, u_3)):
        add_rows(out, slice(i * rows, (i + 1) * rows), (u_own, u_a, u_b, u_c))
    rows = keep.shape[0]
    for i, out in enumerate((keep, give)):
        add_rows(out, slice(i * rows, (i + 1) * rows), (own, got))


def body(plan, *args):
    (tokens, mixer_gain, in_proj, conv_weight, conv_bias, x_proj, dt_proj, dt_bias, a_log, d_skip, out_proj,
     attn_gain, w_query, w_key, w_value, w_output, cotangent) = args
    count = tokens.shape[1]
    tok0, cot0 = tokens.reshape(count, D), cotangent.reshape(count, D)
    chunks = plan.chunks
    devices = plan.dp * plan.ctx
    share, width = E // devices, D // devices
    if plan.fast:
        home = [(s * 8 + c, plan.place(s, c)) for s in range(4) for c in range(8)]
        halo = lax.ppermute(
            tok0[count - HALO :], ALL, [(s * 8 + c, plan.place(s, c + 1)) for s in range(4) for c in range(7)]
        )
        raw = [in_proj, x_proj, dt_proj, a_log.T, conv_weight.T, conv_bias[None], dt_bias[None], d_skip[None],
               mixer_gain[None], attn_gain[None], out_proj, w_query, w_key, w_value, w_output]
        pack_one, pack_two = run(
            pack_kernel, [], [((16, E + 256), BF16), ((32, 4 * D), BF16)],
            [pltpu.VMEM((SMALL_ROWS, 32), F32)] + [pltpu.VMEM(value.shape, F32) for value in raw]
            + [pltpu.SemaphoreType.DMA((len(raw),))], far=raw, limit=60)
        one, tok = join(plan, [spread_out(pack_one, Z_MASKS), [tok0]])
        tok = lax.ppermute(tok, ALL, home)
        near_one = spread_out(one, XY_MASKS)
        (two,) = join(plan, [[pack_two, send(pack_two, 4)]], [one, halo])
        cot = lax.ppermute(cot0, ALL, home)
        one, two = join(plan, [near_one, [two, send(two, 2)]], [tok], (0,))
        one = [one, send(one, CORE)]
        near_two = spread_out(two, XY_MASKS)
    else:
        tok, cot = tok0, cot0
        halo = lax.ppermute(tok0[count - HALO :], "ctx", [(c, c + 1) for c in range(chunks - 1)])
        smalls = jnp.concatenate(
            [x_proj.T, dt_proj, a_log.T, conv_weight.T, conv_bias[None], dt_bias[None], d_skip[None],
             jnp.pad(mixer_gain, (0, share - width))[None], jnp.pad(attn_gain, (0, share - width))[None],
             jnp.zeros((SMALL_ROWS - ROW_G2 - 1, share), F32)], axis=0).astype(BF16)
        small_all = lax.all_gather(smalls, ALL, axis=1, tiled=True)
        apart = lambda row: jnp.pad(
            small_all[row].reshape(devices, share)[:, :width].reshape(BLOCKS, 16), ((0, 0), (0, 16))).reshape(1, E)
        small_all = jnp.concatenate(
            [small_all[:ROW_G1], apart(ROW_G1), apart(ROW_G2), small_all[ROW_G2 + 1 :]], axis=0)
        small_all = small_all.reshape(8, 16, BLOCKS, 32).transpose(2, 1, 0, 3).reshape(BLOCKS * 16, 256)
        whole = lambda value: lax.all_gather(value.astype(BF16), ALL, axis=0, tiled=True)
        in_all = whole(in_proj)
        halves = lambda value: [value.reshape(2, 2, -1, value.shape[1])[:, i].reshape(-1, value.shape[1]) for i in range(2)]
        one = halves(jnp.concatenate([in_all[:, :E], small_all], axis=1))
        out_all, q_all, k_all, v_all, o_all = (whole(w) for w in (out_proj, w_query, w_key, w_value, w_output))
        cut = lambda value: value.reshape(BLOCKS, 16, D)
        side = jnp.concatenate(
            [jnp.concatenate([cut(q_all), cut(k_all)], axis=2), jnp.concatenate([cut(v_all), cut(o_all)], axis=2)], axis=1)
        gate = jnp.concatenate([cut(in_all[:, E : E + D]), cut(in_all[:, E + D :])], axis=1)
        two = halves(jnp.concatenate([out_all.reshape(BLOCKS, 32, D), side, gate], axis=2).reshape(BLOCKS * 32, 4 * D))

    no = len(plan.grad_masks)
    rows3 = count * LG
    (normed, turned, u_pre, conv, act, proj, sig, dt3, au3, a3, state, pm, gains, bx, cx) = run(
        functools.partial(front_kernel, plan),
        [tok, halo, *one],
        [((HALO + count, D), BF16), ((HALO + count, D), BF16), ((HALO + count, E), F32), ((count, E), F32),
         ((count, E), BF16), ((count, 128), F32), ((count, E), F32), ((rows3, 128), F32), ((rows3, 128), F32),
         ((128, 128), F32), ((144, 128), BF16), ((SMALL_ROWS, E), F32), ((8, D), F32),
         ((NS, count, 128), F32), ((NS, count, 128), F32)], us=6,
    )
    entry, firsts = exchange(plan, state, a3, True)
    if plan.fast:
        (held,) = join(plan, [near_two], [*firsts[1:2], cot], (0,))
        two = [held, send(held, CORE)]
    pay, mamba, gated, middle, all_states, z = run(
        functools.partial(mid_kernel, plan),
        [tok, dt3, au3, a3, turned, pm, gains, cot, entry, bx, cx, *two],
        [((HEADS * count, 4 * HDIM), BF16), ((count, E), F32), ((count, E), BF16), ((count, D), F32),
         (((count + 1) * 128, 128), F32), ((count, E), F32)],
        [pltpu.VMEM((rows3, 128), F32)], us=6,
    )
    got = attend(plan, pay, count)
    (att, gq, gk, gv, grad_middle, mix, gz, gy3, later, gain_grad_two) = run(
        functools.partial(turn_kernel, plan),
        [got, middle, cot, gains, z, mamba, dt3, cx, a3, *two, state],
        [((count, D), BF16)] * 4 + [((count, D), F32), ((count, D), BF16), ((count, E), BF16), ((rows3, 128), F32),
                                    ((144, 128), BF16), ((1, D), F32)],
    )
    blocks = [len(masks_of) for masks_of in plan.grad_masks]

    def weight_grads(after):
        return run(
            functools.partial(weights_kernel, plan, no),
            [att, gq, gk, gv, mix, gated, middle, gains, cot, *two, normed, gz],
            [((count, D), BF16)] + [((n * 32, 4 * D), BF16) for n in blocks],
            [pltpu.VMEM((D, D), F32), pltpu.VMEM((E, D), F32), pltpu.VMEM((D, E), F32)], after=after)

    def c_grads(after):
        return run(grad_c_kernel, [gy3, all_states], [((count, 128), F32)], after=after)

    done, extra = [], []

    def beside(step, entry):
        if step == 1:
            done.extend(weight_grads([entry]))
            return done[:1]
        if step == 2:
            extra.extend(c_grads([entry]))
        return list(extra)

    leaving, _ = exchange(plan, later, a3, False, beside)
    result, *one_grads = done or weight_grads([])
    (grad_c,) = extra or c_grads([])
    one_parts = []
    if plan.fast:
        rows = blocks[0] * 32
        one_parts = run(
            cut_one_kernel, [one_grads[0], send(one_grads[1], CORE)], [((rows // 2, 2 * D), BF16)] * 4, after=[leaving])
    small_grads, gu = run(
        functools.partial(back_kernel, plan),
        [dt3, au3, gy3, a3, proj, pm, all_states, sig, act, conv, u_pre, leaving, bx, cx, grad_c],
        [((SMALL_ROWS, E), F32), ((HALO + count, E), BF16)],
        [pltpu.VMEM((count * 128, 128), F32), pltpu.VMEM((rows3, 128), F32), pltpu.VMEM((rows3, 128), F32),
         pltpu.VMEM((128, 128), F32), pltpu.VMEM((8, 128), F32), pltpu.VMEM((count, 128), F32),
         pltpu.VMEM((count + 2 * HALO, E), F32)],
        limit=32, after=one_parts[:1], us=11,
    )
    *two_grads, both, before = run(
        functools.partial(last_kernel, plan, no),
        [tok, halo, gains, gu, gz, grad_middle, *one, *two, normed, small_grads, gain_grad_two, result],
        [((n * 16, E + 256), BF16) for n in blocks] + [((2 * count, D), BF16), ((HALO, D), BF16)],
        [pltpu.VMEM((D, E), F32), pltpu.VMEM((SMALL_ROWS, E), F32)],     )
    if plan.fast:
        a_keep, a_give, b_keep, b_give = one_parts
        one_parts = run(
            cut_two_kernel, [a_keep, send(a_give, 16), b_keep, send(b_give, 1)], [((rows // 4, 2 * D), BF16)] * 4,
            after=[two_grads[0]])
    if plan.fast:
        back = [(b, a) for a, b in home]
        both = lax.ppermute(both, ALL, back)
        tail = lax.ppermute(
            before, ALL, [(plan.place(s, c + 1), s * 8 + c) for s in range(4) for c in range(7)])
        a_keep, a_give, b_keep, b_give = one_parts
        sends = lambda parts, stage: [parts[0]] + [send(part, mask) for part, mask in zip(parts[1:], stage[1:])]
        n = blocks[0]
        *u_parts, keep, give = run(
            cut_three_kernel,
            [two_grads[0], send(two_grads[1], CORE), a_keep, send(a_give, 1), b_keep, send(b_give, 16)],
            [((n * 4, E + 256), BF16)] * 4 + [((n * 4, 4 * D), BF16)] * 2, after=[tail])
        *u_parts, keep, give = run(
            cut_four_kernel, [*sends(u_parts, XY_MASKS), keep, send(give, 2)],
            [((n, E + 256), BF16)] * 4 + [((n * 2, 4 * D), BF16)] * 2, after=[both])
        grad_tok, result, out_g, q_g, k_g, v_g, o_g, in_g, x_g, dt_g, a_g, cw_g, cb_g, db_g, sk_g, g1_g, g2_g = run(
            finish_kernel, [both, tail, *sends(u_parts, Z_MASKS), keep, send(give, 4)],
            [((count, D), BF16)] * 2 + [((32, D), F32)] + [((16, D), F32)] * 4
            + [((16, 2 * E), F32), ((32, 64), F32), ((32, 32), F32), ((NS, 32), F32), ((KW, 32), F32)]
            + [((1, 32), F32)] * 3 + [((1, 16), F32)] * 2,
            [pltpu.VMEM((SMALL_ROWS, 32), F32)], final=True)
        a_g, cw_g = a_g.T, cw_g.T
        vectors = [value[0] for value in (cb_g, db_g, sk_g, g1_g, g2_g)]
    else:
        tail = lax.ppermute(before, "ctx", [(c + 1, c) for c in range(chunks - 1)])
        own, result = both[:count], both[count:]
        end = (own[count - HALO :].astype(F32) + tail.astype(F32)).astype(BF16)
        grad_tok = jnp.concatenate([own[: count - HALO], end], axis=0)
        scatter = lambda value, dim=0: lax.psum_scatter(value.astype(F32), ALL, scatter_dimension=dim, tiled=True)
        blocks_one = one_grads[0].reshape(BLOCKS, 32, 4 * D)
        part = lambda row, rows, col: scatter(blocks_one[:, row : row + rows, col * D : (col + 1) * D].reshape(-1, D))
        out_g, q_g, k_g, v_g, o_g = part(0, 32, 0), part(0, 16, 1), part(0, 16, 2), part(16, 16, 1), part(16, 16, 2)
        in_g = jnp.concatenate([scatter(two_grads[0][:, :E]), part(0, 16, 3), part(16, 16, 3)], axis=1)
        small = two_grads[0][:, E:].reshape(BLOCKS, 16, 8, 32).transpose(2, 1, 0, 3).reshape(SMALL_ROWS, E)
        close = lambda row: scatter(small[row].reshape(BLOCKS, 32)[:, :16].reshape(D))
        g1, g2 = close(ROW_G1), close(ROW_G2)
        mine = scatter(small, 1)
        x_g, dt_g, a_g, cw_g = (
            mine[ROW_X : ROW_X + 64].T, mine[ROW_DT : ROW_DT + RANK], mine[ROW_A : ROW_A + NS].T, mine[ROW_CW : ROW_CW + KW].T)
        vectors = [mine[ROW_CB], mine[ROW_DB], mine[ROW_SK], g1, g2]
    cb_v, db_v, sk_v, g1_v, g2_v = vectors
    return (
        result[None], grad_tok[None], g1_v, in_g, cw_g, cb_v, x_g, dt_g, db_v, a_g, sk_v, out_g, g2_v, q_g, k_g, v_g, o_g,
    )


def attend(plan, pay, count):
    if plan.chunks == HEADS:
        held = plan.swap(pay)
        length = held.shape[0]
        half = pltpu.VMEM((length, HDIM), BF16)
        flat = pltpu.VMEM((HDIM, length), BF16)
        wide = pltpu.VMEM((length, HDIM), F32)
        (back,) = run(
            attention_kernel, [held], [((length, 4 * HDIM), BF16)], [half] * 4 + [flat] * 2 + [wide] * 2, us=4
        )
        return plan.swap(back)
    parts = pay.reshape(HEADS, count, 4, HDIM)
    query, key, value, grad = (parts[:, :, i] for i in range(4))
    key, value = (lax.all_gather(part, "ctx", axis=1, tiled=True) for part in (key, value))
    query_at = lax.axis_index("ctx") * count + jnp.arange(count)
    allowed = jnp.arange(key.shape[1])[None, :] <= query_at[:, None]
    scale = HDIM**-0.5
    dots = functools.partial(jnp.einsum, preferred_element_type=F32)
    scores = jnp.where(allowed, dots("hqd,hkd->hqk", query, key) * scale, -1e30)
    soft = jax.nn.softmax(scores, axis=-1)
    soft_low = soft.astype(BF16)
    grad_p = dots("hqd,hkd->hqk", grad, value)
    grad_s = (soft * (grad_p - jnp.sum(soft * grad_p, axis=-1, keepdims=True))).astype(BF16)
    raw = dots("hqk,hkd->hqd", soft_low, value).astype(BF16)
    grad_q = (dots("hqk,hkd->hqd", grad_s, key) * scale).astype(BF16)
    grads = (dots("hqk,hqd->hkd", grad_s, query) * scale, dots("hqk,hqd->hkd", soft_low, grad))
    grad_k, grad_v = (
        lax.psum_scatter(part.astype(BF16), "ctx", scatter_dimension=1, tiled=True) for part in grads
    )
    return jnp.concatenate([raw, grad_q, grad_k, grad_v], axis=-1).reshape(HEADS * count, 4 * HDIM)


def solution(mesh):
    plan = Plan(mesh)
    split, rows, cols = P(ALL), P(ALL, None), P(None, ALL)
    acts = P("dp", "ctx", None)
    return jax.shard_map(
        functools.partial(body, plan),
        mesh=mesh,
        in_specs=(acts, split, rows, rows, split, rows, cols, split, rows, split, rows, split, rows, rows, rows, rows, acts),
        out_specs=(acts, acts, split, rows, rows, split, rows, cols, split, rows, split, rows, split, rows, rows, rows, rows),
        check_vma=False,
    )
```
